32 devices in a mesh: groups: 2 (over y), dp: 8 (over z, x), tensor: 2 (over core).
Axes of the slice: x: 2, y: 2, z: 4, core: 2. Of those that a mesh axis runs over, the one named last changes fastest.
Arguments:
- inputs: bfloat16 [2048, 4096], P(('groups', 'dp', 'tensor')), parts along dimension 0, may hold values from -6 to 6
- output_gradient: bfloat16 [2048, 512], P(('groups', 'dp')), parts along dimension 0, may hold values from -6 to 6
- frozen_weight: bfloat16 [4096, 512], P('tensor'), may hold values from -0.25 to 0.25
- down_maps: bfloat16 [8192, 128], P(('groups', 'dp')), parts along dimension 0, may hold values from -0.09375 to 0.09375
- up_maps: bfloat16 [256, 512], P(('groups', 'dp')), parts along dimension 0, may hold values from -0.25 to 0.25
- segment_start: int32 [16, 2], P('groups'), parts along dimension 0, may hold values from 0 to 96, as said below
- segment_adapter: int32 [16, 2], P('groups'), parts along dimension 0, may hold values from 0 to 7
- adapter_slot: int32 [16], P('groups'), parts along dimension 0, may hold values from 0 to 7, each once
- token_count: int32 [16], P('groups'), parts along dimension 0, may hold values from 64 to 128, as said below
Outputs:
- grad_x: bfloat16 [2048, 4096], P(('groups', 'dp'), 'tensor'), parts along dimension 0
- grad_a: float32 [8192, 128], P(('groups', 'dp')), parts along dimension 0
- up_map_gradient: float32 [256, 512], P(('groups', 'dp'), 'tensor'), parts along dimension 0
The draws below stay inside these ranges and needn't reach their ends.
There are 2 independent parts, one for each index of `groups`. The reference program is written for one: setup_inputs(seed, part) draws one part's arguments, and reference() takes and returns one part's arrays. A program takes and returns all parts, laid end to end along the dimension named above; an argument that names none is the same for every part. Nothing has to cross between parts.
Inputs may be any that keep to these rules, and one draw needn't show every extreme that they name: `segment_start`: column 0 is 0; the second start lies between 32 and 96, the latter on some rank. `token_count`: rows at or past a rank's count are padding; some rank is full.
All inputs are finite; a program needn't handle non-finite values.
Results may differ from the reference program's by a relative error of at most 0.0034.
Values may be sent and summed in bfloat16 or wider, within the bound.
No kernel may reach another device: no remote copies, remote signals or barrier semaphores. Data moves between devices by JAX's collectives and lax.ppermute only.
A program may use at most 64 MiB of HBM per device.

```python
import math
import jax
import jax.numpy as jnp
import numpy as np
from jax import lax

MODEL_WIDTH = 4096
VALUE_OUT_WIDTH = 512
ADAPTER_RANK = 16
TOK_DEV = 128
SEGS = 2
ADAPTER_TOTAL = 8
TOKENS = 1024
N_DP = 8


def draw_segment_start(key, part):
    key = jax.random.fold_in(key, 11)
    cut_key, top_key = jax.random.split(key)
    cut_points = jax.random.randint(cut_key, (N_DP,), TOK_DEV // 4, TOK_DEV - TOK_DEV // 4 + 1)
    widest = jax.random.randint(top_key, (), 0, N_DP)
    cut_points = cut_points.at[widest].set(TOK_DEV - TOK_DEV // 4)
    first_col = jnp.zeros((N_DP,), jnp.int32)
    return jnp.stack([first_col, cut_points.astype(jnp.int32)], axis=1).astype(jnp.int32)


def draw_token_count(key, part):
    key = jax.random.fold_in(key, 23)
    first_key, second_key = jax.random.split(key)
    rank_counts = jax.random.randint(first_key, (N_DP,), TOK_DEV // 2, TOK_DEV + 1)
    fullest = jax.random.randint(second_key, (), 0, N_DP)
    return rank_counts.at[fullest].set(TOK_DEV).astype(jnp.int32)


def place_ends(array, key, smallest, largest):
    shape = array.shape
    index_at = [jax.random.randint(jax.random.fold_in(key, axis), (), 0, shape[axis]) for axis in range(len(shape))]
    array = array.at[tuple(index_at)].set(smallest)
    longest = shape.index(max(shape))
    index_at[longest] = (index_at[longest] + 1) % shape[longest]
    return array.at[tuple(index_at)].set(largest)


def levels(stream_key, extent, cuts, least, top_value):
    def one(dim, parts):
        steps = jax.random.uniform(jax.random.fold_in(jax.random.fold_in(stream_key, 6), dim), (parts,), jnp.float32, least / len(cuts), top_value / len(cuts))
        return jnp.repeat(jnp.exp(steps), extent[dim] // parts).reshape((-1,) + (1,) * (len(extent) - dim - 1))

    factor_of = one(*cuts[0])
    for cut in cuts[1:]:
        factor_of = factor_of * one(*cut)
    return factor_of


def rank_bounds(number_of, lean):
    portions = [(1 << 20) // math.isqrt(grade ** lean) + 1 for grade in range(1, number_of + 1)]
    width = 1 + sum(portions) // (1 << 30)
    return np.cumsum(np.array([max(1, weight // width) for weight in portions]))


def ranked(own_key, shape, amount, skew):
    listing = rank_bounds(amount, skew)
    ticket = jax.random.randint(jax.random.fold_in(own_key, 1), shape, 0, int(listing[amount - 1]))
    rank = jnp.searchsorted(jnp.asarray(listing, jnp.int32), ticket, side="right")
    return jax.random.permutation(jax.random.fold_in(own_key, 2), amount)[rank].astype(jnp.int32)


def noise(rng, shape, deviation, most, cuts=(), held_as=jnp.bfloat16):
    values = jax.random.normal(rng, shape, jnp.float32) * deviation
    if len(cuts) > 0:
        values = levels(rng, shape, cuts, -0.22, 0.18) * values
    return jnp.clip(values, min=-most, max=most).astype(held_as)


def setup_inputs(seed: int = 0, part: int = 0) -> dict:
    keys = jax.random.split(jax.random.key(seed), 10)
    part_keys = jax.random.split(jax.random.fold_in(keys[9], part), 10)
    inputs = noise(part_keys[0], (TOKENS, MODEL_WIDTH), 1.0, 6.0, ((0, 16),))
    output_gradient = noise(part_keys[1], (TOKENS, VALUE_OUT_WIDTH), 1.0, 6.0, ((0, 8),))
    frozen_weight = noise(keys[2], (MODEL_WIDTH, VALUE_OUT_WIDTH), VALUE_OUT_WIDTH ** -0.5, 0.25, ((0, 2),))
    down_maps = noise(part_keys[3], (MODEL_WIDTH, ADAPTER_TOTAL * ADAPTER_RANK), MODEL_WIDTH ** -0.5, 0.09375, ((0, 8),))
    up_maps = noise(part_keys[4], (ADAPTER_TOTAL * ADAPTER_RANK, VALUE_OUT_WIDTH), VALUE_OUT_WIDTH ** -0.5, 0.25, ((0, 8),))
    segment_start = draw_segment_start(jax.random.fold_in(jax.random.fold_in(keys[9], part), 71), part)
    segment_adapter = place_ends(ranked(part_keys[6], (N_DP, SEGS), ADAPTER_TOTAL, 2), jax.random.fold_in(part_keys[6], 3), 0, ADAPTER_TOTAL - 1).astype(jnp.int32)
    adapter_slot = jax.random.permutation(part_keys[7], ADAPTER_TOTAL).astype(jnp.int32)
    token_count = draw_token_count(jax.random.fold_in(jax.random.fold_in(keys[9], part), 71), part)
    return {"inputs": inputs, "output_gradient": output_gradient, "frozen_weight": frozen_weight, "down_maps": down_maps, "up_maps": up_maps, "segment_start": segment_start, "segment_adapter": segment_adapter, "adapter_slot": adapter_slot, "token_count": token_count}


adapter_scale = 2.0


def token_slots(starts, chosen, table, live_count, tok_rows):
    position = jnp.arange(tok_rows, dtype=jnp.int32)
    segment = jnp.sum((starts[None, :] <= position[:, None]).astype(jnp.int32), axis=1) - 1
    seg_ids = jnp.arange(starts.shape[0], dtype=jnp.int32)
    adapter = jnp.sum(jnp.where(segment[:, None] == seg_ids[None, :], chosen[None, :], 0), axis=1)
    adapter_ids = jnp.arange(table.shape[0], dtype=jnp.int32)
    row_slot_index = jnp.sum(jnp.where(adapter[:, None] == adapter_ids[None, :], table[None, :], 0), axis=1)
    return row_slot_index.astype(jnp.int32), position < live_count


def reference(inputs, output_gradient, frozen_weight, down_maps, up_maps, segment_start, segment_adapter, adapter_slot, token_count):
    down_stack = down_maps.reshape(MODEL_WIDTH, ADAPTER_TOTAL, ADAPTER_RANK)
    up_stack = up_maps.reshape(ADAPTER_TOTAL, ADAPTER_RANK, VALUE_OUT_WIDTH)
    x_blocks = inputs.reshape(N_DP, TOK_DEV, MODEL_WIDTH)
    dy_blocks = output_gradient.reshape(N_DP, TOK_DEV, VALUE_OUT_WIDTH)

    def one_rank(carry, block_items):
        grad_a, up_map_gradient = carry
        x_rank, dy_rank, starts, chosen, live_count = block_items
        row_slot_index, live_mask = token_slots(starts, chosen, adapter_slot, live_count, TOK_DEV)
        grads_out = jnp.where(live_mask[:, None], dy_rank, jnp.zeros_like(dy_rank))
        a_rows = jnp.take(down_stack, row_slot_index, axis=1).astype(jnp.float32)
        up_rows = jnp.take(up_stack, row_slot_index, axis=0).astype(jnp.float32)
        x_wide = x_rank.astype(jnp.float32)
        gradient_wide = grads_out.astype(jnp.float32)
        low_rank_input = jnp.einsum("td,dtr->tr", x_wide, a_rows).astype(jnp.bfloat16)
        low_gradient = (adapter_scale * jnp.einsum("lk,lsk->ls", gradient_wide, up_rows)).astype(jnp.bfloat16)
        base_grad = jnp.dot(grads_out, frozen_weight.T, preferred_element_type=jnp.float32)
        adapter_grad = jnp.einsum("tr,dtr->td", low_gradient.astype(jnp.float32), a_rows)
        grad_x = (base_grad + adapter_grad).astype(jnp.bfloat16)
        grad_a = grad_a.at[:, row_slot_index, :].add(jnp.einsum("td,tr->dtr", x_wide, low_gradient.astype(jnp.float32)))
        up_map_gradient = up_map_gradient.at[row_slot_index].add(adapter_scale * jnp.einsum("sk,sb->skb", low_rank_input.astype(jnp.float32), gradient_wide))
        return (grad_a, up_map_gradient), grad_x

    init = (jnp.zeros((MODEL_WIDTH, ADAPTER_TOTAL, ADAPTER_RANK), jnp.float32), jnp.zeros((ADAPTER_TOTAL, ADAPTER_RANK, VALUE_OUT_WIDTH), jnp.float32))
    (grad_a, up_map_gradient), grad_x = lax.scan(one_rank, init, (x_blocks, dy_blocks, segment_start, segment_adapter, token_count))
    return grad_x.reshape(TOKENS, MODEL_WIDTH), grad_a.reshape(MODEL_WIDTH, ADAPTER_TOTAL * ADAPTER_RANK), up_map_gradient.reshape(ADAPTER_TOTAL * ADAPTER_RANK, VALUE_OUT_WIDTH)
```

```python
import jax
import jax.numpy as jnp
from jax import lax
from jax.sharding import PartitionSpec as P

ADAPTER_RANK = 16
adapter_scale = 2.0


def dot(a, b, ca, cb):
    return lax.dot_general(a, b, (((ca,), (cb,)), ((), ())), preferred_element_type=jnp.float32)


def local(
    inputs,
    output_gradient,
    frozen_weight,
    down_maps,
    up_maps,
    segment_start,
    segment_adapter,
    adapter_slot,
    token_count,
):
    bf16, f32, i32 = jnp.bfloat16, jnp.float32, jnp.int32
    tok_half = inputs.shape[0]
    tok_rows, out_width = output_gradient.shape
    column_total = down_maps.shape[0]
    adapter_list = adapter_slot.shape[0]
    segs = segment_start.shape[1]
    dp_size = lax.axis_size("dp")
    tp_size = lax.axis_size("tensor")
    my_rank = lax.axis_index("dp")
    core_idx = lax.axis_index("tensor")
    picked = segs * ADAPTER_RANK
    piece_out = out_width // tp_size
    half = frozen_weight.shape[0]

    x_other = lax.ppermute(inputs, "tensor", [(0, 1), (1, 0)])

    adapter_ids = jnp.arange(adapter_list, dtype=i32)
    slot_table = jnp.sum(
        jnp.where(segment_adapter[..., None] == adapter_ids, adapter_slot, 0), axis=-1
    )
    column = slot_table[:, :, None] * ADAPTER_RANK + jnp.arange(ADAPTER_RANK, dtype=i32)
    onehot = (
        column.reshape(-1)[:, None] == jnp.arange(adapter_list * ADAPTER_RANK, dtype=i32)
    ).astype(bf16)

    a_send = dot(onehot, down_maps, 1, 1).astype(bf16).reshape(dp_size, picked, column_total)
    b_send = jnp.broadcast_to(up_maps[None], (dp_size,) + up_maps.shape)
    if column_total == out_width:
        got = lax.all_to_all(jnp.concatenate([a_send, b_send], axis=1), "dp", 0, 0, tiled=True)
        a_got, b_got = got[:, :picked], got[:, picked:]
    else:
        a_got = lax.all_to_all(a_send, "dp", 0, 0, tiled=True)
        b_got = lax.all_to_all(b_send, "dp", 0, 0, tiled=True)

    position = jnp.arange(tok_rows, dtype=i32)
    starts = lax.dynamic_index_in_dim(segment_start, my_rank, 0, keepdims=False)
    live = position < lax.dynamic_index_in_dim(token_count, my_rank, 0, keepdims=False)
    my_seg = jnp.sum((starts[None, :] <= position[:, None]).astype(i32), axis=1) - 1
    in_seg = my_seg[:, None] == (jnp.arange(picked, dtype=i32) // ADAPTER_RANK)[None, :]
    my_onehot = lax.dynamic_slice_in_dim(onehot, my_rank * picked, picked, 0)
    g = jnp.where(live[:, None], output_gradient, jnp.zeros_like(output_gradient))
    base = dot(g, frozen_weight, 1, 1)

    b_sel = dot(my_onehot, b_got.reshape(-1, out_width), 1, 0).astype(bf16)
    dlow = (adapter_scale * dot(g, b_sel, 1, 1)).astype(bf16)
    dlow = jnp.where(in_seg, dlow, jnp.zeros_like(dlow))
    a_sel = jnp.moveaxis(a_got, 0, 1).reshape(picked, -1)
    first = core_idx == 0
    x = jnp.concatenate(
        [jnp.where(first, inputs, x_other), jnp.where(first, x_other, inputs)], axis=0
    )
    low = dot(x, a_sel, 1, 1).astype(bf16)
    low = jnp.where(in_seg, low, jnp.zeros_like(low))
    low_wide = dot(low, my_onehot, 1, 0).astype(bf16)

    ga_send = dot(dlow, x, 0, 0).astype(bf16).reshape(picked, dp_size, column_total)
    ga_send = jnp.moveaxis(ga_send, 1, 0)
    g_piece = lax.dynamic_slice_in_dim(g, core_idx * piece_out, piece_out, 1)
    up_send = (adapter_scale * dot(low_wide, g_piece, 0, 0)).astype(bf16)
    up_send = up_send.reshape(dp_size, -1, piece_out)
    if column_total % piece_out == 0:
        parts = column_total // piece_out
        folded = [ga_send[:, :, k * piece_out : (k + 1) * piece_out] for k in range(parts)]
        got = lax.all_to_all(jnp.concatenate(folded + [up_send], axis=1), "dp", 0, 0, tiled=True)
        ga_got = jnp.concatenate(
            [got[:, k * picked : (k + 1) * picked] for k in range(parts)], axis=2
        )
        up_got = got[:, parts * picked :]
    else:
        ga_got = lax.all_to_all(ga_send, "dp", 0, 0, tiled=True)
        up_got = lax.all_to_all(up_send, "dp", 0, 0, tiled=True)

    a_half = lax.dynamic_slice_in_dim(a_sel, core_idx * half, half, 1)
    grad_x = (base + dot(dlow, a_half, 1, 0)).astype(bf16)

    grad_a = dot(ga_got.reshape(dp_size * picked, column_total), onehot, 0, 0)
    up_map_gradient = jnp.sum(up_got.astype(f32), axis=0)
    return grad_x, grad_a, up_map_gradient


def solution(mesh):
    in_specs = (
        P(("groups", "dp", "tensor"), None),
        P(("groups", "dp"), None),
        P("tensor", None),
        P(("groups", "dp"), None),
        P(("groups", "dp"), None),
        P("groups", None),
        P("groups", None),
        P("groups"),
        P("groups"),
    )
    out_specs = (
        P(("groups", "dp"), "tensor"),
        P(("groups", "dp"), None),
        P(("groups", "dp"), "tensor"),
    )
    return jax.shard_map(local, mesh=mesh, in_specs=in_specs, out_specs=out_specs, check_vma=False)
```

```python
import functools

import jax
import jax.numpy as jnp
from jax import lax
from jax.experimental import pallas as pl
from jax.experimental.pallas import tpu as pltpu
from jax.sharding import PartitionSpec as P

ADAPTER_RANK = 16
adapter_scale = 2.0

bf16, f32, i32 = jnp.bfloat16, jnp.float32, jnp.int32

SMEM = pl.BlockSpec(memory_space=pltpu.SMEM)
VMEM = pl.BlockSpec(memory_space=pltpu.VMEM)


def dot(a, b, ca, cb):
    return lax.dot_general(a, b, (((ca,), (cb,)), ((), ())), preferred_element_type=f32)


def params(mib):
    return pltpu.CompilerParams(vmem_limit_bytes=mib << 20)


def slot_rows(chosen_ref, slot_ref, ranks, width):
    segs = chosen_ref.shape[1]
    lane = lax.broadcasted_iota(i32, (ADAPTER_RANK, width), 1)
    row = lax.broadcasted_iota(i32, (ADAPTER_RANK, width), 0)
    rows = []
    for rank in ranks:
        for k in range(segs):
            first = slot_ref[chosen_ref[rank, k]] * ADAPTER_RANK
            rows.append(jnp.where(lane == row + first, 1.0, 0.0))
    return jnp.concatenate(rows, axis=0).astype(bf16)


def others(me, n, sign):
    return [lax.rem(me + (sign * d) % n, n) for d in range(n)]


def pack_kernel(n, chosen_ref, slot_ref, down_ref, up_ref, *send):
    me = lax.axis_index("dp")
    onehot = slot_rows(chosen_ref, slot_ref, others(me, n, 1), down_ref.shape[1])
    picked = onehot.shape[0] // n
    columns = dot(onehot, down_ref[...], 1, 1).astype(bf16)
    for d in range(n):
        send[d][:picked, :] = columns[d * picked : (d + 1) * picked]
        send[d][picked:, :] = up_ref[...]


def middle_kernel(n, piece, start_ref, chosen_ref, slot_ref, count_ref, x_mine, x_other, g_ref, *refs):
    got, (dlow_ref, a_ref), send = refs[:n], refs[n : n + 2], refs[n + 2 : 2 * n + 2]
    x_ref, b_ref, up_ref = refs[2 * n + 2 :]
    me, core = lax.axis_index("dp"), lax.axis_index("tensor")
    segs = start_ref.shape[1]
    picked = segs * ADAPTER_RANK
    half, rows, width = x_mine.shape[0], g_ref.shape[0], got[0].shape[1]

    x_ref[pl.ds(pl.multiple_of(core * half, half), half), :] = x_mine[...]
    x_ref[pl.ds(pl.multiple_of((1 - core) * half, half), half), :] = x_other[...]
    sources = others(me, n, -1)
    for d in range(n):
        a_ref[sources[d]] = got[d][:picked, :]
        b_ref[sources[d]] = got[d][picked:, :]

    position = lax.broadcasted_iota(i32, (rows, picked), 0)
    group = lax.broadcasted_iota(i32, (rows, picked), 1) // ADAPTER_RANK
    segment = jnp.full((rows, picked), -1, i32)
    for k in range(segs):
        segment += jnp.where(position >= start_ref[me, k], 1, 0)
    in_seg = segment == group
    live = lax.broadcasted_iota(i32, g_ref.shape, 0) < count_ref[me]
    g = jnp.where(live, g_ref[...], jnp.zeros(g_ref.shape, bf16))

    b_sel = jnp.concatenate([b_ref[slot_ref[chosen_ref[me, k]]] for k in range(segs)], axis=0)
    dlow = jnp.where(in_seg, adapter_scale * dot(g, b_sel, 1, 1), 0.0).astype(bf16)
    dlow_ref[...] = dlow
    targets = others(me, n, 1)
    for d in range(n):
        at = pl.multiple_of(targets[d] * width, width)
        part = dot(dlow, x_ref[:, pl.ds(at, width)], 0, 0).astype(bf16)
        for k in range(width // piece):
            send[d][k * picked : (k + 1) * picked, :] = part[:, k * piece : (k + 1) * piece]

    low = jnp.zeros((rows, picked), f32)
    for q in range(n):
        low += dot(x_ref[:, q * width : (q + 1) * width], a_ref[q], 1, 1)
    low = jnp.where(in_seg, low, 0.0).astype(bf16)
    onehot = slot_rows(chosen_ref, slot_ref, [me], n * ADAPTER_RANK)
    low_wide = dot(low, onehot, 1, 0).astype(bf16)
    g_piece = g_ref[:, pl.ds(pl.multiple_of(core * piece, piece), piece)]
    g_piece = jnp.where(live[:, :piece], g_piece, jnp.zeros(g_piece.shape, bf16))
    up = (adapter_scale * dot(low_wide, g_piece, 0, 0)).astype(bf16)
    for s in range(n):
        up_ref[s] = up[s * ADAPTER_RANK : (s + 1) * ADAPTER_RANK]
    for d in range(n):
        send[d][width // piece * picked :, :] = up_ref[targets[d]]


def grad_x_kernel(count_ref, g_ref, w_ref, dlow_ref, a_ref, out_ref):
    me, core = lax.axis_index("dp"), lax.axis_index("tensor")
    live = lax.broadcasted_iota(i32, g_ref.shape, 0) < count_ref[me]
    g = jnp.where(live, g_ref[...], jnp.zeros(g_ref.shape, bf16))
    block = core * pl.num_programs(0) + pl.program_id(0)
    total = dot(g, w_ref[...], 1, 1) + dot(dlow_ref[...], a_ref[block], 1, 0)
    out_ref[...] = total.astype(bf16)


def final_kernel(n, chosen_ref, slot_ref, *refs):
    got, (a_ref, up_ref) = refs[:n], refs[n:]
    me = lax.axis_index("dp")
    onehot = slot_rows(chosen_ref, slot_ref, others(me, n, -1), a_ref.shape[1])
    picked = onehot.shape[0] // n
    piece = got[0].shape[1]
    parts = a_ref.shape[0] // piece
    for k in range(parts):
        rows = jnp.concatenate([r[k * picked : (k + 1) * picked, :] for r in got], axis=0)
        a_ref[k * piece : (k + 1) * piece, :] = dot(rows, onehot, 0, 0)
    up = got[0][parts * picked :, :].astype(f32)
    for r in got[1:]:
        up += r[parts * picked :, :].astype(f32)
    up_ref[...] = up


def exchange(messages):
    n = len(messages)
    return [messages[0]] + [
        lax.ppermute(messages[d], "dp", [(i, (i + d) % n) for i in range(n)]) for d in range(1, n)
    ]


def local_kernels(
    inputs,
    output_gradient,
    frozen_weight,
    down_maps,
    up_maps,
    segment_start,
    segment_adapter,
    adapter_slot,
    token_count,
):
    tok_half, model_width = inputs.shape
    tok_rows, out_width = output_gradient.shape
    column_total, slot_width = down_maps.shape
    half = frozen_weight.shape[0]
    n = lax.axis_size("dp")
    piece = out_width // lax.axis_size("tensor")
    picked = segment_start.shape[1] * ADAPTER_RANK
    shape = jax.ShapeDtypeStruct

    x_other = lax.ppermute(inputs, "tensor", [(0, 1), (1, 0)])

    sent = pl.pallas_call(
        functools.partial(pack_kernel, n),
        out_shape=[shape((picked + ADAPTER_RANK, column_total), bf16)] * n,
        in_specs=[SMEM, SMEM, VMEM, VMEM],
        out_specs=[VMEM] * n,
        compiler_params=params(8),
    )(segment_adapter, adapter_slot, down_maps, up_maps)
    got = exchange(sent)

    rows = column_total // piece * picked + ADAPTER_RANK
    dlow, a_all, *sent = pl.pallas_call(
        functools.partial(middle_kernel, n, piece),
        out_shape=[
            shape((tok_rows, picked), bf16),
            shape((n, picked, column_total), bf16),
        ]
        + [shape((rows, piece), bf16)] * n,
        in_specs=[SMEM] * 4 + [VMEM] * (3 + n),
        out_specs=[VMEM] * (2 + n),
        scratch_shapes=[
            pltpu.VMEM((tok_rows, model_width), bf16),
            pltpu.VMEM((n, ADAPTER_RANK, out_width), bf16),
            pltpu.VMEM((n, ADAPTER_RANK, piece), bf16),
        ],
        compiler_params=params(16),
    )(
        segment_start,
        segment_adapter,
        adapter_slot,
        token_count,
        inputs,
        x_other,
        output_gradient,
        *got,
    )
    got = exchange(sent)

    grad_x = pl.pallas_call(
        grad_x_kernel,
        out_shape=shape((tok_rows, half), bf16),
        grid=(half // column_total,),
        in_specs=[
            SMEM,
            pl.BlockSpec((tok_rows, out_width), lambda j: (0, 0)),
            pl.BlockSpec((column_total, out_width), lambda j: (j, 0)),
            pl.BlockSpec((tok_rows, picked), lambda j: (0, 0)),
            pl.BlockSpec((n, picked, column_total), lambda j: (0, 0, 0)),
        ],
        out_specs=pl.BlockSpec((tok_rows, column_total), lambda j: (0, j)),
        compiler_params=params(16),
        cost_estimate=pl.CostEstimate(
            flops=2 * tok_rows * half * (out_width + picked),
            bytes_accessed=2 * half * (out_width + tok_rows),
            transcendentals=0,
        ),
    )(token_count, output_gradient, frozen_weight, dlow, a_all)

    grad_a, up_map_gradient = pl.pallas_call(
        functools.partial(final_kernel, n),
        out_shape=[shape((column_total, slot_width), f32), shape((ADAPTER_RANK, piece), f32)],
        in_specs=[SMEM, SMEM] + [VMEM] * n,
        out_specs=[VMEM, VMEM],
        compiler_params=params(8),
    )(segment_adapter, adapter_slot, *got)
    return grad_x, grad_a, up_map_gradient


def local_plain(
    inputs,
    output_gradient,
    frozen_weight,
    down_maps,
    up_maps,
    segment_start,
    segment_adapter,
    adapter_slot,
    token_count,
):
    tok_rows, out_width = output_gradient.shape
    column_total = down_maps.shape[0]
    adapter_list = adapter_slot.shape[0]
    segs = segment_start.shape[1]
    dp_size = lax.axis_size("dp")
    my_rank = lax.axis_index("dp")
    core_idx = lax.axis_index("tensor")
    picked = segs * ADAPTER_RANK
    piece_out = out_width // lax.axis_size("tensor")
    half = frozen_weight.shape[0]

    x_other = lax.ppermute(inputs, "tensor", [(0, 1), (1, 0)])
    adapter_ids = jnp.arange(adapter_list, dtype=i32)
    slot_table = jnp.sum(
        jnp.where(segment_adapter[..., None] == adapter_ids, adapter_slot, 0), axis=-1
    )
    column = slot_table[:, :, None] * ADAPTER_RANK + jnp.arange(ADAPTER_RANK, dtype=i32)
    onehot = (
        column.reshape(-1)[:, None] == jnp.arange(adapter_list * ADAPTER_RANK, dtype=i32)
    ).astype(bf16)

    a_send = dot(onehot, down_maps, 1, 1).astype(bf16).reshape(dp_size, picked, column_total)
    b_send = jnp.broadcast_to(up_maps[None], (dp_size,) + up_maps.shape)
    a_got = lax.all_to_all(a_send, "dp", 0, 0, tiled=True)
    b_got = lax.all_to_all(b_send, "dp", 0, 0, tiled=True)

    position = jnp.arange(tok_rows, dtype=i32)
    starts = lax.dynamic_index_in_dim(segment_start, my_rank, 0, keepdims=False)
    live = position < lax.dynamic_index_in_dim(token_count, my_rank, 0, keepdims=False)
    my_seg = jnp.sum((starts[None, :] <= position[:, None]).astype(i32), axis=1) - 1
    in_seg = my_seg[:, None] == (jnp.arange(picked, dtype=i32) // ADAPTER_RANK)[None, :]
    my_onehot = lax.dynamic_slice_in_dim(onehot, my_rank * picked, picked, 0)
    g = jnp.where(live[:, None], output_gradient, jnp.zeros_like(output_gradient))
    base = dot(g, frozen_weight, 1, 1)

    b_sel = dot(my_onehot, b_got.reshape(-1, out_width), 1, 0).astype(bf16)
    dlow = (adapter_scale * dot(g, b_sel, 1, 1)).astype(bf16)
    dlow = jnp.where(in_seg, dlow, jnp.zeros_like(dlow))
    a_sel = jnp.moveaxis(a_got, 0, 1).reshape(picked, -1)
    first = core_idx == 0
    x = jnp.concatenate(
        [jnp.where(first, inputs, x_other), jnp.where(first, x_other, inputs)], axis=0
    )
    low = dot(x, a_sel, 1, 1).astype(bf16)
    low = jnp.where(in_seg, low, jnp.zeros_like(low))
    low_wide = dot(low, my_onehot, 1, 0).astype(bf16)

    ga_send = dot(dlow, x, 0, 0).astype(bf16).reshape(picked, dp_size, column_total)
    ga_got = lax.all_to_all(jnp.moveaxis(ga_send, 1, 0), "dp", 0, 0, tiled=True)
    g_piece = lax.dynamic_slice_in_dim(g, core_idx * piece_out, piece_out, 1)
    up_send = (adapter_scale * dot(low_wide, g_piece, 0, 0)).astype(bf16)
    up_got = lax.all_to_all(up_send.reshape(dp_size, -1, piece_out), "dp", 0, 0, tiled=True)

    a_half = lax.dynamic_slice_in_dim(a_sel, core_idx * half, half, 1)
    grad_x = (base + dot(dlow, a_half, 1, 0)).astype(bf16)
    grad_a = dot(ga_got.reshape(dp_size * picked, column_total), onehot, 0, 0)
    up_map_gradient = jnp.sum(up_got.astype(f32), axis=0)
    return grad_x, grad_a, up_map_gradient


def local(*args):
    down_maps, up_maps = args[3], args[4]
    n, tp = lax.axis_size("dp"), lax.axis_size("tensor")
    out_width = up_maps.shape[1]
    kernels_fit = (
        n <= 16
        and tp == 2
        and down_maps.shape[0] == out_width
        and down_maps.shape[1] == n * up_maps.shape[0]
        and out_width % (128 * tp) == 0
    )
    return (local_kernels if kernels_fit else local_plain)(*args)


def solution(mesh):
    in_specs = (
        P(("groups", "dp", "tensor"), None),
        P(("groups", "dp"), None),
        P("tensor", None),
        P(("groups", "dp"), None),
        P(("groups", "dp"), None),
        P("groups", None),
        P("groups", None),
        P("groups"),
        P("groups"),
    )
    out_specs = (
        P(("groups", "dp"), "tensor"),
        P(("groups", "dp"), None),
        P(("groups", "dp"), "tensor"),
    )
    return jax.shard_map(local, mesh=mesh, in_specs=in_specs, out_specs=out_specs, check_vma=False)
```

```python
import functools

import jax
import jax.numpy as jnp
from jax import lax
from jax.experimental import pallas as pl
from jax.experimental.pallas import tpu as pltpu
from jax.sharding import PartitionSpec as P

ADAPTER_RANK = 16
adapter_scale = 2.0

bf16, f32, i32 = jnp.bfloat16, jnp.float32, jnp.int32

HBM = pl.BlockSpec(memory_space=pltpu.HBM)
VMEM = pl.BlockSpec(memory_space=pltpu.VMEM)


def dot(a, b, ca, cb):
    return lax.dot_general(a, b, (((ca,), (cb,)), ((), ())), preferred_element_type=f32)


def params(mib):
    return pltpu.CompilerParams(vmem_limit_bytes=mib << 20)


def slot_rows(chosen_ref, slot_ref, ranks, width):
    lane = lax.broadcasted_iota(i32, (ADAPTER_RANK, width), 1)
    row = lax.broadcasted_iota(i32, (ADAPTER_RANK, width), 0)
    rows = []
    for rank in ranks:
        for k in range(chosen_ref.shape[0]):
            first = slot_ref[chosen_ref[k, rank]] * ADAPTER_RANK
            rows.append(jnp.where(lane == row + first, 1.0, 0.0))
    return jnp.concatenate(rows, axis=0).astype(bf16)


def fetch(sources, targets, sems):
    copies = [
        pltpu.make_async_copy(source, target, sems.at[k])
        for k, (source, target) in enumerate(zip(sources, targets))
    ]
    for copy in copies:
        copy.start()
    for copy in copies:
        copy.wait()


def pairs(n, core):
    return [n - 1 - 2 * j - core for j in range(n // 2 - 1)]


def partners(n, me, core):
    steps = [jnp.where(core == 0, a, b) for a, b in zip(pairs(n, 0), pairs(n, 1))]
    return [me] + [me ^ d for d in steps] + [me ^ 1]


def senders(n, me, core):
    return partners(n, me, core) + partners(n, me, 1 - core)[1:-1]


def pack_kernel(n, chosen_hbm, slot_hbm, down_hbm, up_hbm, *refs):
    count = n // 2 + 1
    send, (chosen_ref, slot_ref, down_ref, up_ref, sems) = refs[:count], refs[count:]
    fetch([chosen_hbm, slot_hbm, down_hbm, up_hbm], [chosen_ref, slot_ref, down_ref, up_ref], sems)
    ranks = partners(n, lax.axis_index("dp"), lax.axis_index("tensor"))
    onehot = slot_rows(chosen_ref, slot_ref, ranks, down_ref.shape[1])
    picked = onehot.shape[0] // count
    columns = dot(onehot, down_ref[...], 1, 1).astype(bf16)
    for k in range(count):
        send[k][:picked, :] = columns[k * picked : (k + 1) * picked]
        send[k][picked:, :] = up_ref[...]


def stage_kernel(
    n, start_hbm, chosen_hbm, slot_hbm, count_hbm, g_hbm, x_mine, x_other,
    x_ref, g_ref, seg_ref, own_ref, all_ref,
    start_ref, chosen_ref, slot_ref, count_ref, sems,
):
    me, core = lax.axis_index("dp"), lax.axis_index("tensor")
    half = x_mine.shape[0]
    rows, picked = seg_ref.shape
    mine = pl.ds(pl.multiple_of(core * half, half), half)
    other = pl.ds(pl.multiple_of((1 - core) * half, half), half)
    fetch(
        [start_hbm, chosen_hbm, slot_hbm, count_hbm, g_hbm, x_mine, x_other],
        [start_ref, chosen_ref, slot_ref, count_ref, g_ref, x_ref.at[mine], x_ref.at[other]],
        sems,
    )
    position = lax.broadcasted_iota(i32, (rows, picked), 0)
    group = lax.broadcasted_iota(i32, (rows, picked), 1) // ADAPTER_RANK
    segment = jnp.full((rows, picked), -1, i32)
    for k in range(start_ref.shape[0]):
        segment += jnp.where(position >= start_ref[k, me], 1, 0)
    seg_ref[...] = jnp.where(segment == group, 1.0, 0.0)
    live = lax.broadcasted_iota(i32, g_ref.shape, 0) < count_ref[me]
    g_ref[...] = jnp.where(live, g_ref[...], jnp.zeros(g_ref.shape, bf16))
    own_ref[...] = slot_rows(chosen_ref, slot_ref, [me], own_ref.shape[1])
    all_ref[...] = slot_rows(chosen_ref, slot_ref, range(n), all_ref.shape[1])


def middle_kernel(n, x_ref, g_ref, seg_ref, own_ref, *refs):
    got, (dlow_ref, a_ref), send = refs[:n], refs[n : n + 2], refs[n + 2 : n + 3 + n // 2]
    b_ref, up_ref = refs[n + 3 + n // 2 :]
    me, core = lax.axis_index("dp"), lax.axis_index("tensor")
    rows, picked = seg_ref.shape
    width = got[0].shape[1]
    for sender, message in zip(senders(n, me, core), got):
        a_ref[sender] = message[:picked, :]
        b_ref[sender] = message[picked:, :]

    in_seg = seg_ref[...] > 0.0
    b_sel = dot(own_ref[...], b_ref[...].reshape(-1, width), 1, 0).astype(bf16)
    dlow = jnp.where(in_seg, adapter_scale * dot(g_ref[...], b_sel, 1, 1), 0.0).astype(bf16)
    dlow_ref[...] = dlow
    targets = partners(n, me, core)
    for target, message in zip(targets, send):
        at = pl.ds(pl.multiple_of(target * width, width), width)
        message[:picked, :] = dot(dlow, x_ref[:, at], 0, 0).astype(bf16)

    low = jnp.zeros((rows, picked), f32)
    for q in range(n):
        low += dot(x_ref[:, q * width : (q + 1) * width], a_ref[q], 1, 1)
    low = jnp.where(in_seg, low, 0.0).astype(bf16)
    low_wide = dot(low, own_ref[...], 1, 0).astype(bf16)
    up = (adapter_scale * dot(low_wide, g_ref[...], 0, 0)).astype(bf16)
    up_ref[...] = up.reshape(up_ref.shape)
    for target, message in zip(targets, send):
        message[picked:, :] = up_ref[target]


def grad_x_kernel(g_ref, w_ref, dlow_ref, a_ref, out_ref):
    block = lax.axis_index("tensor") * pl.num_programs(0) + pl.program_id(0)
    total = dot(g_ref[...], w_ref[...], 1, 1) + dot(dlow_ref[...], a_ref[block], 1, 0)
    out_ref[...] = total.astype(bf16)


def final_kernel(n, all_ref, *refs):
    got, (a_ref, up_ref, rows_ref) = refs[:n], refs[n:]
    me, core = lax.axis_index("dp"), lax.axis_index("tensor")
    piece = up_ref.shape[1]
    picked = all_ref.shape[0] // n
    for sender, message in zip(senders(n, me, core), got):
        rows_ref[sender] = message[...]
    rows = rows_ref[:, :picked, :].reshape(n * picked, rows_ref.shape[2])
    a_ref[...] = dot(rows, all_ref[...], 0, 0)
    at = pl.ds(pl.multiple_of(core * piece, piece), piece)
    up_ref[...] = jnp.sum(rows_ref[:, picked:, at].astype(f32), axis=0)


def exchange(messages):
    n = 2 * (len(messages) - 1)
    steps = list(zip(pairs(n, 0), pairs(n, 1))) + [(1, 1)]
    got = [
        lax.ppermute(
            message,
            ("dp", "tensor"),
            [(2 * i + c, 2 * (i ^ step[c]) + c) for i in range(n) for c in range(2)],
        )
        for message, step in zip(messages[1:], steps)
    ]
    passed = [lax.ppermute(message, "tensor", [(0, 1), (1, 0)]) for message in got[:-1]]
    return [messages[0]] + got + passed


def local_kernels(
    inputs,
    output_gradient,
    frozen_weight,
    down_maps,
    up_maps,
    segment_start,
    segment_adapter,
    adapter_slot,
    token_count,
):
    model_width = inputs.shape[1]
    tok_rows, out_width = output_gradient.shape
    column_total, slot_width = down_maps.shape
    half = frozen_weight.shape[0]
    n = lax.axis_size("dp")
    piece = out_width // lax.axis_size("tensor")
    segs = segment_start.shape[1]
    picked = segs * ADAPTER_RANK
    shape = jax.ShapeDtypeStruct
    message = shape((picked + ADAPTER_RANK, column_total), bf16)
    count = n // 2 + 1
    starts, chosen = segment_start.T, segment_adapter.T

    sent = pl.pallas_call(
        functools.partial(pack_kernel, n),
        out_shape=[message] * count,
        in_specs=[HBM] * 4,
        out_specs=[VMEM] * count,
        scratch_shapes=[
            pltpu.SMEM(chosen.shape, i32),
            pltpu.SMEM(adapter_slot.shape, i32),
            pltpu.VMEM(down_maps.shape, bf16),
            pltpu.VMEM(up_maps.shape, bf16),
            pltpu.SemaphoreType.DMA((4,)),
        ],
        compiler_params=params(8),
    )(chosen, adapter_slot, down_maps, up_maps)
    x_other = lax.ppermute(inputs, "tensor", [(0, 1), (1, 0)])
    got = exchange(sent)

    x, g, in_seg, own_rows, all_rows = pl.pallas_call(
        functools.partial(stage_kernel, n),
        out_shape=[
            shape((tok_rows, model_width), bf16),
            shape((tok_rows, out_width), bf16),
            shape((tok_rows, picked), f32),
            shape((picked, slot_width), bf16),
            shape((n * picked, slot_width), bf16),
        ],
        in_specs=[HBM] * 6 + [pl.BlockSpec(memory_space=pl.ANY)],
        out_specs=[VMEM] * 5,
        scratch_shapes=[
            pltpu.SMEM(starts.shape, i32),
            pltpu.SMEM(chosen.shape, i32),
            pltpu.SMEM(adapter_slot.shape, i32),
            pltpu.SMEM(token_count.shape, i32),
            pltpu.SemaphoreType.DMA((7,)),
        ],
        compiler_params=params(8),
        cost_estimate=pl.CostEstimate(flops=0, bytes_accessed=1 << 22, transcendentals=0),
    )(starts, chosen, adapter_slot, token_count, output_gradient, inputs, x_other)

    dlow, a_all, *sent = pl.pallas_call(
        functools.partial(middle_kernel, n),
        out_shape=[shape((tok_rows, picked), bf16), shape((n, picked, column_total), bf16)]
        + [message] * count,
        in_specs=[VMEM] * (4 + n),
        out_specs=[VMEM] * (2 + count),
        scratch_shapes=[
            pltpu.VMEM((n, ADAPTER_RANK, out_width), bf16),
            pltpu.VMEM((n, ADAPTER_RANK, out_width), bf16),
        ],
        compiler_params=params(8),
    )(x, g, in_seg, own_rows, *got)
    got = exchange(sent)

    grad_x = pl.pallas_call(
        grad_x_kernel,
        out_shape=shape((tok_rows, half), bf16),
        grid=(half // column_total,),
        in_specs=[
            pl.BlockSpec((tok_rows, out_width), lambda j: (0, 0)),
            pl.BlockSpec((column_total, out_width), lambda j: (j, 0)),
            pl.BlockSpec((tok_rows, picked), lambda j: (0, 0)),
            pl.BlockSpec((n, picked, column_total), lambda j: (0, 0, 0)),
        ],
        out_specs=pl.BlockSpec((tok_rows, column_total), lambda j: (0, j)),
        compiler_params=params(8),
        cost_estimate=pl.CostEstimate(
            flops=2 * tok_rows * half * (out_width + picked),
            bytes_accessed=2 * half * (out_width + tok_rows),
            transcendentals=0,
        ),
    )(g, frozen_weight, dlow, a_all)

    grad_a, up_map_gradient = pl.pallas_call(
        functools.partial(final_kernel, n),
        out_shape=[shape((column_total, slot_width), f32), shape((ADAPTER_RANK, piece), f32)],
        in_specs=[VMEM] * (1 + n),
        out_specs=[VMEM, VMEM],
        scratch_shapes=[pltpu.VMEM((n,) + message.shape, bf16)],
        compiler_params=params(8),
    )(all_rows, *got)
    return grad_x, grad_a, up_map_gradient


def local_plain(
    inputs,
    output_gradient,
    frozen_weight,
    down_maps,
    up_maps,
    segment_start,
    segment_adapter,
    adapter_slot,
    token_count,
):
    tok_rows, out_width = output_gradient.shape
    column_total = down_maps.shape[0]
    adapter_list = adapter_slot.shape[0]
    segs = segment_start.shape[1]
    dp_size = lax.axis_size("dp")
    my_rank = lax.axis_index("dp")
    core_idx = lax.axis_index("tensor")
    picked = segs * ADAPTER_RANK
    piece_out = out_width // lax.axis_size("tensor")
    half = frozen_weight.shape[0]

    x_other = lax.ppermute(inputs, "tensor", [(0, 1), (1, 0)])
    adapter_ids = jnp.arange(adapter_list, dtype=i32)
    slot_table = jnp.sum(
        jnp.where(segment_adapter[..., None] == adapter_ids, adapter_slot, 0), axis=-1
    )
    column = slot_table[:, :, None] * ADAPTER_RANK + jnp.arange(ADAPTER_RANK, dtype=i32)
    onehot = (
        column.reshape(-1)[:, None] == jnp.arange(adapter_list * ADAPTER_RANK, dtype=i32)
    ).astype(bf16)

    a_send = dot(onehot, down_maps, 1, 1).astype(bf16).reshape(dp_size, picked, column_total)
    b_send = jnp.broadcast_to(up_maps[None], (dp_size,) + up_maps.shape)
    a_got = lax.all_to_all(a_send, "dp", 0, 0, tiled=True)
    b_got = lax.all_to_all(b_send, "dp", 0, 0, tiled=True)

    position = jnp.arange(tok_rows, dtype=i32)
    starts = lax.dynamic_index_in_dim(segment_start, my_rank, 0, keepdims=False)
    live = position < lax.dynamic_index_in_dim(token_count, my_rank, 0, keepdims=False)
    my_seg = jnp.sum((starts[None, :] <= position[:, None]).astype(i32), axis=1) - 1
    in_seg = my_seg[:, None] == (jnp.arange(picked, dtype=i32) // ADAPTER_RANK)[None, :]
    my_onehot = lax.dynamic_slice_in_dim(onehot, my_rank * picked, picked, 0)
    g = jnp.where(live[:, None], output_gradient, jnp.zeros_like(output_gradient))
    base = dot(g, frozen_weight, 1, 1)

    b_sel = dot(my_onehot, b_got.reshape(-1, out_width), 1, 0).astype(bf16)
    dlow = (adapter_scale * dot(g, b_sel, 1, 1)).astype(bf16)
    dlow = jnp.where(in_seg, dlow, jnp.zeros_like(dlow))
    a_sel = jnp.moveaxis(a_got, 0, 1).reshape(picked, -1)
    first = core_idx == 0
    x = jnp.concatenate(
        [jnp.where(first, inputs, x_other), jnp.where(first, x_other, inputs)], axis=0
    )
    low = dot(x, a_sel, 1, 1).astype(bf16)
    low = jnp.where(in_seg, low, jnp.zeros_like(low))
    low_wide = dot(low, my_onehot, 1, 0).astype(bf16)

    ga_send = dot(dlow, x, 0, 0).astype(bf16).reshape(picked, dp_size, column_total)
    ga_got = lax.all_to_all(jnp.moveaxis(ga_send, 1, 0), "dp", 0, 0, tiled=True)
    g_piece = lax.dynamic_slice_in_dim(g, core_idx * piece_out, piece_out, 1)
    up_send = (adapter_scale * dot(low_wide, g_piece, 0, 0)).astype(bf16)
    up_got = lax.all_to_all(up_send.reshape(dp_size, -1, piece_out), "dp", 0, 0, tiled=True)

    a_half = lax.dynamic_slice_in_dim(a_sel, core_idx * half, half, 1)
    grad_x = (base + dot(dlow, a_half, 1, 0)).astype(bf16)
    grad_a = dot(ga_got.reshape(dp_size * picked, column_total), onehot, 0, 0)
    up_map_gradient = jnp.sum(up_got.astype(f32), axis=0)
    return grad_x, grad_a, up_map_gradient


def local(*args):
    down_maps, up_maps = args[3], args[4]
    n, tp = lax.axis_size("dp"), lax.axis_size("tensor")
    out_width = up_maps.shape[1]
    kernels_fit = (
        n in (4, 8, 16)
        and tp == 2
        and down_maps.shape[0] == out_width
        and down_maps.shape[1] == n * up_maps.shape[0]
        and out_width % (128 * tp) == 0
    )
    return (local_kernels if kernels_fit else local_plain)(*args)


def solution(mesh):
    in_specs = (
        P(("groups", "dp", "tensor"), None),
        P(("groups", "dp"), None),
        P("tensor", None),
        P(("groups", "dp"), None),
        P(("groups", "dp"), None),
        P("groups", None),
        P("groups", None),
        P("groups"),
        P("groups"),
    )
    out_specs = (
        P(("groups", "dp"), "tensor"),
        P(("groups", "dp"), None),
        P(("groups", "dp"), "tensor"),
    )
    return jax.shard_map(local, mesh=mesh, in_specs=in_specs, out_specs=out_specs, check_vma=False)
```

```python
import functools

import jax
import jax.numpy as jnp
from jax import lax
from jax.experimental import pallas as pl
from jax.experimental.pallas import tpu as pltpu
from jax.sharding import PartitionSpec as P

ADAPTER_RANK = 16
adapter_scale = 2.0

bf16, f32, i32 = jnp.bfloat16, jnp.float32, jnp.int32

HBM = pl.BlockSpec(memory_space=pltpu.HBM)
VMEM = pl.BlockSpec(memory_space=pltpu.VMEM)


def dot(a, b, ca, cb):
    return lax.dot_general(a, b, (((ca,), (cb,)), ((), ())), preferred_element_type=f32)


def params(mib):
    return pltpu.CompilerParams(vmem_limit_bytes=mib << 20)


def slot_rows(chosen_ref, slot_ref, ranks, width):
    lane = lax.broadcasted_iota(i32, (ADAPTER_RANK, width), 1)
    row = lax.broadcasted_iota(i32, (ADAPTER_RANK, width), 0)
    rows = []
    for rank in ranks:
        for k in range(chosen_ref.shape[0]):
            first = slot_ref[chosen_ref[k, rank]] * ADAPTER_RANK
            rows.append(jnp.where(lane == row + first, 1.0, 0.0))
    return jnp.concatenate(rows, axis=0).astype(bf16)


def start_all(sources, targets, sems, first=0):
    copies = [
        pltpu.make_async_copy(source, target, sems.at[first + k])
        for k, (source, target) in enumerate(zip(sources, targets))
    ]
    for copy in copies:
        copy.start()
    return copies


def wait_all(copies):
    for copy in copies:
        copy.wait()


def pairs(n, core):
    return [n - 1 - 2 * j - core for j in range(n // 2 - 1)]


def partners(n, me, core):
    steps = [jnp.where(core == 0, a, b) for a, b in zip(pairs(n, 0), pairs(n, 1))]
    return [me] + [me ^ d for d in steps] + [me ^ 1]


def senders(n, me, core):
    return partners(n, me, core) + partners(n, me, 1 - core)[1:-1]


class Staged:
    def __init__(self, n, half, rows, picked, width, slots):
        self.n, self.half, self.rows, self.picked, self.slots = n, half, rows, picked, slots
        self.g = n * half
        self.mask = self.g + rows
        self.message = self.mask + rows
        self.shape = (self.message + picked + ADAPTER_RANK, width)

    def x(self, q):
        return pl.ds(q * self.half, self.half)

    def own_rows(self, ref):
        return ref[self.mask : self.mask + self.picked, self.slots : 2 * self.slots]

    def all_rows(self, kept):
        parts = self.n * self.picked // self.rows
        at = [pl.ds((2 + k) * self.slots, self.slots) for k in range(parts)]
        return jnp.concatenate([kept[self.rows :, k] for k in at], axis=0)


def pack_kernel(n, lay, start_hbm, chosen_hbm, slot_hbm, count_hbm, g_hbm, x_hbm, down_hbm, up_hbm, *refs):
    count = n // 2 + 1
    send, stage = refs[: count - 1], refs[count - 1]
    start_ref, chosen_ref, slot_ref, count_ref, down_ref, up_ref, out_ref, extra_ref, sems = refs[count:]
    width = down_hbm.shape[0]
    rows, picked, slots = lay.rows, lay.picked, lay.slots
    tables = start_all(
        [chosen_hbm, slot_hbm, start_hbm, count_hbm], [chosen_ref, slot_ref, start_ref, count_ref], sems
    )
    maps = start_all([down_hbm, up_hbm], [down_ref, up_ref], sems, 4)
    gradient = start_all([g_hbm], [extra_ref.at[pl.ds(0, rows)]], sems, 6)
    tokens = start_all(
        [x_hbm.at[:, pl.ds(q * width, width)] for q in range(n)],
        [stage.at[lay.x(q)] for q in range(n)],
        sems,
        7,
    )
    me = lax.axis_index("dp")
    ranks = partners(n, me, lax.axis_index("tensor"))
    wait_all(tables)
    onehot = slot_rows(chosen_ref, slot_ref, ranks, slots)
    wait_all(maps)
    columns = dot(onehot, down_ref[...], 1, 1).astype(bf16)
    for k in range(count):
        out_ref[k, :picked, :] = columns[k * picked : (k + 1) * picked]
        out_ref[k, picked:, :] = up_ref[...]
    done = start_all([out_ref.at[k] for k in range(1, count)], send, sems, 7 + n)
    own = stage.at[pl.ds(lay.message, picked + ADAPTER_RANK)]
    done += start_all([out_ref.at[0]], [own], sems, 6 + n + count)

    position = lax.broadcasted_iota(i32, (rows, slots), 0)
    group = lax.broadcasted_iota(i32, (rows, slots), 1) // ADAPTER_RANK
    segment = jnp.full((rows, slots), -1, i32)
    for k in range(start_ref.shape[0]):
        segment += jnp.where(position >= start_ref[k, me], 1, 0)
    extra_ref[rows:, :slots] = jnp.where(segment == group, 1.0, 0.0).astype(bf16)
    extra_ref[rows : rows + picked, slots : 2 * slots] = onehot[:picked]
    every = slot_rows(chosen_ref, slot_ref, range(n), slots)
    for k in range(n * picked // rows):
        extra_ref[rows:, (2 + k) * slots : (3 + k) * slots] = every[k * rows : (k + 1) * rows]
    wait_all(gradient)
    live = lax.broadcasted_iota(i32, (rows, width), 0) < count_ref[me]
    g = extra_ref[:rows, :]
    extra_ref[:rows, :] = jnp.where(live, g, jnp.zeros_like(g))
    done += start_all([extra_ref], [stage.at[pl.ds(lay.g, 2 * rows)]], sems, 7 + n + count)
    wait_all(tokens + done)


def middle_kernel(n, lay, stage, x_other, *refs):
    count = n // 2 + 1
    got, (dlow_ref, a_ref, kept_ref) = refs[: n - 1], refs[n - 1 : n + 2]
    send, (x_ref, got_ref, up_ref) = refs[n + 2 : n + 2 + count], refs[n + 2 + count :]
    me, core = lax.axis_index("dp"), lax.axis_index("tensor")
    half, rows, picked = lay.half, lay.rows, lay.picked
    width = stage.shape[1]
    mine = pl.ds(pl.multiple_of(core * half, half), half)
    other = pl.ds(pl.multiple_of((1 - core) * half, half), half)
    for q in range(n):
        x_ref[mine, q * width : (q + 1) * width] = stage[lay.x(q), :]
    x_ref[other, :] = x_other[...]
    ranks = senders(n, me, core)
    got_ref[me] = stage[lay.message :, :]
    for sender, message in zip(ranks[1:], got):
        got_ref[sender] = message[...]

    in_seg = stage[lay.mask : lay.mask + rows, :picked].astype(f32) > 0.0
    g = stage[lay.g : lay.g + rows, :]
    onehot = lay.own_rows(stage)
    up_maps = got_ref[:, picked:, :].reshape(-1, width)
    b_sel = dot(onehot, up_maps, 1, 0).astype(bf16)
    dlow = jnp.where(in_seg, adapter_scale * dot(g, b_sel, 1, 1), 0.0).astype(bf16)
    dlow_ref[...] = dlow
    parts = n // 2
    a_ref[...] = got_ref[pl.ds(pl.multiple_of(core * parts, parts), parts), :picked, :]
    kept_ref[...] = stage[lay.g : lay.message, :]
    targets = partners(n, me, core)
    for target, message in zip(targets, send):
        at = pl.ds(pl.multiple_of(target * width, width), width)
        message[:picked, :] = dot(dlow, x_ref[:, at], 0, 0).astype(bf16)

    low = jnp.zeros((rows, picked), f32)
    for q in range(n):
        low += dot(x_ref[:, q * width : (q + 1) * width], got_ref[q, :picked, :], 1, 1)
    low = jnp.where(in_seg, low, 0.0).astype(bf16)
    low_wide = dot(low, onehot, 1, 0).astype(bf16)
    up = (adapter_scale * dot(low_wide, g, 0, 0)).astype(bf16)
    up_ref[...] = up.reshape(up_ref.shape)
    for target, message in zip(targets, send):
        message[picked:, :] = up_ref[target]


def grad_x_kernel(kept_ref, w_hbm, dlow_ref, a_ref, out_hbm, w_ref, out_ref, sems):
    steps, picked, width = a_ref.shape
    blocks = [pl.ds(j * width, width) for j in range(steps)]
    weights = start_all([w_hbm.at[k] for k in blocks], [w_ref.at[k] for k in blocks], sems)
    g = kept_ref[: out_ref.shape[0], :]
    done = []
    for j, at in enumerate(blocks):
        total = dot(dlow_ref[...], a_ref[j], 1, 0)
        weights[j].wait()
        total += dot(g, w_ref[at, :], 1, 1)
        out_ref[:, at] = total.astype(bf16)
        done += start_all([out_ref.at[:, at]], [out_hbm.at[:, at]], sems, steps + j)
    wait_all(done)


def final_kernel(n, lay, kept_ref, *refs):
    got, (a_ref, up_ref, rows_ref) = refs[:n], refs[n:]
    me, core = lax.axis_index("dp"), lax.axis_index("tensor")
    piece, picked = up_ref.shape[1], lay.picked
    for sender, message in zip(senders(n, me, core), got):
        rows_ref[sender] = message[...]
    rows = rows_ref[:, :picked, :].reshape(n * picked, rows_ref.shape[2])
    a_ref[...] = dot(rows, lay.all_rows(kept_ref), 0, 0)
    at = pl.ds(pl.multiple_of(core * piece, piece), piece)
    up_ref[...] = jnp.sum(rows_ref[:, picked:, at].astype(f32), axis=0)


def exchange(messages):
    n = 2 * len(messages)
    steps = list(zip(pairs(n, 0), pairs(n, 1))) + [(1, 1)]
    got = [
        lax.ppermute(
            message,
            ("dp", "tensor"),
            [(2 * i + c, 2 * (i ^ step[c]) + c) for i in range(n) for c in range(2)],
        )
        for message, step in zip(messages, steps)
    ]
    passed = [lax.ppermute(message, "tensor", [(0, 1), (1, 0)]) for message in got[:-1]]
    return got + passed


def local_kernels(
    inputs,
    output_gradient,
    frozen_weight,
    down_maps,
    up_maps,
    segment_start,
    segment_adapter,
    adapter_slot,
    token_count,
):
    tok_half, model_width = inputs.shape
    tok_rows, out_width = output_gradient.shape
    column_total, slot_width = down_maps.shape
    half = frozen_weight.shape[0]
    n = lax.axis_size("dp")
    piece = out_width // lax.axis_size("tensor")
    segs = segment_start.shape[1]
    picked = segs * ADAPTER_RANK
    shape = jax.ShapeDtypeStruct
    message = shape((picked + ADAPTER_RANK, column_total), bf16)
    count = n // 2 + 1
    starts, chosen = segment_start.T, segment_adapter.T

    tables = [
        pltpu.SMEM(starts.shape, i32),
        pltpu.SMEM(chosen.shape, i32),
        pltpu.SMEM(adapter_slot.shape, i32),
        pltpu.SMEM(token_count.shape, i32),
    ]
    dma = pltpu.SemaphoreType.DMA

    lay = Staged(n, tok_half, tok_rows, picked, column_total, slot_width)
    *sent, stage = pl.pallas_call(
        functools.partial(pack_kernel, n, lay),
        out_shape=[message] * (count - 1) + [shape(lay.shape, bf16)],
        in_specs=[HBM] * 8,
        out_specs=[HBM] * count,
        scratch_shapes=tables
        + [
            pltpu.VMEM(down_maps.shape, bf16),
            pltpu.VMEM(up_maps.shape, bf16),
            pltpu.VMEM((count,) + message.shape, bf16),
            pltpu.VMEM((2 * tok_rows, out_width), bf16),
            dma((8 + n + count,)),
        ],
        compiler_params=params(56),
    )(
        starts,
        chosen,
        adapter_slot,
        token_count,
        output_gradient,
        inputs,
        down_maps,
        up_maps,
    )
    sent, x_late = lax.optimization_barrier((sent, inputs))
    got = exchange(sent)
    x_other = lax.ppermute(x_late, "tensor", [(0, 1), (1, 0)])

    dlow, a_half, kept, own, *sent = pl.pallas_call(
        functools.partial(middle_kernel, n, lay),
        out_shape=[
            shape((tok_rows, picked), bf16),
            shape((n // 2, picked, column_total), bf16),
            shape((2 * tok_rows, out_width), bf16),
        ]
        + [message] * count,
        in_specs=[VMEM] * (1 + n),
        out_specs=[VMEM] * (3 + count),
        scratch_shapes=[
            pltpu.VMEM((tok_rows, model_width), bf16),
            pltpu.VMEM((n,) + message.shape, bf16),
            pltpu.VMEM((n, ADAPTER_RANK, out_width), bf16),
        ],
        compiler_params=params(8),
    )(stage, x_other, *got)
    got = exchange(sent)

    grad_x = pl.pallas_call(
        grad_x_kernel,
        out_shape=shape((tok_rows, half), bf16),
        in_specs=[VMEM, HBM, VMEM, VMEM],
        out_specs=HBM,
        scratch_shapes=[
            pltpu.VMEM(frozen_weight.shape, bf16),
            pltpu.VMEM((tok_rows, half), bf16),
            dma((n,)),
        ],
        compiler_params=params(52),
        cost_estimate=pl.CostEstimate(
            flops=2 * tok_rows * half * (out_width + picked),
            bytes_accessed=2 * half * (out_width + tok_rows),
            transcendentals=0,
        ),
    )(kept, frozen_weight, dlow, a_half)

    grad_a, up_map_gradient = pl.pallas_call(
        functools.partial(final_kernel, n, lay),
        out_shape=[shape((column_total, slot_width), f32), shape((ADAPTER_RANK, piece), f32)],
        in_specs=[VMEM] * (1 + n),
        out_specs=[VMEM, VMEM],
        scratch_shapes=[pltpu.VMEM((n,) + message.shape, bf16)],
        compiler_params=params(8),
    )(kept, own, *got)
    return grad_x, grad_a, up_map_gradient


def local_plain(
    inputs,
    output_gradient,
    frozen_weight,
    down_maps,
    up_maps,
    segment_start,
    segment_adapter,
    adapter_slot,
    token_count,
):
    tok_rows, out_width = output_gradient.shape
    column_total = down_maps.shape[0]
    adapter_list = adapter_slot.shape[0]
    segs = segment_start.shape[1]
    dp_size = lax.axis_size("dp")
    my_rank = lax.axis_index("dp")
    core_idx = lax.axis_index("tensor")
    picked = segs * ADAPTER_RANK
    piece_out = out_width // lax.axis_size("tensor")
    half = frozen_weight.shape[0]

    x_other = lax.ppermute(inputs, "tensor", [(0, 1), (1, 0)])
    adapter_ids = jnp.arange(adapter_list, dtype=i32)
    slot_table = jnp.sum(
        jnp.where(segment_adapter[..., None] == adapter_ids, adapter_slot, 0), axis=-1
    )
    column = slot_table[:, :, None] * ADAPTER_RANK + jnp.arange(ADAPTER_RANK, dtype=i32)
    onehot = (
        column.reshape(-1)[:, None] == jnp.arange(adapter_list * ADAPTER_RANK, dtype=i32)
    ).astype(bf16)

    a_send = dot(onehot, down_maps, 1, 1).astype(bf16).reshape(dp_size, picked, column_total)
    b_send = jnp.broadcast_to(up_maps[None], (dp_size,) + up_maps.shape)
    a_got = lax.all_to_all(a_send, "dp", 0, 0, tiled=True)
    b_got = lax.all_to_all(b_send, "dp", 0, 0, tiled=True)

    position = jnp.arange(tok_rows, dtype=i32)
    starts = lax.dynamic_index_in_dim(segment_start, my_rank, 0, keepdims=False)
    live = position < lax.dynamic_index_in_dim(token_count, my_rank, 0, keepdims=False)
    my_seg = jnp.sum((starts[None, :] <= position[:, None]).astype(i32), axis=1) - 1
    in_seg = my_seg[:, None] == (jnp.arange(picked, dtype=i32) // ADAPTER_RANK)[None, :]
    my_onehot = lax.dynamic_slice_in_dim(onehot, my_rank * picked, picked, 0)
    g = jnp.where(live[:, None], output_gradient, jnp.zeros_like(output_gradient))
    base = dot(g, frozen_weight, 1, 1)

    b_sel = dot(my_onehot, b_got.reshape(-1, out_width), 1, 0).astype(bf16)
    dlow = (adapter_scale * dot(g, b_sel, 1, 1)).astype(bf16)
    dlow = jnp.where(in_seg, dlow, jnp.zeros_like(dlow))
    a_sel = jnp.moveaxis(a_got, 0, 1).reshape(picked, -1)
    first = core_idx == 0
    x = jnp.concatenate(
        [jnp.where(first, inputs, x_other), jnp.where(first, x_other, inputs)], axis=0
    )
    low = dot(x, a_sel, 1, 1).astype(bf16)
    low = jnp.where(in_seg, low, jnp.zeros_like(low))
    low_wide = dot(low, my_onehot, 1, 0).astype(bf16)

    ga_send = dot(dlow, x, 0, 0).astype(bf16).reshape(picked, dp_size, column_total)
    ga_got = lax.all_to_all(jnp.moveaxis(ga_send, 1, 0), "dp", 0, 0, tiled=True)
    g_piece = lax.dynamic_slice_in_dim(g, core_idx * piece_out, piece_out, 1)
    up_send = (adapter_scale * dot(low_wide, g_piece, 0, 0)).astype(bf16)
    up_got = lax.all_to_all(up_send.reshape(dp_size, -1, piece_out), "dp", 0, 0, tiled=True)

    a_half = lax.dynamic_slice_in_dim(a_sel, core_idx * half, half, 1)
    grad_x = (base + dot(dlow, a_half, 1, 0)).astype(bf16)
    grad_a = dot(ga_got.reshape(dp_size * picked, column_total), onehot, 0, 0)
    up_map_gradient = jnp.sum(up_got.astype(f32), axis=0)
    return grad_x, grad_a, up_map_gradient


def local(*args):
    down_maps, up_maps = args[3], args[4]
    n, tp = lax.axis_size("dp"), lax.axis_size("tensor")
    out_width = up_maps.shape[1]
    kernels_fit = (
        n == 8
        and tp == 2
        and down_maps.shape[0] == out_width
        and down_maps.shape[1] == n * up_maps.shape[0]
        and out_width % (128 * tp) == 0
        and out_width >= 4 * down_maps.shape[1]
        and args[1].shape[0] == 2 * args[0].shape[0] == down_maps.shape[1]
        and args[5].shape[1] * ADAPTER_RANK * n == 2 * down_maps.shape[1]
    )
    return (local_kernels if kernels_fit else local_plain)(*args)


def solution(mesh):
    in_specs = (
        P(("groups", "dp", "tensor"), None),
        P(("groups", "dp"), None),
        P("tensor", None),
        P(("groups", "dp"), None),
        P(("groups", "dp"), None),
        P("groups", None),
        P("groups", None),
        P("groups"),
        P("groups"),
    )
    out_specs = (
        P(("groups", "dp"), "tensor"),
        P(("groups", "dp"), None),
        P(("groups", "dp"), "tensor"),
    )
    return jax.shard_map(local, mesh=mesh, in_specs=in_specs, out_specs=out_specs, check_vma=False)
```

```python
import functools

import jax
import jax.numpy as jnp
from jax import lax
from jax.experimental import pallas as pl
from jax.experimental.pallas import tpu as pltpu
from jax.sharding import PartitionSpec as P

ADAPTER_RANK = 16
adapter_scale = 2.0

bf16, f32, i32 = jnp.bfloat16, jnp.float32, jnp.int32

HBM = pl.BlockSpec(memory_space=pltpu.HBM)
VMEM = pl.BlockSpec(memory_space=pltpu.VMEM)


def dot(a, b, ca, cb):
    return lax.dot_general(a, b, (((ca,), (cb,)), ((), ())), preferred_element_type=f32)


def params(mib):
    return pltpu.CompilerParams(vmem_limit_bytes=mib << 20)


def slot_rows(chosen_ref, slot_ref, ranks, width):
    lane = lax.broadcasted_iota(i32, (ADAPTER_RANK, width), 1)
    row = lax.broadcasted_iota(i32, (ADAPTER_RANK, width), 0)
    rows = []
    for rank in ranks:
        for k in range(chosen_ref.shape[0]):
            first = slot_ref[chosen_ref[k, rank]] * ADAPTER_RANK
            rows.append(jnp.where(lane == row + first, 1.0, 0.0))
    return jnp.concatenate(rows, axis=0).astype(bf16)


def start_all(sources, targets, sems, first=0):
    copies = [
        pltpu.make_async_copy(source, target, sems.at[first + k])
        for k, (source, target) in enumerate(zip(sources, targets))
    ]
    for copy in copies:
        copy.start()
    return copies


def wait_all(copies):
    for copy in copies:
        copy.wait()


def pairs(n, core):
    return [n - 1 - 2 * j - core for j in range(n // 2 - 1)]


def partners(n, me, core):
    steps = [jnp.where(core == 0, a, b) for a, b in zip(pairs(n, 0), pairs(n, 1))]
    return [me] + [me ^ d for d in steps] + [me ^ 1]


def senders(n, me, core):
    return partners(n, me, core) + partners(n, me, 1 - core)[1:-1]


class Staged:
    def __init__(self, n, half, rows, picked, width, slots):
        self.n, self.half, self.rows, self.picked, self.slots = n, half, rows, picked, slots
        self.g = n * half
        self.mask = self.g + rows
        self.message = self.mask + rows
        self.shape = (self.message + picked + ADAPTER_RANK, width)

    def x(self, q):
        return pl.ds(q * self.half, self.half)

    def own_rows(self, ref):
        return ref[self.mask : self.mask + self.picked, self.slots : 2 * self.slots]

    def all_rows(self, kept):
        parts = self.n * self.picked // self.rows
        at = [pl.ds((2 + k) * self.slots, self.slots) for k in range(parts)]
        return jnp.concatenate([kept[self.rows :, k] for k in at], axis=0)


def pack_kernel(n, lay, start_hbm, chosen_hbm, slot_hbm, count_hbm, g_hbm, x_hbm, down_hbm, up_hbm, *refs):
    count = n // 2 + 1
    send, stage_hbm = refs[: count - 1], refs[count - 1]
    start_ref, chosen_ref, slot_ref, count_ref, down_ref, up_ref, out_ref, stage, sems = refs[count:]
    width = down_hbm.shape[0]
    rows, picked, slots = lay.rows, lay.picked, lay.slots
    tables = start_all(
        [chosen_hbm, slot_hbm, start_hbm, count_hbm], [chosen_ref, slot_ref, start_ref, count_ref], sems
    )
    maps = start_all([down_hbm, up_hbm], [down_ref, up_ref], sems, 4)
    gradient = start_all([g_hbm], [stage.at[pl.ds(lay.g, rows)]], sems, 6)
    tokens = start_all(
        [x_hbm.at[:, pl.ds(q * width, width)] for q in range(n)],
        [stage.at[lay.x(q)] for q in range(n)],
        sems,
        7,
    )
    me = lax.axis_index("dp")
    ranks = partners(n, me, lax.axis_index("tensor"))
    wait_all(tables)
    onehot = slot_rows(chosen_ref, slot_ref, ranks, slots)
    wait_all(maps)
    columns = dot(onehot, down_ref[...], 1, 1).astype(bf16)
    for k in range(1, count):
        out_ref[k - 1, :picked, :] = columns[k * picked : (k + 1) * picked]
        out_ref[k - 1, picked:, :] = up_ref[...]
    done = start_all([out_ref.at[k] for k in range(count - 1)], send, sems, 7 + n)
    stage[lay.message : lay.message + picked, :] = columns[:picked]
    stage[lay.message + picked :, :] = up_ref[...]

    position = lax.broadcasted_iota(i32, (rows, slots), 0)
    group = lax.broadcasted_iota(i32, (rows, slots), 1) // ADAPTER_RANK
    segment = jnp.full((rows, slots), -1, i32)
    segs = start_ref.shape[0]
    for k in range(segs):
        segment += jnp.where(position >= start_ref[k, me], 1, 0)
    flag = (segment == group) | ((group == segs) & (position < count_ref[me]))
    stage[lay.mask : lay.mask + rows, :slots] = jnp.where(flag, 1.0, 0.0).astype(bf16)
    stage[lay.mask : lay.mask + picked, slots : 2 * slots] = onehot[:picked]
    every = slot_rows(chosen_ref, slot_ref, range(n), slots)
    for k in range(n * picked // rows):
        at = pl.ds((2 + k) * slots, slots)
        stage[lay.mask : lay.mask + rows, at] = every[k * rows : (k + 1) * rows]
    wait_all(gradient)
    live = lax.broadcasted_iota(i32, (rows, width), 0) < count_ref[me]
    g = stage[lay.g : lay.g + rows, :]
    stage[lay.g : lay.g + rows, :] = jnp.where(live, g, jnp.zeros_like(g))
    wait_all(tokens)
    done += start_all([stage], [stage_hbm], sems, 6 + n + count)
    wait_all(done)


def hand_on_kernel(stage, out_ref):
    out_ref[...] = stage[...]


def middle_kernel(n, lay, stage, x_other, *refs):
    count = n // 2 + 1
    got, (dlow_ref, a_ref, kept_ref) = refs[: n - 1], refs[n - 1 : n + 2]
    send, (x_ref, got_ref, up_ref) = refs[n + 2 : n + 2 + count], refs[n + 2 + count :]
    me, core = lax.axis_index("dp"), lax.axis_index("tensor")
    half, rows, picked = lay.half, lay.rows, lay.picked
    width = stage.shape[1]
    mine = pl.ds(pl.multiple_of(core * half, half), half)
    other = pl.ds(pl.multiple_of((1 - core) * half, half), half)
    for q in range(n):
        x_ref[mine, q * width : (q + 1) * width] = stage[lay.x(q), :]
    x_ref[other, :] = x_other[...]
    ranks = senders(n, me, core)
    got_ref[me] = stage[lay.message :, :]
    for sender, message in zip(ranks[1:], got):
        got_ref[sender] = message[...]

    in_seg = stage[lay.mask : lay.mask + rows, :picked].astype(f32) > 0.0
    g = stage[lay.g : lay.g + rows, :]
    onehot = lay.own_rows(stage)
    up_maps = got_ref[:, picked:, :].reshape(-1, width)
    b_sel = dot(onehot, up_maps, 1, 0).astype(bf16)
    dlow = jnp.where(in_seg, adapter_scale * dot(g, b_sel, 1, 1), 0.0).astype(bf16)
    dlow_ref[...] = dlow
    parts = n // 2
    a_ref[...] = got_ref[pl.ds(pl.multiple_of(core * parts, parts), parts), :picked, :]
    kept_ref[...] = stage[lay.g : lay.message, :]
    targets = partners(n, me, core)
    for target, message in zip(targets, send):
        at = pl.ds(pl.multiple_of(target * width, width), width)
        message[:picked, :] = dot(dlow, x_ref[:, at], 0, 0).astype(bf16)

    low = jnp.zeros((rows, picked), f32)
    for q in range(n):
        low += dot(x_ref[:, q * width : (q + 1) * width], got_ref[q, :picked, :], 1, 1)
    low = jnp.where(in_seg, low, 0.0).astype(bf16)
    low_wide = dot(low, onehot, 1, 0).astype(bf16)
    up = (adapter_scale * dot(low_wide, g, 0, 0)).astype(bf16)
    up_ref[...] = up.reshape(up_ref.shape)
    for target, message in zip(targets, send):
        message[picked:, :] = up_ref[target]


def grad_x_kernel(kept_ref, base_ref, dlow_ref, a_ref, out_hbm, out_ref, sems):
    steps, picked, width = a_ref.shape
    rows = out_ref.shape[0]
    live = kept_ref[rows:, picked : picked + 1].astype(f32) > 0.0
    done = []
    for j in range(steps):
        at = pl.ds(j * width, width)
        total = jnp.where(live, base_ref[:, at], 0.0) + dot(dlow_ref[...], a_ref[j], 1, 0)
        out_ref[:, at] = total.astype(bf16)
        done += start_all([out_ref.at[:, at]], [out_hbm.at[:, at]], sems, j)
    wait_all(done)


def final_kernel(n, lay, kept_ref, *refs):
    got, (a_ref, up_ref, rows_ref) = refs[:n], refs[n:]
    me, core = lax.axis_index("dp"), lax.axis_index("tensor")
    piece, picked = up_ref.shape[1], lay.picked
    for sender, message in zip(senders(n, me, core), got):
        rows_ref[sender] = message[...]
    rows = rows_ref[:, :picked, :].reshape(n * picked, rows_ref.shape[2])
    a_ref[...] = dot(rows, lay.all_rows(kept_ref), 0, 0)
    at = pl.ds(pl.multiple_of(core * piece, piece), piece)
    up_ref[...] = jnp.sum(rows_ref[:, picked:, at].astype(f32), axis=0)


def exchange(messages):
    n = 2 * len(messages)
    steps = list(zip(pairs(n, 0), pairs(n, 1))) + [(1, 1)]
    got = [
        lax.ppermute(
            message,
            ("dp", "tensor"),
            [(2 * i + c, 2 * (i ^ step[c]) + c) for i in range(n) for c in range(2)],
        )
        for message, step in zip(messages, steps)
    ]
    passed = [lax.ppermute(message, "tensor", [(0, 1), (1, 0)]) for message in got[:-1]]
    return got + passed


def local_kernels(
    inputs,
    output_gradient,
    frozen_weight,
    down_maps,
    up_maps,
    segment_start,
    segment_adapter,
    adapter_slot,
    token_count,
):
    tok_half, model_width = inputs.shape
    tok_rows, out_width = output_gradient.shape
    column_total, slot_width = down_maps.shape
    half = frozen_weight.shape[0]
    n = lax.axis_size("dp")
    piece = out_width // lax.axis_size("tensor")
    segs = segment_start.shape[1]
    picked = segs * ADAPTER_RANK
    shape = jax.ShapeDtypeStruct
    message = shape((picked + ADAPTER_RANK, column_total), bf16)
    count = n // 2 + 1
    starts, chosen = segment_start.T, segment_adapter.T

    tables = [
        pltpu.SMEM(starts.shape, i32),
        pltpu.SMEM(chosen.shape, i32),
        pltpu.SMEM(adapter_slot.shape, i32),
        pltpu.SMEM(token_count.shape, i32),
    ]
    dma = pltpu.SemaphoreType.DMA

    lay = Staged(n, tok_half, tok_rows, picked, column_total, slot_width)
    *sent, stage = pl.pallas_call(
        functools.partial(pack_kernel, n, lay),
        out_shape=[message] * (count - 1) + [shape(lay.shape, bf16)],
        in_specs=[HBM] * 8,
        out_specs=[HBM] * count,
        scratch_shapes=tables
        + [
            pltpu.VMEM(down_maps.shape, bf16),
            pltpu.VMEM(up_maps.shape, bf16),
            pltpu.VMEM((count - 1,) + message.shape, bf16),
            pltpu.VMEM(lay.shape, bf16),
            dma((7 + n + count,)),
        ],
        compiler_params=params(56),
    )(
        starts,
        chosen,
        adapter_slot,
        token_count,
        output_gradient,
        inputs,
        down_maps,
        up_maps,
    )
    sent, x_late = lax.optimization_barrier((sent, inputs))
    got = exchange(sent)
    x_other = lax.ppermute(x_late, "tensor", [(0, 1), (1, 0)])
    stage = pl.pallas_call(
        hand_on_kernel,
        out_shape=shape(lay.shape, bf16),
        in_specs=[VMEM],
        out_specs=VMEM,
        compiler_params=params(8),
        cost_estimate=pl.CostEstimate(flops=0, bytes_accessed=1 << 21, transcendentals=0),
    )(stage)
    base = dot(output_gradient, frozen_weight, 1, 1)

    dlow, a_half, kept, own, *sent = pl.pallas_call(
        functools.partial(middle_kernel, n, lay),
        out_shape=[
            shape((tok_rows, picked), bf16),
            shape((n // 2, picked, column_total), bf16),
            shape((2 * tok_rows, out_width), bf16),
        ]
        + [message] * count,
        in_specs=[VMEM] * (1 + n),
        out_specs=[VMEM] * (3 + count),
        scratch_shapes=[
            pltpu.VMEM((tok_rows, model_width), bf16),
            pltpu.VMEM((n,) + message.shape, bf16),
            pltpu.VMEM((n, ADAPTER_RANK, out_width), bf16),
        ],
        compiler_params=params(8),
    )(stage, x_other, *got)
    got = exchange(sent)

    grad_x = pl.pallas_call(
        grad_x_kernel,
        out_shape=shape((tok_rows, half), bf16),
        in_specs=[VMEM] * 4,
        out_specs=HBM,
        scratch_shapes=[pltpu.VMEM((tok_rows, half), bf16), dma((n // 2,))],
        compiler_params=params(8),
        cost_estimate=pl.CostEstimate(
            flops=2 * tok_rows * half * picked,
            bytes_accessed=6 * half * tok_rows,
            transcendentals=0,
        ),
    )(kept, base, dlow, a_half)

    grad_a, up_map_gradient = pl.pallas_call(
        functools.partial(final_kernel, n, lay),
        out_shape=[shape((column_total, slot_width), f32), shape((ADAPTER_RANK, piece), f32)],
        in_specs=[VMEM] * (1 + n),
        out_specs=[VMEM, VMEM],
        scratch_shapes=[pltpu.VMEM((n,) + message.shape, bf16)],
        compiler_params=params(8),
    )(kept, own, *got)
    return grad_x, grad_a, up_map_gradient


def local_plain(
    inputs,
    output_gradient,
    frozen_weight,
    down_maps,
    up_maps,
    segment_start,
    segment_adapter,
    adapter_slot,
    token_count,
):
    tok_rows, out_width = output_gradient.shape
    column_total = down_maps.shape[0]
    adapter_list = adapter_slot.shape[0]
    segs = segment_start.shape[1]
    dp_size = lax.axis_size("dp")
    my_rank = lax.axis_index("dp")
    core_idx = lax.axis_index("tensor")
    picked = segs * ADAPTER_RANK
    piece_out = out_width // lax.axis_size("tensor")
    half = frozen_weight.shape[0]

    x_other = lax.ppermute(inputs, "tensor", [(0, 1), (1, 0)])
    adapter_ids = jnp.arange(adapter_list, dtype=i32)
    slot_table = jnp.sum(
        jnp.where(segment_adapter[..., None] == adapter_ids, adapter_slot, 0), axis=-1
    )
    column = slot_table[:, :, None] * ADAPTER_RANK + jnp.arange(ADAPTER_RANK, dtype=i32)
    onehot = (
        column.reshape(-1)[:, None] == jnp.arange(adapter_list * ADAPTER_RANK, dtype=i32)
    ).astype(bf16)

    a_send = dot(onehot, down_maps, 1, 1).astype(bf16).reshape(dp_size, picked, column_total)
    b_send = jnp.broadcast_to(up_maps[None], (dp_size,) + up_maps.shape)
    a_got = lax.all_to_all(a_send, "dp", 0, 0, tiled=True)
    b_got = lax.all_to_all(b_send, "dp", 0, 0, tiled=True)

    position = jnp.arange(tok_rows, dtype=i32)
    starts = lax.dynamic_index_in_dim(segment_start, my_rank, 0, keepdims=False)
    live = position < lax.dynamic_index_in_dim(token_count, my_rank, 0, keepdims=False)
    my_seg = jnp.sum((starts[None, :] <= position[:, None]).astype(i32), axis=1) - 1
    in_seg = my_seg[:, None] == (jnp.arange(picked, dtype=i32) // ADAPTER_RANK)[None, :]
    my_onehot = lax.dynamic_slice_in_dim(onehot, my_rank * picked, picked, 0)
    g = jnp.where(live[:, None], output_gradient, jnp.zeros_like(output_gradient))
    base = dot(g, frozen_weight, 1, 1)

    b_sel = dot(my_onehot, b_got.reshape(-1, out_width), 1, 0).astype(bf16)
    dlow = (adapter_scale * dot(g, b_sel, 1, 1)).astype(bf16)
    dlow = jnp.where(in_seg, dlow, jnp.zeros_like(dlow))
    a_sel = jnp.moveaxis(a_got, 0, 1).reshape(picked, -1)
    first = core_idx == 0
    x = jnp.concatenate(
        [jnp.where(first, inputs, x_other), jnp.where(first, x_other, inputs)], axis=0
    )
    low = dot(x, a_sel, 1, 1).astype(bf16)
    low = jnp.where(in_seg, low, jnp.zeros_like(low))
    low_wide = dot(low, my_onehot, 1, 0).astype(bf16)

    ga_send = dot(dlow, x, 0, 0).astype(bf16).reshape(picked, dp_size, column_total)
    ga_got = lax.all_to_all(jnp.moveaxis(ga_send, 1, 0), "dp", 0, 0, tiled=True)
    g_piece = lax.dynamic_slice_in_dim(g, core_idx * piece_out, piece_out, 1)
    up_send = (adapter_scale * dot(low_wide, g_piece, 0, 0)).astype(bf16)
    up_got = lax.all_to_all(up_send.reshape(dp_size, -1, piece_out), "dp", 0, 0, tiled=True)

    a_half = lax.dynamic_slice_in_dim(a_sel, core_idx * half, half, 1)
    grad_x = (base + dot(dlow, a_half, 1, 0)).astype(bf16)
    grad_a = dot(ga_got.reshape(dp_size * picked, column_total), onehot, 0, 0)
    up_map_gradient = jnp.sum(up_got.astype(f32), axis=0)
    return grad_x, grad_a, up_map_gradient


def local(*args):
    down_maps, up_maps = args[3], args[4]
    n, tp = lax.axis_size("dp"), lax.axis_size("tensor")
    out_width = up_maps.shape[1]
    kernels_fit = (
        n == 8
        and tp == 2
        and down_maps.shape[0] == out_width
        and down_maps.shape[1] == n * up_maps.shape[0]
        and out_width % (128 * tp) == 0
        and out_width >= 4 * down_maps.shape[1]
        and args[1].shape[0] == 2 * args[0].shape[0] == down_maps.shape[1]
        and args[5].shape[1] * ADAPTER_RANK * n == 2 * down_maps.shape[1]
    )
    return (local_kernels if kernels_fit else local_plain)(*args)


def solution(mesh):
    in_specs = (
        P(("groups", "dp", "tensor"), None),
        P(("groups", "dp"), None),
        P("tensor", None),
        P(("groups", "dp"), None),
        P(("groups", "dp"), None),
        P("groups", None),
        P("groups", None),
        P("groups"),
        P("groups"),
    )
    out_specs = (
        P(("groups", "dp"), "tensor"),
        P(("groups", "dp"), None),
        P(("groups", "dp"), "tensor"),
    )
    return jax.shard_map(local, mesh=mesh, in_specs=in_specs, out_specs=out_specs, check_vma=False)
```

```python
import functools

import jax
import jax.numpy as jnp
from jax import lax
from jax.experimental import pallas as pl
from jax.experimental.pallas import tpu as pltpu
from jax.sharding import PartitionSpec as P

ADAPTER_RANK = 16
adapter_scale = 2.0

bf16, f32, i32 = jnp.bfloat16, jnp.float32, jnp.int32

HBM = pl.BlockSpec(memory_space=pltpu.HBM)
VMEM = pl.BlockSpec(memory_space=pltpu.VMEM)


def dot(a, b, ca, cb):
    return lax.dot_general(a, b, (((ca,), (cb,)), ((), ())), preferred_element_type=f32)


def params(mib):
    return pltpu.CompilerParams(vmem_limit_bytes=mib << 20)


def slot_rows(chosen_ref, slot_ref, ranks, width):
    lane = lax.broadcasted_iota(i32, (ADAPTER_RANK, width), 1)
    row = lax.broadcasted_iota(i32, (ADAPTER_RANK, width), 0)
    rows = []
    for rank in ranks:
        for k in range(chosen_ref.shape[0]):
            first = slot_ref[chosen_ref[k, rank]] * ADAPTER_RANK
            rows.append(jnp.where(lane == row + first, 1.0, 0.0))
    return jnp.concatenate(rows, axis=0).astype(bf16)


def start_all(sources, targets, sems, first=0):
    copies = [
        pltpu.make_async_copy(source, target, sems.at[first + k])
        for k, (source, target) in enumerate(zip(sources, targets))
    ]
    for copy in copies:
        copy.start()
    return copies


def wait_all(copies):
    for copy in copies:
        copy.wait()


def pairs(n, core):
    return [n - 1 - 2 * j - (core if j == 0 else 1 - core) for j in range(n // 2 - 1)]


def partners(n, me, core):
    steps = [jnp.where(core == 0, a, b) for a, b in zip(pairs(n, 0), pairs(n, 1))]
    return [me] + [me ^ d for d in steps] + [me ^ 1]


def senders(n, me, core):
    return partners(n, me, core) + partners(n, me, 1 - core)[1:-1]


class Staged:
    def __init__(self, n, half, rows, picked, width, slots):
        self.n, self.half, self.rows, self.picked, self.slots = n, half, rows, picked, slots
        self.g = n * half
        self.mask = self.g + rows
        self.message = self.mask + rows
        self.shape = (self.message + picked + ADAPTER_RANK, width)

    def x(self, q):
        return pl.ds(q * self.half, self.half)

    def own_rows(self, ref):
        return ref[self.mask : self.mask + self.picked, self.slots : 2 * self.slots]

    def all_rows(self, kept):
        parts = self.n * self.picked // self.rows
        at = [pl.ds((2 + k) * self.slots, self.slots) for k in range(parts)]
        return jnp.concatenate([kept[self.rows :, k] for k in at], axis=0)


def pack_kernel(n, lay, start_hbm, chosen_hbm, slot_hbm, count_hbm, g_hbm, x_hbm, down_hbm, up_hbm, *refs):
    count = n // 2 + 1
    send, stage_hbm = refs[: count - 1], refs[count - 1]
    start_ref, chosen_ref, slot_ref, count_ref, down_ref, up_ref, out_ref, stage, sems = refs[count:]
    width = down_hbm.shape[0]
    rows, picked, slots = lay.rows, lay.picked, lay.slots
    tables = start_all(
        [chosen_hbm, slot_hbm, start_hbm, count_hbm], [chosen_ref, slot_ref, start_ref, count_ref], sems
    )
    maps = start_all([down_hbm, up_hbm], [down_ref, up_ref], sems, 4)
    gradient = start_all([g_hbm], [stage.at[pl.ds(lay.g, rows)]], sems, 6)
    tokens = start_all(
        [x_hbm.at[:, pl.ds(q * width, width)] for q in range(n)],
        [stage.at[lay.x(q)] for q in range(n)],
        sems,
        7,
    )
    me = lax.axis_index("dp")
    ranks = partners(n, me, lax.axis_index("tensor"))
    wait_all(tables)
    onehot = slot_rows(chosen_ref, slot_ref, ranks, slots)
    wait_all(maps)
    columns = dot(onehot, down_ref[...], 1, 1).astype(bf16)
    for k in range(1, count):
        out_ref[k - 1, :picked, :] = columns[k * picked : (k + 1) * picked]
        out_ref[k - 1, picked:, :] = up_ref[...]
    done = start_all([out_ref.at[k] for k in range(count - 1)], send, sems, 7 + n)
    stage[lay.message : lay.message + picked, :] = columns[:picked]
    stage[lay.message + picked :, :] = up_ref[...]

    position = lax.broadcasted_iota(i32, (rows, slots), 0)
    group = lax.broadcasted_iota(i32, (rows, slots), 1) // ADAPTER_RANK
    segment = jnp.full((rows, slots), -1, i32)
    segs = start_ref.shape[0]
    for k in range(segs):
        segment += jnp.where(position >= start_ref[k, me], 1, 0)
    flag = (segment == group) | ((group == segs) & (position < count_ref[me]))
    stage[lay.mask : lay.mask + rows, :slots] = jnp.where(flag, 1.0, 0.0).astype(bf16)
    stage[lay.mask : lay.mask + picked, slots : 2 * slots] = onehot[:picked]
    every = slot_rows(chosen_ref, slot_ref, range(n), slots)
    for k in range(n * picked // rows):
        at = pl.ds((2 + k) * slots, slots)
        stage[lay.mask : lay.mask + rows, at] = every[k * rows : (k + 1) * rows]
    wait_all(gradient)
    live = lax.broadcasted_iota(i32, (rows, width), 0) < count_ref[me]
    g = stage[lay.g : lay.g + rows, :]
    stage[lay.g : lay.g + rows, :] = jnp.where(live, g, jnp.zeros_like(g))
    wait_all(tokens)
    done += start_all([stage], [stage_hbm], sems, 6 + n + count)
    wait_all(done)


def hand_on_kernel(stage, out_ref):
    out_ref[...] = stage[...]


def middle_kernel(n, lay, stage, x_other, *refs):
    count = n // 2 + 1
    got, (dlow_ref, a_ref, kept_ref) = refs[: n - 1], refs[n - 1 : n + 2]
    send, (x_ref, got_ref, up_ref) = refs[n + 2 : n + 2 + count], refs[n + 2 + count :]
    me, core = lax.axis_index("dp"), lax.axis_index("tensor")
    half, rows, picked = lay.half, lay.rows, lay.picked
    width = stage.shape[1]
    mine = pl.ds(pl.multiple_of(core * half, half), half)
    other = pl.ds(pl.multiple_of((1 - core) * half, half), half)
    for q in range(n):
        x_ref[mine, q * width : (q + 1) * width] = stage[lay.x(q), :]
    x_ref[other, :] = x_other[...]
    ranks = senders(n, me, core)
    got_ref[me] = stage[lay.message :, :]
    for sender, message in zip(ranks[1:], got):
        got_ref[sender] = message[...]

    in_seg = stage[lay.mask : lay.mask + rows, :picked].astype(f32) > 0.0
    g = stage[lay.g : lay.g + rows, :]
    onehot = lay.own_rows(stage)
    up_maps = got_ref[:, picked:, :].reshape(-1, width)
    b_sel = dot(onehot, up_maps, 1, 0).astype(bf16)
    dlow = jnp.where(in_seg, adapter_scale * dot(g, b_sel, 1, 1), 0.0).astype(bf16)
    dlow_ref[...] = dlow
    parts = n // 2
    a_ref[...] = got_ref[pl.ds(pl.multiple_of(core * parts, parts), parts), :picked, :]
    kept_ref[...] = stage[lay.g : lay.message, :]
    targets = partners(n, me, core)
    for target, message in zip(targets, send):
        at = pl.ds(pl.multiple_of(target * width, width), width)
        message[:picked, :] = dot(dlow, x_ref[:, at], 0, 0).astype(bf16)

    low = jnp.zeros((rows, picked), f32)
    for q in range(n):
        low += dot(x_ref[:, q * width : (q + 1) * width], got_ref[q, :picked, :], 1, 1)
    low = jnp.where(in_seg, low, 0.0).astype(bf16)
    low_wide = dot(low, onehot, 1, 0).astype(bf16)
    up = (adapter_scale * dot(low_wide, g, 0, 0)).astype(bf16)
    up_ref[...] = up.reshape(up_ref.shape)
    for target, message in zip(targets, send):
        message[picked:, :] = up_ref[target]


def base_kernel(kept_ref, w_ref, after_ref, out_ref):
    out_ref[...] = dot(kept_ref[: out_ref.shape[0], :], w_ref[...], 1, 1)


def grad_x_kernel(base_ref, dlow_ref, a_ref, out_hbm, out_ref, sems):
    steps, picked, width = a_ref.shape
    done = []
    for j in range(steps):
        at = pl.ds(j * width, width)
        total = base_ref[:, at] + dot(dlow_ref[...], a_ref[j], 1, 0)
        out_ref[:, at] = total.astype(bf16)
        done += start_all([out_ref.at[:, at]], [out_hbm.at[:, at]], sems, j)
    wait_all(done)


def final_kernel(n, lay, kept_ref, *refs):
    got, (a_ref, up_ref, rows_ref) = refs[:n], refs[n:]
    me, core = lax.axis_index("dp"), lax.axis_index("tensor")
    piece, picked = up_ref.shape[1], lay.picked
    for sender, message in zip(senders(n, me, core), got):
        rows_ref[sender] = message[...]
    rows = rows_ref[:, :picked, :].reshape(n * picked, rows_ref.shape[2])
    a_ref[...] = dot(rows, lay.all_rows(kept_ref), 0, 0)
    at = pl.ds(pl.multiple_of(core * piece, piece), piece)
    up_ref[...] = jnp.sum(rows_ref[:, picked:, at].astype(f32), axis=0)


def exchange(messages, beside=None):
    n = 2 * len(messages)
    steps = list(zip(pairs(n, 0), pairs(n, 1))) + [(1, 1)]
    got = [
        lax.ppermute(
            message,
            ("dp", "tensor"),
            [(2 * i + c, 2 * (i ^ step[c]) + c) for i in range(n) for c in range(2)],
        )
        for message, step in zip(messages, steps)
    ]
    made = None
    if beside is not None:
        made = beside(got[0])
        got[1], made = lax.optimization_barrier((got[1], made))
    passed = [lax.ppermute(message, "tensor", [(0, 1), (1, 0)]) for message in got[:-1]]
    return got + passed, made


def local_kernels(
    inputs,
    output_gradient,
    frozen_weight,
    down_maps,
    up_maps,
    segment_start,
    segment_adapter,
    adapter_slot,
    token_count,
):
    tok_half, model_width = inputs.shape
    tok_rows, out_width = output_gradient.shape
    column_total, slot_width = down_maps.shape
    half = frozen_weight.shape[0]
    n = lax.axis_size("dp")
    piece = out_width // lax.axis_size("tensor")
    segs = segment_start.shape[1]
    picked = segs * ADAPTER_RANK
    shape = jax.ShapeDtypeStruct
    message = shape((picked + ADAPTER_RANK, column_total), bf16)
    count = n // 2 + 1
    starts, chosen = segment_start.T, segment_adapter.T

    tables = [
        pltpu.SMEM(starts.shape, i32),
        pltpu.SMEM(chosen.shape, i32),
        pltpu.SMEM(adapter_slot.shape, i32),
        pltpu.SMEM(token_count.shape, i32),
    ]
    dma = pltpu.SemaphoreType.DMA

    lay = Staged(n, tok_half, tok_rows, picked, column_total, slot_width)
    *sent, stage = pl.pallas_call(
        functools.partial(pack_kernel, n, lay),
        out_shape=[message] * (count - 1) + [shape(lay.shape, bf16)],
        in_specs=[HBM] * 8,
        out_specs=[HBM] * count,
        scratch_shapes=tables
        + [
            pltpu.VMEM(down_maps.shape, bf16),
            pltpu.VMEM(up_maps.shape, bf16),
            pltpu.VMEM((count - 1,) + message.shape, bf16),
            pltpu.VMEM(lay.shape, bf16),
            dma((7 + n + count,)),
        ],
        compiler_params=params(56),
    )(
        starts,
        chosen,
        adapter_slot,
        token_count,
        output_gradient,
        inputs,
        down_maps,
        up_maps,
    )
    sent, x_late = lax.optimization_barrier((sent, inputs))
    got, _ = exchange(sent)
    x_other = lax.ppermute(x_late, "tensor", [(0, 1), (1, 0)])
    stage = pl.pallas_call(
        hand_on_kernel,
        out_shape=shape(lay.shape, bf16),
        in_specs=[VMEM],
        out_specs=VMEM,
        compiler_params=params(8),
        cost_estimate=pl.CostEstimate(flops=0, bytes_accessed=1 << 21, transcendentals=0),
    )(stage)

    dlow, a_half, kept, own, *sent = pl.pallas_call(
        functools.partial(middle_kernel, n, lay),
        out_shape=[
            shape((tok_rows, picked), bf16),
            shape((n // 2, picked, column_total), bf16),
            shape((2 * tok_rows, out_width), bf16),
        ]
        + [message] * count,
        in_specs=[VMEM] * (1 + n),
        out_specs=[VMEM] * (3 + count),
        scratch_shapes=[
            pltpu.VMEM((tok_rows, model_width), bf16),
            pltpu.VMEM((n,) + message.shape, bf16),
            pltpu.VMEM((n, ADAPTER_RANK, out_width), bf16),
        ],
        compiler_params=params(8),
    )(stage, x_other, *got)
    frozen = pl.pallas_call(
        base_kernel,
        out_shape=shape((tok_rows, half), f32),
        in_specs=[VMEM, VMEM, pl.BlockSpec(memory_space=pl.ANY)],
        out_specs=VMEM,
        compiler_params=params(8),
        cost_estimate=pl.CostEstimate(
            flops=2 * tok_rows * half * out_width,
            bytes_accessed=4 * half * tok_rows + 2 * half * out_width,
            transcendentals=0,
        ),
    )
    got, base = exchange(sent, functools.partial(frozen, kept, frozen_weight))

    grad_x = pl.pallas_call(
        grad_x_kernel,
        out_shape=shape((tok_rows, half), bf16),
        in_specs=[VMEM] * 3,
        out_specs=HBM,
        scratch_shapes=[pltpu.VMEM((tok_rows, half), bf16), dma((n // 2,))],
        compiler_params=params(8),
        cost_estimate=pl.CostEstimate(
            flops=2 * tok_rows * half * picked,
            bytes_accessed=6 * half * tok_rows,
            transcendentals=0,
        ),
    )(base, dlow, a_half)

    grad_a, up_map_gradient = pl.pallas_call(
        functools.partial(final_kernel, n, lay),
        out_shape=[shape((column_total, slot_width), f32), shape((ADAPTER_RANK, piece), f32)],
        in_specs=[VMEM] * (1 + n),
        out_specs=[VMEM, VMEM],
        scratch_shapes=[pltpu.VMEM((n,) + message.shape, bf16)],
        compiler_params=params(8),
    )(kept, own, *got)
    return grad_x, grad_a, up_map_gradient


def local_plain(
    inputs,
    output_gradient,
    frozen_weight,
    down_maps,
    up_maps,
    segment_start,
    segment_adapter,
    adapter_slot,
    token_count,
):
    tok_rows, out_width = output_gradient.shape
    column_total = down_maps.shape[0]
    adapter_list = adapter_slot.shape[0]
    segs = segment_start.shape[1]
    dp_size = lax.axis_size("dp")
    my_rank = lax.axis_index("dp")
    core_idx = lax.axis_index("tensor")
    picked = segs * ADAPTER_RANK
    piece_out = out_width // lax.axis_size("tensor")
    half = frozen_weight.shape[0]

    x_other = lax.ppermute(inputs, "tensor", [(0, 1), (1, 0)])
    adapter_ids = jnp.arange(adapter_list, dtype=i32)
    slot_table = jnp.sum(
        jnp.where(segment_adapter[..., None] == adapter_ids, adapter_slot, 0), axis=-1
    )
    column = slot_table[:, :, None] * ADAPTER_RANK + jnp.arange(ADAPTER_RANK, dtype=i32)
    onehot = (
        column.reshape(-1)[:, None] == jnp.arange(adapter_list * ADAPTER_RANK, dtype=i32)
    ).astype(bf16)

    a_send = dot(onehot, down_maps, 1, 1).astype(bf16).reshape(dp_size, picked, column_total)
    b_send = jnp.broadcast_to(up_maps[None], (dp_size,) + up_maps.shape)
    a_got = lax.all_to_all(a_send, "dp", 0, 0, tiled=True)
    b_got = lax.all_to_all(b_send, "dp", 0, 0, tiled=True)

    position = jnp.arange(tok_rows, dtype=i32)
    starts = lax.dynamic_index_in_dim(segment_start, my_rank, 0, keepdims=False)
    live = position < lax.dynamic_index_in_dim(token_count, my_rank, 0, keepdims=False)
    my_seg = jnp.sum((starts[None, :] <= position[:, None]).astype(i32), axis=1) - 1
    in_seg = my_seg[:, None] == (jnp.arange(picked, dtype=i32) // ADAPTER_RANK)[None, :]
    my_onehot = lax.dynamic_slice_in_dim(onehot, my_rank * picked, picked, 0)
    g = jnp.where(live[:, None], output_gradient, jnp.zeros_like(output_gradient))
    base = dot(g, frozen_weight, 1, 1)

    b_sel = dot(my_onehot, b_got.reshape(-1, out_width), 1, 0).astype(bf16)
    dlow = (adapter_scale * dot(g, b_sel, 1, 1)).astype(bf16)
    dlow = jnp.where(in_seg, dlow, jnp.zeros_like(dlow))
    a_sel = jnp.moveaxis(a_got, 0, 1).reshape(picked, -1)
    first = core_idx == 0
    x = jnp.concatenate(
        [jnp.where(first, inputs, x_other), jnp.where(first, x_other, inputs)], axis=0
    )
    low = dot(x, a_sel, 1, 1).astype(bf16)
    low = jnp.where(in_seg, low, jnp.zeros_like(low))
    low_wide = dot(low, my_onehot, 1, 0).astype(bf16)

    ga_send = dot(dlow, x, 0, 0).astype(bf16).reshape(picked, dp_size, column_total)
    ga_got = lax.all_to_all(jnp.moveaxis(ga_send, 1, 0), "dp", 0, 0, tiled=True)
    g_piece = lax.dynamic_slice_in_dim(g, core_idx * piece_out, piece_out, 1)
    up_send = (adapter_scale * dot(low_wide, g_piece, 0, 0)).astype(bf16)
    up_got = lax.all_to_all(up_send.reshape(dp_size, -1, piece_out), "dp", 0, 0, tiled=True)

    a_half = lax.dynamic_slice_in_dim(a_sel, core_idx * half, half, 1)
    grad_x = (base + dot(dlow, a_half, 1, 0)).astype(bf16)
    grad_a = dot(ga_got.reshape(dp_size * picked, column_total), onehot, 0, 0)
    up_map_gradient = jnp.sum(up_got.astype(f32), axis=0)
    return grad_x, grad_a, up_map_gradient


def local(*args):
    down_maps, up_maps = args[3], args[4]
    n, tp = lax.axis_size("dp"), lax.axis_size("tensor")
    out_width = up_maps.shape[1]
    kernels_fit = (
        n == 8
        and tp == 2
        and down_maps.shape[0] == out_width
        and down_maps.shape[1] == n * up_maps.shape[0]
        and out_width % (128 * tp) == 0
        and out_width >= 4 * down_maps.shape[1]
        and args[1].shape[0] == 2 * args[0].shape[0] == down_maps.shape[1]
        and args[5].shape[1] * ADAPTER_RANK * n == 2 * down_maps.shape[1]
    )
    return (local_kernels if kernels_fit else local_plain)(*args)


def solution(mesh):
    in_specs = (
        P(("groups", "dp", "tensor"), None),
        P(("groups", "dp"), None),
        P("tensor", None),
        P(("groups", "dp"), None),
        P(("groups", "dp"), None),
        P("groups", None),
        P("groups", None),
        P("groups"),
        P("groups"),
    )
    out_specs = (
        P(("groups", "dp"), "tensor"),
        P(("groups", "dp"), None),
        P(("groups", "dp"), "tensor"),
    )
    return jax.shard_map(local, mesh=mesh, in_specs=in_specs, out_specs=out_specs, check_vma=False)
```

```python
import functools

import jax
import jax.numpy as jnp
from jax import lax
from jax.experimental import pallas as pl
from jax.experimental.pallas import tpu as pltpu
from jax.sharding import PartitionSpec as P

ADAPTER_RANK = 16
adapter_scale = 2.0

bf16, f32, i32 = jnp.bfloat16, jnp.float32, jnp.int32

HBM = pl.BlockSpec(memory_space=pltpu.HBM)
VMEM = pl.BlockSpec(memory_space=pltpu.VMEM)


def dot(a, b, ca, cb):
    return lax.dot_general(a, b, (((ca,), (cb,)), ((), ())), preferred_element_type=f32)


def params(mib):
    return pltpu.CompilerParams(vmem_limit_bytes=mib << 20)


def slot_rows(chosen_ref, slot_ref, ranks, width):
    lane = lax.broadcasted_iota(i32, (ADAPTER_RANK, width), 1)
    row = lax.broadcasted_iota(i32, (ADAPTER_RANK, width), 0)
    rows = []
    for rank in ranks:
        for k in range(chosen_ref.shape[0]):
            first = slot_ref[chosen_ref[k, rank]] * ADAPTER_RANK
            rows.append(jnp.where(lane == row + first, 1.0, 0.0))
    return jnp.concatenate(rows, axis=0).astype(bf16)


def start_all(sources, targets, sems, first=0):
    copies = [
        pltpu.make_async_copy(source, target, sems.at[first + k])
        for k, (source, target) in enumerate(zip(sources, targets))
    ]
    for copy in copies:
        copy.start()
    return copies


def wait_all(copies):
    for copy in copies:
        copy.wait()


def steps(n):
    return [(n // 2, n // 2 + 1), (n - 1, n - 2), (2, 3), (1, 1)]


def partners(n, me, core):
    return [me] + [me ^ jnp.where(core == 0, a, b) for a, b in steps(n)]


def senders(n, me, core):
    passed = [me ^ jnp.where(core == 0, b, a) for a, b in steps(n) if a != b]
    return partners(n, me, core) + passed


class Staged:
    def __init__(self, n, half, rows, picked, width, slots):
        self.n, self.half, self.rows, self.picked, self.slots = n, half, rows, picked, slots
        self.g = n * half
        self.mask = self.g + rows
        self.message = self.mask + rows
        self.shape = (self.message + picked + ADAPTER_RANK, width)

    def x(self, q):
        return pl.ds(q * self.half, self.half)

    def own_rows(self, ref):
        return ref[self.mask : self.mask + self.picked, self.slots : 2 * self.slots]

    def all_rows(self, kept):
        parts = self.n * self.picked // self.rows
        at = [pl.ds((2 + k) * self.slots, self.slots) for k in range(parts)]
        return jnp.concatenate([kept[self.rows :, k] for k in at], axis=0)


def pack_kernel(n, chosen_hbm, slot_hbm, down_hbm, up_hbm, *refs):
    count = n // 2 + 1
    send, (chosen_ref, slot_ref, down_ref, up_ref, out_ref, sems) = refs[:count], refs[count:]
    tables = start_all([chosen_hbm, slot_hbm], [chosen_ref, slot_ref], sems)
    maps = start_all([down_hbm, up_hbm], [down_ref, up_ref], sems, 2)
    ranks = partners(n, lax.axis_index("dp"), lax.axis_index("tensor"))
    wait_all(tables)
    onehot = slot_rows(chosen_ref, slot_ref, ranks, down_ref.shape[1])
    picked = onehot.shape[0] // count
    wait_all(maps)
    columns = dot(onehot, down_ref[...], 1, 1).astype(bf16)
    for k in range(count):
        out_ref[k, :picked, :] = columns[k * picked : (k + 1) * picked]
        out_ref[k, picked:, :] = up_ref[...]
    wait_all(start_all([out_ref.at[k] for k in range(count)], send, sems, 4))


def stage_kernel(
    n, lay, start_hbm, chosen_hbm, slot_hbm, count_hbm, g_hbm, x_hbm, own_hbm,
    stage_hbm, start_ref, chosen_ref, slot_ref, count_ref, stage, sems,
):
    rows, picked, slots = lay.rows, lay.picked, lay.slots
    width = stage.shape[1]
    tables = start_all(
        [chosen_hbm, slot_hbm, start_hbm, count_hbm], [chosen_ref, slot_ref, start_ref, count_ref], sems
    )
    gradient = start_all([g_hbm], [stage.at[pl.ds(lay.g, rows)]], sems, 4)
    other = start_all(
        [own_hbm] + [x_hbm.at[:, pl.ds(q * width, width)] for q in range(n)],
        [stage.at[pl.ds(lay.message, picked + ADAPTER_RANK)]] + [stage.at[lay.x(q)] for q in range(n)],
        sems,
        5,
    )
    me = lax.axis_index("dp")
    wait_all(tables)
    position = lax.broadcasted_iota(i32, (rows, slots), 0)
    group = lax.broadcasted_iota(i32, (rows, slots), 1) // ADAPTER_RANK
    segment = jnp.full((rows, slots), -1, i32)
    for k in range(start_ref.shape[0]):
        segment += jnp.where(position >= start_ref[k, me], 1, 0)
    stage[lay.mask : lay.mask + rows, :slots] = jnp.where(segment == group, 1.0, 0.0).astype(bf16)
    mine = slot_rows(chosen_ref, slot_ref, [me], slots)
    stage[lay.mask : lay.mask + picked, slots : 2 * slots] = mine
    every = slot_rows(chosen_ref, slot_ref, range(n), slots)
    for k in range(n * picked // rows):
        at = pl.ds((2 + k) * slots, slots)
        stage[lay.mask : lay.mask + rows, at] = every[k * rows : (k + 1) * rows]
    wait_all(gradient)
    live = lax.broadcasted_iota(i32, (rows, width), 0) < count_ref[me]
    g = stage[lay.g : lay.g + rows, :]
    stage[lay.g : lay.g + rows, :] = jnp.where(live, g, jnp.zeros_like(g))
    wait_all(other)
    wait_all(start_all([stage], [stage_hbm], sems, 6 + n))


def hand_on_kernel(stage, out_ref):
    out_ref[...] = stage[...]


def middle_kernel(n, lay, stage, x_other, *refs):
    count = n // 2 + 1
    got, (dlow_ref, a_ref, kept_ref) = refs[: n - 1], refs[n - 1 : n + 2]
    send, (x_ref, got_ref, up_ref) = refs[n + 2 : n + 2 + count], refs[n + 2 + count :]
    me, core = lax.axis_index("dp"), lax.axis_index("tensor")
    half, rows, picked = lay.half, lay.rows, lay.picked
    width = stage.shape[1]
    mine = pl.ds(pl.multiple_of(core * half, half), half)
    other = pl.ds(pl.multiple_of((1 - core) * half, half), half)
    for q in range(n):
        x_ref[mine, q * width : (q + 1) * width] = stage[lay.x(q), :]
    x_ref[other, :] = x_other[...]
    ranks = senders(n, me, core)
    got_ref[me] = stage[lay.message :, :]
    for sender, message in zip(ranks[1:], got):
        got_ref[sender] = message[...]

    in_seg = stage[lay.mask : lay.mask + rows, :picked].astype(f32) > 0.0
    g = stage[lay.g : lay.g + rows, :]
    onehot = lay.own_rows(stage)
    up_maps = got_ref[:, picked:, :].reshape(-1, width)
    b_sel = dot(onehot, up_maps, 1, 0).astype(bf16)
    dlow = jnp.where(in_seg, adapter_scale * dot(g, b_sel, 1, 1), 0.0).astype(bf16)
    dlow_ref[...] = dlow
    parts = n // 2
    a_ref[...] = got_ref[pl.ds(pl.multiple_of(core * parts, parts), parts), :picked, :]
    kept_ref[...] = stage[lay.g : lay.message, :]
    targets = partners(n, me, core)
    for target, message in zip(targets, send):
        at = pl.ds(pl.multiple_of(target * width, width), width)
        message[:picked, :] = dot(dlow, x_ref[:, at], 0, 0).astype(bf16)

    low = jnp.zeros((rows, picked), f32)
    for q in range(n):
        low += dot(x_ref[:, q * width : (q + 1) * width], got_ref[q, :picked, :], 1, 1)
    low = jnp.where(in_seg, low, 0.0).astype(bf16)
    low_wide = dot(low, onehot, 1, 0).astype(bf16)
    up = (adapter_scale * dot(low_wide, g, 0, 0)).astype(bf16)
    up_ref[...] = up.reshape(up_ref.shape)
    for target, message in zip(targets, send):
        message[picked:, :] = up_ref[target]


def base_kernel(kept_ref, w_ref, out_ref):
    out_ref[...] = dot(kept_ref[: out_ref.shape[0], :], w_ref[...], 1, 1)


def grad_x_kernel(base_ref, dlow_ref, a_ref, out_hbm, out_ref, sems):
    steps, picked, width = a_ref.shape
    done = []
    for j in range(steps):
        at = pl.ds(j * width, width)
        total = base_ref[:, at] + dot(dlow_ref[...], a_ref[j], 1, 0)
        out_ref[:, at] = total.astype(bf16)
        done += start_all([out_ref.at[:, at]], [out_hbm.at[:, at]], sems, j)
    wait_all(done)


def final_kernel(n, lay, kept_ref, *refs):
    got, (a_ref, up_ref, rows_ref) = refs[:n], refs[n:]
    me, core = lax.axis_index("dp"), lax.axis_index("tensor")
    piece, picked = up_ref.shape[1], lay.picked
    for sender, message in zip(senders(n, me, core), got):
        rows_ref[sender] = message[...]
    rows = rows_ref[:, :picked, :].reshape(n * picked, rows_ref.shape[2])
    a_ref[...] = dot(rows, lay.all_rows(kept_ref), 0, 0)
    at = pl.ds(pl.multiple_of(core * piece, piece), piece)
    up_ref[...] = jnp.sum(rows_ref[:, picked:, at].astype(f32), axis=0)


def exchange(messages, beside):
    n = 2 * len(messages)
    got = [
        lax.ppermute(
            message,
            ("dp", "tensor"),
            [(2 * i + c, 2 * (i ^ step[c]) + c) for i in range(n) for c in range(2)],
        )
        for message, step in zip(messages, steps(n))
    ]
    got[0], beside = lax.optimization_barrier((got[0], beside))
    passed = [
        lax.ppermute(message, "tensor", [(0, 1), (1, 0)])
        for message, (a, b) in zip(got, steps(n))
        if a != b
    ]
    return got + passed, beside


def local_kernels(
    inputs,
    output_gradient,
    frozen_weight,
    down_maps,
    up_maps,
    segment_start,
    segment_adapter,
    adapter_slot,
    token_count,
):
    tok_half, model_width = inputs.shape
    tok_rows, out_width = output_gradient.shape
    column_total, slot_width = down_maps.shape
    half = frozen_weight.shape[0]
    n = lax.axis_size("dp")
    piece = out_width // lax.axis_size("tensor")
    segs = segment_start.shape[1]
    picked = segs * ADAPTER_RANK
    shape = jax.ShapeDtypeStruct
    message = shape((picked + ADAPTER_RANK, column_total), bf16)
    count = n // 2 + 1
    starts, chosen = segment_start.T, segment_adapter.T

    tables = [
        pltpu.SMEM(starts.shape, i32),
        pltpu.SMEM(chosen.shape, i32),
        pltpu.SMEM(adapter_slot.shape, i32),
        pltpu.SMEM(token_count.shape, i32),
    ]
    dma = pltpu.SemaphoreType.DMA

    lay = Staged(n, tok_half, tok_rows, picked, column_total, slot_width)
    own, *sent = pl.pallas_call(
        functools.partial(pack_kernel, n),
        out_shape=[message] * count,
        in_specs=[HBM] * 4,
        out_specs=[HBM] * count,
        scratch_shapes=tables[1:3]
        + [
            pltpu.VMEM(down_maps.shape, bf16),
            pltpu.VMEM(up_maps.shape, bf16),
            pltpu.VMEM((count,) + message.shape, bf16),
            dma((4 + count,)),
        ],
        compiler_params=params(56),
    )(chosen, adapter_slot, down_maps, up_maps)
    sent, x_late = lax.optimization_barrier((sent, inputs))
    x_other = lax.ppermute(x_late, "tensor", [(0, 1), (1, 0)])
    stage = pl.pallas_call(
        functools.partial(stage_kernel, n, lay),
        out_shape=shape(lay.shape, bf16),
        in_specs=[HBM] * 7,
        out_specs=HBM,
        scratch_shapes=tables + [pltpu.VMEM(lay.shape, bf16), dma((7 + n,))],
        compiler_params=params(56),
        cost_estimate=pl.CostEstimate(flops=0, bytes_accessed=1 << 21, transcendentals=0),
    )(starts, chosen, adapter_slot, token_count, output_gradient, inputs, own)
    got, stage = exchange(sent, stage)
    stage = pl.pallas_call(
        hand_on_kernel,
        out_shape=shape(lay.shape, bf16),
        in_specs=[VMEM],
        out_specs=VMEM,
        compiler_params=params(8),
        cost_estimate=pl.CostEstimate(flops=0, bytes_accessed=1 << 21, transcendentals=0),
    )(stage)

    dlow, a_half, kept, own, *sent = pl.pallas_call(
        functools.partial(middle_kernel, n, lay),
        out_shape=[
            shape((tok_rows, picked), bf16),
            shape((n // 2, picked, column_total), bf16),
            shape((2 * tok_rows, out_width), bf16),
        ]
        + [message] * count,
        in_specs=[VMEM] * (1 + n),
        out_specs=[VMEM] * (3 + count),
        scratch_shapes=[
            pltpu.VMEM((tok_rows, model_width), bf16),
            pltpu.VMEM((n,) + message.shape, bf16),
            pltpu.VMEM((n, ADAPTER_RANK, out_width), bf16),
        ],
        compiler_params=params(8),
    )(stage, x_other, *got)
    base = pl.pallas_call(
        base_kernel,
        out_shape=shape((tok_rows, half), f32),
        in_specs=[VMEM, VMEM],
        out_specs=VMEM,
        compiler_params=params(8),
        cost_estimate=pl.CostEstimate(
            flops=2 * tok_rows * half * out_width,
            bytes_accessed=4 * half * tok_rows + 2 * half * out_width,
            transcendentals=0,
        ),
    )(kept, frozen_weight)
    got, base = exchange(sent, base)

    grad_x = pl.pallas_call(
        grad_x_kernel,
        out_shape=shape((tok_rows, half), bf16),
        in_specs=[VMEM] * 3,
        out_specs=HBM,
        scratch_shapes=[pltpu.VMEM((tok_rows, half), bf16), dma((n // 2,))],
        compiler_params=params(8),
        cost_estimate=pl.CostEstimate(
            flops=2 * tok_rows * half * picked,
            bytes_accessed=6 * half * tok_rows,
            transcendentals=0,
        ),
    )(base, dlow, a_half)

    grad_a, up_map_gradient = pl.pallas_call(
        functools.partial(final_kernel, n, lay),
        out_shape=[shape((column_total, slot_width), f32), shape((ADAPTER_RANK, piece), f32)],
        in_specs=[VMEM] * (1 + n),
        out_specs=[VMEM, VMEM],
        scratch_shapes=[pltpu.VMEM((n,) + message.shape, bf16)],
        compiler_params=params(8),
    )(kept, own, *got)
    return grad_x, grad_a, up_map_gradient


def local_plain(
    inputs,
    output_gradient,
    frozen_weight,
    down_maps,
    up_maps,
    segment_start,
    segment_adapter,
    adapter_slot,
    token_count,
):
    tok_rows, out_width = output_gradient.shape
    column_total = down_maps.shape[0]
    adapter_list = adapter_slot.shape[0]
    segs = segment_start.shape[1]
    dp_size = lax.axis_size("dp")
    my_rank = lax.axis_index("dp")
    core_idx = lax.axis_index("tensor")
    picked = segs * ADAPTER_RANK
    piece_out = out_width // lax.axis_size("tensor")
    half = frozen_weight.shape[0]

    x_other = lax.ppermute(inputs, "tensor", [(0, 1), (1, 0)])
    adapter_ids = jnp.arange(adapter_list, dtype=i32)
    slot_table = jnp.sum(
        jnp.where(segment_adapter[..., None] == adapter_ids, adapter_slot, 0), axis=-1
    )
    column = slot_table[:, :, None] * ADAPTER_RANK + jnp.arange(ADAPTER_RANK, dtype=i32)
    onehot = (
        column.reshape(-1)[:, None] == jnp.arange(adapter_list * ADAPTER_RANK, dtype=i32)
    ).astype(bf16)

    a_send = dot(onehot, down_maps, 1, 1).astype(bf16).reshape(dp_size, picked, column_total)
    b_send = jnp.broadcast_to(up_maps[None], (dp_size,) + up_maps.shape)
    a_got = lax.all_to_all(a_send, "dp", 0, 0, tiled=True)
    b_got = lax.all_to_all(b_send, "dp", 0, 0, tiled=True)

    position = jnp.arange(tok_rows, dtype=i32)
    starts = lax.dynamic_index_in_dim(segment_start, my_rank, 0, keepdims=False)
    live = position < lax.dynamic_index_in_dim(token_count, my_rank, 0, keepdims=False)
    my_seg = jnp.sum((starts[None, :] <= position[:, None]).astype(i32), axis=1) - 1
    in_seg = my_seg[:, None] == (jnp.arange(picked, dtype=i32) // ADAPTER_RANK)[None, :]
    my_onehot = lax.dynamic_slice_in_dim(onehot, my_rank * picked, picked, 0)
    g = jnp.where(live[:, None], output_gradient, jnp.zeros_like(output_gradient))
    base = dot(g, frozen_weight, 1, 1)

    b_sel = dot(my_onehot, b_got.reshape(-1, out_width), 1, 0).astype(bf16)
    dlow = (adapter_scale * dot(g, b_sel, 1, 1)).astype(bf16)
    dlow = jnp.where(in_seg, dlow, jnp.zeros_like(dlow))
    a_sel = jnp.moveaxis(a_got, 0, 1).reshape(picked, -1)
    first = core_idx == 0
    x = jnp.concatenate(
        [jnp.where(first, inputs, x_other), jnp.where(first, x_other, inputs)], axis=0
    )
    low = dot(x, a_sel, 1, 1).astype(bf16)
    low = jnp.where(in_seg, low, jnp.zeros_like(low))
    low_wide = dot(low, my_onehot, 1, 0).astype(bf16)

    ga_send = dot(dlow, x, 0, 0).astype(bf16).reshape(picked, dp_size, column_total)
    ga_got = lax.all_to_all(jnp.moveaxis(ga_send, 1, 0), "dp", 0, 0, tiled=True)
    g_piece = lax.dynamic_slice_in_dim(g, core_idx * piece_out, piece_out, 1)
    up_send = (adapter_scale * dot(low_wide, g_piece, 0, 0)).astype(bf16)
    up_got = lax.all_to_all(up_send.reshape(dp_size, -1, piece_out), "dp", 0, 0, tiled=True)

    a_half = lax.dynamic_slice_in_dim(a_sel, core_idx * half, half, 1)
    grad_x = (base + dot(dlow, a_half, 1, 0)).astype(bf16)
    grad_a = dot(ga_got.reshape(dp_size * picked, column_total), onehot, 0, 0)
    up_map_gradient = jnp.sum(up_got.astype(f32), axis=0)
    return grad_x, grad_a, up_map_gradient


def local(*args):
    down_maps, up_maps = args[3], args[4]
    n, tp = lax.axis_size("dp"), lax.axis_size("tensor")
    out_width = up_maps.shape[1]
    kernels_fit = (
        n == 8
        and tp == 2
        and down_maps.shape[0] == out_width
        and down_maps.shape[1] == n * up_maps.shape[0]
        and out_width % (128 * tp) == 0
        and out_width >= 4 * down_maps.shape[1]
        and args[1].shape[0] == 2 * args[0].shape[0] == down_maps.shape[1]
        and args[5].shape[1] * ADAPTER_RANK * n == 2 * down_maps.shape[1]
    )
    return (local_kernels if kernels_fit else local_plain)(*args)


def solution(mesh):
    in_specs = (
        P(("groups", "dp", "tensor"), None),
        P(("groups", "dp"), None),
        P("tensor", None),
        P(("groups", "dp"), None),
        P(("groups", "dp"), None),
        P("groups", None),
        P("groups", None),
        P("groups"),
        P("groups"),
    )
    out_specs = (
        P(("groups", "dp"), "tensor"),
        P(("groups", "dp"), None),
        P(("groups", "dp"), "tensor"),
    )
    return jax.shard_map(local, mesh=mesh, in_specs=in_specs, out_specs=out_specs, check_vma=False)
```

```python
import functools

import jax
import jax.numpy as jnp
from jax import lax
from jax.experimental import pallas as pl
from jax.experimental.pallas import tpu as pltpu
from jax.sharding import PartitionSpec as P

ADAPTER_RANK = 16
adapter_scale = 2.0

bf16, f32, i32 = jnp.bfloat16, jnp.float32, jnp.int32

HBM = pl.BlockSpec(memory_space=pltpu.HBM)
VMEM = pl.BlockSpec(memory_space=pltpu.VMEM)


def dot(a, b, ca, cb):
    return lax.dot_general(a, b, (((ca,), (cb,)), ((), ())), preferred_element_type=f32)


def params(mib):
    return pltpu.CompilerParams(vmem_limit_bytes=mib << 20)


def slot_rows(chosen_ref, slot_ref, ranks, width):
    lane = lax.broadcasted_iota(i32, (ADAPTER_RANK, width), 1)
    row = lax.broadcasted_iota(i32, (ADAPTER_RANK, width), 0)
    rows = []
    for rank in ranks:
        for k in range(chosen_ref.shape[0]):
            first = slot_ref[chosen_ref[k, rank]] * ADAPTER_RANK
            rows.append(jnp.where(lane == row + first, 1.0, 0.0))
    return jnp.concatenate(rows, axis=0).astype(bf16)


def start_all(sources, targets, sems, first=0):
    copies = [
        pltpu.make_async_copy(source, target, sems.at[first + k])
        for k, (source, target) in enumerate(zip(sources, targets))
    ]
    for copy in copies:
        copy.start()
    return copies


def wait_all(copies):
    for copy in copies:
        copy.wait()


def steps(n):
    return [(n - 1, n - 2), (n // 2, n // 2 + 1), (2, 3), (1, 1)]


def partners(n, me, core):
    return [me] + [me ^ jnp.where(core == 0, a, b) for a, b in steps(n)]


def senders(n, me, core):
    passed = [me ^ jnp.where(core == 0, b, a) for a, b in steps(n) if a != b]
    return partners(n, me, core) + passed


class Staged:
    def __init__(self, n, half, rows, picked, width, slots):
        self.n, self.half, self.rows, self.picked, self.slots = n, half, rows, picked, slots
        self.g = n * half
        self.mask = self.g + rows
        self.message = self.mask + rows
        self.shape = (self.message + picked + ADAPTER_RANK, width)

    def x(self, q):
        return pl.ds(q * self.half, self.half)

    def own_rows(self, ref):
        return ref[self.mask : self.mask + self.picked, self.slots : 2 * self.slots]

    def all_rows(self, kept):
        parts = self.n * self.picked // self.rows
        at = [pl.ds((2 + k) * self.slots, self.slots) for k in range(parts)]
        return jnp.concatenate([kept[self.rows :, k] for k in at], axis=0)


def pack_kernel(n, chosen_hbm, slot_hbm, down_hbm, up_hbm, *refs):
    count = n // 2 + 1
    send, (chosen_ref, slot_ref, down_ref, up_ref, out_ref, sems) = refs[:count], refs[count:]
    tables = start_all([chosen_hbm, slot_hbm], [chosen_ref, slot_ref], sems)
    maps = start_all([down_hbm, up_hbm], [down_ref, up_ref], sems, 2)
    ranks = partners(n, lax.axis_index("dp"), lax.axis_index("tensor"))
    wait_all(tables)
    onehot = slot_rows(chosen_ref, slot_ref, ranks, down_ref.shape[1])
    picked = onehot.shape[0] // count
    wait_all(maps)
    columns = dot(onehot, down_ref[...], 1, 1).astype(bf16)
    for k in range(count):
        out_ref[k, :picked, :] = columns[k * picked : (k + 1) * picked]
        out_ref[k, picked:, :] = up_ref[...]
    wait_all(start_all([out_ref.at[k] for k in range(count)], send, sems, 4))


def stage_kernel(
    n, lay, start_hbm, chosen_hbm, slot_hbm, count_hbm, g_hbm, x_hbm, own_hbm,
    stage_hbm, start_ref, chosen_ref, slot_ref, count_ref, stage, sems,
):
    rows, picked, slots = lay.rows, lay.picked, lay.slots
    width = stage.shape[1]
    tables = start_all(
        [chosen_hbm, slot_hbm, start_hbm, count_hbm], [chosen_ref, slot_ref, start_ref, count_ref], sems
    )
    gradient = start_all([g_hbm], [stage.at[pl.ds(lay.g, rows)]], sems, 4)
    other = start_all(
        [own_hbm] + [x_hbm.at[:, pl.ds(q * width, width)] for q in range(n)],
        [stage.at[pl.ds(lay.message, picked + ADAPTER_RANK)]] + [stage.at[lay.x(q)] for q in range(n)],
        sems,
        5,
    )
    me = lax.axis_index("dp")
    wait_all(tables)
    position = lax.broadcasted_iota(i32, (rows, slots), 0)
    group = lax.broadcasted_iota(i32, (rows, slots), 1) // ADAPTER_RANK
    segment = jnp.full((rows, slots), -1, i32)
    for k in range(start_ref.shape[0]):
        segment += jnp.where(position >= start_ref[k, me], 1, 0)
    stage[lay.mask : lay.mask + rows, :slots] = jnp.where(segment == group, 1.0, 0.0).astype(bf16)
    mine = slot_rows(chosen_ref, slot_ref, [me], slots)
    stage[lay.mask : lay.mask + picked, slots : 2 * slots] = mine
    every = slot_rows(chosen_ref, slot_ref, range(n), slots)
    for k in range(n * picked // rows):
        at = pl.ds((2 + k) * slots, slots)
        stage[lay.mask : lay.mask + rows, at] = every[k * rows : (k + 1) * rows]
    wait_all(gradient)
    live = lax.broadcasted_iota(i32, (rows, width), 0) < count_ref[me]
    g = stage[lay.g : lay.g + rows, :]
    stage[lay.g : lay.g + rows, :] = jnp.where(live, g, jnp.zeros_like(g))
    wait_all(other)
    wait_all(start_all([stage], [stage_hbm], sems, 6 + n))


def hand_on_kernel(stage, out_ref):
    out_ref[...] = stage[...]


def middle_kernel(n, lay, stage, x_other, *refs):
    count = n // 2 + 1
    got, (dlow_ref, a_ref, kept_ref) = refs[: n - 1], refs[n - 1 : n + 2]
    send, (x_ref, got_ref, up_ref) = refs[n + 2 : n + 2 + count], refs[n + 2 + count :]
    me, core = lax.axis_index("dp"), lax.axis_index("tensor")
    half, rows, picked = lay.half, lay.rows, lay.picked
    width = stage.shape[1]
    mine = pl.ds(pl.multiple_of(core * half, half), half)
    other = pl.ds(pl.multiple_of((1 - core) * half, half), half)
    for q in range(n):
        x_ref[mine, q * width : (q + 1) * width] = stage[lay.x(q), :]
    x_ref[other, :] = x_other[...]
    ranks = senders(n, me, core)
    got_ref[me] = stage[lay.message :, :]
    for sender, message in zip(ranks[1:], got):
        got_ref[sender] = message[...]

    in_seg = stage[lay.mask : lay.mask + rows, :picked].astype(f32) > 0.0
    g = stage[lay.g : lay.g + rows, :]
    onehot = lay.own_rows(stage)
    up_maps = got_ref[:, picked:, :].reshape(-1, width)
    b_sel = dot(onehot, up_maps, 1, 0).astype(bf16)
    dlow = jnp.where(in_seg, adapter_scale * dot(g, b_sel, 1, 1), 0.0).astype(bf16)
    dlow_ref[...] = dlow
    parts = n // 2
    a_ref[...] = got_ref[pl.ds(pl.multiple_of(core * parts, parts), parts), :picked, :]
    kept_ref[...] = stage[lay.g : lay.message, :]
    targets = partners(n, me, core)
    for target, message in zip(targets, send):
        at = pl.ds(pl.multiple_of(target * width, width), width)
        message[:picked, :] = dot(dlow, x_ref[:, at], 0, 0).astype(bf16)

    low = jnp.zeros((rows, picked), f32)
    for q in range(n):
        low += dot(x_ref[:, q * width : (q + 1) * width], got_ref[q, :picked, :], 1, 1)
    low = jnp.where(in_seg, low, 0.0).astype(bf16)
    low_wide = dot(low, onehot, 1, 0).astype(bf16)
    up = (adapter_scale * dot(low_wide, g, 0, 0)).astype(bf16)
    up_ref[...] = up.reshape(up_ref.shape)
    for target, message in zip(targets, send):
        message[picked:, :] = up_ref[target]


def base_kernel(kept_ref, w_ref, out_ref):
    out_ref[...] = dot(kept_ref[: out_ref.shape[0], :], w_ref[...], 1, 1)


def grad_x_kernel(base_ref, dlow_ref, a_ref, out_hbm, out_ref, sems):
    steps, picked, width = a_ref.shape
    done = []
    for j in range(steps):
        at = pl.ds(j * width, width)
        total = base_ref[:, at] + dot(dlow_ref[...], a_ref[j], 1, 0)
        out_ref[:, at] = total.astype(bf16)
        done += start_all([out_ref.at[:, at]], [out_hbm.at[:, at]], sems, j)
    wait_all(done)


def final_kernel(n, lay, kept_ref, *refs):
    got, (a_ref, up_ref, rows_ref) = refs[:n], refs[n:]
    me, core = lax.axis_index("dp"), lax.axis_index("tensor")
    piece, picked = up_ref.shape[1], lay.picked
    for sender, message in zip(senders(n, me, core), got):
        rows_ref[sender] = message[...]
    rows = rows_ref[:, :picked, :].reshape(n * picked, rows_ref.shape[2])
    a_ref[...] = dot(rows, lay.all_rows(kept_ref), 0, 0)
    at = pl.ds(pl.multiple_of(core * piece, piece), piece)
    up_ref[...] = jnp.sum(rows_ref[:, picked:, at].astype(f32), axis=0)


def exchange(messages, beside):
    n = 2 * len(messages)
    got = [
        lax.ppermute(
            message,
            ("dp", "tensor"),
            [(2 * i + c, 2 * (i ^ step[c]) + c) for i in range(n) for c in range(2)],
        )
        for message, step in zip(messages, steps(n))
    ]
    got[0], beside = lax.optimization_barrier((got[0], beside))
    passed = [
        lax.ppermute(message, "tensor", [(0, 1), (1, 0)])
        for message, (a, b) in zip(got, steps(n))
        if a != b
    ]
    return got + passed, beside


def local_kernels(
    inputs,
    output_gradient,
    frozen_weight,
    down_maps,
    up_maps,
    segment_start,
    segment_adapter,
    adapter_slot,
    token_count,
):
    tok_half, model_width = inputs.shape
    tok_rows, out_width = output_gradient.shape
    column_total, slot_width = down_maps.shape
    half = frozen_weight.shape[0]
    n = lax.axis_size("dp")
    piece = out_width // lax.axis_size("tensor")
    segs = segment_start.shape[1]
    picked = segs * ADAPTER_RANK
    shape = jax.ShapeDtypeStruct
    message = shape((picked + ADAPTER_RANK, column_total), bf16)
    count = n // 2 + 1
    starts, chosen = segment_start.T, segment_adapter.T

    tables = [
        pltpu.SMEM(starts.shape, i32),
        pltpu.SMEM(chosen.shape, i32),
        pltpu.SMEM(adapter_slot.shape, i32),
        pltpu.SMEM(token_count.shape, i32),
    ]
    dma = pltpu.SemaphoreType.DMA

    lay = Staged(n, tok_half, tok_rows, picked, column_total, slot_width)
    own, *sent = pl.pallas_call(
        functools.partial(pack_kernel, n),
        out_shape=[message] * count,
        in_specs=[HBM] * 4,
        out_specs=[HBM] * count,
        scratch_shapes=tables[1:3]
        + [
            pltpu.VMEM(down_maps.shape, bf16),
            pltpu.VMEM(up_maps.shape, bf16),
            pltpu.VMEM((count,) + message.shape, bf16),
            dma((4 + count,)),
        ],
        compiler_params=params(56),
    )(chosen, adapter_slot, down_maps, up_maps)
    sent, x_late = lax.optimization_barrier((sent, inputs))
    x_other = lax.ppermute(x_late, "tensor", [(0, 1), (1, 0)])
    stage = pl.pallas_call(
        functools.partial(stage_kernel, n, lay),
        out_shape=shape(lay.shape, bf16),
        in_specs=[HBM] * 7,
        out_specs=HBM,
        scratch_shapes=tables + [pltpu.VMEM(lay.shape, bf16), dma((7 + n,))],
        compiler_params=params(56),
        cost_estimate=pl.CostEstimate(flops=0, bytes_accessed=1 << 21, transcendentals=0),
    )(starts, chosen, adapter_slot, token_count, output_gradient, inputs, own)
    got, stage = exchange(sent, stage)
    stage = pl.pallas_call(
        hand_on_kernel,
        out_shape=shape(lay.shape, bf16),
        in_specs=[VMEM],
        out_specs=VMEM,
        compiler_params=params(8),
        cost_estimate=pl.CostEstimate(flops=0, bytes_accessed=1 << 21, transcendentals=0),
    )(stage)

    dlow, a_half, kept, own, *sent = pl.pallas_call(
        functools.partial(middle_kernel, n, lay),
        out_shape=[
            shape((tok_rows, picked), bf16),
            shape((n // 2, picked, column_total), bf16),
            shape((2 * tok_rows, out_width), bf16),
        ]
        + [message] * count,
        in_specs=[VMEM] * (1 + n),
        out_specs=[VMEM] * (3 + count),
        scratch_shapes=[
            pltpu.VMEM((tok_rows, model_width), bf16),
            pltpu.VMEM((n,) + message.shape, bf16),
            pltpu.VMEM((n, ADAPTER_RANK, out_width), bf16),
        ],
        compiler_params=params(8),
    )(stage, x_other, *got)
    base = pl.pallas_call(
        base_kernel,
        out_shape=shape((tok_rows, half), f32),
        in_specs=[VMEM, VMEM],
        out_specs=VMEM,
        compiler_params=params(8),
        cost_estimate=pl.CostEstimate(
            flops=2 * tok_rows * half * out_width,
            bytes_accessed=4 * half * tok_rows + 2 * half * out_width,
            transcendentals=0,
        ),
    )(kept, frozen_weight)
    got, base = exchange(sent, base)

    grad_x = pl.pallas_call(
        grad_x_kernel,
        out_shape=shape((tok_rows, half), bf16),
        in_specs=[VMEM] * 3,
        out_specs=HBM,
        scratch_shapes=[pltpu.VMEM((tok_rows, half), bf16), dma((n // 2,))],
        compiler_params=params(8),
        cost_estimate=pl.CostEstimate(
            flops=2 * tok_rows * half * picked,
            bytes_accessed=6 * half * tok_rows,
            transcendentals=0,
        ),
    )(base, dlow, a_half)

    grad_a, up_map_gradient = pl.pallas_call(
        functools.partial(final_kernel, n, lay),
        out_shape=[shape((column_total, slot_width), f32), shape((ADAPTER_RANK, piece), f32)],
        in_specs=[VMEM] * (1 + n),
        out_specs=[VMEM, VMEM],
        scratch_shapes=[pltpu.VMEM((n,) + message.shape, bf16)],
        compiler_params=params(8),
    )(kept, own, *got)
    return grad_x, grad_a, up_map_gradient


def local_plain(
    inputs,
    output_gradient,
    frozen_weight,
    down_maps,
    up_maps,
    segment_start,
    segment_adapter,
    adapter_slot,
    token_count,
):
    tok_rows, out_width = output_gradient.shape
    column_total = down_maps.shape[0]
    adapter_list = adapter_slot.shape[0]
    segs = segment_start.shape[1]
    dp_size = lax.axis_size("dp")
    my_rank = lax.axis_index("dp")
    core_idx = lax.axis_index("tensor")
    picked = segs * ADAPTER_RANK
    piece_out = out_width // lax.axis_size("tensor")
    half = frozen_weight.shape[0]

    x_other = lax.ppermute(inputs, "tensor", [(0, 1), (1, 0)])
    adapter_ids = jnp.arange(adapter_list, dtype=i32)
    slot_table = jnp.sum(
        jnp.where(segment_adapter[..., None] == adapter_ids, adapter_slot, 0), axis=-1
    )
    column = slot_table[:, :, None] * ADAPTER_RANK + jnp.arange(ADAPTER_RANK, dtype=i32)
    onehot = (
        column.reshape(-1)[:, None] == jnp.arange(adapter_list * ADAPTER_RANK, dtype=i32)
    ).astype(bf16)

    a_send = dot(onehot, down_maps, 1, 1).astype(bf16).reshape(dp_size, picked, column_total)
    b_send = jnp.broadcast_to(up_maps[None], (dp_size,) + up_maps.shape)
    a_got = lax.all_to_all(a_send, "dp", 0, 0, tiled=True)
    b_got = lax.all_to_all(b_send, "dp", 0, 0, tiled=True)

    position = jnp.arange(tok_rows, dtype=i32)
    starts = lax.dynamic_index_in_dim(segment_start, my_rank, 0, keepdims=False)
    live = position < lax.dynamic_index_in_dim(token_count, my_rank, 0, keepdims=False)
    my_seg = jnp.sum((starts[None, :] <= position[:, None]).astype(i32), axis=1) - 1
    in_seg = my_seg[:, None] == (jnp.arange(picked, dtype=i32) // ADAPTER_RANK)[None, :]
    my_onehot = lax.dynamic_slice_in_dim(onehot, my_rank * picked, picked, 0)
    g = jnp.where(live[:, None], output_gradient, jnp.zeros_like(output_gradient))
    base = dot(g, frozen_weight, 1, 1)

    b_sel = dot(my_onehot, b_got.reshape(-1, out_width), 1, 0).astype(bf16)
    dlow = (adapter_scale * dot(g, b_sel, 1, 1)).astype(bf16)
    dlow = jnp.where(in_seg, dlow, jnp.zeros_like(dlow))
    a_sel = jnp.moveaxis(a_got, 0, 1).reshape(picked, -1)
    first = core_idx == 0
    x = jnp.concatenate(
        [jnp.where(first, inputs, x_other), jnp.where(first, x_other, inputs)], axis=0
    )
    low = dot(x, a_sel, 1, 1).astype(bf16)
    low = jnp.where(in_seg, low, jnp.zeros_like(low))
    low_wide = dot(low, my_onehot, 1, 0).astype(bf16)

    ga_send = dot(dlow, x, 0, 0).astype(bf16).reshape(picked, dp_size, column_total)
    ga_got = lax.all_to_all(jnp.moveaxis(ga_send, 1, 0), "dp", 0, 0, tiled=True)
    g_piece = lax.dynamic_slice_in_dim(g, core_idx * piece_out, piece_out, 1)
    up_send = (adapter_scale * dot(low_wide, g_piece, 0, 0)).astype(bf16)
    up_got = lax.all_to_all(up_send.reshape(dp_size, -1, piece_out), "dp", 0, 0, tiled=True)

    a_half = lax.dynamic_slice_in_dim(a_sel, core_idx * half, half, 1)
    grad_x = (base + dot(dlow, a_half, 1, 0)).astype(bf16)
    grad_a = dot(ga_got.reshape(dp_size * picked, column_total), onehot, 0, 0)
    up_map_gradient = jnp.sum(up_got.astype(f32), axis=0)
    return grad_x, grad_a, up_map_gradient


def local(*args):
    down_maps, up_maps = args[3], args[4]
    n, tp = lax.axis_size("dp"), lax.axis_size("tensor")
    out_width = up_maps.shape[1]
    kernels_fit = (
        n == 8
        and tp == 2
        and down_maps.shape[0] == out_width
        and down_maps.shape[1] == n * up_maps.shape[0]
        and out_width % (128 * tp) == 0
        and out_width >= 4 * down_maps.shape[1]
        and args[1].shape[0] == 2 * args[0].shape[0] == down_maps.shape[1]
        and args[5].shape[1] * ADAPTER_RANK * n == 2 * down_maps.shape[1]
    )
    return (local_kernels if kernels_fit else local_plain)(*args)


def solution(mesh):
    in_specs = (
        P(("groups", "dp", "tensor"), None),
        P(("groups", "dp"), None),
        P("tensor", None),
        P(("groups", "dp"), None),
        P(("groups", "dp"), None),
        P("groups", None),
        P("groups", None),
        P("groups"),
        P("groups"),
    )
    out_specs = (
        P(("groups", "dp"), "tensor"),
        P(("groups", "dp"), None),
        P(("groups", "dp"), "tensor"),
    )
    return jax.shard_map(local, mesh=mesh, in_specs=in_specs, out_specs=out_specs, check_vma=False)
```

```python
import functools

import jax
import jax.numpy as jnp
from jax import lax
from jax.experimental import pallas as pl
from jax.experimental.pallas import tpu as pltpu
from jax.sharding import PartitionSpec as P

ADAPTER_RANK = 16
adapter_scale = 2.0

bf16, f32, i32 = jnp.bfloat16, jnp.float32, jnp.int32

HBM = pl.BlockSpec(memory_space=pltpu.HBM)
VMEM = pl.BlockSpec(memory_space=pltpu.VMEM)


def dot(a, b, ca, cb):
    return lax.dot_general(a, b, (((ca,), (cb,)), ((), ())), preferred_element_type=f32)


def params(mib):
    return pltpu.CompilerParams(vmem_limit_bytes=mib << 20)


def slot_rows(chosen_ref, slot_ref, ranks, width):
    lane = lax.broadcasted_iota(i32, (ADAPTER_RANK, width), 1)
    row = lax.broadcasted_iota(i32, (ADAPTER_RANK, width), 0)
    rows = []
    for rank in ranks:
        for k in range(chosen_ref.shape[0]):
            first = slot_ref[chosen_ref[k, rank]] * ADAPTER_RANK
            rows.append(jnp.where(lane == row + first, 1.0, 0.0))
    return jnp.concatenate(rows, axis=0).astype(bf16)


def start_all(sources, targets, sems, first=0):
    copies = [
        pltpu.make_async_copy(source, target, sems.at[first + k])
        for k, (source, target) in enumerate(zip(sources, targets))
    ]
    for copy in copies:
        copy.start()
    return copies


def wait_all(copies):
    for copy in copies:
        copy.wait()


def steps(n):
    return [(n - 1, n // 2 + 1), (3, n - 2), (2, n // 2), (1, 1)]


def partners(n, me, core):
    return [me] + [me ^ jnp.where(core == 0, a, b) for a, b in steps(n)]


def senders(n, me, core):
    passed = [me ^ jnp.where(core == 0, b, a) for a, b in steps(n) if a != b]
    return partners(n, me, core) + passed


class Staged:
    def __init__(self, n, half, rows, picked, width, slots):
        self.n, self.half, self.rows, self.picked, self.slots = n, half, rows, picked, slots
        self.g = n * half
        self.mask = self.g + rows
        self.message = self.mask + rows
        self.shape = (self.message + picked + ADAPTER_RANK, width)

    def x(self, q):
        return pl.ds(q * self.half, self.half)

    def own_rows(self, ref):
        return ref[self.mask : self.mask + self.picked, self.slots : 2 * self.slots]

    def all_rows(self, kept):
        parts = self.n * self.picked // self.rows
        at = [pl.ds((2 + k) * self.slots, self.slots) for k in range(parts)]
        return jnp.concatenate([kept[self.rows :, k] for k in at], axis=0)


def pack_kernel(n, chosen_hbm, slot_hbm, down_hbm, up_hbm, *refs):
    count = n // 2 + 1
    send, (chosen_ref, slot_ref, down_ref, up_ref, out_ref, sems) = refs[:count], refs[count:]
    tables = start_all([chosen_hbm, slot_hbm], [chosen_ref, slot_ref], sems)
    maps = start_all([down_hbm, up_hbm], [down_ref, up_ref], sems, 2)
    ranks = partners(n, lax.axis_index("dp"), lax.axis_index("tensor"))
    wait_all(tables)
    onehot = slot_rows(chosen_ref, slot_ref, ranks, down_ref.shape[1])
    picked = onehot.shape[0] // count
    wait_all(maps)
    columns = dot(onehot, down_ref[...], 1, 1).astype(bf16)
    for k in range(count):
        out_ref[k, :picked, :] = columns[k * picked : (k + 1) * picked]
        out_ref[k, picked:, :] = up_ref[...]
    wait_all(start_all([out_ref.at[k] for k in range(count)], send, sems, 4))


def stage_kernel(
    n, lay, start_hbm, chosen_hbm, slot_hbm, count_hbm, g_hbm, x_hbm, own_hbm,
    stage_hbm, start_ref, chosen_ref, slot_ref, count_ref, stage, sems,
):
    rows, picked, slots = lay.rows, lay.picked, lay.slots
    width = stage.shape[1]
    tables = start_all(
        [chosen_hbm, slot_hbm, start_hbm, count_hbm], [chosen_ref, slot_ref, start_ref, count_ref], sems
    )
    gradient = start_all([g_hbm], [stage.at[pl.ds(lay.g, rows)]], sems, 4)
    other = start_all(
        [own_hbm] + [x_hbm.at[:, pl.ds(q * width, width)] for q in range(n)],
        [stage.at[pl.ds(lay.message, picked + ADAPTER_RANK)]] + [stage.at[lay.x(q)] for q in range(n)],
        sems,
        5,
    )
    me = lax.axis_index("dp")
    wait_all(tables)
    position = lax.broadcasted_iota(i32, (rows, slots), 0)
    group = lax.broadcasted_iota(i32, (rows, slots), 1) // ADAPTER_RANK
    segment = jnp.full((rows, slots), -1, i32)
    for k in range(start_ref.shape[0]):
        segment += jnp.where(position >= start_ref[k, me], 1, 0)
    stage[lay.mask : lay.mask + rows, :slots] = jnp.where(segment == group, 1.0, 0.0).astype(bf16)
    mine = slot_rows(chosen_ref, slot_ref, [me], slots)
    stage[lay.mask : lay.mask + picked, slots : 2 * slots] = mine
    every = slot_rows(chosen_ref, slot_ref, range(n), slots)
    for k in range(n * picked // rows):
        at = pl.ds((2 + k) * slots, slots)
        stage[lay.mask : lay.mask + rows, at] = every[k * rows : (k + 1) * rows]
    wait_all(gradient)
    live = lax.broadcasted_iota(i32, (rows, width), 0) < count_ref[me]
    g = stage[lay.g : lay.g + rows, :]
    stage[lay.g : lay.g + rows, :] = jnp.where(live, g, jnp.zeros_like(g))
    wait_all(other)
    wait_all(start_all([stage], [stage_hbm], sems, 6 + n))


def hand_on_kernel(stage, out_ref):
    out_ref[...] = stage[...]


def middle_kernel(n, lay, stage, x_other, *refs):
    count = n // 2 + 1
    got, (dlow_ref, a_ref, kept_ref) = refs[: n - 1], refs[n - 1 : n + 2]
    send, (x_ref, got_ref, up_ref) = refs[n + 2 : n + 2 + count], refs[n + 2 + count :]
    me, core = lax.axis_index("dp"), lax.axis_index("tensor")
    half, rows, picked = lay.half, lay.rows, lay.picked
    width = stage.shape[1]
    mine = pl.ds(pl.multiple_of(core * half, half), half)
    other = pl.ds(pl.multiple_of((1 - core) * half, half), half)
    for q in range(n):
        x_ref[mine, q * width : (q + 1) * width] = stage[lay.x(q), :]
    x_ref[other, :] = x_other[...]
    ranks = senders(n, me, core)
    got_ref[me] = stage[lay.message :, :]
    for sender, message in zip(ranks[1:], got):
        got_ref[sender] = message[...]

    in_seg = stage[lay.mask : lay.mask + rows, :picked].astype(f32) > 0.0
    g = stage[lay.g : lay.g + rows, :]
    onehot = lay.own_rows(stage)
    up_maps = got_ref[:, picked:, :].reshape(-1, width)
    b_sel = dot(onehot, up_maps, 1, 0).astype(bf16)
    dlow = jnp.where(in_seg, adapter_scale * dot(g, b_sel, 1, 1), 0.0).astype(bf16)
    dlow_ref[...] = dlow
    parts = n // 2
    a_ref[...] = got_ref[pl.ds(pl.multiple_of(core * parts, parts), parts), :picked, :]
    kept_ref[...] = stage[lay.g : lay.message, :]
    targets = partners(n, me, core)
    for target, message in zip(targets, send):
        at = pl.ds(pl.multiple_of(target * width, width), width)
        message[:picked, :] = dot(dlow, x_ref[:, at], 0, 0).astype(bf16)

    low = jnp.zeros((rows, picked), f32)
    for q in range(n):
        low += dot(x_ref[:, q * width : (q + 1) * width], got_ref[q, :picked, :], 1, 1)
    low = jnp.where(in_seg, low, 0.0).astype(bf16)
    low_wide = dot(low, onehot, 1, 0).astype(bf16)
    up = (adapter_scale * dot(low_wide, g, 0, 0)).astype(bf16)
    up_ref[...] = up.reshape(up_ref.shape)
    for target, message in zip(targets, send):
        message[picked:, :] = up_ref[target]


def base_kernel(kept_ref, w_ref, out_ref):
    out_ref[...] = dot(kept_ref[: out_ref.shape[0], :], w_ref[...], 1, 1)


def grad_x_kernel(base_ref, dlow_ref, a_ref, out_hbm, out_ref, sems):
    steps, picked, width = a_ref.shape
    done = []
    for j in range(steps):
        at = pl.ds(j * width, width)
        total = base_ref[:, at] + dot(dlow_ref[...], a_ref[j], 1, 0)
        out_ref[:, at] = total.astype(bf16)
        done += start_all([out_ref.at[:, at]], [out_hbm.at[:, at]], sems, j)
    wait_all(done)


def final_kernel(n, lay, kept_ref, *refs):
    got, (a_ref, up_ref, rows_ref) = refs[:n], refs[n:]
    me, core = lax.axis_index("dp"), lax.axis_index("tensor")
    piece, picked = up_ref.shape[1], lay.picked
    for sender, message in zip(senders(n, me, core), got):
        rows_ref[sender] = message[...]
    rows = rows_ref[:, :picked, :].reshape(n * picked, rows_ref.shape[2])
    a_ref[...] = dot(rows, lay.all_rows(kept_ref), 0, 0)
    at = pl.ds(pl.multiple_of(core * piece, piece), piece)
    up_ref[...] = jnp.sum(rows_ref[:, picked:, at].astype(f32), axis=0)


def exchange(messages, beside):
    n = 2 * len(messages)
    got = [
        lax.ppermute(
            message,
            ("dp", "tensor"),
            [(2 * i + c, 2 * (i ^ step[c]) + c) for i in range(n) for c in range(2)],
        )
        for message, step in zip(messages, steps(n))
    ]
    got[0], beside = lax.optimization_barrier((got[0], beside))
    passed = [
        lax.ppermute(message, "tensor", [(0, 1), (1, 0)])
        for message, (a, b) in zip(got, steps(n))
        if a != b
    ]
    return got + passed, beside


def local_kernels(
    inputs,
    output_gradient,
    frozen_weight,
    down_maps,
    up_maps,
    segment_start,
    segment_adapter,
    adapter_slot,
    token_count,
):
    tok_half, model_width = inputs.shape
    tok_rows, out_width = output_gradient.shape
    column_total, slot_width = down_maps.shape
    half = frozen_weight.shape[0]
    n = lax.axis_size("dp")
    piece = out_width // lax.axis_size("tensor")
    segs = segment_start.shape[1]
    picked = segs * ADAPTER_RANK
    shape = jax.ShapeDtypeStruct
    message = shape((picked + ADAPTER_RANK, column_total), bf16)
    count = n // 2 + 1
    starts, chosen = segment_start.T, segment_adapter.T

    tables = [
        pltpu.SMEM(starts.shape, i32),
        pltpu.SMEM(chosen.shape, i32),
        pltpu.SMEM(adapter_slot.shape, i32),
        pltpu.SMEM(token_count.shape, i32),
    ]
    dma = pltpu.SemaphoreType.DMA

    lay = Staged(n, tok_half, tok_rows, picked, column_total, slot_width)
    own, *sent = pl.pallas_call(
        functools.partial(pack_kernel, n),
        out_shape=[message] * count,
        in_specs=[HBM] * 4,
        out_specs=[HBM] * count,
        scratch_shapes=tables[1:3]
        + [
            pltpu.VMEM(down_maps.shape, bf16),
            pltpu.VMEM(up_maps.shape, bf16),
            pltpu.VMEM((count,) + message.shape, bf16),
            dma((4 + count,)),
        ],
        compiler_params=params(56),
    )(chosen, adapter_slot, down_maps, up_maps)
    sent, x_late = lax.optimization_barrier((sent, inputs))
    x_other = lax.ppermute(x_late, "tensor", [(0, 1), (1, 0)])
    stage = pl.pallas_call(
        functools.partial(stage_kernel, n, lay),
        out_shape=shape(lay.shape, bf16),
        in_specs=[HBM] * 7,
        out_specs=HBM,
        scratch_shapes=tables + [pltpu.VMEM(lay.shape, bf16), dma((7 + n,))],
        compiler_params=params(56),
        cost_estimate=pl.CostEstimate(flops=0, bytes_accessed=1 << 21, transcendentals=0),
    )(starts, chosen, adapter_slot, token_count, output_gradient, inputs, own)
    got, stage = exchange(sent, stage)
    stage = pl.pallas_call(
        hand_on_kernel,
        out_shape=shape(lay.shape, bf16),
        in_specs=[VMEM],
        out_specs=VMEM,
        compiler_params=params(8),
        cost_estimate=pl.CostEstimate(flops=0, bytes_accessed=1 << 21, transcendentals=0),
    )(stage)

    dlow, a_half, kept, own, *sent = pl.pallas_call(
        functools.partial(middle_kernel, n, lay),
        out_shape=[
            shape((tok_rows, picked), bf16),
            shape((n // 2, picked, column_total), bf16),
            shape((2 * tok_rows, out_width), bf16),
        ]
        + [message] * count,
        in_specs=[VMEM] * (1 + n),
        out_specs=[VMEM] * (3 + count),
        scratch_shapes=[
            pltpu.VMEM((tok_rows, model_width), bf16),
            pltpu.VMEM((n,) + message.shape, bf16),
            pltpu.VMEM((n, ADAPTER_RANK, out_width), bf16),
        ],
        compiler_params=params(8),
    )(stage, x_other, *got)
    base = pl.pallas_call(
        base_kernel,
        out_shape=shape((tok_rows, half), f32),
        in_specs=[VMEM, VMEM],
        out_specs=VMEM,
        compiler_params=params(8),
        cost_estimate=pl.CostEstimate(
            flops=2 * tok_rows * half * out_width,
            bytes_accessed=4 * half * tok_rows + 2 * half * out_width,
            transcendentals=0,
        ),
    )(kept, frozen_weight)
    grad_x = pl.pallas_call(
        grad_x_kernel,
        out_shape=shape((tok_rows, half), bf16),
        in_specs=[VMEM] * 3,
        out_specs=HBM,
        scratch_shapes=[pltpu.VMEM((tok_rows, half), bf16), dma((n // 2,))],
        compiler_params=params(8),
        cost_estimate=pl.CostEstimate(
            flops=2 * tok_rows * half * picked,
            bytes_accessed=6 * half * tok_rows,
            transcendentals=0,
        ),
    )(base, dlow, a_half)

    got, grad_x = exchange(sent, grad_x)

    grad_a, up_map_gradient = pl.pallas_call(
        functools.partial(final_kernel, n, lay),
        out_shape=[shape((column_total, slot_width), f32), shape((ADAPTER_RANK, piece), f32)],
        in_specs=[VMEM] * (1 + n),
        out_specs=[VMEM, VMEM],
        scratch_shapes=[pltpu.VMEM((n,) + message.shape, bf16)],
        compiler_params=params(8),
    )(kept, own, *got)
    return grad_x, grad_a, up_map_gradient


def local_plain(
    inputs,
    output_gradient,
    frozen_weight,
    down_maps,
    up_maps,
    segment_start,
    segment_adapter,
    adapter_slot,
    token_count,
):
    tok_rows, out_width = output_gradient.shape
    column_total = down_maps.shape[0]
    adapter_list = adapter_slot.shape[0]
    segs = segment_start.shape[1]
    dp_size = lax.axis_size("dp")
    my_rank = lax.axis_index("dp")
    core_idx = lax.axis_index("tensor")
    picked = segs * ADAPTER_RANK
    piece_out = out_width // lax.axis_size("tensor")
    half = frozen_weight.shape[0]

    x_other = lax.ppermute(inputs, "tensor", [(0, 1), (1, 0)])
    adapter_ids = jnp.arange(adapter_list, dtype=i32)
    slot_table = jnp.sum(
        jnp.where(segment_adapter[..., None] == adapter_ids, adapter_slot, 0), axis=-1
    )
    column = slot_table[:, :, None] * ADAPTER_RANK + jnp.arange(ADAPTER_RANK, dtype=i32)
    onehot = (
        column.reshape(-1)[:, None] == jnp.arange(adapter_list * ADAPTER_RANK, dtype=i32)
    ).astype(bf16)

    a_send = dot(onehot, down_maps, 1, 1).astype(bf16).reshape(dp_size, picked, column_total)
    b_send = jnp.broadcast_to(up_maps[None], (dp_size,) + up_maps.shape)
    a_got = lax.all_to_all(a_send, "dp", 0, 0, tiled=True)
    b_got = lax.all_to_all(b_send, "dp", 0, 0, tiled=True)

    position = jnp.arange(tok_rows, dtype=i32)
    starts = lax.dynamic_index_in_dim(segment_start, my_rank, 0, keepdims=False)
    live = position < lax.dynamic_index_in_dim(token_count, my_rank, 0, keepdims=False)
    my_seg = jnp.sum((starts[None, :] <= position[:, None]).astype(i32), axis=1) - 1
    in_seg = my_seg[:, None] == (jnp.arange(picked, dtype=i32) // ADAPTER_RANK)[None, :]
    my_onehot = lax.dynamic_slice_in_dim(onehot, my_rank * picked, picked, 0)
    g = jnp.where(live[:, None], output_gradient, jnp.zeros_like(output_gradient))
    base = dot(g, frozen_weight, 1, 1)

    b_sel = dot(my_onehot, b_got.reshape(-1, out_width), 1, 0).astype(bf16)
    dlow = (adapter_scale * dot(g, b_sel, 1, 1)).astype(bf16)
    dlow = jnp.where(in_seg, dlow, jnp.zeros_like(dlow))
    a_sel = jnp.moveaxis(a_got, 0, 1).reshape(picked, -1)
    first = core_idx == 0
    x = jnp.concatenate(
        [jnp.where(first, inputs, x_other), jnp.where(first, x_other, inputs)], axis=0
    )
    low = dot(x, a_sel, 1, 1).astype(bf16)
    low = jnp.where(in_seg, low, jnp.zeros_like(low))
    low_wide = dot(low, my_onehot, 1, 0).astype(bf16)

    ga_send = dot(dlow, x, 0, 0).astype(bf16).reshape(picked, dp_size, column_total)
    ga_got = lax.all_to_all(jnp.moveaxis(ga_send, 1, 0), "dp", 0, 0, tiled=True)
    g_piece = lax.dynamic_slice_in_dim(g, core_idx * piece_out, piece_out, 1)
    up_send = (adapter_scale * dot(low_wide, g_piece, 0, 0)).astype(bf16)
    up_got = lax.all_to_all(up_send.reshape(dp_size, -1, piece_out), "dp", 0, 0, tiled=True)

    a_half = lax.dynamic_slice_in_dim(a_sel, core_idx * half, half, 1)
    grad_x = (base + dot(dlow, a_half, 1, 0)).astype(bf16)
    grad_a = dot(ga_got.reshape(dp_size * picked, column_total), onehot, 0, 0)
    up_map_gradient = jnp.sum(up_got.astype(f32), axis=0)
    return grad_x, grad_a, up_map_gradient


def local(*args):
    down_maps, up_maps = args[3], args[4]
    n, tp = lax.axis_size("dp"), lax.axis_size("tensor")
    out_width = up_maps.shape[1]
    kernels_fit = (
        n == 8
        and tp == 2
        and down_maps.shape[0] == out_width
        and down_maps.shape[1] == n * up_maps.shape[0]
        and out_width % (128 * tp) == 0
        and out_width >= 4 * down_maps.shape[1]
        and args[1].shape[0] == 2 * args[0].shape[0] == down_maps.shape[1]
        and args[5].shape[1] * ADAPTER_RANK * n == 2 * down_maps.shape[1]
    )
    return (local_kernels if kernels_fit else local_plain)(*args)


def solution(mesh):
    in_specs = (
        P(("groups", "dp", "tensor"), None),
        P(("groups", "dp"), None),
        P("tensor", None),
        P(("groups", "dp"), None),
        P(("groups", "dp"), None),
        P("groups", None),
        P("groups", None),
        P("groups"),
        P("groups"),
    )
    out_specs = (
        P(("groups", "dp"), "tensor"),
        P(("groups", "dp"), None),
        P(("groups", "dp"), "tensor"),
    )
    return jax.shard_map(local, mesh=mesh, in_specs=in_specs, out_specs=out_specs, check_vma=False)
```

```python
import functools

import jax
import jax.numpy as jnp
from jax import lax
from jax.experimental import pallas as pl
from jax.experimental.pallas import tpu as pltpu
from jax.sharding import PartitionSpec as P

ADAPTER_RANK = 16
adapter_scale = 2.0

bf16, f32, i32 = jnp.bfloat16, jnp.float32, jnp.int32

HBM = pl.BlockSpec(memory_space=pltpu.HBM)
VMEM = pl.BlockSpec(memory_space=pltpu.VMEM)


def dot(a, b, ca, cb):
    return lax.dot_general(a, b, (((ca,), (cb,)), ((), ())), preferred_element_type=f32)


def params(mib):
    return pltpu.CompilerParams(vmem_limit_bytes=mib << 20)


def slot_rows(chosen_ref, slot_ref, ranks, width):
    lane = lax.broadcasted_iota(i32, (ADAPTER_RANK, width), 1)
    row = lax.broadcasted_iota(i32, (ADAPTER_RANK, width), 0)
    rows = []
    for rank in ranks:
        for k in range(chosen_ref.shape[0]):
            first = slot_ref[chosen_ref[k, rank]] * ADAPTER_RANK
            rows.append(jnp.where(lane == row + first, 1.0, 0.0))
    return jnp.concatenate(rows, axis=0).astype(bf16)


def start_all(sources, targets, sems, first=0):
    copies = [
        pltpu.make_async_copy(source, target, sems.at[first + k])
        for k, (source, target) in enumerate(zip(sources, targets))
    ]
    for copy in copies:
        copy.start()
    return copies


def wait_all(copies):
    for copy in copies:
        copy.wait()


def steps(n, turn):
    half = n // 2
    if turn == 0:
        return [(half, half + 1), (n - 1, n - 2), (2, 3), (1, 1)]
    return [(n - 1, half + 1), (2, half), (n - 2, 3), (1, 1)]


def partners(n, turn, me, core):
    return [me] + [me ^ jnp.where(core == 0, a, b) for a, b in steps(n, turn)]


def senders(n, turn, me, core):
    passed = [me ^ jnp.where(core == 0, b, a) for a, b in steps(n, turn) if a != b]
    return partners(n, turn, me, core) + passed


class Staged:
    def __init__(self, n, half, rows, picked, width, slots):
        self.n, self.half, self.rows, self.picked, self.slots = n, half, rows, picked, slots
        self.g = n * half
        self.mask = self.g + rows
        self.message = self.mask + rows
        self.shape = (self.message + picked + ADAPTER_RANK, width)

    def x(self, q):
        return pl.ds(q * self.half, self.half)

    def own_rows(self, ref):
        return ref[self.mask : self.mask + self.picked, self.slots : 2 * self.slots]

    def all_rows(self, kept):
        parts = self.n * self.picked // self.rows
        at = [pl.ds((2 + k) * self.slots, self.slots) for k in range(parts)]
        return jnp.concatenate([kept[self.rows :, k] for k in at], axis=0)


def pack_kernel(n, chosen_hbm, slot_hbm, down_hbm, up_hbm, *refs):
    count = n // 2 + 1
    send, (chosen_ref, slot_ref, down_ref, up_ref, out_ref, sems) = refs[:count], refs[count:]
    tables = start_all([chosen_hbm, slot_hbm], [chosen_ref, slot_ref], sems)
    maps = start_all([down_hbm, up_hbm], [down_ref, up_ref], sems, 2)
    ranks = partners(n, 0, lax.axis_index("dp"), lax.axis_index("tensor"))
    wait_all(tables)
    onehot = slot_rows(chosen_ref, slot_ref, ranks, down_ref.shape[1])
    picked = onehot.shape[0] // count
    wait_all(maps)
    columns = dot(onehot, down_ref[...], 1, 1).astype(bf16)
    for k in range(count):
        out_ref[k, :picked, :] = columns[k * picked : (k + 1) * picked]
        out_ref[k, picked:, :] = up_ref[...]
    wait_all(start_all([out_ref.at[k] for k in range(count)], send, sems, 4))


def stage_kernel(
    n, lay, start_hbm, chosen_hbm, slot_hbm, count_hbm, g_hbm, x_hbm, own_hbm,
    stage_hbm, start_ref, chosen_ref, slot_ref, count_ref, stage, sems,
):
    rows, picked, slots = lay.rows, lay.picked, lay.slots
    width = stage.shape[1]
    tables = start_all(
        [chosen_hbm, slot_hbm, start_hbm, count_hbm], [chosen_ref, slot_ref, start_ref, count_ref], sems
    )
    gradient = start_all([g_hbm], [stage.at[pl.ds(lay.g, rows)]], sems, 4)
    other = start_all(
        [own_hbm] + [x_hbm.at[:, pl.ds(q * width, width)] for q in range(n)],
        [stage.at[pl.ds(lay.message, picked + ADAPTER_RANK)]] + [stage.at[lay.x(q)] for q in range(n)],
        sems,
        5,
    )
    me = lax.axis_index("dp")
    wait_all(tables)
    position = lax.broadcasted_iota(i32, (rows, slots), 0)
    group = lax.broadcasted_iota(i32, (rows, slots), 1) // ADAPTER_RANK
    segment = jnp.full((rows, slots), -1, i32)
    for k in range(start_ref.shape[0]):
        segment += jnp.where(position >= start_ref[k, me], 1, 0)
    stage[lay.mask : lay.mask + rows, :slots] = jnp.where(segment == group, 1.0, 0.0).astype(bf16)
    mine = slot_rows(chosen_ref, slot_ref, [me], slots)
    stage[lay.mask : lay.mask + picked, slots : 2 * slots] = mine
    every = slot_rows(chosen_ref, slot_ref, range(n), slots)
    for k in range(n * picked // rows):
        at = pl.ds((2 + k) * slots, slots)
        stage[lay.mask : lay.mask + rows, at] = every[k * rows : (k + 1) * rows]
    wait_all(gradient)
    live = lax.broadcasted_iota(i32, (rows, width), 0) < count_ref[me]
    g = stage[lay.g : lay.g + rows, :]
    stage[lay.g : lay.g + rows, :] = jnp.where(live, g, jnp.zeros_like(g))
    wait_all(other)
    wait_all(start_all([stage], [stage_hbm], sems, 6 + n))


def hand_on_kernel(stage, out_ref):
    out_ref[...] = stage[...]


def middle_kernel(n, lay, stage, x_other, *refs):
    count = n // 2 + 1
    got, (dlow_ref, a_ref, kept_ref) = refs[: n - 1], refs[n - 1 : n + 2]
    send, (x_ref, got_ref, up_ref) = refs[n + 2 : n + 2 + count], refs[n + 2 + count :]
    me, core = lax.axis_index("dp"), lax.axis_index("tensor")
    half, rows, picked = lay.half, lay.rows, lay.picked
    width = stage.shape[1]
    mine = pl.ds(pl.multiple_of(core * half, half), half)
    other = pl.ds(pl.multiple_of((1 - core) * half, half), half)
    for q in range(n):
        x_ref[mine, q * width : (q + 1) * width] = stage[lay.x(q), :]
    x_ref[other, :] = x_other[...]
    ranks = senders(n, 0, me, core)
    got_ref[me] = stage[lay.message :, :]
    for sender, message in zip(ranks[1:], got):
        got_ref[sender] = message[...]

    in_seg = stage[lay.mask : lay.mask + rows, :picked].astype(f32) > 0.0
    g = stage[lay.g : lay.g + rows, :]
    onehot = lay.own_rows(stage)
    up_maps = got_ref[:, picked:, :].reshape(-1, width)
    b_sel = dot(onehot, up_maps, 1, 0).astype(bf16)
    dlow = jnp.where(in_seg, adapter_scale * dot(g, b_sel, 1, 1), 0.0).astype(bf16)
    dlow_ref[...] = dlow
    parts = n // 2
    a_ref[...] = got_ref[pl.ds(pl.multiple_of(core * parts, parts), parts), :picked, :]
    kept_ref[...] = stage[lay.g : lay.message, :]
    targets = partners(n, 1, me, core)
    for target, message in zip(targets, send):
        at = pl.ds(pl.multiple_of(target * width, width), width)
        message[:picked, :] = dot(dlow, x_ref[:, at], 0, 0).astype(bf16)

    low = jnp.zeros((rows, picked), f32)
    for q in range(n):
        low += dot(x_ref[:, q * width : (q + 1) * width], got_ref[q, :picked, :], 1, 1)
    low = jnp.where(in_seg, low, 0.0).astype(bf16)
    low_wide = dot(low, onehot, 1, 0).astype(bf16)
    up = (adapter_scale * dot(low_wide, g, 0, 0)).astype(bf16)
    up_ref[...] = up.reshape(up_ref.shape)
    for target, message in zip(targets, send):
        message[picked:, :] = up_ref[target]


def base_kernel(kept_ref, w_ref, out_ref):
    out_ref[...] = dot(kept_ref[: out_ref.shape[0], :], w_ref[...], 1, 1)


def grad_x_kernel(base_ref, dlow_ref, a_ref, out_hbm, out_ref, sems):
    steps, picked, width = a_ref.shape
    done = []
    for j in range(steps):
        at = pl.ds(j * width, width)
        total = base_ref[:, at] + dot(dlow_ref[...], a_ref[j], 1, 0)
        out_ref[:, at] = total.astype(bf16)
        done += start_all([out_ref.at[:, at]], [out_hbm.at[:, at]], sems, j)
    wait_all(done)


def final_kernel(n, lay, kept_ref, *refs):
    got, (a_ref, up_ref, rows_ref) = refs[:n], refs[n:]
    me, core = lax.axis_index("dp"), lax.axis_index("tensor")
    piece, picked = up_ref.shape[1], lay.picked
    for sender, message in zip(senders(n, 1, me, core), got):
        rows_ref[sender] = message[...]
    rows = rows_ref[:, :picked, :].reshape(n * picked, rows_ref.shape[2])
    a_ref[...] = dot(rows, lay.all_rows(kept_ref), 0, 0)
    at = pl.ds(pl.multiple_of(core * piece, piece), piece)
    up_ref[...] = jnp.sum(rows_ref[:, picked:, at].astype(f32), axis=0)


def exchange(messages, turn, beside):
    n = 2 * len(messages)
    got = [
        lax.ppermute(
            message,
            ("dp", "tensor"),
            [(2 * i + c, 2 * (i ^ step[c]) + c) for i in range(n) for c in range(2)],
        )
        for message, step in zip(messages, steps(n, turn))
    ]
    got[0], beside = lax.optimization_barrier((got[0], beside))
    passed = [
        lax.ppermute(message, "tensor", [(0, 1), (1, 0)])
        for message, (a, b) in zip(got, steps(n, turn))
        if a != b
    ]
    return got + passed, beside


def local_kernels(
    inputs,
    output_gradient,
    frozen_weight,
    down_maps,
    up_maps,
    segment_start,
    segment_adapter,
    adapter_slot,
    token_count,
):
    tok_half, model_width = inputs.shape
    tok_rows, out_width = output_gradient.shape
    column_total, slot_width = down_maps.shape
    half = frozen_weight.shape[0]
    n = lax.axis_size("dp")
    piece = out_width // lax.axis_size("tensor")
    segs = segment_start.shape[1]
    picked = segs * ADAPTER_RANK
    shape = jax.ShapeDtypeStruct
    message = shape((picked + ADAPTER_RANK, column_total), bf16)
    count = n // 2 + 1
    starts, chosen = segment_start.T, segment_adapter.T

    tables = [
        pltpu.SMEM(starts.shape, i32),
        pltpu.SMEM(chosen.shape, i32),
        pltpu.SMEM(adapter_slot.shape, i32),
        pltpu.SMEM(token_count.shape, i32),
    ]
    dma = pltpu.SemaphoreType.DMA

    lay = Staged(n, tok_half, tok_rows, picked, column_total, slot_width)
    own, *sent = pl.pallas_call(
        functools.partial(pack_kernel, n),
        out_shape=[message] * count,
        in_specs=[HBM] * 4,
        out_specs=[HBM] * count,
        scratch_shapes=tables[1:3]
        + [
            pltpu.VMEM(down_maps.shape, bf16),
            pltpu.VMEM(up_maps.shape, bf16),
            pltpu.VMEM((count,) + message.shape, bf16),
            dma((4 + count,)),
        ],
        compiler_params=params(56),
    )(chosen, adapter_slot, down_maps, up_maps)
    sent, x_late = lax.optimization_barrier((sent, inputs))
    x_other = lax.ppermute(x_late, "tensor", [(0, 1), (1, 0)])
    stage = pl.pallas_call(
        functools.partial(stage_kernel, n, lay),
        out_shape=shape(lay.shape, bf16),
        in_specs=[HBM] * 7,
        out_specs=HBM,
        scratch_shapes=tables + [pltpu.VMEM(lay.shape, bf16), dma((7 + n,))],
        compiler_params=params(56),
        cost_estimate=pl.CostEstimate(flops=0, bytes_accessed=1 << 21, transcendentals=0),
    )(starts, chosen, adapter_slot, token_count, output_gradient, inputs, own)
    got, stage = exchange(sent, 0, stage)
    stage = pl.pallas_call(
        hand_on_kernel,
        out_shape=shape(lay.shape, bf16),
        in_specs=[VMEM],
        out_specs=VMEM,
        compiler_params=params(8),
        cost_estimate=pl.CostEstimate(flops=0, bytes_accessed=1 << 21, transcendentals=0),
    )(stage)

    dlow, a_half, kept, own, *sent = pl.pallas_call(
        functools.partial(middle_kernel, n, lay),
        out_shape=[
            shape((tok_rows, picked), bf16),
            shape((n // 2, picked, column_total), bf16),
            shape((2 * tok_rows, out_width), bf16),
        ]
        + [message] * count,
        in_specs=[VMEM] * (1 + n),
        out_specs=[VMEM] * (3 + count),
        scratch_shapes=[
            pltpu.VMEM((tok_rows, model_width), bf16),
            pltpu.VMEM((n,) + message.shape, bf16),
            pltpu.VMEM((n, ADAPTER_RANK, out_width), bf16),
        ],
        compiler_params=params(8),
    )(stage, x_other, *got)
    base = pl.pallas_call(
        base_kernel,
        out_shape=shape((tok_rows, half), f32),
        in_specs=[VMEM, VMEM],
        out_specs=VMEM,
        compiler_params=params(8),
        cost_estimate=pl.CostEstimate(
            flops=2 * tok_rows * half * out_width,
            bytes_accessed=4 * half * tok_rows + 2 * half * out_width,
            transcendentals=0,
        ),
    )(kept, frozen_weight)
    grad_x = pl.pallas_call(
        grad_x_kernel,
        out_shape=shape((tok_rows, half), bf16),
        in_specs=[VMEM] * 3,
        out_specs=HBM,
        scratch_shapes=[pltpu.VMEM((tok_rows, half), bf16), dma((n // 2,))],
        compiler_params=params(8),
        cost_estimate=pl.CostEstimate(
            flops=2 * tok_rows * half * picked,
            bytes_accessed=6 * half * tok_rows,
            transcendentals=0,
        ),
    )(base, dlow, a_half)

    got, grad_x = exchange(sent, 1, grad_x)

    grad_a, up_map_gradient = pl.pallas_call(
        functools.partial(final_kernel, n, lay),
        out_shape=[shape((column_total, slot_width), f32), shape((ADAPTER_RANK, piece), f32)],
        in_specs=[VMEM] * (1 + n),
        out_specs=[VMEM, VMEM],
        scratch_shapes=[pltpu.VMEM((n,) + message.shape, bf16)],
        compiler_params=params(8),
    )(kept, own, *got)
    return grad_x, grad_a, up_map_gradient


def local_plain(
    inputs,
    output_gradient,
    frozen_weight,
    down_maps,
    up_maps,
    segment_start,
    segment_adapter,
    adapter_slot,
    token_count,
):
    tok_rows, out_width = output_gradient.shape
    column_total = down_maps.shape[0]
    adapter_list = adapter_slot.shape[0]
    segs = segment_start.shape[1]
    dp_size = lax.axis_size("dp")
    my_rank = lax.axis_index("dp")
    core_idx = lax.axis_index("tensor")
    picked = segs * ADAPTER_RANK
    piece_out = out_width // lax.axis_size("tensor")
    half = frozen_weight.shape[0]

    x_other = lax.ppermute(inputs, "tensor", [(0, 1), (1, 0)])
    adapter_ids = jnp.arange(adapter_list, dtype=i32)
    slot_table = jnp.sum(
        jnp.where(segment_adapter[..., None] == adapter_ids, adapter_slot, 0), axis=-1
    )
    column = slot_table[:, :, None] * ADAPTER_RANK + jnp.arange(ADAPTER_RANK, dtype=i32)
    onehot = (
        column.reshape(-1)[:, None] == jnp.arange(adapter_list * ADAPTER_RANK, dtype=i32)
    ).astype(bf16)

    a_send = dot(onehot, down_maps, 1, 1).astype(bf16).reshape(dp_size, picked, column_total)
    b_send = jnp.broadcast_to(up_maps[None], (dp_size,) + up_maps.shape)
    a_got = lax.all_to_all(a_send, "dp", 0, 0, tiled=True)
    b_got = lax.all_to_all(b_send, "dp", 0, 0, tiled=True)

    position = jnp.arange(tok_rows, dtype=i32)
    starts = lax.dynamic_index_in_dim(segment_start, my_rank, 0, keepdims=False)
    live = position < lax.dynamic_index_in_dim(token_count, my_rank, 0, keepdims=False)
    my_seg = jnp.sum((starts[None, :] <= position[:, None]).astype(i32), axis=1) - 1
    in_seg = my_seg[:, None] == (jnp.arange(picked, dtype=i32) // ADAPTER_RANK)[None, :]
    my_onehot = lax.dynamic_slice_in_dim(onehot, my_rank * picked, picked, 0)
    g = jnp.where(live[:, None], output_gradient, jnp.zeros_like(output_gradient))
    base = dot(g, frozen_weight, 1, 1)

    b_sel = dot(my_onehot, b_got.reshape(-1, out_width), 1, 0).astype(bf16)
    dlow = (adapter_scale * dot(g, b_sel, 1, 1)).astype(bf16)
    dlow = jnp.where(in_seg, dlow, jnp.zeros_like(dlow))
    a_sel = jnp.moveaxis(a_got, 0, 1).reshape(picked, -1)
    first = core_idx == 0
    x = jnp.concatenate(
        [jnp.where(first, inputs, x_other), jnp.where(first, x_other, inputs)], axis=0
    )
    low = dot(x, a_sel, 1, 1).astype(bf16)
    low = jnp.where(in_seg, low, jnp.zeros_like(low))
    low_wide = dot(low, my_onehot, 1, 0).astype(bf16)

    ga_send = dot(dlow, x, 0, 0).astype(bf16).reshape(picked, dp_size, column_total)
    ga_got = lax.all_to_all(jnp.moveaxis(ga_send, 1, 0), "dp", 0, 0, tiled=True)
    g_piece = lax.dynamic_slice_in_dim(g, core_idx * piece_out, piece_out, 1)
    up_send = (adapter_scale * dot(low_wide, g_piece, 0, 0)).astype(bf16)
    up_got = lax.all_to_all(up_send.reshape(dp_size, -1, piece_out), "dp", 0, 0, tiled=True)

    a_half = lax.dynamic_slice_in_dim(a_sel, core_idx * half, half, 1)
    grad_x = (base + dot(dlow, a_half, 1, 0)).astype(bf16)
    grad_a = dot(ga_got.reshape(dp_size * picked, column_total), onehot, 0, 0)
    up_map_gradient = jnp.sum(up_got.astype(f32), axis=0)
    return grad_x, grad_a, up_map_gradient


def local(*args):
    down_maps, up_maps = args[3], args[4]
    n, tp = lax.axis_size("dp"), lax.axis_size("tensor")
    out_width = up_maps.shape[1]
    kernels_fit = (
        n == 8
        and tp == 2
        and down_maps.shape[0] == out_width
        and down_maps.shape[1] == n * up_maps.shape[0]
        and out_width % (128 * tp) == 0
        and out_width >= 4 * down_maps.shape[1]
        and args[1].shape[0] == 2 * args[0].shape[0] == down_maps.shape[1]
        and args[5].shape[1] * ADAPTER_RANK * n == 2 * down_maps.shape[1]
    )
    return (local_kernels if kernels_fit else local_plain)(*args)


def solution(mesh):
    in_specs = (
        P(("groups", "dp", "tensor"), None),
        P(("groups", "dp"), None),
        P("tensor", None),
        P(("groups", "dp"), None),
        P(("groups", "dp"), None),
        P("groups", None),
        P("groups", None),
        P("groups"),
        P("groups"),
    )
    out_specs = (
        P(("groups", "dp"), "tensor"),
        P(("groups", "dp"), None),
        P(("groups", "dp"), "tensor"),
    )
    return jax.shard_map(local, mesh=mesh, in_specs=in_specs, out_specs=out_specs, check_vma=False)
```

```python
import functools

import jax
import jax.numpy as jnp
from jax import lax
from jax.experimental import pallas as pl
from jax.experimental.pallas import tpu as pltpu
from jax.sharding import PartitionSpec as P

ADAPTER_RANK = 16
adapter_scale = 2.0

bf16, f32, i32 = jnp.bfloat16, jnp.float32, jnp.int32

HBM = pl.BlockSpec(memory_space=pltpu.HBM)
VMEM = pl.BlockSpec(memory_space=pltpu.VMEM)


def dot(a, b, ca, cb):
    return lax.dot_general(a, b, (((ca,), (cb,)), ((), ())), preferred_element_type=f32)


def params(mib):
    return pltpu.CompilerParams(vmem_limit_bytes=mib << 20)


def slot_rows(chosen_ref, slot_ref, ranks, width):
    lane = lax.broadcasted_iota(i32, (ADAPTER_RANK, width), 1)
    row = lax.broadcasted_iota(i32, (ADAPTER_RANK, width), 0)
    rows = []
    for rank in ranks:
        for k in range(chosen_ref.shape[0]):
            first = slot_ref[chosen_ref[k, rank]] * ADAPTER_RANK
            rows.append(jnp.where(lane == row + first, 1.0, 0.0))
    return jnp.concatenate(rows, axis=0).astype(bf16)


def start_all(sources, targets, sems, first=0):
    copies = [
        pltpu.make_async_copy(source, target, sems.at[first + k])
        for k, (source, target) in enumerate(zip(sources, targets))
    ]
    for copy in copies:
        copy.start()
    return copies


def wait_all(copies):
    for copy in copies:
        copy.wait()


def steps(n, turn):
    half = n // 2
    if turn == 0:
        return [(half, half + 1), (n - 1, n - 2), (2, 3), (1, 1)]
    return [(n - 1, half + 1), (3, n - 2), (2, half), (1, 1)]


def partners(n, turn, me, core):
    return [me] + [me ^ jnp.where(core == 0, a, b) for a, b in steps(n, turn)]


def senders(n, turn, me, core):
    passed = [me ^ jnp.where(core == 0, b, a) for a, b in steps(n, turn) if a != b]
    return partners(n, turn, me, core) + passed


class Staged:
    def __init__(self, n, half, rows, picked, width, slots):
        self.n, self.half, self.rows, self.picked, self.slots = n, half, rows, picked, slots
        self.g = n * half
        self.mask = self.g + rows
        self.message = self.mask + rows
        self.shape = (self.message + picked + ADAPTER_RANK, width)

    def x(self, q):
        return pl.ds(q * self.half, self.half)

    def own_rows(self, ref):
        return ref[self.mask : self.mask + self.picked, self.slots : 2 * self.slots]

    def all_rows(self, kept):
        parts = self.n * self.picked // self.rows
        at = [pl.ds((2 + k) * self.slots, self.slots) for k in range(parts)]
        return jnp.concatenate([kept[self.rows :, k] for k in at], axis=0)


def pack_kernel(n, chosen_hbm, slot_hbm, down_hbm, up_hbm, *refs):
    count = n // 2 + 1
    send, (chosen_ref, slot_ref, down_ref, up_ref, out_ref, sems) = refs[:count], refs[count:]
    tables = start_all([chosen_hbm, slot_hbm], [chosen_ref, slot_ref], sems)
    maps = start_all([down_hbm, up_hbm], [down_ref, up_ref], sems, 2)
    ranks = partners(n, 0, lax.axis_index("dp"), lax.axis_index("tensor"))
    wait_all(tables)
    onehot = slot_rows(chosen_ref, slot_ref, ranks, down_ref.shape[1])
    picked = onehot.shape[0] // count
    wait_all(maps)
    columns = dot(onehot, down_ref[...], 1, 1).astype(bf16)
    for k in range(count):
        out_ref[k, :picked, :] = columns[k * picked : (k + 1) * picked]
        out_ref[k, picked:, :] = up_ref[...]
    wait_all(start_all([out_ref.at[k] for k in range(count)], send, sems, 4))


def stage_kernel(
    n, lay, start_hbm, chosen_hbm, slot_hbm, count_hbm, g_hbm, x_hbm, own_hbm,
    stage_hbm, start_ref, chosen_ref, slot_ref, count_ref, stage, sems,
):
    rows, picked, slots = lay.rows, lay.picked, lay.slots
    width = stage.shape[1]
    tables = start_all(
        [chosen_hbm, slot_hbm, start_hbm, count_hbm], [chosen_ref, slot_ref, start_ref, count_ref], sems
    )
    gradient = start_all([g_hbm], [stage.at[pl.ds(lay.g, rows)]], sems, 4)
    other = start_all(
        [own_hbm] + [x_hbm.at[:, pl.ds(q * width, width)] for q in range(n)],
        [stage.at[pl.ds(lay.message, picked + ADAPTER_RANK)]] + [stage.at[lay.x(q)] for q in range(n)],
        sems,
        5,
    )
    me = lax.axis_index("dp")
    wait_all(tables)
    position = lax.broadcasted_iota(i32, (rows, slots), 0)
    group = lax.broadcasted_iota(i32, (rows, slots), 1) // ADAPTER_RANK
    segment = jnp.full((rows, slots), -1, i32)
    for k in range(start_ref.shape[0]):
        segment += jnp.where(position >= start_ref[k, me], 1, 0)
    stage[lay.mask : lay.mask + rows, :slots] = jnp.where(segment == group, 1.0, 0.0).astype(bf16)
    mine = slot_rows(chosen_ref, slot_ref, [me], slots)
    stage[lay.mask : lay.mask + picked, slots : 2 * slots] = mine
    every = slot_rows(chosen_ref, slot_ref, range(n), slots)
    for k in range(n * picked // rows):
        at = pl.ds((2 + k) * slots, slots)
        stage[lay.mask : lay.mask + rows, at] = every[k * rows : (k + 1) * rows]
    wait_all(gradient)
    live = lax.broadcasted_iota(i32, (rows, width), 0) < count_ref[me]
    g = stage[lay.g : lay.g + rows, :]
    stage[lay.g : lay.g + rows, :] = jnp.where(live, g, jnp.zeros_like(g))
    wait_all(other)
    wait_all(start_all([stage], [stage_hbm], sems, 6 + n))


def hand_on_kernel(stage, out_ref):
    out_ref[...] = stage[...]


def middle_kernel(n, lay, stage, x_other, *refs):
    count = n // 2 + 1
    got, (dlow_ref, a_ref, kept_ref) = refs[: n - 1], refs[n - 1 : n + 2]
    send, (x_ref, got_ref, up_ref) = refs[n + 2 : n + 2 + count], refs[n + 2 + count :]
    me, core = lax.axis_index("dp"), lax.axis_index("tensor")
    half, rows, picked = lay.half, lay.rows, lay.picked
    width = stage.shape[1]
    mine = pl.ds(pl.multiple_of(core * half, half), half)
    other = pl.ds(pl.multiple_of((1 - core) * half, half), half)
    for q in range(n):
        x_ref[mine, q * width : (q + 1) * width] = stage[lay.x(q), :]
    x_ref[other, :] = x_other[...]
    ranks = senders(n, 0, me, core)
    got_ref[me] = stage[lay.message :, :]
    for sender, message in zip(ranks[1:], got):
        got_ref[sender] = message[...]

    in_seg = stage[lay.mask : lay.mask + rows, :picked].astype(f32) > 0.0
    g = stage[lay.g : lay.g + rows, :]
    onehot = lay.own_rows(stage)
    up_maps = got_ref[:, picked:, :].reshape(-1, width)
    b_sel = dot(onehot, up_maps, 1, 0).astype(bf16)
    dlow = jnp.where(in_seg, adapter_scale * dot(g, b_sel, 1, 1), 0.0).astype(bf16)
    dlow_ref[...] = dlow
    parts = n // 2
    a_ref[...] = got_ref[pl.ds(pl.multiple_of(core * parts, parts), parts), :picked, :]
    kept_ref[...] = stage[lay.g : lay.message, :]
    targets = partners(n, 1, me, core)
    for target, message in zip(targets, send):
        at = pl.ds(pl.multiple_of(target * width, width), width)
        message[:picked, :] = dot(dlow, x_ref[:, at], 0, 0).astype(bf16)

    low = jnp.zeros((rows, picked), f32)
    for q in range(n):
        low += dot(x_ref[:, q * width : (q + 1) * width], got_ref[q, :picked, :], 1, 1)
    low = jnp.where(in_seg, low, 0.0).astype(bf16)
    low_wide = dot(low, onehot, 1, 0).astype(bf16)
    up = (adapter_scale * dot(low_wide, g, 0, 0)).astype(bf16)
    up_ref[...] = up.reshape(up_ref.shape)
    for target, message in zip(targets, send):
        message[picked:, :] = up_ref[target]


def base_kernel(kept_ref, w_ref, out_ref):
    out_ref[...] = dot(kept_ref[: out_ref.shape[0], :], w_ref[...], 1, 1)


def grad_x_kernel(base_ref, dlow_ref, a_ref, out_hbm, out_ref, sems):
    steps, picked, width = a_ref.shape
    done = []
    for j in range(steps):
        at = pl.ds(j * width, width)
        total = base_ref[:, at] + dot(dlow_ref[...], a_ref[j], 1, 0)
        out_ref[:, at] = total.astype(bf16)
        done += start_all([out_ref.at[:, at]], [out_hbm.at[:, at]], sems, j)
    wait_all(done)


def final_kernel(n, lay, kept_ref, *refs):
    got, (a_ref, up_ref, rows_ref) = refs[:n], refs[n:]
    me, core = lax.axis_index("dp"), lax.axis_index("tensor")
    piece, picked = up_ref.shape[1], lay.picked
    for sender, message in zip(senders(n, 1, me, core), got):
        rows_ref[sender] = message[...]
    rows = rows_ref[:, :picked, :].reshape(n * picked, rows_ref.shape[2])
    a_ref[...] = dot(rows, lay.all_rows(kept_ref), 0, 0)
    at = pl.ds(pl.multiple_of(core * piece, piece), piece)
    up_ref[...] = jnp.sum(rows_ref[:, picked:, at].astype(f32), axis=0)


def exchange(messages, turn, beside):
    n = 2 * len(messages)
    got = [
        lax.ppermute(
            message,
            ("dp", "tensor"),
            [(2 * i + c, 2 * (i ^ step[c]) + c) for i in range(n) for c in range(2)],
        )
        for message, step in zip(messages, steps(n, turn))
    ]
    got[0], beside = lax.optimization_barrier((got[0], beside))
    passed = [
        lax.ppermute(message, "tensor", [(0, 1), (1, 0)])
        for message, (a, b) in zip(got, steps(n, turn))
        if a != b
    ]
    return got + passed, beside


def local_kernels(
    inputs,
    output_gradient,
    frozen_weight,
    down_maps,
    up_maps,
    segment_start,
    segment_adapter,
    adapter_slot,
    token_count,
):
    tok_half, model_width = inputs.shape
    tok_rows, out_width = output_gradient.shape
    column_total, slot_width = down_maps.shape
    half = frozen_weight.shape[0]
    n = lax.axis_size("dp")
    piece = out_width // lax.axis_size("tensor")
    segs = segment_start.shape[1]
    picked = segs * ADAPTER_RANK
    shape = jax.ShapeDtypeStruct
    message = shape((picked + ADAPTER_RANK, column_total), bf16)
    count = n // 2 + 1
    starts, chosen = segment_start.T, segment_adapter.T

    tables = [
        pltpu.SMEM(starts.shape, i32),
        pltpu.SMEM(chosen.shape, i32),
        pltpu.SMEM(adapter_slot.shape, i32),
        pltpu.SMEM(token_count.shape, i32),
    ]
    dma = pltpu.SemaphoreType.DMA

    lay = Staged(n, tok_half, tok_rows, picked, column_total, slot_width)
    own, *sent = pl.pallas_call(
        functools.partial(pack_kernel, n),
        out_shape=[message] * count,
        in_specs=[HBM] * 4,
        out_specs=[HBM] * count,
        scratch_shapes=tables[1:3]
        + [
            pltpu.VMEM(down_maps.shape, bf16),
            pltpu.VMEM(up_maps.shape, bf16),
            pltpu.VMEM((count,) + message.shape, bf16),
            dma((4 + count,)),
        ],
        compiler_params=params(56),
    )(chosen, adapter_slot, down_maps, up_maps)
    sent, x_late = lax.optimization_barrier((sent, inputs))
    x_other = lax.ppermute(x_late, "tensor", [(0, 1), (1, 0)])
    stage = pl.pallas_call(
        functools.partial(stage_kernel, n, lay),
        out_shape=shape(lay.shape, bf16),
        in_specs=[HBM] * 7,
        out_specs=HBM,
        scratch_shapes=tables + [pltpu.VMEM(lay.shape, bf16), dma((7 + n,))],
        compiler_params=params(56),
        cost_estimate=pl.CostEstimate(flops=0, bytes_accessed=1 << 21, transcendentals=0),
    )(starts, chosen, adapter_slot, token_count, output_gradient, inputs, own)
    got, stage = exchange(sent, 0, stage)
    stage = pl.pallas_call(
        hand_on_kernel,
        out_shape=shape(lay.shape, bf16),
        in_specs=[VMEM],
        out_specs=VMEM,
        compiler_params=params(8),
        cost_estimate=pl.CostEstimate(flops=0, bytes_accessed=1 << 21, transcendentals=0),
    )(stage)

    dlow, a_half, kept, own, *sent = pl.pallas_call(
        functools.partial(middle_kernel, n, lay),
        out_shape=[
            shape((tok_rows, picked), bf16),
            shape((n // 2, picked, column_total), bf16),
            shape((2 * tok_rows, out_width), bf16),
        ]
        + [message] * count,
        in_specs=[VMEM] * (1 + n),
        out_specs=[VMEM] * (3 + count),
        scratch_shapes=[
            pltpu.VMEM((tok_rows, model_width), bf16),
            pltpu.VMEM((n,) + message.shape, bf16),
            pltpu.VMEM((n, ADAPTER_RANK, out_width), bf16),
        ],
        compiler_params=params(8),
    )(stage, x_other, *got)
    base = pl.pallas_call(
        base_kernel,
        out_shape=shape((tok_rows, half), f32),
        in_specs=[VMEM, VMEM],
        out_specs=VMEM,
        compiler_params=params(8),
        cost_estimate=pl.CostEstimate(
            flops=2 * tok_rows * half * out_width,
            bytes_accessed=4 * half * tok_rows + 2 * half * out_width,
            transcendentals=0,
        ),
    )(kept, frozen_weight)
    grad_x = pl.pallas_call(
        grad_x_kernel,
        out_shape=shape((tok_rows, half), bf16),
        in_specs=[VMEM] * 3,
        out_specs=HBM,
        scratch_shapes=[pltpu.VMEM((tok_rows, half), bf16), dma((n // 2,))],
        compiler_params=params(8),
        cost_estimate=pl.CostEstimate(
            flops=2 * tok_rows * half * picked,
            bytes_accessed=6 * half * tok_rows,
            transcendentals=0,
        ),
    )(base, dlow, a_half)

    got, grad_x = exchange(sent, 1, grad_x)

    grad_a, up_map_gradient = pl.pallas_call(
        functools.partial(final_kernel, n, lay),
        out_shape=[shape((column_total, slot_width), f32), shape((ADAPTER_RANK, piece), f32)],
        in_specs=[VMEM] * (1 + n),
        out_specs=[VMEM, VMEM],
        scratch_shapes=[pltpu.VMEM((n,) + message.shape, bf16)],
        compiler_params=params(8),
    )(kept, own, *got)
    return grad_x, grad_a, up_map_gradient


def local_plain(
    inputs,
    output_gradient,
    frozen_weight,
    down_maps,
    up_maps,
    segment_start,
    segment_adapter,
    adapter_slot,
    token_count,
):
    tok_rows, out_width = output_gradient.shape
    column_total = down_maps.shape[0]
    adapter_list = adapter_slot.shape[0]
    segs = segment_start.shape[1]
    dp_size = lax.axis_size("dp")
    my_rank = lax.axis_index("dp")
    core_idx = lax.axis_index("tensor")
    picked = segs * ADAPTER_RANK
    piece_out = out_width // lax.axis_size("tensor")
    half = frozen_weight.shape[0]

    x_other = lax.ppermute(inputs, "tensor", [(0, 1), (1, 0)])
    adapter_ids = jnp.arange(adapter_list, dtype=i32)
    slot_table = jnp.sum(
        jnp.where(segment_adapter[..., None] == adapter_ids, adapter_slot, 0), axis=-1
    )
    column = slot_table[:, :, None] * ADAPTER_RANK + jnp.arange(ADAPTER_RANK, dtype=i32)
    onehot = (
        column.reshape(-1)[:, None] == jnp.arange(adapter_list * ADAPTER_RANK, dtype=i32)
    ).astype(bf16)

    a_send = dot(onehot, down_maps, 1, 1).astype(bf16).reshape(dp_size, picked, column_total)
    b_send = jnp.broadcast_to(up_maps[None], (dp_size,) + up_maps.shape)
    a_got = lax.all_to_all(a_send, "dp", 0, 0, tiled=True)
    b_got = lax.all_to_all(b_send, "dp", 0, 0, tiled=True)

    position = jnp.arange(tok_rows, dtype=i32)
    starts = lax.dynamic_index_in_dim(segment_start, my_rank, 0, keepdims=False)
    live = position < lax.dynamic_index_in_dim(token_count, my_rank, 0, keepdims=False)
    my_seg = jnp.sum((starts[None, :] <= position[:, None]).astype(i32), axis=1) - 1
    in_seg = my_seg[:, None] == (jnp.arange(picked, dtype=i32) // ADAPTER_RANK)[None, :]
    my_onehot = lax.dynamic_slice_in_dim(onehot, my_rank * picked, picked, 0)
    g = jnp.where(live[:, None], output_gradient, jnp.zeros_like(output_gradient))
    base = dot(g, frozen_weight, 1, 1)

    b_sel = dot(my_onehot, b_got.reshape(-1, out_width), 1, 0).astype(bf16)
    dlow = (adapter_scale * dot(g, b_sel, 1, 1)).astype(bf16)
    dlow = jnp.where(in_seg, dlow, jnp.zeros_like(dlow))
    a_sel = jnp.moveaxis(a_got, 0, 1).reshape(picked, -1)
    first = core_idx == 0
    x = jnp.concatenate(
        [jnp.where(first, inputs, x_other), jnp.where(first, x_other, inputs)], axis=0
    )
    low = dot(x, a_sel, 1, 1).astype(bf16)
    low = jnp.where(in_seg, low, jnp.zeros_like(low))
    low_wide = dot(low, my_onehot, 1, 0).astype(bf16)

    ga_send = dot(dlow, x, 0, 0).astype(bf16).reshape(picked, dp_size, column_total)
    ga_got = lax.all_to_all(jnp.moveaxis(ga_send, 1, 0), "dp", 0, 0, tiled=True)
    g_piece = lax.dynamic_slice_in_dim(g, core_idx * piece_out, piece_out, 1)
    up_send = (adapter_scale * dot(low_wide, g_piece, 0, 0)).astype(bf16)
    up_got = lax.all_to_all(up_send.reshape(dp_size, -1, piece_out), "dp", 0, 0, tiled=True)

    a_half = lax.dynamic_slice_in_dim(a_sel, core_idx * half, half, 1)
    grad_x = (base + dot(dlow, a_half, 1, 0)).astype(bf16)
    grad_a = dot(ga_got.reshape(dp_size * picked, column_total), onehot, 0, 0)
    up_map_gradient = jnp.sum(up_got.astype(f32), axis=0)
    return grad_x, grad_a, up_map_gradient


def local(*args):
    down_maps, up_maps = args[3], args[4]
    n, tp = lax.axis_size("dp"), lax.axis_size("tensor")
    out_width = up_maps.shape[1]
    kernels_fit = (
        n == 8
        and tp == 2
        and down_maps.shape[0] == out_width
        and down_maps.shape[1] == n * up_maps.shape[0]
        and out_width % (128 * tp) == 0
        and out_width >= 4 * down_maps.shape[1]
        and args[1].shape[0] == 2 * args[0].shape[0] == down_maps.shape[1]
        and args[5].shape[1] * ADAPTER_RANK * n == 2 * down_maps.shape[1]
    )
    return (local_kernels if kernels_fit else local_plain)(*args)


def solution(mesh):
    in_specs = (
        P(("groups", "dp", "tensor"), None),
        P(("groups", "dp"), None),
        P("tensor", None),
        P(("groups", "dp"), None),
        P(("groups", "dp"), None),
        P("groups", None),
        P("groups", None),
        P("groups"),
        P("groups"),
    )
    out_specs = (
        P(("groups", "dp"), "tensor"),
        P(("groups", "dp"), None),
        P(("groups", "dp"), "tensor"),
    )
    return jax.shard_map(local, mesh=mesh, in_specs=in_specs, out_specs=out_specs, check_vma=False)
```

```python
import functools

import jax
import jax.numpy as jnp
from jax import lax
from jax.experimental import pallas as pl
from jax.experimental.pallas import tpu as pltpu
from jax.sharding import PartitionSpec as P

ADAPTER_RANK = 16
adapter_scale = 2.0

bf16, f32, i32 = jnp.bfloat16, jnp.float32, jnp.int32

HBM = pl.BlockSpec(memory_space=pltpu.HBM)
VMEM = pl.BlockSpec(memory_space=pltpu.VMEM)


def dot(a, b, ca, cb):
    return lax.dot_general(a, b, (((ca,), (cb,)), ((), ())), preferred_element_type=f32)


def params(mib):
    return pltpu.CompilerParams(vmem_limit_bytes=mib << 20)


def slot_rows(chosen_ref, slot_ref, ranks, width):
    lane = lax.broadcasted_iota(i32, (ADAPTER_RANK, width), 1)
    row = lax.broadcasted_iota(i32, (ADAPTER_RANK, width), 0)
    rows = []
    for rank in ranks:
        for k in range(chosen_ref.shape[0]):
            first = slot_ref[chosen_ref[k, rank]] * ADAPTER_RANK
            rows.append(jnp.where(lane == row + first, 1.0, 0.0))
    return jnp.concatenate(rows, axis=0).astype(bf16)


def start_all(sources, targets, sems, first=0):
    copies = [
        pltpu.make_async_copy(source, target, sems.at[first + k])
        for k, (source, target) in enumerate(zip(sources, targets))
    ]
    for copy in copies:
        copy.start()
    return copies


def wait_all(copies):
    for copy in copies:
        copy.wait()


def steps(n, turn):
    half = n // 2
    if turn == 0:
        return [(n - 1, half + 1), (3, n - 2), (2, half), (1, 1)]
    return [(n - 1, half + 1), (3, n - 2), (2, half), (1, 1)]


def partners(n, turn, me, core):
    return [me] + [me ^ jnp.where(core == 0, a, b) for a, b in steps(n, turn)]


def senders(n, turn, me, core):
    passed = [me ^ jnp.where(core == 0, b, a) for a, b in steps(n, turn) if a != b]
    return partners(n, turn, me, core) + passed


def pack_kernel(n, chosen_hbm, slot_hbm, down_hbm, up_hbm, *refs):
    count = n // 2 + 1
    send, (chosen_ref, slot_ref, down_ref, up_ref, out_ref, sems) = refs[:count], refs[count:]
    tables = start_all([chosen_hbm, slot_hbm], [chosen_ref, slot_ref], sems)
    maps = start_all([down_hbm, up_hbm], [down_ref, up_ref], sems, 2)
    ranks = partners(n, 0, lax.axis_index("dp"), lax.axis_index("tensor"))
    wait_all(tables)
    onehot = slot_rows(chosen_ref, slot_ref, ranks, down_ref.shape[1])
    picked = onehot.shape[0] // count
    wait_all(maps)
    columns = dot(onehot, down_ref[...], 1, 1).astype(bf16)
    for k in range(count):
        out_ref[k, :picked, :] = columns[k * picked : (k + 1) * picked]
        out_ref[k, picked:, :] = up_ref[...]
    wait_all(start_all([out_ref.at[k] for k in range(count)], send, sems, 4))


def table_kernel(
    n, picked, start_hbm, chosen_hbm, slot_hbm, count_hbm, out_hbm, start_ref, chosen_ref, slot_ref, count_ref, out_ref, sems,
):
    rows, width = out_ref.shape
    slots = width // 4
    wait_all(
        start_all(
            [start_hbm, chosen_hbm, slot_hbm, count_hbm], [start_ref, chosen_ref, slot_ref, count_ref], sems
        )
    )
    me = lax.axis_index("dp")
    position = lax.broadcasted_iota(i32, (rows, slots), 0)
    group = lax.broadcasted_iota(i32, (rows, slots), 1) // ADAPTER_RANK
    segs = start_ref.shape[0]
    segment = jnp.full((rows, slots), -1, i32)
    for k in range(segs):
        segment += jnp.where(position >= start_ref[k, me], 1, 0)
    flag = (segment == group) | ((group == segs) & (position < count_ref[me]))
    out_ref[:, :slots] = jnp.where(flag, 1.0, 0.0).astype(bf16)
    out_ref[:picked, slots : 2 * slots] = slot_rows(chosen_ref, slot_ref, [me], slots)
    every = slot_rows(chosen_ref, slot_ref, range(n), slots)
    out_ref[:, 2 * slots : 3 * slots] = every[:rows]
    out_ref[:, 3 * slots :] = every[rows:]
    wait_all(start_all([out_ref], [out_hbm], sems, 4))


def hand_on_kernel(in_ref, out_ref):
    out_ref[...] = in_ref[...]


def middle_kernel(n, table_ref, g_ref, x_mine, x_other, own_ref, *refs):
    count = n // 2 + 1
    got, (dlow_ref, a_ref, kept_ref) = refs[: n - 1], refs[n - 1 : n + 2]
    send, (x_ref, got_ref, up_ref) = refs[n + 2 : n + 2 + count], refs[n + 2 + count :]
    me, core = lax.axis_index("dp"), lax.axis_index("tensor")
    half = x_mine.shape[0]
    rows, picked = dlow_ref.shape
    width = g_ref.shape[1]
    slots = width // 4
    x_ref[pl.ds(pl.multiple_of(core * half, half), half), :] = x_mine[...]
    x_ref[pl.ds(pl.multiple_of((1 - core) * half, half), half), :] = x_other[...]
    for sender, message in zip(senders(n, 0, me, core), (own_ref,) + got):
        got_ref[sender] = message[...]

    flags = table_ref[:, :slots].astype(f32)
    in_seg = flags[:, :picked] > 0.0
    live = flags[:, picked : picked + 1] > 0.0
    g = jnp.where(live, g_ref[...], jnp.zeros(g_ref.shape, bf16))
    onehot = table_ref[:picked, slots : 2 * slots]
    up_maps = got_ref[:, picked:, :].reshape(-1, width)
    b_sel = dot(onehot, up_maps, 1, 0).astype(bf16)
    dlow = jnp.where(in_seg, adapter_scale * dot(g, b_sel, 1, 1), 0.0).astype(bf16)
    dlow_ref[...] = dlow
    parts = n // 2
    a_ref[...] = got_ref[pl.ds(pl.multiple_of(core * parts, parts), parts), :picked, :]
    kept_ref[:rows, :] = g
    kept_ref[rows:, :] = table_ref[...]
    targets = partners(n, 1, me, core)
    for target, message in zip(targets, send):
        at = pl.ds(pl.multiple_of(target * width, width), width)
        message[:picked, :] = dot(dlow, x_ref[:, at], 0, 0).astype(bf16)

    low = jnp.zeros((rows, picked), f32)
    for q in range(n):
        low += dot(x_ref[:, q * width : (q + 1) * width], got_ref[q, :picked, :], 1, 1)
    low = jnp.where(in_seg, low, 0.0).astype(bf16)
    low_wide = dot(low, onehot, 1, 0).astype(bf16)
    up = (adapter_scale * dot(low_wide, g, 0, 0)).astype(bf16)
    up_ref[...] = up.reshape(up_ref.shape)
    for target, message in zip(targets, send):
        message[picked:, :] = up_ref[target]


def base_kernel(kept_ref, w_ref, out_ref):
    out_ref[...] = dot(kept_ref[: out_ref.shape[0], :], w_ref[...], 1, 1)


def grad_x_kernel(base_ref, dlow_ref, a_ref, out_hbm, out_ref, sems):
    steps, picked, width = a_ref.shape
    done = []
    for j in range(steps):
        at = pl.ds(j * width, width)
        total = base_ref[:, at] + dot(dlow_ref[...], a_ref[j], 1, 0)
        out_ref[:, at] = total.astype(bf16)
        done += start_all([out_ref.at[:, at]], [out_hbm.at[:, at]], sems, j)
    wait_all(done)


def final_kernel(n, kept_ref, *refs):
    got, (a_ref, up_ref, rows_ref) = refs[:n], refs[n:]
    me, core = lax.axis_index("dp"), lax.axis_index("tensor")
    piece, picked = up_ref.shape[1], rows_ref.shape[1] - ADAPTER_RANK
    rows, slots = kept_ref.shape[0] // 2, kept_ref.shape[1] // 4
    for sender, message in zip(senders(n, 1, me, core), got):
        rows_ref[sender] = message[...]
    sums = rows_ref[:, :picked, :].reshape(n * picked, rows_ref.shape[2])
    onehot = jnp.concatenate(
        [kept_ref[rows:, 2 * slots : 3 * slots], kept_ref[rows:, 3 * slots :]], axis=0
    )
    a_ref[...] = dot(sums, onehot, 0, 0)
    at = pl.ds(pl.multiple_of(core * piece, piece), piece)
    up_ref[...] = jnp.sum(rows_ref[:, picked:, at].astype(f32), axis=0)


def swap(array):
    return lax.ppermute(array, "tensor", [(0, 1), (1, 0)])


def exchange(messages, turn, beside):
    n = 2 * len(messages)
    got = [
        lax.ppermute(
            message,
            ("dp", "tensor"),
            [(2 * i + c, 2 * (i ^ step[c]) + c) for i in range(n) for c in range(2)],
        )
        for message, step in zip(messages, steps(n, turn))
    ]
    got[0], beside = lax.optimization_barrier((got[0], beside))
    passed = [
        swap(message)
        for message, (a, b) in zip(got, steps(n, turn))
        if a != b
    ]
    return got + passed, beside


def local_kernels(
    inputs,
    output_gradient,
    frozen_weight,
    down_maps,
    up_maps,
    segment_start,
    segment_adapter,
    adapter_slot,
    token_count,
):
    model_width = inputs.shape[1]
    tok_rows, out_width = output_gradient.shape
    column_total, slot_width = down_maps.shape
    half = frozen_weight.shape[0]
    n = lax.axis_size("dp")
    piece = out_width // lax.axis_size("tensor")
    segs = segment_start.shape[1]
    picked = segs * ADAPTER_RANK
    shape = jax.ShapeDtypeStruct
    message = shape((picked + ADAPTER_RANK, column_total), bf16)
    count = n // 2 + 1
    starts, chosen = segment_start.T, segment_adapter.T

    tables = [
        pltpu.SMEM(starts.shape, i32),
        pltpu.SMEM(chosen.shape, i32),
        pltpu.SMEM(adapter_slot.shape, i32),
        pltpu.SMEM(token_count.shape, i32),
    ]
    dma = pltpu.SemaphoreType.DMA

    own, *sent = pl.pallas_call(
        functools.partial(pack_kernel, n),
        out_shape=[message] * count,
        in_specs=[HBM] * 4,
        out_specs=[HBM] * count,
        scratch_shapes=tables[1:3]
        + [
            pltpu.VMEM(down_maps.shape, bf16),
            pltpu.VMEM(up_maps.shape, bf16),
            pltpu.VMEM((count,) + message.shape, bf16),
            dma((4 + count,)),
        ],
        compiler_params=params(56),
    )(chosen, adapter_slot, down_maps, up_maps)
    table = pl.pallas_call(
        functools.partial(table_kernel, n, picked),
        out_shape=shape((tok_rows, 4 * slot_width), bf16),
        in_specs=[HBM] * 4,
        out_specs=HBM,
        scratch_shapes=tables + [pltpu.VMEM((tok_rows, 4 * slot_width), bf16), dma((5,))],
        compiler_params=params(56),
        cost_estimate=pl.CostEstimate(flops=0, bytes_accessed=1 << 21, transcendentals=0),
    )(starts, chosen, adapter_slot, token_count)
    sent, x_late, g_late = lax.optimization_barrier((sent, inputs, output_gradient))
    x_other = swap(x_late)
    g = swap(g_late)
    own = swap(own)
    got, table = exchange(sent, 0, table)
    table = swap(table)
    x_mine = pl.pallas_call(
        hand_on_kernel,
        out_shape=shape(inputs.shape, bf16),
        in_specs=[VMEM],
        out_specs=VMEM,
        compiler_params=params(8),
        cost_estimate=pl.CostEstimate(flops=0, bytes_accessed=1 << 21, transcendentals=0),
    )(inputs)

    dlow, a_half, kept, own, *sent = pl.pallas_call(
        functools.partial(middle_kernel, n),
        out_shape=[
            shape((tok_rows, picked), bf16),
            shape((n // 2, picked, column_total), bf16),
            shape((2 * tok_rows, out_width), bf16),
        ]
        + [message] * count,
        in_specs=[VMEM] * (4 + n),
        out_specs=[VMEM] * (3 + count),
        scratch_shapes=[
            pltpu.VMEM((tok_rows, model_width), bf16),
            pltpu.VMEM((n,) + message.shape, bf16),
            pltpu.VMEM((n, ADAPTER_RANK, out_width), bf16),
        ],
        compiler_params=params(8),
        cost_estimate=pl.CostEstimate(
            flops=6 * tok_rows * model_width * picked,
            bytes_accessed=4 * tok_rows * model_width,
            transcendentals=0,
        ),
    )(table, g, x_mine, x_other, own, *got)
    base = pl.pallas_call(
        base_kernel,
        out_shape=shape((tok_rows, half), f32),
        in_specs=[VMEM, VMEM],
        out_specs=VMEM,
        compiler_params=params(8),
        cost_estimate=pl.CostEstimate(
            flops=2 * tok_rows * half * out_width,
            bytes_accessed=4 * half * tok_rows + 2 * half * out_width,
            transcendentals=0,
        ),
    )(kept, frozen_weight)
    grad_x = pl.pallas_call(
        grad_x_kernel,
        out_shape=shape((tok_rows, half), bf16),
        in_specs=[VMEM] * 3,
        out_specs=HBM,
        scratch_shapes=[pltpu.VMEM((tok_rows, half), bf16), dma((n // 2,))],
        compiler_params=params(8),
        cost_estimate=pl.CostEstimate(
            flops=2 * tok_rows * half * picked,
            bytes_accessed=6 * half * tok_rows,
            transcendentals=0,
        ),
    )(base, dlow, a_half)

    got, grad_x = exchange(sent, 1, grad_x)

    grad_a, up_map_gradient = pl.pallas_call(
        functools.partial(final_kernel, n),
        out_shape=[shape((column_total, slot_width), f32), shape((ADAPTER_RANK, piece), f32)],
        in_specs=[VMEM] * (1 + n),
        out_specs=[VMEM, VMEM],
        scratch_shapes=[pltpu.VMEM((n,) + message.shape, bf16)],
        compiler_params=params(8),
    )(kept, own, *got)
    return grad_x, grad_a, up_map_gradient


def local_plain(
    inputs,
    output_gradient,
    frozen_weight,
    down_maps,
    up_maps,
    segment_start,
    segment_adapter,
    adapter_slot,
    token_count,
):
    tok_rows, out_width = output_gradient.shape
    column_total = down_maps.shape[0]
    adapter_list = adapter_slot.shape[0]
    segs = segment_start.shape[1]
    dp_size = lax.axis_size("dp")
    my_rank = lax.axis_index("dp")
    core_idx = lax.axis_index("tensor")
    picked = segs * ADAPTER_RANK
    piece_out = out_width // lax.axis_size("tensor")
    half = frozen_weight.shape[0]

    x_other = lax.ppermute(inputs, "tensor", [(0, 1), (1, 0)])
    adapter_ids = jnp.arange(adapter_list, dtype=i32)
    slot_table = jnp.sum(
        jnp.where(segment_adapter[..., None] == adapter_ids, adapter_slot, 0), axis=-1
    )
    column = slot_table[:, :, None] * ADAPTER_RANK + jnp.arange(ADAPTER_RANK, dtype=i32)
    onehot = (
        column.reshape(-1)[:, None] == jnp.arange(adapter_list * ADAPTER_RANK, dtype=i32)
    ).astype(bf16)

    a_send = dot(onehot, down_maps, 1, 1).astype(bf16).reshape(dp_size, picked, column_total)
    b_send = jnp.broadcast_to(up_maps[None], (dp_size,) + up_maps.shape)
    a_got = lax.all_to_all(a_send, "dp", 0, 0, tiled=True)
    b_got = lax.all_to_all(b_send, "dp", 0, 0, tiled=True)

    position = jnp.arange(tok_rows, dtype=i32)
    starts = lax.dynamic_index_in_dim(segment_start, my_rank, 0, keepdims=False)
    live = position < lax.dynamic_index_in_dim(token_count, my_rank, 0, keepdims=False)
    my_seg = jnp.sum((starts[None, :] <= position[:, None]).astype(i32), axis=1) - 1
    in_seg = my_seg[:, None] == (jnp.arange(picked, dtype=i32) // ADAPTER_RANK)[None, :]
    my_onehot = lax.dynamic_slice_in_dim(onehot, my_rank * picked, picked, 0)
    g = jnp.where(live[:, None], output_gradient, jnp.zeros_like(output_gradient))
    base = dot(g, frozen_weight, 1, 1)

    b_sel = dot(my_onehot, b_got.reshape(-1, out_width), 1, 0).astype(bf16)
    dlow = (adapter_scale * dot(g, b_sel, 1, 1)).astype(bf16)
    dlow = jnp.where(in_seg, dlow, jnp.zeros_like(dlow))
    a_sel = jnp.moveaxis(a_got, 0, 1).reshape(picked, -1)
    first = core_idx == 0
    x = jnp.concatenate(
        [jnp.where(first, inputs, x_other), jnp.where(first, x_other, inputs)], axis=0
    )
    low = dot(x, a_sel, 1, 1).astype(bf16)
    low = jnp.where(in_seg, low, jnp.zeros_like(low))
    low_wide = dot(low, my_onehot, 1, 0).astype(bf16)

    ga_send = dot(dlow, x, 0, 0).astype(bf16).reshape(picked, dp_size, column_total)
    ga_got = lax.all_to_all(jnp.moveaxis(ga_send, 1, 0), "dp", 0, 0, tiled=True)
    g_piece = lax.dynamic_slice_in_dim(g, core_idx * piece_out, piece_out, 1)
    up_send = (adapter_scale * dot(low_wide, g_piece, 0, 0)).astype(bf16)
    up_got = lax.all_to_all(up_send.reshape(dp_size, -1, piece_out), "dp", 0, 0, tiled=True)

    a_half = lax.dynamic_slice_in_dim(a_sel, core_idx * half, half, 1)
    grad_x = (base + dot(dlow, a_half, 1, 0)).astype(bf16)
    grad_a = dot(ga_got.reshape(dp_size * picked, column_total), onehot, 0, 0)
    up_map_gradient = jnp.sum(up_got.astype(f32), axis=0)
    return grad_x, grad_a, up_map_gradient


def local(*args):
    down_maps, up_maps = args[3], args[4]
    n, tp = lax.axis_size("dp"), lax.axis_size("tensor")
    out_width = up_maps.shape[1]
    kernels_fit = (
        n == 8
        and tp == 2
        and down_maps.shape[0] == out_width
        and down_maps.shape[1] == n * up_maps.shape[0]
        and out_width % (128 * tp) == 0
        and out_width == 4 * down_maps.shape[1]
        and args[1].shape[0] == 2 * args[0].shape[0] == down_maps.shape[1]
        and args[5].shape[1] * ADAPTER_RANK * n == 2 * down_maps.shape[1]
    )
    return (local_kernels if kernels_fit else local_plain)(*args)


def solution(mesh):
    in_specs = (
        P(("groups", "dp", "tensor"), None),
        P(("groups", "dp"), None),
        P("tensor", None),
        P(("groups", "dp"), None),
        P(("groups", "dp"), None),
        P("groups", None),
        P("groups", None),
        P("groups"),
        P("groups"),
    )
    out_specs = (
        P(("groups", "dp"), "tensor"),
        P(("groups", "dp"), None),
        P(("groups", "dp"), "tensor"),
    )
    return jax.shard_map(local, mesh=mesh, in_specs=in_specs, out_specs=out_specs, check_vma=False)
```

```python
import functools

import jax
import jax.numpy as jnp
from jax import lax
from jax.experimental import pallas as pl
from jax.experimental.pallas import tpu as pltpu
from jax.sharding import PartitionSpec as P

ADAPTER_RANK = 16
adapter_scale = 2.0

bf16, f32, i32 = jnp.bfloat16, jnp.float32, jnp.int32

HBM = pl.BlockSpec(memory_space=pltpu.HBM)
VMEM = pl.BlockSpec(memory_space=pltpu.VMEM)


def dot(a, b, ca, cb):
    return lax.dot_general(a, b, (((ca,), (cb,)), ((), ())), preferred_element_type=f32)


def params(mib):
    return pltpu.CompilerParams(vmem_limit_bytes=mib << 20)


def slot_rows(chosen_ref, slot_ref, ranks, width):
    lane = lax.broadcasted_iota(i32, (ADAPTER_RANK, width), 1)
    row = lax.broadcasted_iota(i32, (ADAPTER_RANK, width), 0)
    rows = []
    for rank in ranks:
        for k in range(chosen_ref.shape[0]):
            first = slot_ref[chosen_ref[k, rank]] * ADAPTER_RANK
            rows.append(jnp.where(lane == row + first, 1.0, 0.0))
    return jnp.concatenate(rows, axis=0).astype(bf16)


def start_all(sources, targets, sems, first=0):
    copies = [
        pltpu.make_async_copy(source, target, sems.at[first + k])
        for k, (source, target) in enumerate(zip(sources, targets))
    ]
    for copy in copies:
        copy.start()
    return copies


def wait_all(copies):
    for copy in copies:
        copy.wait()


def steps(n):
    return [(n - 1, n // 2 + 1), (3, n - 2), (2, n // 2), (1, 1)]


def partners(n, me, core):
    return [me] + [me ^ jnp.where(core == 0, a, b) for a, b in steps(n)]


def senders(n, me, core):
    passed = [me ^ jnp.where(core == 0, b, a) for a, b in steps(n) if a != b]
    return partners(n, me, core) + passed


class Staged:
    def __init__(self, n, half, rows, picked, width, slots):
        self.n, self.half, self.rows, self.picked, self.slots = n, half, rows, picked, slots
        self.g = n * half
        self.mask = self.g + rows
        self.message = self.mask + rows
        self.shape = (self.message + picked + ADAPTER_RANK, width)

    def x(self, q):
        return pl.ds(q * self.half, self.half)

    def own_rows(self, ref):
        return ref[self.mask : self.mask + self.picked, self.slots : 2 * self.slots]

    def all_rows(self, kept):
        parts = self.n * self.picked // self.rows
        at = [pl.ds((2 + k) * self.slots, self.slots) for k in range(parts)]
        return jnp.concatenate([kept[self.rows :, k] for k in at], axis=0)


def pack_kernel(n, chosen_hbm, slot_hbm, down_hbm, up_hbm, *refs):
    count = n // 2 + 1
    send, (chosen_ref, slot_ref, down_ref, up_ref, out_ref, sems) = refs[:count], refs[count:]
    tables = start_all([chosen_hbm, slot_hbm], [chosen_ref, slot_ref], sems)
    maps = start_all([down_hbm, up_hbm], [down_ref, up_ref], sems, 2)
    ranks = partners(n, lax.axis_index("dp"), lax.axis_index("tensor"))
    wait_all(tables)
    onehot = slot_rows(chosen_ref, slot_ref, ranks, down_ref.shape[1])
    picked = onehot.shape[0] // count
    wait_all(maps)
    columns = dot(onehot, down_ref[...], 1, 1).astype(bf16)
    for k in range(count):
        out_ref[k, :picked, :] = columns[k * picked : (k + 1) * picked]
        out_ref[k, picked:, :] = up_ref[...]
    wait_all(start_all([out_ref.at[k] for k in range(count)], send, sems, 4))


def stage_kernel(
    n, lay, start_hbm, chosen_hbm, slot_hbm, count_hbm, g_hbm, x_hbm, own_hbm,
    stage_hbm, start_ref, chosen_ref, slot_ref, count_ref, stage, sems,
):
    rows, picked, slots = lay.rows, lay.picked, lay.slots
    width = stage.shape[1]
    tables = start_all(
        [chosen_hbm, slot_hbm, start_hbm, count_hbm], [chosen_ref, slot_ref, start_ref, count_ref], sems
    )
    gradient = start_all([g_hbm], [stage.at[pl.ds(lay.g, rows)]], sems, 4)
    other = start_all(
        [own_hbm] + [x_hbm.at[:, pl.ds(q * width, width)] for q in range(n)],
        [stage.at[pl.ds(lay.message, picked + ADAPTER_RANK)]] + [stage.at[lay.x(q)] for q in range(n)],
        sems,
        5,
    )
    me = lax.axis_index("dp")
    wait_all(other)
    parts = [pl.ds(0, lay.g), pl.ds(lay.message, picked + ADAPTER_RANK), pl.ds(lay.g, 2 * rows)]
    done = start_all([stage.at[at] for at in parts[:2]], [stage_hbm.at[at] for at in parts[:2]], sems, 6 + n)
    wait_all(tables)
    position = lax.broadcasted_iota(i32, (rows, slots), 0)
    group = lax.broadcasted_iota(i32, (rows, slots), 1) // ADAPTER_RANK
    segment = jnp.full((rows, slots), -1, i32)
    for k in range(start_ref.shape[0]):
        segment += jnp.where(position >= start_ref[k, me], 1, 0)
    stage[lay.mask : lay.mask + rows, :slots] = jnp.where(segment == group, 1.0, 0.0).astype(bf16)
    mine = slot_rows(chosen_ref, slot_ref, [me], slots)
    stage[lay.mask : lay.mask + picked, slots : 2 * slots] = mine
    every = slot_rows(chosen_ref, slot_ref, range(n), slots)
    for k in range(n * picked // rows):
        at = pl.ds((2 + k) * slots, slots)
        stage[lay.mask : lay.mask + rows, at] = every[k * rows : (k + 1) * rows]
    wait_all(gradient)
    live = lax.broadcasted_iota(i32, (rows, width), 0) < count_ref[me]
    g = stage[lay.g : lay.g + rows, :]
    stage[lay.g : lay.g + rows, :] = jnp.where(live, g, jnp.zeros_like(g))
    done += start_all([stage.at[parts[2]]], [stage_hbm.at[parts[2]]], sems, 8 + n)
    wait_all(done)


def hand_on_kernel(stage, out_ref):
    out_ref[...] = stage[...]


def middle_kernel(n, lay, stage, x_other, *refs):
    count = n // 2 + 1
    got, (dlow_ref, a_ref, kept_ref) = refs[: n - 1], refs[n - 1 : n + 2]
    send, (x_ref, got_ref, up_ref) = refs[n + 2 : n + 2 + count], refs[n + 2 + count :]
    me, core = lax.axis_index("dp"), lax.axis_index("tensor")
    half, rows, picked = lay.half, lay.rows, lay.picked
    width = stage.shape[1]
    mine = pl.ds(pl.multiple_of(core * half, half), half)
    other = pl.ds(pl.multiple_of((1 - core) * half, half), half)
    for q in range(n):
        x_ref[mine, q * width : (q + 1) * width] = stage[lay.x(q), :]
    x_ref[other, :] = x_other[...]
    ranks = senders(n, me, core)
    got_ref[me] = stage[lay.message :, :]
    for sender, message in zip(ranks[1:], got):
        got_ref[sender] = message[...]

    in_seg = stage[lay.mask : lay.mask + rows, :picked].astype(f32) > 0.0
    g = stage[lay.g : lay.g + rows, :]
    onehot = lay.own_rows(stage)
    up_maps = got_ref[:, picked:, :].reshape(-1, width)
    b_sel = dot(onehot, up_maps, 1, 0).astype(bf16)
    dlow = jnp.where(in_seg, adapter_scale * dot(g, b_sel, 1, 1), 0.0).astype(bf16)
    dlow_ref[...] = dlow
    parts = n // 2
    a_ref[...] = got_ref[pl.ds(pl.multiple_of(core * parts, parts), parts), :picked, :]
    kept_ref[...] = stage[lay.g : lay.message, :]
    targets = partners(n, me, core)
    for target, message in zip(targets, send):
        at = pl.ds(pl.multiple_of(target * width, width), width)
        message[:picked, :] = dot(dlow, x_ref[:, at], 0, 0).astype(bf16)

    low = jnp.zeros((rows, picked), f32)
    for q in range(n):
        low += dot(x_ref[:, q * width : (q + 1) * width], got_ref[q, :picked, :], 1, 1)
    low = jnp.where(in_seg, low, 0.0).astype(bf16)
    low_wide = dot(low, onehot, 1, 0).astype(bf16)
    up = (adapter_scale * dot(low_wide, g, 0, 0)).astype(bf16)
    up_ref[...] = up.reshape(up_ref.shape)
    for target, message in zip(targets, send):
        message[picked:, :] = up_ref[target]


def base_kernel(kept_ref, w_ref, out_ref):
    out_ref[...] = dot(kept_ref[: out_ref.shape[0], :], w_ref[...], 1, 1)


def grad_x_kernel(base_ref, dlow_ref, a_ref, out_hbm, out_ref, sems):
    steps, picked, width = a_ref.shape
    done = []
    for j in range(steps):
        at = pl.ds(j * width, width)
        total = base_ref[:, at] + dot(dlow_ref[...], a_ref[j], 1, 0)
        out_ref[:, at] = total.astype(bf16)
        done += start_all([out_ref.at[:, at]], [out_hbm.at[:, at]], sems, j)
    wait_all(done)


def final_kernel(n, lay, kept_ref, *refs):
    got, (a_hbm, up_ref, rows_ref, a_ref, sems) = refs[:n], refs[n:]
    me, core = lax.axis_index("dp"), lax.axis_index("tensor")
    piece, picked = up_ref.shape[1], lay.picked
    for sender, message in zip(senders(n, me, core), got):
        rows_ref[sender] = message[...]
    onehot = lay.all_rows(kept_ref)
    done = []
    part = a_ref.shape[0] // 2
    for k in range(2):
        at = pl.ds(k * part, part)
        rows = rows_ref[:, :picked, at].reshape(n * picked, part)
        a_ref[at, :] = dot(rows, onehot, 0, 0)
        done += start_all([a_ref.at[at]], [a_hbm.at[at]], sems, k)
    at = pl.ds(pl.multiple_of(core * piece, piece), piece)
    up_ref[...] = jnp.sum(rows_ref[:, picked:, at].astype(f32), axis=0)
    wait_all(done)


def exchange(messages, beside):
    n = 2 * len(messages)
    got = [
        lax.ppermute(
            message,
            ("dp", "tensor"),
            [(2 * i + c, 2 * (i ^ step[c]) + c) for i in range(n) for c in range(2)],
        )
        for message, step in zip(messages, steps(n))
    ]
    got[0], beside = lax.optimization_barrier((got[0], beside))
    passed = [
        lax.ppermute(message, "tensor", [(0, 1), (1, 0)])
        for message, (a, b) in zip(got, steps(n))
        if a != b
    ]
    return got + passed, beside


def local_kernels(
    inputs,
    output_gradient,
    frozen_weight,
    down_maps,
    up_maps,
    segment_start,
    segment_adapter,
    adapter_slot,
    token_count,
):
    tok_half, model_width = inputs.shape
    tok_rows, out_width = output_gradient.shape
    column_total, slot_width = down_maps.shape
    half = frozen_weight.shape[0]
    n = lax.axis_size("dp")
    piece = out_width // lax.axis_size("tensor")
    segs = segment_start.shape[1]
    picked = segs * ADAPTER_RANK
    shape = jax.ShapeDtypeStruct
    message = shape((picked + ADAPTER_RANK, column_total), bf16)
    count = n // 2 + 1
    starts, chosen = segment_start.T, segment_adapter.T

    tables = [
        pltpu.SMEM(starts.shape, i32),
        pltpu.SMEM(chosen.shape, i32),
        pltpu.SMEM(adapter_slot.shape, i32),
        pltpu.SMEM(token_count.shape, i32),
    ]
    dma = pltpu.SemaphoreType.DMA

    lay = Staged(n, tok_half, tok_rows, picked, column_total, slot_width)
    own, *sent = pl.pallas_call(
        functools.partial(pack_kernel, n),
        out_shape=[message] * count,
        in_specs=[HBM] * 4,
        out_specs=[HBM] * count,
        scratch_shapes=tables[1:3]
        + [
            pltpu.VMEM(down_maps.shape, bf16),
            pltpu.VMEM(up_maps.shape, bf16),
            pltpu.VMEM((count,) + message.shape, bf16),
            dma((4 + count,)),
        ],
        compiler_params=params(56),
    )(chosen, adapter_slot, down_maps, up_maps)
    sent, x_late = lax.optimization_barrier((sent, inputs))
    x_other = lax.ppermute(x_late, "tensor", [(0, 1), (1, 0)])
    stage = pl.pallas_call(
        functools.partial(stage_kernel, n, lay),
        out_shape=shape(lay.shape, bf16),
        in_specs=[HBM] * 7,
        out_specs=HBM,
        scratch_shapes=tables + [pltpu.VMEM(lay.shape, bf16), dma((9 + n,))],
        compiler_params=params(56),
        cost_estimate=pl.CostEstimate(flops=0, bytes_accessed=1 << 21, transcendentals=0),
    )(starts, chosen, adapter_slot, token_count, output_gradient, inputs, own)
    got, stage = exchange(sent, stage)
    stage = pl.pallas_call(
        hand_on_kernel,
        out_shape=shape(lay.shape, bf16),
        in_specs=[VMEM],
        out_specs=VMEM,
        compiler_params=params(8),
        cost_estimate=pl.CostEstimate(flops=0, bytes_accessed=1 << 21, transcendentals=0),
    )(stage)

    dlow, a_half, kept, own, *sent = pl.pallas_call(
        functools.partial(middle_kernel, n, lay),
        out_shape=[
            shape((tok_rows, picked), bf16),
            shape((n // 2, picked, column_total), bf16),
            shape((2 * tok_rows, out_width), bf16),
        ]
        + [message] * count,
        in_specs=[VMEM] * (1 + n),
        out_specs=[VMEM] * (3 + count),
        scratch_shapes=[
            pltpu.VMEM((tok_rows, model_width), bf16),
            pltpu.VMEM((n,) + message.shape, bf16),
            pltpu.VMEM((n, ADAPTER_RANK, out_width), bf16),
        ],
        compiler_params=params(8),
    )(stage, x_other, *got)
    base = pl.pallas_call(
        base_kernel,
        out_shape=shape((tok_rows, half), f32),
        in_specs=[VMEM, VMEM],
        out_specs=VMEM,
        compiler_params=params(8),
        cost_estimate=pl.CostEstimate(
            flops=2 * tok_rows * half * out_width,
            bytes_accessed=4 * half * tok_rows + 2 * half * out_width,
            transcendentals=0,
        ),
    )(kept, frozen_weight)
    grad_x = pl.pallas_call(
        grad_x_kernel,
        out_shape=shape((tok_rows, half), bf16),
        in_specs=[VMEM] * 3,
        out_specs=HBM,
        scratch_shapes=[pltpu.VMEM((tok_rows, half), bf16), dma((n // 2,))],
        compiler_params=params(8),
        cost_estimate=pl.CostEstimate(
            flops=2 * tok_rows * half * picked,
            bytes_accessed=6 * half * tok_rows,
            transcendentals=0,
        ),
    )(base, dlow, a_half)

    got, grad_x = exchange(sent, grad_x)

    grad_a, up_map_gradient = pl.pallas_call(
        functools.partial(final_kernel, n, lay),
        out_shape=[shape((column_total, slot_width), f32), shape((ADAPTER_RANK, piece), f32)],
        in_specs=[VMEM] * (1 + n),
        out_specs=[HBM, VMEM],
        scratch_shapes=[
            pltpu.VMEM((n,) + message.shape, bf16),
            pltpu.VMEM((column_total, slot_width), f32),
            dma((2,)),
        ],
        compiler_params=params(8),
    )(kept, own, *got)
    return grad_x, grad_a, up_map_gradient


def local_plain(
    inputs,
    output_gradient,
    frozen_weight,
    down_maps,
    up_maps,
    segment_start,
    segment_adapter,
    adapter_slot,
    token_count,
):
    tok_rows, out_width = output_gradient.shape
    column_total = down_maps.shape[0]
    adapter_list = adapter_slot.shape[0]
    segs = segment_start.shape[1]
    dp_size = lax.axis_size("dp")
    my_rank = lax.axis_index("dp")
    core_idx = lax.axis_index("tensor")
    picked = segs * ADAPTER_RANK
    piece_out = out_width // lax.axis_size("tensor")
    half = frozen_weight.shape[0]

    x_other = lax.ppermute(inputs, "tensor", [(0, 1), (1, 0)])
    adapter_ids = jnp.arange(adapter_list, dtype=i32)
    slot_table = jnp.sum(
        jnp.where(segment_adapter[..., None] == adapter_ids, adapter_slot, 0), axis=-1
    )
    column = slot_table[:, :, None] * ADAPTER_RANK + jnp.arange(ADAPTER_RANK, dtype=i32)
    onehot = (
        column.reshape(-1)[:, None] == jnp.arange(adapter_list * ADAPTER_RANK, dtype=i32)
    ).astype(bf16)

    a_send = dot(onehot, down_maps, 1, 1).astype(bf16).reshape(dp_size, picked, column_total)
    b_send = jnp.broadcast_to(up_maps[None], (dp_size,) + up_maps.shape)
    a_got = lax.all_to_all(a_send, "dp", 0, 0, tiled=True)
    b_got = lax.all_to_all(b_send, "dp", 0, 0, tiled=True)

    position = jnp.arange(tok_rows, dtype=i32)
    starts = lax.dynamic_index_in_dim(segment_start, my_rank, 0, keepdims=False)
    live = position < lax.dynamic_index_in_dim(token_count, my_rank, 0, keepdims=False)
    my_seg = jnp.sum((starts[None, :] <= position[:, None]).astype(i32), axis=1) - 1
    in_seg = my_seg[:, None] == (jnp.arange(picked, dtype=i32) // ADAPTER_RANK)[None, :]
    my_onehot = lax.dynamic_slice_in_dim(onehot, my_rank * picked, picked, 0)
    g = jnp.where(live[:, None], output_gradient, jnp.zeros_like(output_gradient))
    base = dot(g, frozen_weight, 1, 1)

    b_sel = dot(my_onehot, b_got.reshape(-1, out_width), 1, 0).astype(bf16)
    dlow = (adapter_scale * dot(g, b_sel, 1, 1)).astype(bf16)
    dlow = jnp.where(in_seg, dlow, jnp.zeros_like(dlow))
    a_sel = jnp.moveaxis(a_got, 0, 1).reshape(picked, -1)
    first = core_idx == 0
    x = jnp.concatenate(
        [jnp.where(first, inputs, x_other), jnp.where(first, x_other, inputs)], axis=0
    )
    low = dot(x, a_sel, 1, 1).astype(bf16)
    low = jnp.where(in_seg, low, jnp.zeros_like(low))
    low_wide = dot(low, my_onehot, 1, 0).astype(bf16)

    ga_send = dot(dlow, x, 0, 0).astype(bf16).reshape(picked, dp_size, column_total)
    ga_got = lax.all_to_all(jnp.moveaxis(ga_send, 1, 0), "dp", 0, 0, tiled=True)
    g_piece = lax.dynamic_slice_in_dim(g, core_idx * piece_out, piece_out, 1)
    up_send = (adapter_scale * dot(low_wide, g_piece, 0, 0)).astype(bf16)
    up_got = lax.all_to_all(up_send.reshape(dp_size, -1, piece_out), "dp", 0, 0, tiled=True)

    a_half = lax.dynamic_slice_in_dim(a_sel, core_idx * half, half, 1)
    grad_x = (base + dot(dlow, a_half, 1, 0)).astype(bf16)
    grad_a = dot(ga_got.reshape(dp_size * picked, column_total), onehot, 0, 0)
    up_map_gradient = jnp.sum(up_got.astype(f32), axis=0)
    return grad_x, grad_a, up_map_gradient


def local(*args):
    down_maps, up_maps = args[3], args[4]
    n, tp = lax.axis_size("dp"), lax.axis_size("tensor")
    out_width = up_maps.shape[1]
    kernels_fit = (
        n == 8
        and tp == 2
        and down_maps.shape[0] == out_width
        and down_maps.shape[1] == n * up_maps.shape[0]
        and out_width % (128 * tp) == 0
        and out_width >= 4 * down_maps.shape[1]
        and args[1].shape[0] == 2 * args[0].shape[0] == down_maps.shape[1]
        and args[5].shape[1] * ADAPTER_RANK * n == 2 * down_maps.shape[1]
    )
    return (local_kernels if kernels_fit else local_plain)(*args)


def solution(mesh):
    in_specs = (
        P(("groups", "dp", "tensor"), None),
        P(("groups", "dp"), None),
        P("tensor", None),
        P(("groups", "dp"), None),
        P(("groups", "dp"), None),
        P("groups", None),
        P("groups", None),
        P("groups"),
        P("groups"),
    )
    out_specs = (
        P(("groups", "dp"), "tensor"),
        P(("groups", "dp"), None),
        P(("groups", "dp"), "tensor"),
    )
    return jax.shard_map(local, mesh=mesh, in_specs=in_specs, out_specs=out_specs, check_vma=False)
```

```python
import functools

import jax
import jax.numpy as jnp
from jax import lax
from jax.experimental import pallas as pl
from jax.experimental.pallas import tpu as pltpu
from jax.sharding import PartitionSpec as P

ADAPTER_RANK = 16
adapter_scale = 2.0

bf16, f32, i32 = jnp.bfloat16, jnp.float32, jnp.int32

HBM = pl.BlockSpec(memory_space=pltpu.HBM)
VMEM = pl.BlockSpec(memory_space=pltpu.VMEM)


def dot(a, b, ca, cb):
    return lax.dot_general(a, b, (((ca,), (cb,)), ((), ())), preferred_element_type=f32)


def params(mib):
    return pltpu.CompilerParams(vmem_limit_bytes=mib << 20)


def slot_rows(chosen_ref, slot_ref, ranks, width):
    lane = lax.broadcasted_iota(i32, (ADAPTER_RANK, width), 1)
    row = lax.broadcasted_iota(i32, (ADAPTER_RANK, width), 0)
    rows = []
    for rank in ranks:
        for k in range(chosen_ref.shape[0]):
            first = slot_ref[chosen_ref[k, rank]] * ADAPTER_RANK
            rows.append(jnp.where(lane == row + first, 1.0, 0.0))
    return jnp.concatenate(rows, axis=0).astype(bf16)


def start_all(sources, targets, sems, first=0):
    copies = [
        pltpu.make_async_copy(source, target, sems.at[first + k])
        for k, (source, target) in enumerate(zip(sources, targets))
    ]
    for copy in copies:
        copy.start()
    return copies


def wait_all(copies):
    for copy in copies:
        copy.wait()


def steps(n, turn):
    half = n // 2
    if turn == 0:
        return [(n - 1, half), (3, half + 1), (n - 2, 2), (1, 1)]
    return [(n - 1, half + 1), (2, n - 2), (half, 3), (1, 1)]


def partners(n, turn, me, core):
    return [me] + [me ^ jnp.where(core == 0, a, b) for a, b in steps(n, turn)]


def senders(n, turn, me, core):
    passed = [me ^ jnp.where(core == 0, b, a) for a, b in steps(n, turn) if a != b]
    return partners(n, turn, me, core) + passed


class Staged:
    def __init__(self, n, half, rows, picked, width, slots):
        self.n, self.half, self.rows, self.picked, self.slots = n, half, rows, picked, slots
        self.g = n * half
        self.mask = self.g + rows
        self.message = self.mask + rows
        self.shape = (self.message + picked + ADAPTER_RANK, width)

    def x(self, q):
        return pl.ds(q * self.half, self.half)

    def own_rows(self, ref):
        return ref[self.mask : self.mask + self.picked, self.slots : 2 * self.slots]

    def all_rows(self, kept):
        parts = self.n * self.picked // self.rows
        at = [pl.ds((2 + k) * self.slots, self.slots) for k in range(parts)]
        return jnp.concatenate([kept[self.rows :, k] for k in at], axis=0)


def pack_kernel(n, chosen_hbm, slot_hbm, down_hbm, up_hbm, *refs):
    count = n // 2 + 1
    send, (chosen_ref, slot_ref, down_ref, up_ref, out_ref, sems) = refs[:count], refs[count:]
    tables = start_all([chosen_hbm, slot_hbm], [chosen_ref, slot_ref], sems)
    maps = start_all([down_hbm, up_hbm], [down_ref, up_ref], sems, 2)
    ranks = partners(n, 0, lax.axis_index("dp"), lax.axis_index("tensor"))
    wait_all(tables)
    onehot = slot_rows(chosen_ref, slot_ref, ranks, down_ref.shape[1])
    picked = onehot.shape[0] // count
    wait_all(maps)
    columns = dot(onehot, down_ref[...], 1, 1).astype(bf16)
    for k in range(count):
        out_ref[k, :picked, :] = columns[k * picked : (k + 1) * picked]
        out_ref[k, picked:, :] = up_ref[...]
    wait_all(start_all([out_ref.at[k] for k in range(count)], send, sems, 4))


def stage_kernel(
    n, lay, start_hbm, chosen_hbm, slot_hbm, count_hbm, g_hbm, x_hbm, own_hbm,
    stage_hbm, start_ref, chosen_ref, slot_ref, count_ref, stage, sems,
):
    rows, picked, slots = lay.rows, lay.picked, lay.slots
    width = stage.shape[1]
    tables = start_all(
        [chosen_hbm, slot_hbm, start_hbm, count_hbm], [chosen_ref, slot_ref, start_ref, count_ref], sems
    )
    gradient = start_all([g_hbm], [stage.at[pl.ds(lay.g, rows)]], sems, 4)
    other = start_all(
        [own_hbm] + [x_hbm.at[:, pl.ds(q * width, width)] for q in range(n)],
        [stage.at[pl.ds(lay.message, picked + ADAPTER_RANK)]] + [stage.at[lay.x(q)] for q in range(n)],
        sems,
        5,
    )
    me = lax.axis_index("dp")
    wait_all(tables)
    position = lax.broadcasted_iota(i32, (rows, slots), 0)
    group = lax.broadcasted_iota(i32, (rows, slots), 1) // ADAPTER_RANK
    segment = jnp.full((rows, slots), -1, i32)
    for k in range(start_ref.shape[0]):
        segment += jnp.where(position >= start_ref[k, me], 1, 0)
    stage[lay.mask : lay.mask + rows, :slots] = jnp.where(segment == group, 1.0, 0.0).astype(bf16)
    mine = slot_rows(chosen_ref, slot_ref, [me], slots)
    stage[lay.mask : lay.mask + picked, slots : 2 * slots] = mine
    every = slot_rows(chosen_ref, slot_ref, range(n), slots)
    for k in range(n * picked // rows):
        at = pl.ds((2 + k) * slots, slots)
        stage[lay.mask : lay.mask + rows, at] = every[k * rows : (k + 1) * rows]
    wait_all(gradient)
    live = lax.broadcasted_iota(i32, (rows, width), 0) < count_ref[me]
    g = stage[lay.g : lay.g + rows, :]
    stage[lay.g : lay.g + rows, :] = jnp.where(live, g, jnp.zeros_like(g))
    wait_all(other)
    wait_all(start_all([stage], [stage_hbm], sems, 6 + n))


def hand_on_kernel(stage, out_ref):
    out_ref[...] = stage[...]


def middle_kernel(n, lay, stage, x_other, *refs):
    count = n // 2 + 1
    got, (dlow_ref, a_ref, kept_ref) = refs[: n - 1], refs[n - 1 : n + 2]
    send, (x_ref, got_ref, up_ref) = refs[n + 2 : n + 2 + count], refs[n + 2 + count :]
    me, core = lax.axis_index("dp"), lax.axis_index("tensor")
    half, rows, picked = lay.half, lay.rows, lay.picked
    width = stage.shape[1]
    mine = pl.ds(pl.multiple_of(core * half, half), half)
    other = pl.ds(pl.multiple_of((1 - core) * half, half), half)
    for q in range(n):
        x_ref[mine, q * width : (q + 1) * width] = stage[lay.x(q), :]
    x_ref[other, :] = x_other[...]
    ranks = senders(n, 0, me, core)
    got_ref[me] = stage[lay.message :, :]
    for sender, message in zip(ranks[1:], got):
        got_ref[sender] = message[...]

    in_seg = stage[lay.mask : lay.mask + rows, :picked].astype(f32) > 0.0
    g = stage[lay.g : lay.g + rows, :]
    onehot = lay.own_rows(stage)
    up_maps = got_ref[:, picked:, :].reshape(-1, width)
    b_sel = dot(onehot, up_maps, 1, 0).astype(bf16)
    dlow = jnp.where(in_seg, adapter_scale * dot(g, b_sel, 1, 1), 0.0).astype(bf16)
    dlow_ref[...] = dlow
    parts = n // 2
    a_ref[...] = got_ref[pl.ds(pl.multiple_of(core * parts, parts), parts), :picked, :]
    kept_ref[...] = stage[lay.g : lay.message, :]
    targets = partners(n, 1, me, core)
    for target, message in zip(targets, send):
        at = pl.ds(pl.multiple_of(target * width, width), width)
        message[:picked, :] = dot(dlow, x_ref[:, at], 0, 0).astype(bf16)

    low = jnp.zeros((rows, picked), f32)
    for q in range(n):
        low += dot(x_ref[:, q * width : (q + 1) * width], got_ref[q, :picked, :], 1, 1)
    low = jnp.where(in_seg, low, 0.0).astype(bf16)
    low_wide = dot(low, onehot, 1, 0).astype(bf16)
    up = (adapter_scale * dot(low_wide, g, 0, 0)).astype(bf16)
    up_ref[...] = up.reshape(up_ref.shape)
    for target, message in zip(targets, send):
        message[picked:, :] = up_ref[target]


def base_kernel(kept_ref, w_ref, out_ref):
    out_ref[...] = dot(kept_ref[: out_ref.shape[0], :], w_ref[...], 1, 1)


def grad_x_kernel(base_ref, dlow_ref, a_ref, out_hbm, out_ref, sems):
    steps, picked, width = a_ref.shape
    done = []
    for j in range(steps):
        at = pl.ds(j * width, width)
        total = base_ref[:, at] + dot(dlow_ref[...], a_ref[j], 1, 0)
        out_ref[:, at] = total.astype(bf16)
        done += start_all([out_ref.at[:, at]], [out_hbm.at[:, at]], sems, j)
    wait_all(done)


def final_kernel(n, lay, kept_ref, *refs):
    got, (a_ref, up_ref, rows_ref) = refs[:n], refs[n:]
    me, core = lax.axis_index("dp"), lax.axis_index("tensor")
    piece, picked = up_ref.shape[1], lay.picked
    for sender, message in zip(senders(n, 1, me, core), got):
        rows_ref[sender] = message[...]
    rows = rows_ref[:, :picked, :].reshape(n * picked, rows_ref.shape[2])
    a_ref[...] = dot(rows, lay.all_rows(kept_ref), 0, 0)
    at = pl.ds(pl.multiple_of(core * piece, piece), piece)
    up_ref[...] = jnp.sum(rows_ref[:, picked:, at].astype(f32), axis=0)


def exchange(messages, turn, beside):
    n = 2 * len(messages)
    got = [
        lax.ppermute(
            message,
            ("dp", "tensor"),
            [(2 * i + c, 2 * (i ^ step[c]) + c) for i in range(n) for c in range(2)],
        )
        for message, step in zip(messages, steps(n, turn))
    ]
    got[0], beside = lax.optimization_barrier((got[0], beside))
    passed = [
        lax.ppermute(message, "tensor", [(0, 1), (1, 0)])
        for message, (a, b) in zip(got, steps(n, turn))
        if a != b
    ]
    return got + passed, beside


def local_kernels(
    inputs,
    output_gradient,
    frozen_weight,
    down_maps,
    up_maps,
    segment_start,
    segment_adapter,
    adapter_slot,
    token_count,
):
    tok_half, model_width = inputs.shape
    tok_rows, out_width = output_gradient.shape
    column_total, slot_width = down_maps.shape
    half = frozen_weight.shape[0]
    n = lax.axis_size("dp")
    piece = out_width // lax.axis_size("tensor")
    segs = segment_start.shape[1]
    picked = segs * ADAPTER_RANK
    shape = jax.ShapeDtypeStruct
    message = shape((picked + ADAPTER_RANK, column_total), bf16)
    count = n // 2 + 1
    starts, chosen = segment_start.T, segment_adapter.T

    tables = [
        pltpu.SMEM(starts.shape, i32),
        pltpu.SMEM(chosen.shape, i32),
        pltpu.SMEM(adapter_slot.shape, i32),
        pltpu.SMEM(token_count.shape, i32),
    ]
    dma = pltpu.SemaphoreType.DMA

    lay = Staged(n, tok_half, tok_rows, picked, column_total, slot_width)
    own, *sent = pl.pallas_call(
        functools.partial(pack_kernel, n),
        out_shape=[message] * count,
        in_specs=[HBM] * 4,
        out_specs=[HBM] * count,
        scratch_shapes=tables[1:3]
        + [
            pltpu.VMEM(down_maps.shape, bf16),
            pltpu.VMEM(up_maps.shape, bf16),
            pltpu.VMEM((count,) + message.shape, bf16),
            dma((4 + count,)),
        ],
        compiler_params=params(56),
    )(chosen, adapter_slot, down_maps, up_maps)
    sent, x_late = lax.optimization_barrier((sent, inputs))
    x_other = lax.ppermute(x_late, "tensor", [(0, 1), (1, 0)])
    stage = pl.pallas_call(
        functools.partial(stage_kernel, n, lay),
        out_shape=shape(lay.shape, bf16),
        in_specs=[HBM] * 7,
        out_specs=HBM,
        scratch_shapes=tables + [pltpu.VMEM(lay.shape, bf16), dma((7 + n,))],
        compiler_params=params(56),
        cost_estimate=pl.CostEstimate(flops=0, bytes_accessed=1 << 21, transcendentals=0),
    )(starts, chosen, adapter_slot, token_count, output_gradient, inputs, own)
    got, stage = exchange(sent, 0, stage)
    stage = pl.pallas_call(
        hand_on_kernel,
        out_shape=shape(lay.shape, bf16),
        in_specs=[VMEM],
        out_specs=VMEM,
        compiler_params=params(8),
        cost_estimate=pl.CostEstimate(flops=0, bytes_accessed=1 << 21, transcendentals=0),
    )(stage)

    dlow, a_half, kept, own, *sent = pl.pallas_call(
        functools.partial(middle_kernel, n, lay),
        out_shape=[
            shape((tok_rows, picked), bf16),
            shape((n // 2, picked, column_total), bf16),
            shape((2 * tok_rows, out_width), bf16),
        ]
        + [message] * count,
        in_specs=[VMEM] * (1 + n),
        out_specs=[VMEM] * (3 + count),
        scratch_shapes=[
            pltpu.VMEM((tok_rows, model_width), bf16),
            pltpu.VMEM((n,) + message.shape, bf16),
            pltpu.VMEM((n, ADAPTER_RANK, out_width), bf16),
        ],
        compiler_params=params(8),
    )(stage, x_other, *got)
    base = pl.pallas_call(
        base_kernel,
        out_shape=shape((tok_rows, half), f32),
        in_specs=[VMEM, VMEM],
        out_specs=VMEM,
        compiler_params=params(8),
        cost_estimate=pl.CostEstimate(
            flops=2 * tok_rows * half * out_width,
            bytes_accessed=4 * half * tok_rows + 2 * half * out_width,
            transcendentals=0,
        ),
    )(kept, frozen_weight)
    grad_x = pl.pallas_call(
        grad_x_kernel,
        out_shape=shape((tok_rows, half), bf16),
        in_specs=[VMEM] * 3,
        out_specs=HBM,
        scratch_shapes=[pltpu.VMEM((tok_rows, half), bf16), dma((n // 2,))],
        compiler_params=params(8),
        cost_estimate=pl.CostEstimate(
            flops=2 * tok_rows * half * picked,
            bytes_accessed=6 * half * tok_rows,
            transcendentals=0,
        ),
    )(base, dlow, a_half)

    got, grad_x = exchange(sent, 1, grad_x)

    grad_a, up_map_gradient = pl.pallas_call(
        functools.partial(final_kernel, n, lay),
        out_shape=[shape((column_total, slot_width), f32), shape((ADAPTER_RANK, piece), f32)],
        in_specs=[VMEM] * (1 + n),
        out_specs=[VMEM, VMEM],
        scratch_shapes=[pltpu.VMEM((n,) + message.shape, bf16)],
        compiler_params=params(8),
    )(kept, own, *got)
    return grad_x, grad_a, up_map_gradient


def local_plain(
    inputs,
    output_gradient,
    frozen_weight,
    down_maps,
    up_maps,
    segment_start,
    segment_adapter,
    adapter_slot,
    token_count,
):
    tok_rows, out_width = output_gradient.shape
    column_total = down_maps.shape[0]
    adapter_list = adapter_slot.shape[0]
    segs = segment_start.shape[1]
    dp_size = lax.axis_size("dp")
    my_rank = lax.axis_index("dp")
    core_idx = lax.axis_index("tensor")
    picked = segs * ADAPTER_RANK
    piece_out = out_width // lax.axis_size("tensor")
    half = frozen_weight.shape[0]

    x_other = lax.ppermute(inputs, "tensor", [(0, 1), (1, 0)])
    adapter_ids = jnp.arange(adapter_list, dtype=i32)
    slot_table = jnp.sum(
        jnp.where(segment_adapter[..., None] == adapter_ids, adapter_slot, 0), axis=-1
    )
    column = slot_table[:, :, None] * ADAPTER_RANK + jnp.arange(ADAPTER_RANK, dtype=i32)
    onehot = (
        column.reshape(-1)[:, None] == jnp.arange(adapter_list * ADAPTER_RANK, dtype=i32)
    ).astype(bf16)

    a_send = dot(onehot, down_maps, 1, 1).astype(bf16).reshape(dp_size, picked, column_total)
    b_send = jnp.broadcast_to(up_maps[None], (dp_size,) + up_maps.shape)
    a_got = lax.all_to_all(a_send, "dp", 0, 0, tiled=True)
    b_got = lax.all_to_all(b_send, "dp", 0, 0, tiled=True)

    position = jnp.arange(tok_rows, dtype=i32)
    starts = lax.dynamic_index_in_dim(segment_start, my_rank, 0, keepdims=False)
    live = position < lax.dynamic_index_in_dim(token_count, my_rank, 0, keepdims=False)
    my_seg = jnp.sum((starts[None, :] <= position[:, None]).astype(i32), axis=1) - 1
    in_seg = my_seg[:, None] == (jnp.arange(picked, dtype=i32) // ADAPTER_RANK)[None, :]
    my_onehot = lax.dynamic_slice_in_dim(onehot, my_rank * picked, picked, 0)
    g = jnp.where(live[:, None], output_gradient, jnp.zeros_like(output_gradient))
    base = dot(g, frozen_weight, 1, 1)

    b_sel = dot(my_onehot, b_got.reshape(-1, out_width), 1, 0).astype(bf16)
    dlow = (adapter_scale * dot(g, b_sel, 1, 1)).astype(bf16)
    dlow = jnp.where(in_seg, dlow, jnp.zeros_like(dlow))
    a_sel = jnp.moveaxis(a_got, 0, 1).reshape(picked, -1)
    first = core_idx == 0
    x = jnp.concatenate(
        [jnp.where(first, inputs, x_other), jnp.where(first, x_other, inputs)], axis=0
    )
    low = dot(x, a_sel, 1, 1).astype(bf16)
    low = jnp.where(in_seg, low, jnp.zeros_like(low))
    low_wide = dot(low, my_onehot, 1, 0).astype(bf16)

    ga_send = dot(dlow, x, 0, 0).astype(bf16).reshape(picked, dp_size, column_total)
    ga_got = lax.all_to_all(jnp.moveaxis(ga_send, 1, 0), "dp", 0, 0, tiled=True)
    g_piece = lax.dynamic_slice_in_dim(g, core_idx * piece_out, piece_out, 1)
    up_send = (adapter_scale * dot(low_wide, g_piece, 0, 0)).astype(bf16)
    up_got = lax.all_to_all(up_send.reshape(dp_size, -1, piece_out), "dp", 0, 0, tiled=True)

    a_half = lax.dynamic_slice_in_dim(a_sel, core_idx * half, half, 1)
    grad_x = (base + dot(dlow, a_half, 1, 0)).astype(bf16)
    grad_a = dot(ga_got.reshape(dp_size * picked, column_total), onehot, 0, 0)
    up_map_gradient = jnp.sum(up_got.astype(f32), axis=0)
    return grad_x, grad_a, up_map_gradient


def local(*args):
    down_maps, up_maps = args[3], args[4]
    n, tp = lax.axis_size("dp"), lax.axis_size("tensor")
    out_width = up_maps.shape[1]
    kernels_fit = (
        n == 8
        and tp == 2
        and down_maps.shape[0] == out_width
        and down_maps.shape[1] == n * up_maps.shape[0]
        and out_width % (128 * tp) == 0
        and out_width >= 4 * down_maps.shape[1]
        and args[1].shape[0] == 2 * args[0].shape[0] == down_maps.shape[1]
        and args[5].shape[1] * ADAPTER_RANK * n == 2 * down_maps.shape[1]
    )
    return (local_kernels if kernels_fit else local_plain)(*args)


def solution(mesh):
    in_specs = (
        P(("groups", "dp", "tensor"), None),
        P(("groups", "dp"), None),
        P("tensor", None),
        P(("groups", "dp"), None),
        P(("groups", "dp"), None),
        P("groups", None),
        P("groups", None),
        P("groups"),
        P("groups"),
    )
    out_specs = (
        P(("groups", "dp"), "tensor"),
        P(("groups", "dp"), None),
        P(("groups", "dp"), "tensor"),
    )
    return jax.shard_map(local, mesh=mesh, in_specs=in_specs, out_specs=out_specs, check_vma=False)
```

```python
import functools

import jax
import jax.numpy as jnp
from jax import lax
from jax.experimental import pallas as pl
from jax.experimental.pallas import tpu as pltpu
from jax.sharding import PartitionSpec as P

ADAPTER_RANK = 16
adapter_scale = 2.0

bf16, f32, i32 = jnp.bfloat16, jnp.float32, jnp.int32

HBM = pl.BlockSpec(memory_space=pltpu.HBM)
VMEM = pl.BlockSpec(memory_space=pltpu.VMEM)


def dot(a, b, ca, cb):
    return lax.dot_general(a, b, (((ca,), (cb,)), ((), ())), preferred_element_type=f32)


def params(mib):
    return pltpu.CompilerParams(vmem_limit_bytes=mib << 20)


def slot_rows(chosen_ref, slot_ref, ranks, width):
    lane = lax.broadcasted_iota(i32, (ADAPTER_RANK, width), 1)
    row = lax.broadcasted_iota(i32, (ADAPTER_RANK, width), 0)
    rows = []
    for rank in ranks:
        for k in range(chosen_ref.shape[0]):
            first = slot_ref[chosen_ref[k, rank]] * ADAPTER_RANK
            rows.append(jnp.where(lane == row + first, 1.0, 0.0))
    return jnp.concatenate(rows, axis=0).astype(bf16)


def start_all(sources, targets, sems, first=0):
    copies = [
        pltpu.make_async_copy(source, target, sems.at[first + k])
        for k, (source, target) in enumerate(zip(sources, targets))
    ]
    for copy in copies:
        copy.start()
    return copies


def wait_all(copies):
    for copy in copies:
        copy.wait()


def steps(n, turn):
    half = n // 2
    if turn == 0:
        return [(half + 1, 3), (n - 1, n - 2), (1, 1), (2, half)]
    return [(n - 1, half + 1), (3, n - 2), (2, half), (1, 1)]


def partners(n, turn, me, core):
    return [me] + [me ^ jnp.where(core == 0, a, b) for a, b in steps(n, turn)]


def senders(n, turn, me, core):
    passed = [me ^ jnp.where(core == 0, b, a) for a, b in steps(n, turn) if a != b]
    return partners(n, turn, me, core) + passed


class Staged:
    def __init__(self, n, half, rows, picked, width, slots):
        self.n, self.half, self.rows, self.picked, self.slots = n, half, rows, picked, slots
        self.g = n * half
        self.mask = self.g + rows
        self.message = self.mask + rows
        self.shape = (self.message + picked + ADAPTER_RANK, width)

    def x(self, q):
        return pl.ds(q * self.half, self.half)

    def own_rows(self, ref):
        return ref[self.mask : self.mask + self.picked, self.slots : 2 * self.slots]

    def all_rows(self, kept):
        parts = self.n * self.picked // self.rows
        at = [pl.ds((2 + k) * self.slots, self.slots) for k in range(parts)]
        return jnp.concatenate([kept[self.rows :, k] for k in at], axis=0)


def pack_kernel(n, chosen_hbm, slot_hbm, down_hbm, up_hbm, *refs):
    count = n // 2 + 1
    send, (chosen_ref, slot_ref, down_ref, up_ref, out_ref, sems) = refs[:count], refs[count:]
    tables = start_all([chosen_hbm, slot_hbm], [chosen_ref, slot_ref], sems)
    maps = start_all([down_hbm, up_hbm], [down_ref, up_ref], sems, 2)
    ranks = partners(n, 0, lax.axis_index("dp"), lax.axis_index("tensor"))
    wait_all(tables)
    onehot = slot_rows(chosen_ref, slot_ref, ranks, down_ref.shape[1])
    picked = onehot.shape[0] // count
    wait_all(maps)
    columns = dot(onehot, down_ref[...], 1, 1).astype(bf16)
    for k in range(count):
        out_ref[k, :picked, :] = columns[k * picked : (k + 1) * picked]
        out_ref[k, picked:, :] = up_ref[...]
    wait_all(start_all([out_ref.at[k] for k in range(count)], send, sems, 4))


def stage_kernel(
    n, lay, start_hbm, chosen_hbm, slot_hbm, count_hbm, g_hbm, x_hbm, own_hbm,
    stage_hbm, start_ref, chosen_ref, slot_ref, count_ref, stage, sems,
):
    rows, picked, slots = lay.rows, lay.picked, lay.slots
    width = stage.shape[1]
    tables = start_all(
        [chosen_hbm, slot_hbm, start_hbm, count_hbm], [chosen_ref, slot_ref, start_ref, count_ref], sems
    )
    gradient = start_all([g_hbm], [stage.at[pl.ds(lay.g, rows)]], sems, 4)
    other = start_all(
        [own_hbm] + [x_hbm.at[:, pl.ds(q * width, width)] for q in range(n)],
        [stage.at[pl.ds(lay.message, picked + ADAPTER_RANK)]] + [stage.at[lay.x(q)] for q in range(n)],
        sems,
        5,
    )
    me = lax.axis_index("dp")
    wait_all(tables)
    position = lax.broadcasted_iota(i32, (rows, slots), 0)
    group = lax.broadcasted_iota(i32, (rows, slots), 1) // ADAPTER_RANK
    segment = jnp.full((rows, slots), -1, i32)
    for k in range(start_ref.shape[0]):
        segment += jnp.where(position >= start_ref[k, me], 1, 0)
    stage[lay.mask : lay.mask + rows, :slots] = jnp.where(segment == group, 1.0, 0.0).astype(bf16)
    mine = slot_rows(chosen_ref, slot_ref, [me], slots)
    stage[lay.mask : lay.mask + picked, slots : 2 * slots] = mine
    every = slot_rows(chosen_ref, slot_ref, range(n), slots)
    for k in range(n * picked // rows):
        at = pl.ds((2 + k) * slots, slots)
        stage[lay.mask : lay.mask + rows, at] = every[k * rows : (k + 1) * rows]
    wait_all(gradient)
    live = lax.broadcasted_iota(i32, (rows, width), 0) < count_ref[me]
    g = stage[lay.g : lay.g + rows, :]
    stage[lay.g : lay.g + rows, :] = jnp.where(live, g, jnp.zeros_like(g))
    wait_all(other)
    wait_all(start_all([stage], [stage_hbm], sems, 6 + n))


def hand_on_kernel(stage, out_ref):
    out_ref[...] = stage[...]


def middle_kernel(n, lay, stage, x_other, *refs):
    count = n // 2 + 1
    got, (dlow_ref, a_ref, kept_ref) = refs[: n - 1], refs[n - 1 : n + 2]
    send, (x_ref, got_ref, up_ref) = refs[n + 2 : n + 2 + count], refs[n + 2 + count :]
    me, core = lax.axis_index("dp"), lax.axis_index("tensor")
    half, rows, picked = lay.half, lay.rows, lay.picked
    width = stage.shape[1]
    mine = pl.ds(pl.multiple_of(core * half, half), half)
    other = pl.ds(pl.multiple_of((1 - core) * half, half), half)
    for q in range(n):
        x_ref[mine, q * width : (q + 1) * width] = stage[lay.x(q), :]
    x_ref[other, :] = x_other[...]
    ranks = senders(n, 0, me, core)
    got_ref[me] = stage[lay.message :, :]
    for sender, message in zip(ranks[1:], got):
        got_ref[sender] = message[...]

    in_seg = stage[lay.mask : lay.mask + rows, :picked].astype(f32) > 0.0
    g = stage[lay.g : lay.g + rows, :]
    onehot = lay.own_rows(stage)
    up_maps = got_ref[:, picked:, :].reshape(-1, width)
    b_sel = dot(onehot, up_maps, 1, 0).astype(bf16)
    dlow = jnp.where(in_seg, adapter_scale * dot(g, b_sel, 1, 1), 0.0).astype(bf16)
    dlow_ref[...] = dlow
    parts = n // 2
    a_ref[...] = got_ref[pl.ds(pl.multiple_of(core * parts, parts), parts), :picked, :]
    kept_ref[...] = stage[lay.g : lay.message, :]
    targets = partners(n, 1, me, core)
    for target, message in zip(targets, send):
        at = pl.ds(pl.multiple_of(target * width, width), width)
        message[:picked, :] = dot(dlow, x_ref[:, at], 0, 0).astype(bf16)

    low = jnp.zeros((rows, picked), f32)
    for q in range(n):
        low += dot(x_ref[:, q * width : (q + 1) * width], got_ref[q, :picked, :], 1, 1)
    low = jnp.where(in_seg, low, 0.0).astype(bf16)
    low_wide = dot(low, onehot, 1, 0).astype(bf16)
    up = (adapter_scale * dot(low_wide, g, 0, 0)).astype(bf16)
    up_ref[...] = up.reshape(up_ref.shape)
    for target, message in zip(targets, send):
        message[picked:, :] = up_ref[target]


def base_kernel(kept_ref, w_ref, out_ref):
    out_ref[...] = dot(kept_ref[: out_ref.shape[0], :], w_ref[...], 1, 1)


def grad_x_kernel(base_ref, dlow_ref, a_ref, out_hbm, out_ref, sems):
    steps, picked, width = a_ref.shape
    done = []
    for j in range(steps):
        at = pl.ds(j * width, width)
        total = base_ref[:, at] + dot(dlow_ref[...], a_ref[j], 1, 0)
        out_ref[:, at] = total.astype(bf16)
        done += start_all([out_ref.at[:, at]], [out_hbm.at[:, at]], sems, j)
    wait_all(done)


def final_kernel(n, lay, kept_ref, *refs):
    got, (a_ref, up_ref, rows_ref) = refs[:n], refs[n:]
    me, core = lax.axis_index("dp"), lax.axis_index("tensor")
    piece, picked = up_ref.shape[1], lay.picked
    for sender, message in zip(senders(n, 1, me, core), got):
        rows_ref[sender] = message[...]
    rows = rows_ref[:, :picked, :].reshape(n * picked, rows_ref.shape[2])
    a_ref[...] = dot(rows, lay.all_rows(kept_ref), 0, 0)
    at = pl.ds(pl.multiple_of(core * piece, piece), piece)
    up_ref[...] = jnp.sum(rows_ref[:, picked:, at].astype(f32), axis=0)


def exchange(messages, turn, beside):
    n = 2 * len(messages)
    got = [
        lax.ppermute(
            message,
            ("dp", "tensor"),
            [(2 * i + c, 2 * (i ^ step[c]) + c) for i in range(n) for c in range(2)],
        )
        for message, step in zip(messages, steps(n, turn))
    ]
    got[0], beside = lax.optimization_barrier((got[0], beside))
    passed = [
        lax.ppermute(message, "tensor", [(0, 1), (1, 0)])
        for message, (a, b) in zip(got, steps(n, turn))
        if a != b
    ]
    return got + passed, beside


def local_kernels(
    inputs,
    output_gradient,
    frozen_weight,
    down_maps,
    up_maps,
    segment_start,
    segment_adapter,
    adapter_slot,
    token_count,
):
    tok_half, model_width = inputs.shape
    tok_rows, out_width = output_gradient.shape
    column_total, slot_width = down_maps.shape
    half = frozen_weight.shape[0]
    n = lax.axis_size("dp")
    piece = out_width // lax.axis_size("tensor")
    segs = segment_start.shape[1]
    picked = segs * ADAPTER_RANK
    shape = jax.ShapeDtypeStruct
    message = shape((picked + ADAPTER_RANK, column_total), bf16)
    count = n // 2 + 1
    starts, chosen = segment_start.T, segment_adapter.T

    tables = [
        pltpu.SMEM(starts.shape, i32),
        pltpu.SMEM(chosen.shape, i32),
        pltpu.SMEM(adapter_slot.shape, i32),
        pltpu.SMEM(token_count.shape, i32),
    ]
    dma = pltpu.SemaphoreType.DMA

    lay = Staged(n, tok_half, tok_rows, picked, column_total, slot_width)
    own, *sent = pl.pallas_call(
        functools.partial(pack_kernel, n),
        out_shape=[message] * count,
        in_specs=[HBM] * 4,
        out_specs=[HBM] * count,
        scratch_shapes=tables[1:3]
        + [
            pltpu.VMEM(down_maps.shape, bf16),
            pltpu.VMEM(up_maps.shape, bf16),
            pltpu.VMEM((count,) + message.shape, bf16),
            dma((4 + count,)),
        ],
        compiler_params=params(56),
    )(chosen, adapter_slot, down_maps, up_maps)
    sent, x_late = lax.optimization_barrier((sent, inputs))
    x_other = lax.ppermute(x_late, "tensor", [(0, 1), (1, 0)])
    stage = pl.pallas_call(
        functools.partial(stage_kernel, n, lay),
        out_shape=shape(lay.shape, bf16),
        in_specs=[HBM] * 7,
        out_specs=HBM,
        scratch_shapes=tables + [pltpu.VMEM(lay.shape, bf16), dma((7 + n,))],
        compiler_params=params(56),
        cost_estimate=pl.CostEstimate(flops=0, bytes_accessed=1 << 21, transcendentals=0),
    )(starts, chosen, adapter_slot, token_count, output_gradient, inputs, own)
    got, stage = exchange(sent, 0, stage)
    stage = pl.pallas_call(
        hand_on_kernel,
        out_shape=shape(lay.shape, bf16),
        in_specs=[VMEM],
        out_specs=VMEM,
        compiler_params=params(8),
        cost_estimate=pl.CostEstimate(flops=0, bytes_accessed=1 << 21, transcendentals=0),
    )(stage)

    dlow, a_half, kept, own, *sent = pl.pallas_call(
        functools.partial(middle_kernel, n, lay),
        out_shape=[
            shape((tok_rows, picked), bf16),
            shape((n // 2, picked, column_total), bf16),
            shape((2 * tok_rows, out_width), bf16),
        ]
        + [message] * count,
        in_specs=[VMEM] * (1 + n),
        out_specs=[VMEM] * (3 + count),
        scratch_shapes=[
            pltpu.VMEM((tok_rows, model_width), bf16),
            pltpu.VMEM((n,) + message.shape, bf16),
            pltpu.VMEM((n, ADAPTER_RANK, out_width), bf16),
        ],
        compiler_params=params(8),
    )(stage, x_other, *got)
    base = pl.pallas_call(
        base_kernel,
        out_shape=shape((tok_rows, half), f32),
        in_specs=[VMEM, VMEM],
        out_specs=VMEM,
        compiler_params=params(8),
        cost_estimate=pl.CostEstimate(
            flops=2 * tok_rows * half * out_width,
            bytes_accessed=4 * half * tok_rows + 2 * half * out_width,
            transcendentals=0,
        ),
    )(kept, frozen_weight)
    grad_x = pl.pallas_call(
        grad_x_kernel,
        out_shape=shape((tok_rows, half), bf16),
        in_specs=[VMEM] * 3,
        out_specs=HBM,
        scratch_shapes=[pltpu.VMEM((tok_rows, half), bf16), dma((n // 2,))],
        compiler_params=params(8),
        cost_estimate=pl.CostEstimate(
            flops=2 * tok_rows * half * picked,
            bytes_accessed=6 * half * tok_rows,
            transcendentals=0,
        ),
    )(base, dlow, a_half)

    got, grad_x = exchange(sent, 1, grad_x)

    grad_a, up_map_gradient = pl.pallas_call(
        functools.partial(final_kernel, n, lay),
        out_shape=[shape((column_total, slot_width), f32), shape((ADAPTER_RANK, piece), f32)],
        in_specs=[VMEM] * (1 + n),
        out_specs=[VMEM, VMEM],
        scratch_shapes=[pltpu.VMEM((n,) + message.shape, bf16)],
        compiler_params=params(8),
    )(kept, own, *got)
    return grad_x, grad_a, up_map_gradient


def local_plain(
    inputs,
    output_gradient,
    frozen_weight,
    down_maps,
    up_maps,
    segment_start,
    segment_adapter,
    adapter_slot,
    token_count,
):
    tok_rows, out_width = output_gradient.shape
    column_total = down_maps.shape[0]
    adapter_list = adapter_slot.shape[0]
    segs = segment_start.shape[1]
    dp_size = lax.axis_size("dp")
    my_rank = lax.axis_index("dp")
    core_idx = lax.axis_index("tensor")
    picked = segs * ADAPTER_RANK
    piece_out = out_width // lax.axis_size("tensor")
    half = frozen_weight.shape[0]

    x_other = lax.ppermute(inputs, "tensor", [(0, 1), (1, 0)])
    adapter_ids = jnp.arange(adapter_list, dtype=i32)
    slot_table = jnp.sum(
        jnp.where(segment_adapter[..., None] == adapter_ids, adapter_slot, 0), axis=-1
    )
    column = slot_table[:, :, None] * ADAPTER_RANK + jnp.arange(ADAPTER_RANK, dtype=i32)
    onehot = (
        column.reshape(-1)[:, None] == jnp.arange(adapter_list * ADAPTER_RANK, dtype=i32)
    ).astype(bf16)

    a_send = dot(onehot, down_maps, 1, 1).astype(bf16).reshape(dp_size, picked, column_total)
    b_send = jnp.broadcast_to(up_maps[None], (dp_size,) + up_maps.shape)
    a_got = lax.all_to_all(a_send, "dp", 0, 0, tiled=True)
    b_got = lax.all_to_all(b_send, "dp", 0, 0, tiled=True)

    position = jnp.arange(tok_rows, dtype=i32)
    starts = lax.dynamic_index_in_dim(segment_start, my_rank, 0, keepdims=False)
    live = position < lax.dynamic_index_in_dim(token_count, my_rank, 0, keepdims=False)
    my_seg = jnp.sum((starts[None, :] <= position[:, None]).astype(i32), axis=1) - 1
    in_seg = my_seg[:, None] == (jnp.arange(picked, dtype=i32) // ADAPTER_RANK)[None, :]
    my_onehot = lax.dynamic_slice_in_dim(onehot, my_rank * picked, picked, 0)
    g = jnp.where(live[:, None], output_gradient, jnp.zeros_like(output_gradient))
    base = dot(g, frozen_weight, 1, 1)

    b_sel = dot(my_onehot, b_got.reshape(-1, out_width), 1, 0).astype(bf16)
    dlow = (adapter_scale * dot(g, b_sel, 1, 1)).astype(bf16)
    dlow = jnp.where(in_seg, dlow, jnp.zeros_like(dlow))
    a_sel = jnp.moveaxis(a_got, 0, 1).reshape(picked, -1)
    first = core_idx == 0
    x = jnp.concatenate(
        [jnp.where(first, inputs, x_other), jnp.where(first, x_other, inputs)], axis=0
    )
    low = dot(x, a_sel, 1, 1).astype(bf16)
    low = jnp.where(in_seg, low, jnp.zeros_like(low))
    low_wide = dot(low, my_onehot, 1, 0).astype(bf16)

    ga_send = dot(dlow, x, 0, 0).astype(bf16).reshape(picked, dp_size, column_total)
    ga_got = lax.all_to_all(jnp.moveaxis(ga_send, 1, 0), "dp", 0, 0, tiled=True)
    g_piece = lax.dynamic_slice_in_dim(g, core_idx * piece_out, piece_out, 1)
    up_send = (adapter_scale * dot(low_wide, g_piece, 0, 0)).astype(bf16)
    up_got = lax.all_to_all(up_send.reshape(dp_size, -1, piece_out), "dp", 0, 0, tiled=True)

    a_half = lax.dynamic_slice_in_dim(a_sel, core_idx * half, half, 1)
    grad_x = (base + dot(dlow, a_half, 1, 0)).astype(bf16)
    grad_a = dot(ga_got.reshape(dp_size * picked, column_total), onehot, 0, 0)
    up_map_gradient = jnp.sum(up_got.astype(f32), axis=0)
    return grad_x, grad_a, up_map_gradient


def local(*args):
    down_maps, up_maps = args[3], args[4]
    n, tp = lax.axis_size("dp"), lax.axis_size("tensor")
    out_width = up_maps.shape[1]
    kernels_fit = (
        n == 8
        and tp == 2
        and down_maps.shape[0] == out_width
        and down_maps.shape[1] == n * up_maps.shape[0]
        and out_width % (128 * tp) == 0
        and out_width >= 4 * down_maps.shape[1]
        and args[1].shape[0] == 2 * args[0].shape[0] == down_maps.shape[1]
        and args[5].shape[1] * ADAPTER_RANK * n == 2 * down_maps.shape[1]
    )
    return (local_kernels if kernels_fit else local_plain)(*args)


def solution(mesh):
    in_specs = (
        P(("groups", "dp", "tensor"), None),
        P(("groups", "dp"), None),
        P("tensor", None),
        P(("groups", "dp"), None),
        P(("groups", "dp"), None),
        P("groups", None),
        P("groups", None),
        P("groups"),
        P("groups"),
    )
    out_specs = (
        P(("groups", "dp"), "tensor"),
        P(("groups", "dp"), None),
        P(("groups", "dp"), "tensor"),
    )
    return jax.shard_map(local, mesh=mesh, in_specs=in_specs, out_specs=out_specs, check_vma=False)
```

```python
import functools

import jax
import jax.numpy as jnp
from jax import lax
from jax.experimental import pallas as pl
from jax.experimental.pallas import tpu as pltpu
from jax.sharding import PartitionSpec as P

ADAPTER_RANK = 16
adapter_scale = 2.0

bf16, f32, i32 = jnp.bfloat16, jnp.float32, jnp.int32

HBM = pl.BlockSpec(memory_space=pltpu.HBM)
VMEM = pl.BlockSpec(memory_space=pltpu.VMEM)


def dot(a, b, ca, cb):
    return lax.dot_general(a, b, (((ca,), (cb,)), ((), ())), preferred_element_type=f32)


def params(mib):
    return pltpu.CompilerParams(vmem_limit_bytes=mib << 20)


def slot_rows(chosen_ref, slot_ref, ranks, width):
    lane = lax.broadcasted_iota(i32, (ADAPTER_RANK, width), 1)
    row = lax.broadcasted_iota(i32, (ADAPTER_RANK, width), 0)
    rows = []
    for rank in ranks:
        for k in range(chosen_ref.shape[0]):
            first = slot_ref[chosen_ref[k, rank]] * ADAPTER_RANK
            rows.append(jnp.where(lane == row + first, 1.0, 0.0))
    return jnp.concatenate(rows, axis=0).astype(bf16)


def start_all(sources, targets, sems, first=0):
    copies = [
        pltpu.make_async_copy(source, target, sems.at[first + k])
        for k, (source, target) in enumerate(zip(sources, targets))
    ]
    for copy in copies:
        copy.start()
    return copies


def wait_all(copies):
    for copy in copies:
        copy.wait()


def steps(n, turn):
    half = n // 2
    if turn == 0:
        return [(half, half + 1), (n - 1, n - 2), (2, 3), (1, 1)]
    return [(n - 1, half + 1), (3, n - 2), (2, half), (1, 1)]


def partners(n, turn, me, core):
    return [me] + [me ^ jnp.where(core == 0, a, b) for a, b in steps(n, turn)]


def senders(n, turn, me, core):
    passed = [me ^ jnp.where(core == 0, b, a) for a, b in steps(n, turn) if a != b]
    return partners(n, turn, me, core) + passed


class Staged:
    def __init__(self, n, half, rows, picked, width, slots):
        self.n, self.half, self.rows, self.picked, self.slots = n, half, rows, picked, slots
        self.g = n * half
        self.mask = self.g + rows
        self.message = self.mask + rows
        self.shape = (self.message + picked + ADAPTER_RANK, width)

    def x(self, q):
        return pl.ds(q * self.half, self.half)

    def own_rows(self, ref):
        return ref[self.mask : self.mask + self.picked, self.slots : 2 * self.slots]

    def all_rows(self, kept):
        parts = self.n * self.picked // self.rows
        at = [pl.ds((2 + k) * self.slots, self.slots) for k in range(parts)]
        return jnp.concatenate([kept[self.rows :, k] for k in at], axis=0)


def pack_kernel(n, chosen_hbm, slot_hbm, down_hbm, up_hbm, *refs):
    count = n // 2 + 1
    send, (chosen_ref, slot_ref, down_ref, up_ref, out_ref, sems) = refs[:count], refs[count:]
    tables = start_all([chosen_hbm, slot_hbm], [chosen_ref, slot_ref], sems)
    maps = start_all([down_hbm, up_hbm], [down_ref, up_ref], sems, 2)
    ranks = partners(n, 0, lax.axis_index("dp"), lax.axis_index("tensor"))
    wait_all(tables)
    onehot = slot_rows(chosen_ref, slot_ref, ranks, down_ref.shape[1])
    picked = onehot.shape[0] // count
    wait_all(maps)
    columns = dot(onehot, down_ref[...], 1, 1).astype(bf16)
    for k in range(count):
        out_ref[k, :picked, :] = columns[k * picked : (k + 1) * picked]
        out_ref[k, picked:, :] = up_ref[...]
    wait_all(start_all([out_ref.at[k] for k in range(count)], send, sems, 4))


def stage_kernel(
    n, lay, start_hbm, chosen_hbm, slot_hbm, count_hbm, g_hbm, x_hbm, own_hbm,
    stage_hbm, start_ref, chosen_ref, slot_ref, count_ref, stage, sems,
):
    rows, picked, slots = lay.rows, lay.picked, lay.slots
    width = stage.shape[1]
    tables = start_all(
        [chosen_hbm, slot_hbm, start_hbm, count_hbm], [chosen_ref, slot_ref, start_ref, count_ref], sems
    )
    gradient = start_all([g_hbm], [stage.at[pl.ds(lay.g, rows)]], sems, 4)
    other = start_all(
        [own_hbm] + [x_hbm.at[:, pl.ds(q * width, width)] for q in range(n)],
        [stage.at[pl.ds(lay.message, picked + ADAPTER_RANK)]] + [stage.at[lay.x(q)] for q in range(n)],
        sems,
        5,
    )
    me = lax.axis_index("dp")
    wait_all(tables)
    position = lax.broadcasted_iota(i32, (rows, slots), 0)
    group = lax.broadcasted_iota(i32, (rows, slots), 1) // ADAPTER_RANK
    segment = jnp.full((rows, slots), -1, i32)
    for k in range(start_ref.shape[0]):
        segment += jnp.where(position >= start_ref[k, me], 1, 0)
    stage[lay.mask : lay.mask + rows, :slots] = jnp.where(segment == group, 1.0, 0.0).astype(bf16)
    mine = slot_rows(chosen_ref, slot_ref, [me], slots)
    stage[lay.mask : lay.mask + picked, slots : 2 * slots] = mine
    every = slot_rows(chosen_ref, slot_ref, range(n), slots)
    for k in range(n * picked // rows):
        at = pl.ds((2 + k) * slots, slots)
        stage[lay.mask : lay.mask + rows, at] = every[k * rows : (k + 1) * rows]
    wait_all(gradient)
    live = lax.broadcasted_iota(i32, (rows, width), 0) < count_ref[me]
    g = stage[lay.g : lay.g + rows, :]
    stage[lay.g : lay.g + rows, :] = jnp.where(live, g, jnp.zeros_like(g))
    wait_all(other)
    wait_all(start_all([stage], [stage_hbm], sems, 6 + n))


def hand_on_kernel(stage, out_ref):
    out_ref[...] = stage[...]


def middle_kernel(n, lay, stage, x_other, *refs):
    count = n // 2 + 1
    got, (dlow_ref, a_ref, kept_ref) = refs[: n - 1], refs[n - 1 : n + 2]
    send, (x_ref, got_ref, up_ref) = refs[n + 2 : n + 2 + count], refs[n + 2 + count :]
    me, core = lax.axis_index("dp"), lax.axis_index("tensor")
    half, rows, picked = lay.half, lay.rows, lay.picked
    width = stage.shape[1]
    mine = pl.ds(pl.multiple_of(core * half, half), half)
    other = pl.ds(pl.multiple_of((1 - core) * half, half), half)
    for q in range(n):
        x_ref[mine, q * width : (q + 1) * width] = stage[lay.x(q), :]
    x_ref[other, :] = x_other[...]
    ranks = senders(n, 0, me, core)
    got_ref[me] = stage[lay.message :, :]
    for sender, message in zip(ranks[1:], got):
        got_ref[sender] = message[...]

    in_seg = stage[lay.mask : lay.mask + rows, :picked].astype(f32) > 0.0
    g = stage[lay.g : lay.g + rows, :]
    onehot = lay.own_rows(stage)
    up_maps = got_ref[:, picked:, :].reshape(-1, width)
    b_sel = dot(onehot, up_maps, 1, 0).astype(bf16)
    dlow = jnp.where(in_seg, adapter_scale * dot(g, b_sel, 1, 1), 0.0).astype(bf16)
    dlow_ref[...] = dlow
    parts = n // 2
    a_ref[...] = got_ref[pl.ds(pl.multiple_of(core * parts, parts), parts), :picked, :]
    kept_ref[...] = stage[lay.g : lay.message, :]
    targets = partners(n, 1, me, core)
    for target, message in zip(targets, send):
        at = pl.ds(pl.multiple_of(target * width, width), width)
        message[:picked, :] = dot(dlow, x_ref[:, at], 0, 0).astype(bf16)

    low = jnp.zeros((rows, picked), f32)
    for q in range(n):
        low += dot(x_ref[:, q * width : (q + 1) * width], got_ref[q, :picked, :], 1, 1)
    low = jnp.where(in_seg, low, 0.0).astype(bf16)
    low_wide = dot(low, onehot, 1, 0).astype(bf16)
    up = (adapter_scale * dot(low_wide, g, 0, 0)).astype(bf16)
    up_ref[...] = up.reshape(up_ref.shape)
    for target, message in zip(targets, send):
        message[picked:, :] = up_ref[target]


def base_kernel(kept_ref, w_ref, out_ref):
    out_ref[...] = dot(kept_ref[: out_ref.shape[0], :], w_ref[...], 1, 1)


def grad_x_kernel(base_ref, dlow_ref, a_ref, out_hbm, out_ref, sems):
    steps, picked, width = a_ref.shape
    done = []
    for j in range(steps):
        at = pl.ds(j * width, width)
        total = base_ref[:, at] + dot(dlow_ref[...], a_ref[j], 1, 0)
        out_ref[:, at] = total.astype(bf16)
        done += start_all([out_ref.at[:, at]], [out_hbm.at[:, at]], sems, j)
    wait_all(done)


def final_kernel(n, lay, kept_ref, *refs):
    got, (a_ref, up_ref, rows_ref) = refs[:n], refs[n:]
    me, core = lax.axis_index("dp"), lax.axis_index("tensor")
    piece, picked = up_ref.shape[1], lay.picked
    for sender, message in zip(senders(n, 1, me, core), got):
        rows_ref[sender] = message[...]
    rows = rows_ref[:, :picked, :].reshape(n * picked, rows_ref.shape[2])
    a_ref[...] = dot(rows, lay.all_rows(kept_ref), 0, 0)
    at = pl.ds(pl.multiple_of(core * piece, piece), piece)
    up_ref[...] = jnp.sum(rows_ref[:, picked:, at].astype(f32), axis=0)


def exchange(messages, turn, beside):
    n = 2 * len(messages)
    got = [
        lax.ppermute(
            message,
            ("dp", "tensor"),
            [(2 * i + c, 2 * (i ^ step[c]) + c) for i in range(n) for c in range(2)],
        )
        for message, step in zip(messages, steps(n, turn))
    ]
    got[0], beside = lax.optimization_barrier((got[0], beside))
    passed = [
        lax.ppermute(message, "tensor", [(0, 1), (1, 0)])
        for message, (a, b) in zip(got, steps(n, turn))
        if a != b
    ]
    return got + passed, beside


def local_kernels(
    inputs,
    output_gradient,
    frozen_weight,
    down_maps,
    up_maps,
    segment_start,
    segment_adapter,
    adapter_slot,
    token_count,
):
    tok_half, model_width = inputs.shape
    tok_rows, out_width = output_gradient.shape
    column_total, slot_width = down_maps.shape
    half = frozen_weight.shape[0]
    n = lax.axis_size("dp")
    piece = out_width // lax.axis_size("tensor")
    segs = segment_start.shape[1]
    picked = segs * ADAPTER_RANK
    shape = jax.ShapeDtypeStruct
    message = shape((picked + ADAPTER_RANK, column_total), bf16)
    count = n // 2 + 1
    starts, chosen = segment_start.T, segment_adapter.T

    tables = [
        pltpu.SMEM(starts.shape, i32),
        pltpu.SMEM(chosen.shape, i32),
        pltpu.SMEM(adapter_slot.shape, i32),
        pltpu.SMEM(token_count.shape, i32),
    ]
    dma = pltpu.SemaphoreType.DMA

    lay = Staged(n, tok_half, tok_rows, picked, column_total, slot_width)
    own, *sent = pl.pallas_call(
        functools.partial(pack_kernel, n),
        out_shape=[message] * count,
        in_specs=[HBM] * 4,
        out_specs=[HBM] * count,
        scratch_shapes=tables[1:3]
        + [
            pltpu.VMEM(down_maps.shape, bf16),
            pltpu.VMEM(up_maps.shape, bf16),
            pltpu.VMEM((count,) + message.shape, bf16),
            dma((4 + count,)),
        ],
        compiler_params=params(56),
    )(chosen, adapter_slot, down_maps, up_maps)
    sent, x_late = lax.optimization_barrier((sent, inputs))
    x_other = lax.ppermute(x_late, "tensor", [(0, 1), (1, 0)])
    stage = pl.pallas_call(
        functools.partial(stage_kernel, n, lay),
        out_shape=shape(lay.shape, bf16),
        in_specs=[HBM] * 7,
        out_specs=HBM,
        scratch_shapes=tables + [pltpu.VMEM(lay.shape, bf16), dma((7 + n,))],
        compiler_params=params(56),
        cost_estimate=pl.CostEstimate(flops=0, bytes_accessed=1 << 21, transcendentals=0),
    )(starts, chosen, adapter_slot, token_count, output_gradient, inputs, own)
    stage = pl.pallas_call(
        hand_on_kernel,
        out_shape=shape(lay.shape, bf16),
        in_specs=[VMEM],
        out_specs=VMEM,
        compiler_params=params(8),
        cost_estimate=pl.CostEstimate(flops=0, bytes_accessed=1 << 21, transcendentals=0),
    )(stage)
    got, stage = exchange(sent, 0, stage)

    dlow, a_half, kept, own, *sent = pl.pallas_call(
        functools.partial(middle_kernel, n, lay),
        out_shape=[
            shape((tok_rows, picked), bf16),
            shape((n // 2, picked, column_total), bf16),
            shape((2 * tok_rows, out_width), bf16),
        ]
        + [message] * count,
        in_specs=[VMEM] * (1 + n),
        out_specs=[VMEM] * (3 + count),
        scratch_shapes=[
            pltpu.VMEM((tok_rows, model_width), bf16),
            pltpu.VMEM((n,) + message.shape, bf16),
            pltpu.VMEM((n, ADAPTER_RANK, out_width), bf16),
        ],
        compiler_params=params(8),
    )(stage, x_other, *got)
    base = pl.pallas_call(
        base_kernel,
        out_shape=shape((tok_rows, half), f32),
        in_specs=[VMEM, VMEM],
        out_specs=VMEM,
        compiler_params=params(8),
        cost_estimate=pl.CostEstimate(
            flops=2 * tok_rows * half * out_width,
            bytes_accessed=4 * half * tok_rows + 2 * half * out_width,
            transcendentals=0,
        ),
    )(kept, frozen_weight)
    grad_x = pl.pallas_call(
        grad_x_kernel,
        out_shape=shape((tok_rows, half), bf16),
        in_specs=[VMEM] * 3,
        out_specs=HBM,
        scratch_shapes=[pltpu.VMEM((tok_rows, half), bf16), dma((n // 2,))],
        compiler_params=params(8),
        cost_estimate=pl.CostEstimate(
            flops=2 * tok_rows * half * picked,
            bytes_accessed=6 * half * tok_rows,
            transcendentals=0,
        ),
    )(base, dlow, a_half)

    got, grad_x = exchange(sent, 1, grad_x)

    grad_a, up_map_gradient = pl.pallas_call(
        functools.partial(final_kernel, n, lay),
        out_shape=[shape((column_total, slot_width), f32), shape((ADAPTER_RANK, piece), f32)],
        in_specs=[VMEM] * (1 + n),
        out_specs=[VMEM, VMEM],
        scratch_shapes=[pltpu.VMEM((n,) + message.shape, bf16)],
        compiler_params=params(8),
    )(kept, own, *got)
    return grad_x, grad_a, up_map_gradient


def local_plain(
    inputs,
    output_gradient,
    frozen_weight,
    down_maps,
    up_maps,
    segment_start,
    segment_adapter,
    adapter_slot,
    token_count,
):
    tok_rows, out_width = output_gradient.shape
    column_total = down_maps.shape[0]
    adapter_list = adapter_slot.shape[0]
    segs = segment_start.shape[1]
    dp_size = lax.axis_size("dp")
    my_rank = lax.axis_index("dp")
    core_idx = lax.axis_index("tensor")
    picked = segs * ADAPTER_RANK
    piece_out = out_width // lax.axis_size("tensor")
    half = frozen_weight.shape[0]

    x_other = lax.ppermute(inputs, "tensor", [(0, 1), (1, 0)])
    adapter_ids = jnp.arange(adapter_list, dtype=i32)
    slot_table = jnp.sum(
        jnp.where(segment_adapter[..., None] == adapter_ids, adapter_slot, 0), axis=-1
    )
    column = slot_table[:, :, None] * ADAPTER_RANK + jnp.arange(ADAPTER_RANK, dtype=i32)
    onehot = (
        column.reshape(-1)[:, None] == jnp.arange(adapter_list * ADAPTER_RANK, dtype=i32)
    ).astype(bf16)

    a_send = dot(onehot, down_maps, 1, 1).astype(bf16).reshape(dp_size, picked, column_total)
    b_send = jnp.broadcast_to(up_maps[None], (dp_size,) + up_maps.shape)
    a_got = lax.all_to_all(a_send, "dp", 0, 0, tiled=True)
    b_got = lax.all_to_all(b_send, "dp", 0, 0, tiled=True)

    position = jnp.arange(tok_rows, dtype=i32)
    starts = lax.dynamic_index_in_dim(segment_start, my_rank, 0, keepdims=False)
    live = position < lax.dynamic_index_in_dim(token_count, my_rank, 0, keepdims=False)
    my_seg = jnp.sum((starts[None, :] <= position[:, None]).astype(i32), axis=1) - 1
    in_seg = my_seg[:, None] == (jnp.arange(picked, dtype=i32) // ADAPTER_RANK)[None, :]
    my_onehot = lax.dynamic_slice_in_dim(onehot, my_rank * picked, picked, 0)
    g = jnp.where(live[:, None], output_gradient, jnp.zeros_like(output_gradient))
    base = dot(g, frozen_weight, 1, 1)

    b_sel = dot(my_onehot, b_got.reshape(-1, out_width), 1, 0).astype(bf16)
    dlow = (adapter_scale * dot(g, b_sel, 1, 1)).astype(bf16)
    dlow = jnp.where(in_seg, dlow, jnp.zeros_like(dlow))
    a_sel = jnp.moveaxis(a_got, 0, 1).reshape(picked, -1)
    first = core_idx == 0
    x = jnp.concatenate(
        [jnp.where(first, inputs, x_other), jnp.where(first, x_other, inputs)], axis=0
    )
    low = dot(x, a_sel, 1, 1).astype(bf16)
    low = jnp.where(in_seg, low, jnp.zeros_like(low))
    low_wide = dot(low, my_onehot, 1, 0).astype(bf16)

    ga_send = dot(dlow, x, 0, 0).astype(bf16).reshape(picked, dp_size, column_total)
    ga_got = lax.all_to_all(jnp.moveaxis(ga_send, 1, 0), "dp", 0, 0, tiled=True)
    g_piece = lax.dynamic_slice_in_dim(g, core_idx * piece_out, piece_out, 1)
    up_send = (adapter_scale * dot(low_wide, g_piece, 0, 0)).astype(bf16)
    up_got = lax.all_to_all(up_send.reshape(dp_size, -1, piece_out), "dp", 0, 0, tiled=True)

    a_half = lax.dynamic_slice_in_dim(a_sel, core_idx * half, half, 1)
    grad_x = (base + dot(dlow, a_half, 1, 0)).astype(bf16)
    grad_a = dot(ga_got.reshape(dp_size * picked, column_total), onehot, 0, 0)
    up_map_gradient = jnp.sum(up_got.astype(f32), axis=0)
    return grad_x, grad_a, up_map_gradient


def local(*args):
    down_maps, up_maps = args[3], args[4]
    n, tp = lax.axis_size("dp"), lax.axis_size("tensor")
    out_width = up_maps.shape[1]
    kernels_fit = (
        n == 8
        and tp == 2
        and down_maps.shape[0] == out_width
        and down_maps.shape[1] == n * up_maps.shape[0]
        and out_width % (128 * tp) == 0
        and out_width >= 4 * down_maps.shape[1]
        and args[1].shape[0] == 2 * args[0].shape[0] == down_maps.shape[1]
        and args[5].shape[1] * ADAPTER_RANK * n == 2 * down_maps.shape[1]
    )
    return (local_kernels if kernels_fit else local_plain)(*args)


def solution(mesh):
    in_specs = (
        P(("groups", "dp", "tensor"), None),
        P(("groups", "dp"), None),
        P("tensor", None),
        P(("groups", "dp"), None),
        P(("groups", "dp"), None),
        P("groups", None),
        P("groups", None),
        P("groups"),
        P("groups"),
    )
    out_specs = (
        P(("groups", "dp"), "tensor"),
        P(("groups", "dp"), None),
        P(("groups", "dp"), "tensor"),
    )
    return jax.shard_map(local, mesh=mesh, in_specs=in_specs, out_specs=out_specs, check_vma=False)
```

```python
import functools

import jax
import jax.numpy as jnp
from jax import lax
from jax.experimental import pallas as pl
from jax.experimental.pallas import tpu as pltpu
from jax.sharding import PartitionSpec as P

ADAPTER_RANK = 16
adapter_scale = 2.0

bf16, f32, i32 = jnp.bfloat16, jnp.float32, jnp.int32

HBM = pl.BlockSpec(memory_space=pltpu.HBM)
VMEM = pl.BlockSpec(memory_space=pltpu.VMEM)


def dot(a, b, ca, cb):
    return lax.dot_general(a, b, (((ca,), (cb,)), ((), ())), preferred_element_type=f32)


def params(mib):
    return pltpu.CompilerParams(vmem_limit_bytes=mib << 20)


def slot_rows(chosen_ref, slot_ref, ranks, width):
    lane = lax.broadcasted_iota(i32, (ADAPTER_RANK, width), 1)
    row = lax.broadcasted_iota(i32, (ADAPTER_RANK, width), 0)
    rows = []
    for rank in ranks:
        for k in range(chosen_ref.shape[0]):
            first = slot_ref[chosen_ref[k, rank]] * ADAPTER_RANK
            rows.append(jnp.where(lane == row + first, 1.0, 0.0))
    return jnp.concatenate(rows, axis=0).astype(bf16)


def start_all(sources, targets, sems, first=0):
    copies = [
        pltpu.make_async_copy(source, target, sems.at[first + k])
        for k, (source, target) in enumerate(zip(sources, targets))
    ]
    for copy in copies:
        copy.start()
    return copies


def wait_all(copies):
    for copy in copies:
        copy.wait()


def steps(n):
    return [(n - 1, n // 2 + 1), (3, n - 2), (2, n // 2), (1, 1)]


def partners(n, me, core):
    return [me] + [me ^ jnp.where(core == 0, a, b) for a, b in steps(n)]


def senders(n, me, core):
    passed = [me ^ jnp.where(core == 0, b, a) for a, b in steps(n) if a != b]
    return partners(n, me, core) + passed


def in_hbm(*arrays):
    return [pltpu.with_memory_space_constraint(array, pltpu.HBM) for array in arrays]


def pack_kernel(n, chosen_hbm, slot_hbm, down_hbm, up_hbm, *refs):
    count = n // 2 + 1
    send, (chosen_ref, slot_ref, down_ref, up_ref, sems) = refs[:count], refs[count:]
    tables = start_all([chosen_hbm, slot_hbm], [chosen_ref, slot_ref], sems)
    maps = start_all([down_hbm, up_hbm], [down_ref, up_ref], sems, 2)
    ranks = partners(n, lax.axis_index("dp"), lax.axis_index("tensor"))
    wait_all(tables)
    onehot = slot_rows(chosen_ref, slot_ref, ranks, down_ref.shape[1])
    picked = onehot.shape[0] // count
    wait_all(maps)
    columns = dot(onehot, down_ref[...], 1, 1).astype(bf16)
    for k in range(count):
        send[k][:picked, :] = columns[k * picked : (k + 1) * picked]
        send[k][picked:, :] = up_ref[...]


def stage_kernel(
    n, picked, start_hbm, chosen_hbm, slot_hbm, count_hbm, g_hbm, x_mine, x_other,
    x_ref, kept_ref, start_ref, chosen_ref, slot_ref, count_ref, sems,
):
    rows, width = g_hbm.shape
    half = x_mine.shape[0]
    slots = width // 4
    me, core = lax.axis_index("dp"), lax.axis_index("tensor")
    tables = start_all(
        [chosen_hbm, slot_hbm, start_hbm, count_hbm], [chosen_ref, slot_ref, start_ref, count_ref], sems
    )
    gradient = start_all([g_hbm], [kept_ref.at[pl.ds(0, rows)]], sems, 4)
    mine = pl.ds(pl.multiple_of(core * half, half), half)
    tokens = start_all([x_mine], [x_ref.at[mine]], sems, 5)
    x_ref[pl.ds(pl.multiple_of((1 - core) * half, half), half), :] = x_other[...]
    wait_all(tables)
    position = lax.broadcasted_iota(i32, (rows, slots), 0)
    group = lax.broadcasted_iota(i32, (rows, slots), 1) // ADAPTER_RANK
    segment = jnp.full((rows, slots), -1, i32)
    for k in range(start_ref.shape[0]):
        segment += jnp.where(position >= start_ref[k, me], 1, 0)
    kept_ref[rows:, :slots] = jnp.where(segment == group, 1.0, 0.0).astype(bf16)
    kept_ref[rows : rows + picked, slots : 2 * slots] = slot_rows(chosen_ref, slot_ref, [me], slots)
    every = slot_rows(chosen_ref, slot_ref, range(n), slots)
    kept_ref[rows:, 2 * slots : 3 * slots] = every[:rows]
    kept_ref[rows:, 3 * slots :] = every[rows:]
    wait_all(gradient)
    live = lax.broadcasted_iota(i32, (rows, width), 0) < count_ref[me]
    g = kept_ref[:rows, :]
    kept_ref[:rows, :] = jnp.where(live, g, jnp.zeros_like(g))
    wait_all(tokens)


def middle_kernel(n, kept_ref, x_ref, *refs):
    count = n // 2 + 1
    got, (dlow_ref, a_ref), send = refs[:n], refs[n : n + 2], refs[n + 2 : n + 2 + count]
    got_ref, up_ref = refs[n + 2 + count :]
    me, core = lax.axis_index("dp"), lax.axis_index("tensor")
    rows, picked = dlow_ref.shape
    width = kept_ref.shape[1]
    slots = width // 4
    for sender, message in zip(senders(n, me, core), got):
        got_ref[sender] = message[...]

    in_seg = kept_ref[rows:, :picked].astype(f32) > 0.0
    g = kept_ref[:rows, :]
    onehot = kept_ref[rows : rows + picked, slots : 2 * slots]
    up_maps = got_ref[:, picked:, :].reshape(-1, width)
    b_sel = dot(onehot, up_maps, 1, 0).astype(bf16)
    dlow = jnp.where(in_seg, adapter_scale * dot(g, b_sel, 1, 1), 0.0).astype(bf16)
    dlow_ref[...] = dlow
    parts = n // 2
    a_ref[...] = got_ref[pl.ds(pl.multiple_of(core * parts, parts), parts), :picked, :]
    targets = partners(n, me, core)
    for target, message in zip(targets, send):
        at = pl.ds(pl.multiple_of(target * width, width), width)
        message[:picked, :] = dot(dlow, x_ref[:, at], 0, 0).astype(bf16)

    low = jnp.zeros((rows, picked), f32)
    for q in range(n):
        low += dot(x_ref[:, q * width : (q + 1) * width], got_ref[q, :picked, :], 1, 1)
    low = jnp.where(in_seg, low, 0.0).astype(bf16)
    low_wide = dot(low, onehot, 1, 0).astype(bf16)
    up = (adapter_scale * dot(low_wide, g, 0, 0)).astype(bf16)
    up_ref[...] = up.reshape(up_ref.shape)
    for target, message in zip(targets, send):
        message[picked:, :] = up_ref[target]


def grad_x_kernel(kept_ref, w_ref, dlow_ref, a_ref, out_hbm, out_ref, sems):
    steps, picked, width = a_ref.shape
    g = kept_ref[: out_ref.shape[0], :]
    done = []
    for j in range(steps):
        at = pl.ds(j * width, width)
        total = dot(g, w_ref[at, :], 1, 1) + dot(dlow_ref[...], a_ref[j], 1, 0)
        out_ref[:, at] = total.astype(bf16)
        done += start_all([out_ref.at[:, at]], [out_hbm.at[:, at]], sems, j)
    wait_all(done)


def final_kernel(n, kept_ref, *refs):
    got, (a_ref, up_ref, rows_ref) = refs[:n], refs[n:]
    me, core = lax.axis_index("dp"), lax.axis_index("tensor")
    piece, picked = up_ref.shape[1], rows_ref.shape[1] - ADAPTER_RANK
    half, slots = kept_ref.shape[0] // 2, kept_ref.shape[1] // 4
    for sender, message in zip(senders(n, me, core), got):
        rows_ref[sender] = message[...]
    rows = rows_ref[:, :picked, :].reshape(n * picked, rows_ref.shape[2])
    onehot = jnp.concatenate(
        [kept_ref[half:, 2 * slots : 3 * slots], kept_ref[half:, 3 * slots :]], axis=0
    )
    a_ref[...] = dot(rows, onehot, 0, 0)
    at = pl.ds(pl.multiple_of(core * piece, piece), piece)
    up_ref[...] = jnp.sum(rows_ref[:, picked:, at].astype(f32), axis=0)


def exchange(messages, beside):
    n = 2 * len(messages)
    got = [
        lax.ppermute(
            message,
            ("dp", "tensor"),
            [(2 * i + c, 2 * (i ^ step[c]) + c) for i in range(n) for c in range(2)],
        )
        for message, step in zip(messages, steps(n))
    ]
    for k, (a, b) in enumerate(steps(n)):
        if a != b:
            got[k], beside = lax.optimization_barrier((got[k], beside))
    passed = [
        lax.ppermute(message, "tensor", [(0, 1), (1, 0)])
        for message, (a, b) in zip(got, steps(n))
        if a != b
    ]
    return got + passed, beside


def local_kernels(
    inputs,
    output_gradient,
    frozen_weight,
    down_maps,
    up_maps,
    segment_start,
    segment_adapter,
    adapter_slot,
    token_count,
):
    model_width = inputs.shape[1]
    tok_rows, out_width = output_gradient.shape
    column_total, slot_width = down_maps.shape
    half = frozen_weight.shape[0]
    n = lax.axis_size("dp")
    piece = out_width // lax.axis_size("tensor")
    segs = segment_start.shape[1]
    picked = segs * ADAPTER_RANK
    shape = jax.ShapeDtypeStruct
    message = shape((picked + ADAPTER_RANK, column_total), bf16)
    count = n // 2 + 1
    starts, chosen = segment_start.T, segment_adapter.T

    tables = [
        pltpu.SMEM(starts.shape, i32),
        pltpu.SMEM(chosen.shape, i32),
        pltpu.SMEM(adapter_slot.shape, i32),
        pltpu.SMEM(token_count.shape, i32),
    ]
    dma = pltpu.SemaphoreType.DMA

    own, *sent = pl.pallas_call(
        functools.partial(pack_kernel, n),
        out_shape=[message] * count,
        in_specs=[HBM] * 4,
        out_specs=[VMEM] * count,
        scratch_shapes=tables[1:3]
        + [pltpu.VMEM(down_maps.shape, bf16), pltpu.VMEM(up_maps.shape, bf16), dma((4,))],
        compiler_params=params(8),
    )(*in_hbm(chosen, adapter_slot, down_maps, up_maps))
    sent, x_late = lax.optimization_barrier((sent, inputs))
    x_other = lax.ppermute(x_late, "tensor", [(0, 1), (1, 0)])
    x, kept = pl.pallas_call(
        functools.partial(stage_kernel, n, picked),
        out_shape=[shape((tok_rows, model_width), bf16), shape((2 * tok_rows, out_width), bf16)],
        in_specs=[HBM] * 6 + [VMEM],
        out_specs=[VMEM] * 2,
        scratch_shapes=tables + [dma((6,))],
        compiler_params=params(8),
        cost_estimate=pl.CostEstimate(flops=0, bytes_accessed=1 << 21, transcendentals=0),
    )(*in_hbm(starts, chosen, adapter_slot, token_count, output_gradient, inputs), x_other)
    got, kept = exchange(sent, kept)

    dlow, a_half, *sent = pl.pallas_call(
        functools.partial(middle_kernel, n),
        out_shape=[shape((tok_rows, picked), bf16), shape((n // 2, picked, column_total), bf16)]
        + [message] * count,
        in_specs=[VMEM] * (2 + n),
        out_specs=[VMEM] * (2 + count),
        scratch_shapes=[
            pltpu.VMEM((n,) + message.shape, bf16),
            pltpu.VMEM((n, ADAPTER_RANK, out_width), bf16),
        ],
        compiler_params=params(8),
    )(kept, x, own, *got)
    own, *sent = sent

    grad_x = pl.pallas_call(
        grad_x_kernel,
        out_shape=shape((tok_rows, half), bf16),
        in_specs=[VMEM] * 4,
        out_specs=HBM,
        scratch_shapes=[pltpu.VMEM((tok_rows, half), bf16), dma((n // 2,))],
        compiler_params=params(8),
        cost_estimate=pl.CostEstimate(
            flops=2 * tok_rows * half * (out_width + picked),
            bytes_accessed=2 * half * (out_width + tok_rows),
            transcendentals=0,
        ),
    )(kept, frozen_weight, dlow, a_half)

    got, grad_x = exchange(sent, grad_x)

    grad_a, up_map_gradient = pl.pallas_call(
        functools.partial(final_kernel, n),
        out_shape=[shape((column_total, slot_width), f32), shape((ADAPTER_RANK, piece), f32)],
        in_specs=[VMEM] * (1 + n),
        out_specs=[VMEM, VMEM],
        scratch_shapes=[pltpu.VMEM((n,) + message.shape, bf16)],
        compiler_params=params(8),
    )(kept, own, *got)
    return grad_x, grad_a, up_map_gradient


def local_plain(
    inputs,
    output_gradient,
    frozen_weight,
    down_maps,
    up_maps,
    segment_start,
    segment_adapter,
    adapter_slot,
    token_count,
):
    tok_rows, out_width = output_gradient.shape
    column_total = down_maps.shape[0]
    adapter_list = adapter_slot.shape[0]
    segs = segment_start.shape[1]
    dp_size = lax.axis_size("dp")
    my_rank = lax.axis_index("dp")
    core_idx = lax.axis_index("tensor")
    picked = segs * ADAPTER_RANK
    piece_out = out_width // lax.axis_size("tensor")
    half = frozen_weight.shape[0]

    x_other = lax.ppermute(inputs, "tensor", [(0, 1), (1, 0)])
    adapter_ids = jnp.arange(adapter_list, dtype=i32)
    slot_table = jnp.sum(
        jnp.where(segment_adapter[..., None] == adapter_ids, adapter_slot, 0), axis=-1
    )
    column = slot_table[:, :, None] * ADAPTER_RANK + jnp.arange(ADAPTER_RANK, dtype=i32)
    onehot = (
        column.reshape(-1)[:, None] == jnp.arange(adapter_list * ADAPTER_RANK, dtype=i32)
    ).astype(bf16)

    a_send = dot(onehot, down_maps, 1, 1).astype(bf16).reshape(dp_size, picked, column_total)
    b_send = jnp.broadcast_to(up_maps[None], (dp_size,) + up_maps.shape)
    a_got = lax.all_to_all(a_send, "dp", 0, 0, tiled=True)
    b_got = lax.all_to_all(b_send, "dp", 0, 0, tiled=True)

    position = jnp.arange(tok_rows, dtype=i32)
    starts = lax.dynamic_index_in_dim(segment_start, my_rank, 0, keepdims=False)
    live = position < lax.dynamic_index_in_dim(token_count, my_rank, 0, keepdims=False)
    my_seg = jnp.sum((starts[None, :] <= position[:, None]).astype(i32), axis=1) - 1
    in_seg = my_seg[:, None] == (jnp.arange(picked, dtype=i32) // ADAPTER_RANK)[None, :]
    my_onehot = lax.dynamic_slice_in_dim(onehot, my_rank * picked, picked, 0)
    g = jnp.where(live[:, None], output_gradient, jnp.zeros_like(output_gradient))
    base = dot(g, frozen_weight, 1, 1)

    b_sel = dot(my_onehot, b_got.reshape(-1, out_width), 1, 0).astype(bf16)
    dlow = (adapter_scale * dot(g, b_sel, 1, 1)).astype(bf16)
    dlow = jnp.where(in_seg, dlow, jnp.zeros_like(dlow))
    a_sel = jnp.moveaxis(a_got, 0, 1).reshape(picked, -1)
    first = core_idx == 0
    x = jnp.concatenate(
        [jnp.where(first, inputs, x_other), jnp.where(first, x_other, inputs)], axis=0
    )
    low = dot(x, a_sel, 1, 1).astype(bf16)
    low = jnp.where(in_seg, low, jnp.zeros_like(low))
    low_wide = dot(low, my_onehot, 1, 0).astype(bf16)

    ga_send = dot(dlow, x, 0, 0).astype(bf16).reshape(picked, dp_size, column_total)
    ga_got = lax.all_to_all(jnp.moveaxis(ga_send, 1, 0), "dp", 0, 0, tiled=True)
    g_piece = lax.dynamic_slice_in_dim(g, core_idx * piece_out, piece_out, 1)
    up_send = (adapter_scale * dot(low_wide, g_piece, 0, 0)).astype(bf16)
    up_got = lax.all_to_all(up_send.reshape(dp_size, -1, piece_out), "dp", 0, 0, tiled=True)

    a_half = lax.dynamic_slice_in_dim(a_sel, core_idx * half, half, 1)
    grad_x = (base + dot(dlow, a_half, 1, 0)).astype(bf16)
    grad_a = dot(ga_got.reshape(dp_size * picked, column_total), onehot, 0, 0)
    up_map_gradient = jnp.sum(up_got.astype(f32), axis=0)
    return grad_x, grad_a, up_map_gradient


def local(*args):
    down_maps, up_maps = args[3], args[4]
    n, tp = lax.axis_size("dp"), lax.axis_size("tensor")
    out_width = up_maps.shape[1]
    kernels_fit = (
        n == 8
        and tp == 2
        and down_maps.shape[0] == out_width
        and down_maps.shape[1] == n * up_maps.shape[0]
        and out_width % (128 * tp) == 0
        and out_width == 4 * down_maps.shape[1]
        and args[1].shape[0] == 2 * args[0].shape[0] == down_maps.shape[1]
        and args[5].shape[1] * ADAPTER_RANK * n == 2 * down_maps.shape[1]
    )
    return (local_kernels if kernels_fit else local_plain)(*args)


def solution(mesh):
    in_specs = (
        P(("groups", "dp", "tensor"), None),
        P(("groups", "dp"), None),
        P("tensor", None),
        P(("groups", "dp"), None),
        P(("groups", "dp"), None),
        P("groups", None),
        P("groups", None),
        P("groups"),
        P("groups"),
    )
    out_specs = (
        P(("groups", "dp"), "tensor"),
        P(("groups", "dp"), None),
        P(("groups", "dp"), "tensor"),
    )
    return jax.shard_map(local, mesh=mesh, in_specs=in_specs, out_specs=out_specs, check_vma=False)
```

```python
import functools

import jax
import jax.numpy as jnp
from jax import lax
from jax.experimental import pallas as pl
from jax.experimental.pallas import tpu as pltpu
from jax.sharding import PartitionSpec as P

ADAPTER_RANK = 16
adapter_scale = 2.0

bf16, f32, i32 = jnp.bfloat16, jnp.float32, jnp.int32

HBM = pl.BlockSpec(memory_space=pltpu.HBM)
VMEM = pl.BlockSpec(memory_space=pltpu.VMEM)


def dot(a, b, ca, cb):
    return lax.dot_general(a, b, (((ca,), (cb,)), ((), ())), preferred_element_type=f32)


def params(mib):
    return pltpu.CompilerParams(vmem_limit_bytes=mib << 20)


def slot_rows(chosen_ref, slot_ref, ranks, width):
    lane = lax.broadcasted_iota(i32, (ADAPTER_RANK, width), 1)
    row = lax.broadcasted_iota(i32, (ADAPTER_RANK, width), 0)
    rows = []
    for rank in ranks:
        for k in range(chosen_ref.shape[0]):
            first = slot_ref[chosen_ref[k, rank]] * ADAPTER_RANK
            rows.append(jnp.where(lane == row + first, 1.0, 0.0))
    return jnp.concatenate(rows, axis=0).astype(bf16)


def start_all(sources, targets, sems, first=0):
    copies = [
        pltpu.make_async_copy(source, target, sems.at[first + k])
        for k, (source, target) in enumerate(zip(sources, targets))
    ]
    for copy in copies:
        copy.start()
    return copies


def wait_all(copies):
    for copy in copies:
        copy.wait()


def steps(n):
    return [(n - 1, n // 2 + 1), (3, n - 2), (2, n // 2), (1, 1)]


def partners(n, me, core):
    return [me] + [me ^ jnp.where(core == 0, a, b) for a, b in steps(n)]


def senders(n, me, core):
    passed = [me ^ jnp.where(core == 0, b, a) for a, b in steps(n) if a != b]
    return partners(n, me, core) + passed


def in_hbm(*arrays):
    return [pltpu.with_memory_space_constraint(array, pltpu.HBM) for array in arrays]


def pack_kernel(n, chosen_hbm, slot_hbm, down_hbm, up_hbm, *refs):
    count = n // 2 + 1
    send, (chosen_ref, slot_ref, down_ref, up_ref, sems) = refs[:count], refs[count:]
    tables = start_all([chosen_hbm, slot_hbm], [chosen_ref, slot_ref], sems)
    maps = start_all([down_hbm, up_hbm], [down_ref, up_ref], sems, 2)
    ranks = partners(n, lax.axis_index("dp"), lax.axis_index("tensor"))
    wait_all(tables)
    onehot = slot_rows(chosen_ref, slot_ref, ranks, down_ref.shape[1])
    picked = onehot.shape[0] // count
    wait_all(maps)
    columns = dot(onehot, down_ref[...], 1, 1).astype(bf16)
    for k in range(count):
        send[k][:picked, :] = columns[k * picked : (k + 1) * picked]
        send[k][picked:, :] = up_ref[...]


def stage_kernel(
    n, picked, start_hbm, chosen_hbm, slot_hbm, count_hbm, g_hbm, x_hbm,
    x_ref, kept_ref, start_ref, chosen_ref, slot_ref, count_ref, sems,
):
    rows, width = g_hbm.shape
    slots = width // 4
    me = lax.axis_index("dp")
    tables = start_all(
        [chosen_hbm, slot_hbm, start_hbm, count_hbm], [chosen_ref, slot_ref, start_ref, count_ref], sems
    )
    gradient = start_all([g_hbm], [kept_ref.at[pl.ds(0, rows)]], sems, 4)
    tokens = start_all([x_hbm], [x_ref], sems, 5)
    wait_all(tables)
    position = lax.broadcasted_iota(i32, (rows, slots), 0)
    group = lax.broadcasted_iota(i32, (rows, slots), 1) // ADAPTER_RANK
    segment = jnp.full((rows, slots), -1, i32)
    for k in range(start_ref.shape[0]):
        segment += jnp.where(position >= start_ref[k, me], 1, 0)
    kept_ref[rows:, :slots] = jnp.where(segment == group, 1.0, 0.0).astype(bf16)
    kept_ref[rows : rows + picked, slots : 2 * slots] = slot_rows(chosen_ref, slot_ref, [me], slots)
    every = slot_rows(chosen_ref, slot_ref, range(n), slots)
    kept_ref[rows:, 2 * slots : 3 * slots] = every[:rows]
    kept_ref[rows:, 3 * slots :] = every[rows:]
    wait_all(gradient)
    live = lax.broadcasted_iota(i32, (rows, width), 0) < count_ref[me]
    g = kept_ref[:rows, :]
    kept_ref[:rows, :] = jnp.where(live, g, jnp.zeros_like(g))
    wait_all(tokens)


def join_kernel(x_mine, x_other, x_ref):
    core, half = lax.axis_index("tensor"), x_mine.shape[0]
    x_ref[pl.ds(pl.multiple_of(core * half, half), half), :] = x_mine[...]
    x_ref[pl.ds(pl.multiple_of((1 - core) * half, half), half), :] = x_other[...]


def middle_kernel(n, kept_ref, x_ref, *refs):
    count = n // 2 + 1
    got, (dlow_ref, a_ref), send = refs[:n], refs[n : n + 2], refs[n + 2 : n + 2 + count]
    got_ref, up_ref = refs[n + 2 + count :]
    me, core = lax.axis_index("dp"), lax.axis_index("tensor")
    rows, picked = dlow_ref.shape
    width = kept_ref.shape[1]
    slots = width // 4
    for sender, message in zip(senders(n, me, core), got):
        got_ref[sender] = message[...]

    in_seg = kept_ref[rows:, :picked].astype(f32) > 0.0
    g = kept_ref[:rows, :]
    onehot = kept_ref[rows : rows + picked, slots : 2 * slots]
    up_maps = got_ref[:, picked:, :].reshape(-1, width)
    b_sel = dot(onehot, up_maps, 1, 0).astype(bf16)
    dlow = jnp.where(in_seg, adapter_scale * dot(g, b_sel, 1, 1), 0.0).astype(bf16)
    dlow_ref[...] = dlow
    parts = n // 2
    a_ref[...] = got_ref[pl.ds(pl.multiple_of(core * parts, parts), parts), :picked, :]
    targets = partners(n, me, core)
    for target, message in zip(targets, send):
        at = pl.ds(pl.multiple_of(target * width, width), width)
        message[:picked, :] = dot(dlow, x_ref[:, at], 0, 0).astype(bf16)

    low = jnp.zeros((rows, picked), f32)
    for q in range(n):
        low += dot(x_ref[:, q * width : (q + 1) * width], got_ref[q, :picked, :], 1, 1)
    low = jnp.where(in_seg, low, 0.0).astype(bf16)
    low_wide = dot(low, onehot, 1, 0).astype(bf16)
    up = (adapter_scale * dot(low_wide, g, 0, 0)).astype(bf16)
    up_ref[...] = up.reshape(up_ref.shape)
    for target, message in zip(targets, send):
        message[picked:, :] = up_ref[target]


def grad_x_kernel(kept_ref, w_ref, dlow_ref, a_ref, out_hbm, out_ref, sems):
    steps, picked, width = a_ref.shape
    g = kept_ref[: out_ref.shape[0], :]
    done = []
    for j in range(steps):
        at = pl.ds(j * width, width)
        total = dot(g, w_ref[at, :], 1, 1) + dot(dlow_ref[...], a_ref[j], 1, 0)
        out_ref[:, at] = total.astype(bf16)
        done += start_all([out_ref.at[:, at]], [out_hbm.at[:, at]], sems, j)
    wait_all(done)


def final_kernel(n, kept_ref, *refs):
    got, (a_ref, up_ref, rows_ref) = refs[:n], refs[n:]
    me, core = lax.axis_index("dp"), lax.axis_index("tensor")
    piece, picked = up_ref.shape[1], rows_ref.shape[1] - ADAPTER_RANK
    half, slots = kept_ref.shape[0] // 2, kept_ref.shape[1] // 4
    for sender, message in zip(senders(n, me, core), got):
        rows_ref[sender] = message[...]
    rows = rows_ref[:, :picked, :].reshape(n * picked, rows_ref.shape[2])
    onehot = jnp.concatenate(
        [kept_ref[half:, 2 * slots : 3 * slots], kept_ref[half:, 3 * slots :]], axis=0
    )
    a_ref[...] = dot(rows, onehot, 0, 0)
    at = pl.ds(pl.multiple_of(core * piece, piece), piece)
    up_ref[...] = jnp.sum(rows_ref[:, picked:, at].astype(f32), axis=0)


def exchange(messages, tied, beside):
    n = 2 * len(messages)
    got = [
        lax.ppermute(
            message,
            ("dp", "tensor"),
            [(2 * i + c, 2 * (i ^ step[c]) + c) for i in range(n) for c in range(2)],
        )
        for message, step in zip(messages, steps(n))
    ]
    for k in tied:
        got[k], beside = lax.optimization_barrier((got[k], beside))
    passed = [
        lax.ppermute(message, "tensor", [(0, 1), (1, 0)])
        for message, (a, b) in zip(got, steps(n))
        if a != b
    ]
    return got + passed, beside


def local_kernels(
    inputs,
    output_gradient,
    frozen_weight,
    down_maps,
    up_maps,
    segment_start,
    segment_adapter,
    adapter_slot,
    token_count,
):
    model_width = inputs.shape[1]
    tok_rows, out_width = output_gradient.shape
    column_total, slot_width = down_maps.shape
    half = frozen_weight.shape[0]
    n = lax.axis_size("dp")
    piece = out_width // lax.axis_size("tensor")
    segs = segment_start.shape[1]
    picked = segs * ADAPTER_RANK
    shape = jax.ShapeDtypeStruct
    message = shape((picked + ADAPTER_RANK, column_total), bf16)
    count = n // 2 + 1
    starts, chosen = segment_start.T, segment_adapter.T

    tables = [
        pltpu.SMEM(starts.shape, i32),
        pltpu.SMEM(chosen.shape, i32),
        pltpu.SMEM(adapter_slot.shape, i32),
        pltpu.SMEM(token_count.shape, i32),
    ]
    dma = pltpu.SemaphoreType.DMA

    own, *sent = pl.pallas_call(
        functools.partial(pack_kernel, n),
        out_shape=[message] * count,
        in_specs=[HBM] * 4,
        out_specs=[VMEM] * count,
        scratch_shapes=tables[1:3]
        + [pltpu.VMEM(down_maps.shape, bf16), pltpu.VMEM(up_maps.shape, bf16), dma((4,))],
        compiler_params=params(8),
    )(*in_hbm(chosen, adapter_slot, down_maps, up_maps))
    sent, x_late = lax.optimization_barrier((sent, inputs))
    x_other = lax.ppermute(x_late, "tensor", [(0, 1), (1, 0)])
    x_mine, kept = pl.pallas_call(
        functools.partial(stage_kernel, n, picked),
        out_shape=[shape(inputs.shape, bf16), shape((2 * tok_rows, out_width), bf16)],
        in_specs=[HBM] * 6,
        out_specs=[VMEM] * 2,
        scratch_shapes=tables + [dma((6,))],
        compiler_params=params(8),
        cost_estimate=pl.CostEstimate(flops=0, bytes_accessed=1 << 21, transcendentals=0),
    )(*in_hbm(starts, chosen, adapter_slot, token_count, output_gradient, inputs))
    got, x_mine = exchange(sent, (0,), x_mine)
    x = pl.pallas_call(
        join_kernel,
        out_shape=shape((tok_rows, model_width), bf16),
        in_specs=[VMEM] * 2,
        out_specs=VMEM,
        compiler_params=params(8),
        cost_estimate=pl.CostEstimate(flops=0, bytes_accessed=1 << 21, transcendentals=0),
    )(x_mine, x_other)

    dlow, a_half, *sent = pl.pallas_call(
        functools.partial(middle_kernel, n),
        out_shape=[shape((tok_rows, picked), bf16), shape((n // 2, picked, column_total), bf16)]
        + [message] * count,
        in_specs=[VMEM] * (2 + n),
        out_specs=[VMEM] * (2 + count),
        scratch_shapes=[
            pltpu.VMEM((n,) + message.shape, bf16),
            pltpu.VMEM((n, ADAPTER_RANK, out_width), bf16),
        ],
        compiler_params=params(8),
    )(kept, x, own, *got)
    own, *sent = sent

    grad_x = pl.pallas_call(
        grad_x_kernel,
        out_shape=shape((tok_rows, half), bf16),
        in_specs=[VMEM] * 4,
        out_specs=HBM,
        scratch_shapes=[pltpu.VMEM((tok_rows, half), bf16), dma((n // 2,))],
        compiler_params=params(8),
        cost_estimate=pl.CostEstimate(
            flops=2 * tok_rows * half * (out_width + picked),
            bytes_accessed=2 * half * (out_width + tok_rows),
            transcendentals=0,
        ),
    )(kept, frozen_weight, dlow, a_half)

    got, grad_x = exchange(sent, (0,), grad_x)

    grad_a, up_map_gradient = pl.pallas_call(
        functools.partial(final_kernel, n),
        out_shape=[shape((column_total, slot_width), f32), shape((ADAPTER_RANK, piece), f32)],
        in_specs=[VMEM] * (1 + n),
        out_specs=[VMEM, VMEM],
        scratch_shapes=[pltpu.VMEM((n,) + message.shape, bf16)],
        compiler_params=params(8),
    )(kept, own, *got)
    return grad_x, grad_a, up_map_gradient


def local_plain(
    inputs,
    output_gradient,
    frozen_weight,
    down_maps,
    up_maps,
    segment_start,
    segment_adapter,
    adapter_slot,
    token_count,
):
    tok_rows, out_width = output_gradient.shape
    column_total = down_maps.shape[0]
    adapter_list = adapter_slot.shape[0]
    segs = segment_start.shape[1]
    dp_size = lax.axis_size("dp")
    my_rank = lax.axis_index("dp")
    core_idx = lax.axis_index("tensor")
    picked = segs * ADAPTER_RANK
    piece_out = out_width // lax.axis_size("tensor")
    half = frozen_weight.shape[0]

    x_other = lax.ppermute(inputs, "tensor", [(0, 1), (1, 0)])
    adapter_ids = jnp.arange(adapter_list, dtype=i32)
    slot_table = jnp.sum(
        jnp.where(segment_adapter[..., None] == adapter_ids, adapter_slot, 0), axis=-1
    )
    column = slot_table[:, :, None] * ADAPTER_RANK + jnp.arange(ADAPTER_RANK, dtype=i32)
    onehot = (
        column.reshape(-1)[:, None] == jnp.arange(adapter_list * ADAPTER_RANK, dtype=i32)
    ).astype(bf16)

    a_send = dot(onehot, down_maps, 1, 1).astype(bf16).reshape(dp_size, picked, column_total)
    b_send = jnp.broadcast_to(up_maps[None], (dp_size,) + up_maps.shape)
    a_got = lax.all_to_all(a_send, "dp", 0, 0, tiled=True)
    b_got = lax.all_to_all(b_send, "dp", 0, 0, tiled=True)

    position = jnp.arange(tok_rows, dtype=i32)
    starts = lax.dynamic_index_in_dim(segment_start, my_rank, 0, keepdims=False)
    live = position < lax.dynamic_index_in_dim(token_count, my_rank, 0, keepdims=False)
    my_seg = jnp.sum((starts[None, :] <= position[:, None]).astype(i32), axis=1) - 1
    in_seg = my_seg[:, None] == (jnp.arange(picked, dtype=i32) // ADAPTER_RANK)[None, :]
    my_onehot = lax.dynamic_slice_in_dim(onehot, my_rank * picked, picked, 0)
    g = jnp.where(live[:, None], output_gradient, jnp.zeros_like(output_gradient))
    base = dot(g, frozen_weight, 1, 1)

    b_sel = dot(my_onehot, b_got.reshape(-1, out_width), 1, 0).astype(bf16)
    dlow = (adapter_scale * dot(g, b_sel, 1, 1)).astype(bf16)
    dlow = jnp.where(in_seg, dlow, jnp.zeros_like(dlow))
    a_sel = jnp.moveaxis(a_got, 0, 1).reshape(picked, -1)
    first = core_idx == 0
    x = jnp.concatenate(
        [jnp.where(first, inputs, x_other), jnp.where(first, x_other, inputs)], axis=0
    )
    low = dot(x, a_sel, 1, 1).astype(bf16)
    low = jnp.where(in_seg, low, jnp.zeros_like(low))
    low_wide = dot(low, my_onehot, 1, 0).astype(bf16)

    ga_send = dot(dlow, x, 0, 0).astype(bf16).reshape(picked, dp_size, column_total)
    ga_got = lax.all_to_all(jnp.moveaxis(ga_send, 1, 0), "dp", 0, 0, tiled=True)
    g_piece = lax.dynamic_slice_in_dim(g, core_idx * piece_out, piece_out, 1)
    up_send = (adapter_scale * dot(low_wide, g_piece, 0, 0)).astype(bf16)
    up_got = lax.all_to_all(up_send.reshape(dp_size, -1, piece_out), "dp", 0, 0, tiled=True)

    a_half = lax.dynamic_slice_in_dim(a_sel, core_idx * half, half, 1)
    grad_x = (base + dot(dlow, a_half, 1, 0)).astype(bf16)
    grad_a = dot(ga_got.reshape(dp_size * picked, column_total), onehot, 0, 0)
    up_map_gradient = jnp.sum(up_got.astype(f32), axis=0)
    return grad_x, grad_a, up_map_gradient


def local(*args):
    down_maps, up_maps = args[3], args[4]
    n, tp = lax.axis_size("dp"), lax.axis_size("tensor")
    out_width = up_maps.shape[1]
    kernels_fit = (
        n == 8
        and tp == 2
        and down_maps.shape[0] == out_width
        and down_maps.shape[1] == n * up_maps.shape[0]
        and out_width % (128 * tp) == 0
        and out_width == 4 * down_maps.shape[1]
        and args[1].shape[0] == 2 * args[0].shape[0] == down_maps.shape[1]
        and args[5].shape[1] * ADAPTER_RANK * n == 2 * down_maps.shape[1]
    )
    return (local_kernels if kernels_fit else local_plain)(*args)


def solution(mesh):
    in_specs = (
        P(("groups", "dp", "tensor"), None),
        P(("groups", "dp"), None),
        P("tensor", None),
        P(("groups", "dp"), None),
        P(("groups", "dp"), None),
        P("groups", None),
        P("groups", None),
        P("groups"),
        P("groups"),
    )
    out_specs = (
        P(("groups", "dp"), "tensor"),
        P(("groups", "dp"), None),
        P(("groups", "dp"), "tensor"),
    )
    return jax.shard_map(local, mesh=mesh, in_specs=in_specs, out_specs=out_specs, check_vma=False)
```

```python
import functools

import jax
import jax.numpy as jnp
from jax import lax
from jax.experimental import pallas as pl
from jax.experimental.pallas import tpu as pltpu
from jax.sharding import PartitionSpec as P

ADAPTER_RANK = 16
adapter_scale = 2.0

bf16, f32, i32 = jnp.bfloat16, jnp.float32, jnp.int32

HBM = pl.BlockSpec(memory_space=pltpu.HBM)
VMEM = pl.BlockSpec(memory_space=pltpu.VMEM)


def dot(a, b, ca, cb):
    return lax.dot_general(a, b, (((ca,), (cb,)), ((), ())), preferred_element_type=f32)


def params(mib):
    return pltpu.CompilerParams(vmem_limit_bytes=mib << 20)


def slot_rows(chosen_ref, slot_ref, ranks, width):
    lane = lax.broadcasted_iota(i32, (ADAPTER_RANK, width), 1)
    row = lax.broadcasted_iota(i32, (ADAPTER_RANK, width), 0)
    rows = []
    for rank in ranks:
        for k in range(chosen_ref.shape[0]):
            first = slot_ref[chosen_ref[k, rank]] * ADAPTER_RANK
            rows.append(jnp.where(lane == row + first, 1.0, 0.0))
    return jnp.concatenate(rows, axis=0).astype(bf16)


def start_all(sources, targets, sems, first=0):
    copies = [
        pltpu.make_async_copy(source, target, sems.at[first + k])
        for k, (source, target) in enumerate(zip(sources, targets))
    ]
    for copy in copies:
        copy.start()
    return copies


def wait_all(copies):
    for copy in copies:
        copy.wait()


def steps(n):
    return [(n - 1, n // 2 + 1), (3, n - 2), (2, n // 2), (1, 1)]


def partners(n, me, core):
    return [me] + [me ^ jnp.where(core == 0, a, b) for a, b in steps(n)]


def senders(n, me, core):
    passed = [me ^ jnp.where(core == 0, b, a) for a, b in steps(n) if a != b]
    return partners(n, me, core) + passed


def in_hbm(*arrays):
    return [pltpu.with_memory_space_constraint(array, pltpu.HBM) for array in arrays]


def pack_kernel(n, chosen_hbm, slot_hbm, down_hbm, up_hbm, *refs):
    count = n // 2 + 1
    send, (chosen_ref, slot_ref, down_ref, up_ref, sems) = refs[:count], refs[count:]
    tables = start_all([chosen_hbm, slot_hbm], [chosen_ref, slot_ref], sems)
    maps = start_all([down_hbm, up_hbm], [down_ref, up_ref], sems, 2)
    ranks = partners(n, lax.axis_index("dp"), lax.axis_index("tensor"))
    wait_all(tables)
    onehot = slot_rows(chosen_ref, slot_ref, ranks, down_ref.shape[1])
    picked = onehot.shape[0] // count
    wait_all(maps)
    columns = dot(onehot, down_ref[...], 1, 1).astype(bf16)
    for k in range(count):
        send[k][:picked, :] = columns[k * picked : (k + 1) * picked]
        send[k][picked:, :] = up_ref[...]


def stage_kernel(
    n, picked, start_hbm, chosen_hbm, slot_hbm, count_hbm, g_hbm, x_hbm,
    x_ref, kept_ref, start_ref, chosen_ref, slot_ref, count_ref, sems,
):
    rows, width = g_hbm.shape
    slots = width // 4
    me = lax.axis_index("dp")
    tables = start_all(
        [chosen_hbm, slot_hbm, start_hbm, count_hbm], [chosen_ref, slot_ref, start_ref, count_ref], sems
    )
    gradient = start_all([g_hbm], [kept_ref.at[pl.ds(0, rows)]], sems, 4)
    tokens = start_all([x_hbm], [x_ref], sems, 5)
    wait_all(tables)
    position = lax.broadcasted_iota(i32, (rows, slots), 0)
    group = lax.broadcasted_iota(i32, (rows, slots), 1) // ADAPTER_RANK
    segment = jnp.full((rows, slots), -1, i32)
    for k in range(start_ref.shape[0]):
        segment += jnp.where(position >= start_ref[k, me], 1, 0)
    kept_ref[rows:, :slots] = jnp.where(segment == group, 1.0, 0.0).astype(bf16)
    kept_ref[rows : rows + picked, slots : 2 * slots] = slot_rows(chosen_ref, slot_ref, [me], slots)
    every = slot_rows(chosen_ref, slot_ref, range(n), slots)
    kept_ref[rows:, 2 * slots : 3 * slots] = every[:rows]
    kept_ref[rows:, 3 * slots :] = every[rows:]
    wait_all(gradient)
    live = lax.broadcasted_iota(i32, (rows, width), 0) < count_ref[me]
    g = kept_ref[:rows, :]
    kept_ref[:rows, :] = jnp.where(live, g, jnp.zeros_like(g))
    wait_all(tokens)


def picked_maps(kept_ref, b_ref, picked, ranks, messages):
    rows, slots = kept_ref.shape[0] // 2, kept_ref.shape[1] // 4
    b_ref[...] = jnp.zeros(b_ref.shape, bf16)
    for rank, message in zip(ranks, messages):
        b_ref[rank] = message[picked:, :]
    onehot = kept_ref[rows : rows + picked, slots : 2 * slots]
    return dot(onehot, b_ref[...].reshape(-1, b_ref.shape[2]), 1, 0).astype(bf16)


def low_terms(x_ref, picked, ranks, messages):
    total = jnp.zeros((x_ref.shape[0], picked), f32)
    for rank, message in zip(ranks, messages):
        width = message.shape[1]
        at = pl.ds(pl.multiple_of(rank * width, width), width)
        total += dot(x_ref[:, at], message[:picked, :], 1, 1)
    return total


def early_kernel(n, picked, kept_ref, x_mine, x_other, *refs):
    count = n // 2 + 1
    here, (x_ref, low_ref, dlow_ref, b_ref) = refs[:count], refs[count:]
    me, core, half = lax.axis_index("dp"), lax.axis_index("tensor"), x_mine.shape[0]
    ranks = senders(n, me, core)[:count]
    x_ref[pl.ds(pl.multiple_of(core * half, half), half), :] = x_mine[...]
    x_ref[pl.ds(pl.multiple_of((1 - core) * half, half), half), :] = x_other[...]
    b_sel = picked_maps(kept_ref, b_ref, picked, ranks, here)
    dlow_ref[...] = dot(kept_ref[: 2 * half, :], b_sel, 1, 1)
    low_ref[...] = low_terms(x_ref, picked, ranks, here)


def middle_kernel(n, kept_ref, x_ref, low_ref, dlow_part, *refs):
    count = n // 2 + 1
    got, dlow_ref, send = refs[: n - count], refs[n - count], refs[n - count + 1 : n + 1]
    b_ref, up_ref = refs[n + 1 :]
    me, core = lax.axis_index("dp"), lax.axis_index("tensor")
    rows, picked = dlow_ref.shape
    width = kept_ref.shape[1]
    slots = width // 4
    ranks = senders(n, me, core)[count:]
    in_seg = kept_ref[rows:, :picked].astype(f32) > 0.0
    g = kept_ref[:rows, :]
    onehot = kept_ref[rows : rows + picked, slots : 2 * slots]
    b_sel = picked_maps(kept_ref, b_ref, picked, ranks, got)
    dlow = dlow_part[...] + dot(g, b_sel, 1, 1)
    dlow = jnp.where(in_seg, adapter_scale * dlow, 0.0).astype(bf16)
    dlow_ref[...] = dlow
    targets = partners(n, me, core)
    for target, message in zip(targets, send):
        at = pl.ds(pl.multiple_of(target * width, width), width)
        message[:picked, :] = dot(dlow, x_ref[:, at], 0, 0).astype(bf16)

    low = low_ref[...] + low_terms(x_ref, picked, ranks, got)
    low = jnp.where(in_seg, low, 0.0).astype(bf16)
    low_wide = dot(low, onehot, 1, 0).astype(bf16)
    up = (adapter_scale * dot(low_wide, g, 0, 0)).astype(bf16)
    up_ref[...] = up.reshape(up_ref.shape)
    for target, message in zip(targets, send):
        message[picked:, :] = up_ref[target]


def grad_x_kernel(n, kept_ref, w_ref, dlow_ref, *refs):
    got, (out_hbm, a_ref, out_ref, sems) = refs[:n], refs[n:]
    me, core = lax.axis_index("dp"), lax.axis_index("tensor")
    picked, width = a_ref.shape[1:]
    for sender, message in zip(senders(n, me, core), got):
        a_ref[sender] = message[:picked, :]
    g = kept_ref[: out_ref.shape[0], :]
    done = []
    for j in range(n // 2):
        at = pl.ds(j * width, width)
        total = dot(g, w_ref[at, :], 1, 1) + dot(dlow_ref[...], a_ref[core * (n // 2) + j], 1, 0)
        out_ref[:, at] = total.astype(bf16)
        done += start_all([out_ref.at[:, at]], [out_hbm.at[:, at]], sems, j)
    wait_all(done)


def final_kernel(n, kept_ref, *refs):
    got, (a_ref, up_ref, rows_ref) = refs[:n], refs[n:]
    me, core = lax.axis_index("dp"), lax.axis_index("tensor")
    piece, picked = up_ref.shape[1], rows_ref.shape[1] - ADAPTER_RANK
    half, slots = kept_ref.shape[0] // 2, kept_ref.shape[1] // 4
    for sender, message in zip(senders(n, me, core), got):
        rows_ref[sender] = message[...]
    rows = rows_ref[:, :picked, :].reshape(n * picked, rows_ref.shape[2])
    onehot = jnp.concatenate(
        [kept_ref[half:, 2 * slots : 3 * slots], kept_ref[half:, 3 * slots :]], axis=0
    )
    a_ref[...] = dot(rows, onehot, 0, 0)
    at = pl.ds(pl.multiple_of(core * piece, piece), piece)
    up_ref[...] = jnp.sum(rows_ref[:, picked:, at].astype(f32), axis=0)


def exchange(messages, tied, beside):
    n = 2 * len(messages)
    got = [
        lax.ppermute(
            message,
            ("dp", "tensor"),
            [(2 * i + c, 2 * (i ^ step[c]) + c) for i in range(n) for c in range(2)],
        )
        for message, step in zip(messages, steps(n))
    ]
    for k in tied:
        got[k], beside = lax.optimization_barrier((got[k], beside))
    passed = [
        lax.ppermute(message, "tensor", [(0, 1), (1, 0)])
        for message, (a, b) in zip(got, steps(n))
        if a != b
    ]
    return got + passed, beside


def local_kernels(
    inputs,
    output_gradient,
    frozen_weight,
    down_maps,
    up_maps,
    segment_start,
    segment_adapter,
    adapter_slot,
    token_count,
):
    model_width = inputs.shape[1]
    tok_rows, out_width = output_gradient.shape
    column_total, slot_width = down_maps.shape
    half = frozen_weight.shape[0]
    n = lax.axis_size("dp")
    piece = out_width // lax.axis_size("tensor")
    segs = segment_start.shape[1]
    picked = segs * ADAPTER_RANK
    shape = jax.ShapeDtypeStruct
    message = shape((picked + ADAPTER_RANK, column_total), bf16)
    count = n // 2 + 1
    starts, chosen = segment_start.T, segment_adapter.T

    tables = [
        pltpu.SMEM(starts.shape, i32),
        pltpu.SMEM(chosen.shape, i32),
        pltpu.SMEM(adapter_slot.shape, i32),
        pltpu.SMEM(token_count.shape, i32),
    ]
    dma = pltpu.SemaphoreType.DMA

    own, *sent = pl.pallas_call(
        functools.partial(pack_kernel, n),
        out_shape=[message] * count,
        in_specs=[HBM] * 4,
        out_specs=[VMEM] * count,
        scratch_shapes=tables[1:3]
        + [pltpu.VMEM(down_maps.shape, bf16), pltpu.VMEM(up_maps.shape, bf16), dma((4,))],
        compiler_params=params(8),
    )(*in_hbm(chosen, adapter_slot, down_maps, up_maps))
    sent, x_late = lax.optimization_barrier((sent, inputs))
    x_other = lax.ppermute(x_late, "tensor", [(0, 1), (1, 0)])
    x_mine, kept = pl.pallas_call(
        functools.partial(stage_kernel, n, picked),
        out_shape=[shape(inputs.shape, bf16), shape((2 * tok_rows, out_width), bf16)],
        in_specs=[HBM] * 6,
        out_specs=[VMEM] * 2,
        scratch_shapes=tables + [dma((6,))],
        compiler_params=params(8),
        cost_estimate=pl.CostEstimate(flops=0, bytes_accessed=1 << 21, transcendentals=0),
    )(*in_hbm(starts, chosen, adapter_slot, token_count, output_gradient, inputs))
    got, x_mine = exchange(sent, (0,), x_mine)
    low = shape((tok_rows, picked), f32)
    maps = pltpu.VMEM((n, ADAPTER_RANK, out_width), bf16)
    got = [own] + got
    x, low, dlow = pl.pallas_call(
        functools.partial(early_kernel, n, picked),
        out_shape=[shape((tok_rows, model_width), bf16), low, low],
        in_specs=[VMEM] * (3 + count),
        out_specs=[VMEM] * 3,
        scratch_shapes=[maps],
        compiler_params=params(8),
        cost_estimate=pl.CostEstimate(flops=0, bytes_accessed=1 << 21, transcendentals=0),
    )(kept, x_mine, x_other, *got[:count])

    dlow, *sent = pl.pallas_call(
        functools.partial(middle_kernel, n),
        out_shape=[shape((tok_rows, picked), bf16)] + [message] * count,
        in_specs=[VMEM] * (4 + n - count),
        out_specs=[VMEM] * (1 + count),
        scratch_shapes=[maps, maps],
        compiler_params=params(8),
    )(kept, x, low, dlow, *got[count:])
    own, *sent = sent

    grad_x = pl.pallas_call(
        functools.partial(grad_x_kernel, n),
        out_shape=shape((tok_rows, half), bf16),
        in_specs=[VMEM] * (3 + n),
        out_specs=HBM,
        scratch_shapes=[
            pltpu.VMEM((n, picked, column_total), bf16),
            pltpu.VMEM((tok_rows, half), bf16),
            dma((n // 2,)),
        ],
        compiler_params=params(8),
        cost_estimate=pl.CostEstimate(
            flops=2 * tok_rows * half * (out_width + picked),
            bytes_accessed=2 * half * (out_width + tok_rows),
            transcendentals=0,
        ),
    )(kept, frozen_weight, dlow, *got)

    got, grad_x = exchange(sent, (0,), grad_x)

    grad_a, up_map_gradient = pl.pallas_call(
        functools.partial(final_kernel, n),
        out_shape=[shape((column_total, slot_width), f32), shape((ADAPTER_RANK, piece), f32)],
        in_specs=[VMEM] * (1 + n),
        out_specs=[VMEM, VMEM],
        scratch_shapes=[pltpu.VMEM((n,) + message.shape, bf16)],
        compiler_params=params(8),
    )(kept, own, *got)
    return grad_x, grad_a, up_map_gradient


def local_plain(
    inputs,
    output_gradient,
    frozen_weight,
    down_maps,
    up_maps,
    segment_start,
    segment_adapter,
    adapter_slot,
    token_count,
):
    tok_rows, out_width = output_gradient.shape
    column_total = down_maps.shape[0]
    adapter_list = adapter_slot.shape[0]
    segs = segment_start.shape[1]
    dp_size = lax.axis_size("dp")
    my_rank = lax.axis_index("dp")
    core_idx = lax.axis_index("tensor")
    picked = segs * ADAPTER_RANK
    piece_out = out_width // lax.axis_size("tensor")
    half = frozen_weight.shape[0]

    x_other = lax.ppermute(inputs, "tensor", [(0, 1), (1, 0)])
    adapter_ids = jnp.arange(adapter_list, dtype=i32)
    slot_table = jnp.sum(
        jnp.where(segment_adapter[..., None] == adapter_ids, adapter_slot, 0), axis=-1
    )
    column = slot_table[:, :, None] * ADAPTER_RANK + jnp.arange(ADAPTER_RANK, dtype=i32)
    onehot = (
        column.reshape(-1)[:, None] == jnp.arange(adapter_list * ADAPTER_RANK, dtype=i32)
    ).astype(bf16)

    a_send = dot(onehot, down_maps, 1, 1).astype(bf16).reshape(dp_size, picked, column_total)
    b_send = jnp.broadcast_to(up_maps[None], (dp_size,) + up_maps.shape)
    a_got = lax.all_to_all(a_send, "dp", 0, 0, tiled=True)
    b_got = lax.all_to_all(b_send, "dp", 0, 0, tiled=True)

    position = jnp.arange(tok_rows, dtype=i32)
    starts = lax.dynamic_index_in_dim(segment_start, my_rank, 0, keepdims=False)
    live = position < lax.dynamic_index_in_dim(token_count, my_rank, 0, keepdims=False)
    my_seg = jnp.sum((starts[None, :] <= position[:, None]).astype(i32), axis=1) - 1
    in_seg = my_seg[:, None] == (jnp.arange(picked, dtype=i32) // ADAPTER_RANK)[None, :]
    my_onehot = lax.dynamic_slice_in_dim(onehot, my_rank * picked, picked, 0)
    g = jnp.where(live[:, None], output_gradient, jnp.zeros_like(output_gradient))
    base = dot(g, frozen_weight, 1, 1)

    b_sel = dot(my_onehot, b_got.reshape(-1, out_width), 1, 0).astype(bf16)
    dlow = (adapter_scale * dot(g, b_sel, 1, 1)).astype(bf16)
    dlow = jnp.where(in_seg, dlow, jnp.zeros_like(dlow))
    a_sel = jnp.moveaxis(a_got, 0, 1).reshape(picked, -1)
    first = core_idx == 0
    x = jnp.concatenate(
        [jnp.where(first, inputs, x_other), jnp.where(first, x_other, inputs)], axis=0
    )
    low = dot(x, a_sel, 1, 1).astype(bf16)
    low = jnp.where(in_seg, low, jnp.zeros_like(low))
    low_wide = dot(low, my_onehot, 1, 0).astype(bf16)

    ga_send = dot(dlow, x, 0, 0).astype(bf16).reshape(picked, dp_size, column_total)
    ga_got = lax.all_to_all(jnp.moveaxis(ga_send, 1, 0), "dp", 0, 0, tiled=True)
    g_piece = lax.dynamic_slice_in_dim(g, core_idx * piece_out, piece_out, 1)
    up_send = (adapter_scale * dot(low_wide, g_piece, 0, 0)).astype(bf16)
    up_got = lax.all_to_all(up_send.reshape(dp_size, -1, piece_out), "dp", 0, 0, tiled=True)

    a_half = lax.dynamic_slice_in_dim(a_sel, core_idx * half, half, 1)
    grad_x = (base + dot(dlow, a_half, 1, 0)).astype(bf16)
    grad_a = dot(ga_got.reshape(dp_size * picked, column_total), onehot, 0, 0)
    up_map_gradient = jnp.sum(up_got.astype(f32), axis=0)
    return grad_x, grad_a, up_map_gradient


def local(*args):
    down_maps, up_maps = args[3], args[4]
    n, tp = lax.axis_size("dp"), lax.axis_size("tensor")
    out_width = up_maps.shape[1]
    kernels_fit = (
        n == 8
        and tp == 2
        and down_maps.shape[0] == out_width
        and down_maps.shape[1] == n * up_maps.shape[0]
        and out_width % (128 * tp) == 0
        and out_width == 4 * down_maps.shape[1]
        and args[1].shape[0] == 2 * args[0].shape[0] == down_maps.shape[1]
        and args[5].shape[1] * ADAPTER_RANK * n == 2 * down_maps.shape[1]
    )
    return (local_kernels if kernels_fit else local_plain)(*args)


def solution(mesh):
    in_specs = (
        P(("groups", "dp", "tensor"), None),
        P(("groups", "dp"), None),
        P("tensor", None),
        P(("groups", "dp"), None),
        P(("groups", "dp"), None),
        P("groups", None),
        P("groups", None),
        P("groups"),
        P("groups"),
    )
    out_specs = (
        P(("groups", "dp"), "tensor"),
        P(("groups", "dp"), None),
        P(("groups", "dp"), "tensor"),
    )
    return jax.shard_map(local, mesh=mesh, in_specs=in_specs, out_specs=out_specs, check_vma=False)
```

```python
import functools

import jax
import jax.numpy as jnp
from jax import lax
from jax.experimental import pallas as pl
from jax.experimental.pallas import tpu as pltpu
from jax.sharding import PartitionSpec as P

ADAPTER_RANK = 16
adapter_scale = 2.0

bf16, f32, i32 = jnp.bfloat16, jnp.float32, jnp.int32

HBM = pl.BlockSpec(memory_space=pltpu.HBM)
VMEM = pl.BlockSpec(memory_space=pltpu.VMEM)


def dot(a, b, ca, cb):
    return lax.dot_general(a, b, (((ca,), (cb,)), ((), ())), preferred_element_type=f32)


def params(mib):
    return pltpu.CompilerParams(vmem_limit_bytes=mib << 20)


def slot_rows(chosen_ref, slot_ref, ranks, width):
    lane = lax.broadcasted_iota(i32, (ADAPTER_RANK, width), 1)
    row = lax.broadcasted_iota(i32, (ADAPTER_RANK, width), 0)
    rows = []
    for rank in ranks:
        for k in range(chosen_ref.shape[0]):
            first = slot_ref[chosen_ref[k, rank]] * ADAPTER_RANK
            rows.append(jnp.where(lane == row + first, 1.0, 0.0))
    return jnp.concatenate(rows, axis=0).astype(bf16)


def start_all(sources, targets, sems, first=0):
    copies = [
        pltpu.make_async_copy(source, target, sems.at[first + k])
        for k, (source, target) in enumerate(zip(sources, targets))
    ]
    for copy in copies:
        copy.start()
    return copies


def wait_all(copies):
    for copy in copies:
        copy.wait()


def steps(n):
    return [(n - 1, n // 2 + 1), (3, n - 2), (2, n // 2), (1, 1)]


def partners(n, me, core):
    return [me] + [me ^ jnp.where(core == 0, a, b) for a, b in steps(n)]


def senders(n, me, core):
    passed = [me ^ jnp.where(core == 0, b, a) for a, b in steps(n) if a != b]
    return partners(n, me, core) + passed


def in_hbm(*arrays):
    return [pltpu.with_memory_space_constraint(array, pltpu.HBM) for array in arrays]


def pack_kernel(n, chosen_hbm, slot_hbm, down_hbm, up_hbm, *refs):
    count = n // 2 + 1
    send, (chosen_ref, slot_ref, down_ref, up_ref, sems) = refs[:count], refs[count:]
    tables = start_all([chosen_hbm, slot_hbm], [chosen_ref, slot_ref], sems)
    maps = start_all([down_hbm, up_hbm], [down_ref, up_ref], sems, 2)
    ranks = partners(n, lax.axis_index("dp"), lax.axis_index("tensor"))
    wait_all(tables)
    onehot = slot_rows(chosen_ref, slot_ref, ranks, down_ref.shape[1])
    picked = onehot.shape[0] // count
    wait_all(maps)
    columns = dot(onehot, down_ref[...], 1, 1).astype(bf16)
    for k in range(count):
        send[k][:picked, :] = columns[k * picked : (k + 1) * picked]
        send[k][picked:, :] = up_ref[...]


def stage_kernel(
    n, picked, start_hbm, chosen_hbm, slot_hbm, count_hbm, g_hbm, x_hbm, w_hbm,
    x_ref, kept_ref, start_ref, chosen_ref, slot_ref, count_ref, sems,
):
    rows, width = g_hbm.shape
    slots = width // 4
    me = lax.axis_index("dp")
    tables = start_all(
        [chosen_hbm, slot_hbm, start_hbm, count_hbm], [chosen_ref, slot_ref, start_ref, count_ref], sems
    )
    gradient = start_all([g_hbm], [kept_ref.at[pl.ds(0, rows)]], sems, 4)
    tokens = start_all([x_hbm], [x_ref], sems, 5)
    wait_all(tables)
    position = lax.broadcasted_iota(i32, (rows, slots), 0)
    group = lax.broadcasted_iota(i32, (rows, slots), 1) // ADAPTER_RANK
    segment = jnp.full((rows, slots), -1, i32)
    for k in range(start_ref.shape[0]):
        segment += jnp.where(position >= start_ref[k, me], 1, 0)
    kept_ref[rows:, :slots] = jnp.where(segment == group, 1.0, 0.0).astype(bf16)
    kept_ref[rows : rows + picked, slots : 2 * slots] = slot_rows(chosen_ref, slot_ref, [me], slots)
    every = slot_rows(chosen_ref, slot_ref, range(n), slots)
    kept_ref[rows:, 2 * slots : 3 * slots] = every[:rows]
    kept_ref[rows:, 3 * slots :] = every[rows:]
    wait_all(gradient)
    live = lax.broadcasted_iota(i32, (rows, width), 0) < count_ref[me]
    g = kept_ref[:rows, :]
    kept_ref[:rows, :] = jnp.where(live, g, jnp.zeros_like(g))
    wait_all(tokens)


def picked_maps(kept_ref, b_ref, picked, ranks, messages):
    rows, slots = kept_ref.shape[0] // 2, kept_ref.shape[1] // 4
    b_ref[...] = jnp.zeros(b_ref.shape, bf16)
    for rank, message in zip(ranks, messages):
        b_ref[rank] = message[picked:, :]
    onehot = kept_ref[rows : rows + picked, slots : 2 * slots]
    return dot(onehot, b_ref[...].reshape(-1, b_ref.shape[2]), 1, 0).astype(bf16)


def low_terms(x_ref, picked, ranks, messages):
    total = jnp.zeros((x_ref.shape[0], picked), f32)
    for rank, message in zip(ranks, messages):
        width = message.shape[1]
        at = pl.ds(pl.multiple_of(rank * width, width), width)
        total += dot(x_ref[:, at], message[:picked, :], 1, 1)
    return total


def early_kernel(n, picked, kept_ref, x_mine, x_other, *refs):
    count = n // 2 + 1
    here, (x_ref, low_ref, dlow_ref, b_ref) = refs[:count], refs[count:]
    me, core, half = lax.axis_index("dp"), lax.axis_index("tensor"), x_mine.shape[0]
    ranks = senders(n, me, core)[:count]
    x_ref[pl.ds(pl.multiple_of(core * half, half), half), :] = x_mine[...]
    x_ref[pl.ds(pl.multiple_of((1 - core) * half, half), half), :] = x_other[...]
    b_sel = picked_maps(kept_ref, b_ref, picked, ranks, here)
    dlow_ref[...] = dot(kept_ref[: 2 * half, :], b_sel, 1, 1)
    low_ref[...] = low_terms(x_ref, picked, ranks, here)


def middle_kernel(n, kept_ref, x_ref, low_ref, dlow_part, *refs):
    count = n // 2 + 1
    got, dlow_ref, send = refs[: n - count], refs[n - count], refs[n - count + 1 : n + 1]
    b_ref, up_ref = refs[n + 1 :]
    me, core = lax.axis_index("dp"), lax.axis_index("tensor")
    rows, picked = dlow_ref.shape
    width = kept_ref.shape[1]
    slots = width // 4
    ranks = senders(n, me, core)[count:]
    in_seg = kept_ref[rows:, :picked].astype(f32) > 0.0
    g = kept_ref[:rows, :]
    onehot = kept_ref[rows : rows + picked, slots : 2 * slots]
    b_sel = picked_maps(kept_ref, b_ref, picked, ranks, got)
    dlow = dlow_part[...] + dot(g, b_sel, 1, 1)
    dlow = jnp.where(in_seg, adapter_scale * dlow, 0.0).astype(bf16)
    dlow_ref[...] = dlow
    targets = partners(n, me, core)
    for target, message in zip(targets, send):
        at = pl.ds(pl.multiple_of(target * width, width), width)
        message[:picked, :] = dot(dlow, x_ref[:, at], 0, 0).astype(bf16)

    low = low_ref[...] + low_terms(x_ref, picked, ranks, got)
    low = jnp.where(in_seg, low, 0.0).astype(bf16)
    low_wide = dot(low, onehot, 1, 0).astype(bf16)
    up = (adapter_scale * dot(low_wide, g, 0, 0)).astype(bf16)
    up_ref[...] = up.reshape(up_ref.shape)
    for target, message in zip(targets, send):
        message[picked:, :] = up_ref[target]


def grad_x_kernel(n, kept_ref, w_ref, dlow_ref, *refs):
    got, (out_hbm, a_ref, out_ref, sems) = refs[:n], refs[n:]
    me, core = lax.axis_index("dp"), lax.axis_index("tensor")
    picked, width = a_ref.shape[1:]
    for sender, message in zip(senders(n, me, core), got):
        a_ref[sender] = message[:picked, :]
    g = kept_ref[: out_ref.shape[0], :]
    done = []
    for j in range(n // 2):
        at = pl.ds(j * width, width)
        total = dot(g, w_ref[at, :], 1, 1) + dot(dlow_ref[...], a_ref[core * (n // 2) + j], 1, 0)
        out_ref[:, at] = total.astype(bf16)
        done += start_all([out_ref.at[:, at]], [out_hbm.at[:, at]], sems, j)
    wait_all(done)


def final_kernel(n, kept_ref, *refs):
    got, (a_ref, up_ref, rows_ref) = refs[:n], refs[n:]
    me, core = lax.axis_index("dp"), lax.axis_index("tensor")
    piece, picked = up_ref.shape[1], rows_ref.shape[1] - ADAPTER_RANK
    half, slots = kept_ref.shape[0] // 2, kept_ref.shape[1] // 4
    for sender, message in zip(senders(n, me, core), got):
        rows_ref[sender] = message[...]
    rows = rows_ref[:, :picked, :].reshape(n * picked, rows_ref.shape[2])
    onehot = jnp.concatenate(
        [kept_ref[half:, 2 * slots : 3 * slots], kept_ref[half:, 3 * slots :]], axis=0
    )
    a_ref[...] = dot(rows, onehot, 0, 0)
    at = pl.ds(pl.multiple_of(core * piece, piece), piece)
    up_ref[...] = jnp.sum(rows_ref[:, picked:, at].astype(f32), axis=0)


def exchange(messages, tied, beside):
    n = 2 * len(messages)
    got = [
        lax.ppermute(
            message,
            ("dp", "tensor"),
            [(2 * i + c, 2 * (i ^ step[c]) + c) for i in range(n) for c in range(2)],
        )
        for message, step in zip(messages, steps(n))
    ]
    for k in tied:
        got[k], beside = lax.optimization_barrier((got[k], beside))
    passed = [
        lax.ppermute(message, "tensor", [(0, 1), (1, 0)])
        for message, (a, b) in zip(got, steps(n))
        if a != b
    ]
    return got + passed, beside


def local_kernels(
    inputs,
    output_gradient,
    frozen_weight,
    down_maps,
    up_maps,
    segment_start,
    segment_adapter,
    adapter_slot,
    token_count,
):
    model_width = inputs.shape[1]
    tok_rows, out_width = output_gradient.shape
    column_total, slot_width = down_maps.shape
    half = frozen_weight.shape[0]
    n = lax.axis_size("dp")
    piece = out_width // lax.axis_size("tensor")
    segs = segment_start.shape[1]
    picked = segs * ADAPTER_RANK
    shape = jax.ShapeDtypeStruct
    message = shape((picked + ADAPTER_RANK, column_total), bf16)
    count = n // 2 + 1
    starts, chosen = segment_start.T, segment_adapter.T

    tables = [
        pltpu.SMEM(starts.shape, i32),
        pltpu.SMEM(chosen.shape, i32),
        pltpu.SMEM(adapter_slot.shape, i32),
        pltpu.SMEM(token_count.shape, i32),
    ]
    dma = pltpu.SemaphoreType.DMA

    own, *sent = pl.pallas_call(
        functools.partial(pack_kernel, n),
        out_shape=[message] * count,
        in_specs=[HBM] * 4,
        out_specs=[VMEM] * count,
        scratch_shapes=tables[1:3]
        + [pltpu.VMEM(down_maps.shape, bf16), pltpu.VMEM(up_maps.shape, bf16), dma((4,))],
        compiler_params=params(8),
    )(*in_hbm(chosen, adapter_slot, down_maps, up_maps))
    sent, x_late = lax.optimization_barrier((sent, inputs))
    x_other = lax.ppermute(x_late, "tensor", [(0, 1), (1, 0)])
    x_mine, kept = pl.pallas_call(
        functools.partial(stage_kernel, n, picked),
        out_shape=[shape(inputs.shape, bf16), shape((2 * tok_rows, out_width), bf16)],
        in_specs=[HBM] * 7,
        out_specs=[VMEM] * 2,
        scratch_shapes=tables + [dma((6,))],
        compiler_params=params(8),
        cost_estimate=pl.CostEstimate(flops=0, bytes_accessed=1 << 21, transcendentals=0),
    )(*in_hbm(starts, chosen, adapter_slot, token_count, output_gradient, inputs, frozen_weight))
    got, x_mine = exchange(sent, (0,), x_mine)
    low = shape((tok_rows, picked), f32)
    maps = pltpu.VMEM((n, ADAPTER_RANK, out_width), bf16)
    got = [own] + got
    x, low, dlow = pl.pallas_call(
        functools.partial(early_kernel, n, picked),
        out_shape=[shape((tok_rows, model_width), bf16), low, low],
        in_specs=[VMEM] * (3 + count),
        out_specs=[VMEM] * 3,
        scratch_shapes=[maps],
        compiler_params=params(8),
        cost_estimate=pl.CostEstimate(flops=0, bytes_accessed=1 << 21, transcendentals=0),
    )(kept, x_mine, x_other, *got[:count])

    dlow, *sent = pl.pallas_call(
        functools.partial(middle_kernel, n),
        out_shape=[shape((tok_rows, picked), bf16)] + [message] * count,
        in_specs=[VMEM] * (4 + n - count),
        out_specs=[VMEM] * (1 + count),
        scratch_shapes=[maps, maps],
        compiler_params=params(8),
    )(kept, x, low, dlow, *got[count:])
    own, *sent = sent

    grad_x = pl.pallas_call(
        functools.partial(grad_x_kernel, n),
        out_shape=shape((tok_rows, half), bf16),
        in_specs=[VMEM] * (3 + n),
        out_specs=HBM,
        scratch_shapes=[
            pltpu.VMEM((n, picked, column_total), bf16),
            pltpu.VMEM((tok_rows, half), bf16),
            dma((n // 2,)),
        ],
        compiler_params=params(8),
        cost_estimate=pl.CostEstimate(
            flops=2 * tok_rows * half * (out_width + picked),
            bytes_accessed=2 * half * (out_width + tok_rows),
            transcendentals=0,
        ),
    )(kept, frozen_weight, dlow, *got)

    got, grad_x = exchange(sent, (0,), grad_x)

    grad_a, up_map_gradient = pl.pallas_call(
        functools.partial(final_kernel, n),
        out_shape=[shape((column_total, slot_width), f32), shape((ADAPTER_RANK, piece), f32)],
        in_specs=[VMEM] * (1 + n),
        out_specs=[VMEM, VMEM],
        scratch_shapes=[pltpu.VMEM((n,) + message.shape, bf16)],
        compiler_params=params(8),
    )(kept, own, *got)
    return grad_x, grad_a, up_map_gradient


def local_plain(
    inputs,
    output_gradient,
    frozen_weight,
    down_maps,
    up_maps,
    segment_start,
    segment_adapter,
    adapter_slot,
    token_count,
):
    tok_rows, out_width = output_gradient.shape
    column_total = down_maps.shape[0]
    adapter_list = adapter_slot.shape[0]
    segs = segment_start.shape[1]
    dp_size = lax.axis_size("dp")
    my_rank = lax.axis_index("dp")
    core_idx = lax.axis_index("tensor")
    picked = segs * ADAPTER_RANK
    piece_out = out_width // lax.axis_size("tensor")
    half = frozen_weight.shape[0]

    x_other = lax.ppermute(inputs, "tensor", [(0, 1), (1, 0)])
    adapter_ids = jnp.arange(adapter_list, dtype=i32)
    slot_table = jnp.sum(
        jnp.where(segment_adapter[..., None] == adapter_ids, adapter_slot, 0), axis=-1
    )
    column = slot_table[:, :, None] * ADAPTER_RANK + jnp.arange(ADAPTER_RANK, dtype=i32)
    onehot = (
        column.reshape(-1)[:, None] == jnp.arange(adapter_list * ADAPTER_RANK, dtype=i32)
    ).astype(bf16)

    a_send = dot(onehot, down_maps, 1, 1).astype(bf16).reshape(dp_size, picked, column_total)
    b_send = jnp.broadcast_to(up_maps[None], (dp_size,) + up_maps.shape)
    a_got = lax.all_to_all(a_send, "dp", 0, 0, tiled=True)
    b_got = lax.all_to_all(b_send, "dp", 0, 0, tiled=True)

    position = jnp.arange(tok_rows, dtype=i32)
    starts = lax.dynamic_index_in_dim(segment_start, my_rank, 0, keepdims=False)
    live = position < lax.dynamic_index_in_dim(token_count, my_rank, 0, keepdims=False)
    my_seg = jnp.sum((starts[None, :] <= position[:, None]).astype(i32), axis=1) - 1
    in_seg = my_seg[:, None] == (jnp.arange(picked, dtype=i32) // ADAPTER_RANK)[None, :]
    my_onehot = lax.dynamic_slice_in_dim(onehot, my_rank * picked, picked, 0)
    g = jnp.where(live[:, None], output_gradient, jnp.zeros_like(output_gradient))
    base = dot(g, frozen_weight, 1, 1)

    b_sel = dot(my_onehot, b_got.reshape(-1, out_width), 1, 0).astype(bf16)
    dlow = (adapter_scale * dot(g, b_sel, 1, 1)).astype(bf16)
    dlow = jnp.where(in_seg, dlow, jnp.zeros_like(dlow))
    a_sel = jnp.moveaxis(a_got, 0, 1).reshape(picked, -1)
    first = core_idx == 0
    x = jnp.concatenate(
        [jnp.where(first, inputs, x_other), jnp.where(first, x_other, inputs)], axis=0
    )
    low = dot(x, a_sel, 1, 1).astype(bf16)
    low = jnp.where(in_seg, low, jnp.zeros_like(low))
    low_wide = dot(low, my_onehot, 1, 0).astype(bf16)

    ga_send = dot(dlow, x, 0, 0).astype(bf16).reshape(picked, dp_size, column_total)
    ga_got = lax.all_to_all(jnp.moveaxis(ga_send, 1, 0), "dp", 0, 0, tiled=True)
    g_piece = lax.dynamic_slice_in_dim(g, core_idx * piece_out, piece_out, 1)
    up_send = (adapter_scale * dot(low_wide, g_piece, 0, 0)).astype(bf16)
    up_got = lax.all_to_all(up_send.reshape(dp_size, -1, piece_out), "dp", 0, 0, tiled=True)

    a_half = lax.dynamic_slice_in_dim(a_sel, core_idx * half, half, 1)
    grad_x = (base + dot(dlow, a_half, 1, 0)).astype(bf16)
    grad_a = dot(ga_got.reshape(dp_size * picked, column_total), onehot, 0, 0)
    up_map_gradient = jnp.sum(up_got.astype(f32), axis=0)
    return grad_x, grad_a, up_map_gradient


def local(*args):
    down_maps, up_maps = args[3], args[4]
    n, tp = lax.axis_size("dp"), lax.axis_size("tensor")
    out_width = up_maps.shape[1]
    kernels_fit = (
        n == 8
        and tp == 2
        and down_maps.shape[0] == out_width
        and down_maps.shape[1] == n * up_maps.shape[0]
        and out_width % (128 * tp) == 0
        and out_width == 4 * down_maps.shape[1]
        and args[1].shape[0] == 2 * args[0].shape[0] == down_maps.shape[1]
        and args[5].shape[1] * ADAPTER_RANK * n == 2 * down_maps.shape[1]
    )
    return (local_kernels if kernels_fit else local_plain)(*args)


def solution(mesh):
    in_specs = (
        P(("groups", "dp", "tensor"), None),
        P(("groups", "dp"), None),
        P("tensor", None),
        P(("groups", "dp"), None),
        P(("groups", "dp"), None),
        P("groups", None),
        P("groups", None),
        P("groups"),
        P("groups"),
    )
    out_specs = (
        P(("groups", "dp"), "tensor"),
        P(("groups", "dp"), None),
        P(("groups", "dp"), "tensor"),
    )
    return jax.shard_map(local, mesh=mesh, in_specs=in_specs, out_specs=out_specs, check_vma=False)
```

```python
import functools

import jax
import jax.numpy as jnp
from jax import lax
from jax.experimental import pallas as pl
from jax.experimental.pallas import tpu as pltpu
from jax.sharding import PartitionSpec as P

ADAPTER_RANK = 16
adapter_scale = 2.0

bf16, f32, i32 = jnp.bfloat16, jnp.float32, jnp.int32

HBM = pl.BlockSpec(memory_space=pltpu.HBM)
VMEM = pl.BlockSpec(memory_space=pltpu.VMEM)


def dot(a, b, ca, cb):
    return lax.dot_general(a, b, (((ca,), (cb,)), ((), ())), preferred_element_type=f32)


def params(mib):
    return pltpu.CompilerParams(vmem_limit_bytes=mib << 20)


def slot_rows(chosen_ref, slot_ref, ranks, width):
    lane = lax.broadcasted_iota(i32, (ADAPTER_RANK, width), 1)
    row = lax.broadcasted_iota(i32, (ADAPTER_RANK, width), 0)
    rows = []
    for rank in ranks:
        for k in range(chosen_ref.shape[0]):
            first = slot_ref[chosen_ref[k, rank]] * ADAPTER_RANK
            rows.append(jnp.where(lane == row + first, 1.0, 0.0))
    return jnp.concatenate(rows, axis=0).astype(bf16)


def start_all(sources, targets, sems, first=0):
    copies = [
        pltpu.make_async_copy(source, target, sems.at[first + k])
        for k, (source, target) in enumerate(zip(sources, targets))
    ]
    for copy in copies:
        copy.start()
    return copies


def wait_all(copies):
    for copy in copies:
        copy.wait()


def steps(n, turn):
    half = n // 2
    if turn == 0:
        return [(n - 1, half), (3, half + 1), (n - 2, 2), (1, 1)]
    return [(n - 1, half + 1), (3, n - 2), (2, half), (1, 1)]


def partners(n, turn, me, core):
    return [me] + [me ^ jnp.where(core == 0, a, b) for a, b in steps(n, turn)]


def senders(n, turn, me, core):
    passed = [me ^ jnp.where(core == 0, b, a) for a, b in steps(n, turn) if a != b]
    return partners(n, turn, me, core) + passed


def in_hbm(*arrays):
    return [pltpu.with_memory_space_constraint(array, pltpu.HBM) for array in arrays]


def pack_kernel(n, chosen_hbm, slot_hbm, down_hbm, up_hbm, *refs):
    count = n // 2 + 1
    send, (chosen_ref, slot_ref, down_ref, up_ref, sems) = refs[:count], refs[count:]
    tables = start_all([chosen_hbm, slot_hbm], [chosen_ref, slot_ref], sems)
    maps = start_all([down_hbm, up_hbm], [down_ref, up_ref], sems, 2)
    ranks = partners(n, 0, lax.axis_index("dp"), lax.axis_index("tensor"))
    wait_all(tables)
    onehot = slot_rows(chosen_ref, slot_ref, ranks, down_ref.shape[1])
    picked = onehot.shape[0] // count
    wait_all(maps)
    columns = dot(onehot, down_ref[...], 1, 1).astype(bf16)
    for k in range(count):
        send[k][:picked, :] = columns[k * picked : (k + 1) * picked]
        send[k][picked:, :] = up_ref[...]


def stage_kernel(
    n, picked, start_hbm, chosen_hbm, slot_hbm, count_hbm, g_hbm, x_hbm, w_hbm,
    x_ref, kept_ref, start_ref, chosen_ref, slot_ref, count_ref, sems,
):
    rows, width = g_hbm.shape
    slots = width // 4
    me = lax.axis_index("dp")
    tables = start_all(
        [chosen_hbm, slot_hbm, start_hbm, count_hbm], [chosen_ref, slot_ref, start_ref, count_ref], sems
    )
    gradient = start_all([g_hbm], [kept_ref.at[pl.ds(0, rows)]], sems, 4)
    tokens = start_all([x_hbm], [x_ref], sems, 5)
    wait_all(tables)
    position = lax.broadcasted_iota(i32, (rows, slots), 0)
    group = lax.broadcasted_iota(i32, (rows, slots), 1) // ADAPTER_RANK
    segment = jnp.full((rows, slots), -1, i32)
    for k in range(start_ref.shape[0]):
        segment += jnp.where(position >= start_ref[k, me], 1, 0)
    kept_ref[rows:, :slots] = jnp.where(segment == group, 1.0, 0.0).astype(bf16)
    kept_ref[rows : rows + picked, slots : 2 * slots] = slot_rows(chosen_ref, slot_ref, [me], slots)
    every = slot_rows(chosen_ref, slot_ref, range(n), slots)
    kept_ref[rows:, 2 * slots : 3 * slots] = every[:rows]
    kept_ref[rows:, 3 * slots :] = every[rows:]
    wait_all(gradient)
    live = lax.broadcasted_iota(i32, (rows, width), 0) < count_ref[me]
    g = kept_ref[:rows, :]
    kept_ref[:rows, :] = jnp.where(live, g, jnp.zeros_like(g))
    wait_all(tokens)


def picked_maps(kept_ref, b_ref, picked, ranks, messages):
    rows, slots = kept_ref.shape[0] // 2, kept_ref.shape[1] // 4
    b_ref[...] = jnp.zeros(b_ref.shape, bf16)
    for rank, message in zip(ranks, messages):
        b_ref[rank] = message[picked:, :]
    onehot = kept_ref[rows : rows + picked, slots : 2 * slots]
    return dot(onehot, b_ref[...].reshape(-1, b_ref.shape[2]), 1, 0).astype(bf16)


def low_terms(x_ref, picked, ranks, messages):
    total = jnp.zeros((x_ref.shape[0], picked), f32)
    for rank, message in zip(ranks, messages):
        width = message.shape[1]
        at = pl.ds(pl.multiple_of(rank * width, width), width)
        total += dot(x_ref[:, at], message[:picked, :], 1, 1)
    return total


def early_kernel(n, picked, kept_ref, x_mine, x_other, *refs):
    count = n // 2 + 1
    here, (x_ref, low_ref, dlow_ref, b_ref) = refs[:count], refs[count:]
    me, core, half = lax.axis_index("dp"), lax.axis_index("tensor"), x_mine.shape[0]
    ranks = senders(n, 0, me, core)[:count]
    x_ref[pl.ds(pl.multiple_of(core * half, half), half), :] = x_mine[...]
    x_ref[pl.ds(pl.multiple_of((1 - core) * half, half), half), :] = x_other[...]
    b_sel = picked_maps(kept_ref, b_ref, picked, ranks, here)
    dlow_ref[...] = dot(kept_ref[: 2 * half, :], b_sel, 1, 1)
    low_ref[...] = low_terms(x_ref, picked, ranks, here)


def middle_kernel(n, kept_ref, x_ref, low_ref, dlow_part, *refs):
    count = n // 2 + 1
    got, dlow_ref, send = refs[: n - count], refs[n - count], refs[n - count + 1 : n + 1]
    b_ref, up_ref = refs[n + 1 :]
    me, core = lax.axis_index("dp"), lax.axis_index("tensor")
    rows, picked = dlow_ref.shape
    width = kept_ref.shape[1]
    slots = width // 4
    ranks = senders(n, 0, me, core)[count:]
    in_seg = kept_ref[rows:, :picked].astype(f32) > 0.0
    g = kept_ref[:rows, :]
    onehot = kept_ref[rows : rows + picked, slots : 2 * slots]
    b_sel = picked_maps(kept_ref, b_ref, picked, ranks, got)
    dlow = dlow_part[...] + dot(g, b_sel, 1, 1)
    dlow = jnp.where(in_seg, adapter_scale * dlow, 0.0).astype(bf16)
    dlow_ref[...] = dlow
    targets = partners(n, 1, me, core)
    for target, message in zip(targets, send):
        at = pl.ds(pl.multiple_of(target * width, width), width)
        message[:picked, :] = dot(dlow, x_ref[:, at], 0, 0).astype(bf16)

    low = low_ref[...] + low_terms(x_ref, picked, ranks, got)
    low = jnp.where(in_seg, low, 0.0).astype(bf16)
    low_wide = dot(low, onehot, 1, 0).astype(bf16)
    up = (adapter_scale * dot(low_wide, g, 0, 0)).astype(bf16)
    up_ref[...] = up.reshape(up_ref.shape)
    for target, message in zip(targets, send):
        message[picked:, :] = up_ref[target]


def grad_x_kernel(n, kept_ref, w_ref, dlow_ref, *refs):
    got, (out_hbm, a_ref, out_ref, sems) = refs[:n], refs[n:]
    me, core = lax.axis_index("dp"), lax.axis_index("tensor")
    picked, width = a_ref.shape[1:]
    for sender, message in zip(senders(n, 0, me, core), got):
        a_ref[sender] = message[:picked, :]
    g = kept_ref[: out_ref.shape[0], :]
    done = []
    for j in range(n // 2):
        at = pl.ds(j * width, width)
        total = dot(g, w_ref[at, :], 1, 1) + dot(dlow_ref[...], a_ref[core * (n // 2) + j], 1, 0)
        out_ref[:, at] = total.astype(bf16)
        done += start_all([out_ref.at[:, at]], [out_hbm.at[:, at]], sems, j)
    wait_all(done)


def final_kernel(n, kept_ref, *refs):
    got, (a_ref, up_ref, rows_ref) = refs[:n], refs[n:]
    me, core = lax.axis_index("dp"), lax.axis_index("tensor")
    piece, picked = up_ref.shape[1], rows_ref.shape[1] - ADAPTER_RANK
    half, slots = kept_ref.shape[0] // 2, kept_ref.shape[1] // 4
    for sender, message in zip(senders(n, 1, me, core), got):
        rows_ref[sender] = message[...]
    rows = rows_ref[:, :picked, :].reshape(n * picked, rows_ref.shape[2])
    onehot = jnp.concatenate(
        [kept_ref[half:, 2 * slots : 3 * slots], kept_ref[half:, 3 * slots :]], axis=0
    )
    a_ref[...] = dot(rows, onehot, 0, 0)
    at = pl.ds(pl.multiple_of(core * piece, piece), piece)
    up_ref[...] = jnp.sum(rows_ref[:, picked:, at].astype(f32), axis=0)


def exchange(messages, turn, tied, beside):
    n = 2 * len(messages)
    got = [
        lax.ppermute(
            message,
            ("dp", "tensor"),
            [(2 * i + c, 2 * (i ^ step[c]) + c) for i in range(n) for c in range(2)],
        )
        for message, step in zip(messages, steps(n, turn))
    ]
    for k in tied:
        got[k], beside = lax.optimization_barrier((got[k], beside))
    passed = [
        lax.ppermute(message, "tensor", [(0, 1), (1, 0)])
        for message, (a, b) in zip(got, steps(n, turn))
        if a != b
    ]
    return got + passed, beside


def local_kernels(
    inputs,
    output_gradient,
    frozen_weight,
    down_maps,
    up_maps,
    segment_start,
    segment_adapter,
    adapter_slot,
    token_count,
):
    model_width = inputs.shape[1]
    tok_rows, out_width = output_gradient.shape
    column_total, slot_width = down_maps.shape
    half = frozen_weight.shape[0]
    n = lax.axis_size("dp")
    piece = out_width // lax.axis_size("tensor")
    segs = segment_start.shape[1]
    picked = segs * ADAPTER_RANK
    shape = jax.ShapeDtypeStruct
    message = shape((picked + ADAPTER_RANK, column_total), bf16)
    count = n // 2 + 1
    starts, chosen = segment_start.T, segment_adapter.T

    tables = [
        pltpu.SMEM(starts.shape, i32),
        pltpu.SMEM(chosen.shape, i32),
        pltpu.SMEM(adapter_slot.shape, i32),
        pltpu.SMEM(token_count.shape, i32),
    ]
    dma = pltpu.SemaphoreType.DMA

    own, *sent = pl.pallas_call(
        functools.partial(pack_kernel, n),
        out_shape=[message] * count,
        in_specs=[HBM] * 4,
        out_specs=[VMEM] * count,
        scratch_shapes=tables[1:3]
        + [pltpu.VMEM(down_maps.shape, bf16), pltpu.VMEM(up_maps.shape, bf16), dma((4,))],
        compiler_params=params(8),
    )(*in_hbm(chosen, adapter_slot, down_maps, up_maps))
    sent, x_late = lax.optimization_barrier((sent, inputs))
    x_other = lax.ppermute(x_late, "tensor", [(0, 1), (1, 0)])
    x_mine, kept = pl.pallas_call(
        functools.partial(stage_kernel, n, picked),
        out_shape=[shape(inputs.shape, bf16), shape((2 * tok_rows, out_width), bf16)],
        in_specs=[HBM] * 7,
        out_specs=[VMEM] * 2,
        scratch_shapes=tables + [dma((6,))],
        compiler_params=params(8),
        cost_estimate=pl.CostEstimate(flops=0, bytes_accessed=1 << 21, transcendentals=0),
    )(*in_hbm(starts, chosen, adapter_slot, token_count, output_gradient, inputs, frozen_weight))
    got, x_mine = exchange(sent, 0, (0,), x_mine)
    low = shape((tok_rows, picked), f32)
    maps = pltpu.VMEM((n, ADAPTER_RANK, out_width), bf16)
    got = [own] + got
    x, low, dlow = pl.pallas_call(
        functools.partial(early_kernel, n, picked),
        out_shape=[shape((tok_rows, model_width), bf16), low, low],
        in_specs=[VMEM] * (3 + count),
        out_specs=[VMEM] * 3,
        scratch_shapes=[maps],
        compiler_params=params(8),
        cost_estimate=pl.CostEstimate(flops=0, bytes_accessed=1 << 21, transcendentals=0),
    )(kept, x_mine, x_other, *got[:count])

    dlow, *sent = pl.pallas_call(
        functools.partial(middle_kernel, n),
        out_shape=[shape((tok_rows, picked), bf16)] + [message] * count,
        in_specs=[VMEM] * (4 + n - count),
        out_specs=[VMEM] * (1 + count),
        scratch_shapes=[maps, maps],
        compiler_params=params(8),
    )(kept, x, low, dlow, *got[count:])
    own, *sent = sent

    grad_x = pl.pallas_call(
        functools.partial(grad_x_kernel, n),
        out_shape=shape((tok_rows, half), bf16),
        in_specs=[VMEM] * (3 + n),
        out_specs=HBM,
        scratch_shapes=[
            pltpu.VMEM((n, picked, column_total), bf16),
            pltpu.VMEM((tok_rows, half), bf16),
            dma((n // 2,)),
        ],
        compiler_params=params(8),
        cost_estimate=pl.CostEstimate(
            flops=2 * tok_rows * half * (out_width + picked),
            bytes_accessed=2 * half * (out_width + tok_rows),
            transcendentals=0,
        ),
    )(kept, frozen_weight, dlow, *got)

    got, grad_x = exchange(sent, 1, (0,), grad_x)

    grad_a, up_map_gradient = pl.pallas_call(
        functools.partial(final_kernel, n),
        out_shape=[shape((column_total, slot_width), f32), shape((ADAPTER_RANK, piece), f32)],
        in_specs=[VMEM] * (1 + n),
        out_specs=[VMEM, VMEM],
        scratch_shapes=[pltpu.VMEM((n,) + message.shape, bf16)],
        compiler_params=params(8),
    )(kept, own, *got)
    return grad_x, grad_a, up_map_gradient


def local_plain(
    inputs,
    output_gradient,
    frozen_weight,
    down_maps,
    up_maps,
    segment_start,
    segment_adapter,
    adapter_slot,
    token_count,
):
    tok_rows, out_width = output_gradient.shape
    column_total = down_maps.shape[0]
    adapter_list = adapter_slot.shape[0]
    segs = segment_start.shape[1]
    dp_size = lax.axis_size("dp")
    my_rank = lax.axis_index("dp")
    core_idx = lax.axis_index("tensor")
    picked = segs * ADAPTER_RANK
    piece_out = out_width // lax.axis_size("tensor")
    half = frozen_weight.shape[0]

    x_other = lax.ppermute(inputs, "tensor", [(0, 1), (1, 0)])
    adapter_ids = jnp.arange(adapter_list, dtype=i32)
    slot_table = jnp.sum(
        jnp.where(segment_adapter[..., None] == adapter_ids, adapter_slot, 0), axis=-1
    )
    column = slot_table[:, :, None] * ADAPTER_RANK + jnp.arange(ADAPTER_RANK, dtype=i32)
    onehot = (
        column.reshape(-1)[:, None] == jnp.arange(adapter_list * ADAPTER_RANK, dtype=i32)
    ).astype(bf16)

    a_send = dot(onehot, down_maps, 1, 1).astype(bf16).reshape(dp_size, picked, column_total)
    b_send = jnp.broadcast_to(up_maps[None], (dp_size,) + up_maps.shape)
    a_got = lax.all_to_all(a_send, "dp", 0, 0, tiled=True)
    b_got = lax.all_to_all(b_send, "dp", 0, 0, tiled=True)

    position = jnp.arange(tok_rows, dtype=i32)
    starts = lax.dynamic_index_in_dim(segment_start, my_rank, 0, keepdims=False)
    live = position < lax.dynamic_index_in_dim(token_count, my_rank, 0, keepdims=False)
    my_seg = jnp.sum((starts[None, :] <= position[:, None]).astype(i32), axis=1) - 1
    in_seg = my_seg[:, None] == (jnp.arange(picked, dtype=i32) // ADAPTER_RANK)[None, :]
    my_onehot = lax.dynamic_slice_in_dim(onehot, my_rank * picked, picked, 0)
    g = jnp.where(live[:, None], output_gradient, jnp.zeros_like(output_gradient))
    base = dot(g, frozen_weight, 1, 1)

    b_sel = dot(my_onehot, b_got.reshape(-1, out_width), 1, 0).astype(bf16)
    dlow = (adapter_scale * dot(g, b_sel, 1, 1)).astype(bf16)
    dlow = jnp.where(in_seg, dlow, jnp.zeros_like(dlow))
    a_sel = jnp.moveaxis(a_got, 0, 1).reshape(picked, -1)
    first = core_idx == 0
    x = jnp.concatenate(
        [jnp.where(first, inputs, x_other), jnp.where(first, x_other, inputs)], axis=0
    )
    low = dot(x, a_sel, 1, 1).astype(bf16)
    low = jnp.where(in_seg, low, jnp.zeros_like(low))
    low_wide = dot(low, my_onehot, 1, 0).astype(bf16)

    ga_send = dot(dlow, x, 0, 0).astype(bf16).reshape(picked, dp_size, column_total)
    ga_got = lax.all_to_all(jnp.moveaxis(ga_send, 1, 0), "dp", 0, 0, tiled=True)
    g_piece = lax.dynamic_slice_in_dim(g, core_idx * piece_out, piece_out, 1)
    up_send = (adapter_scale * dot(low_wide, g_piece, 0, 0)).astype(bf16)
    up_got = lax.all_to_all(up_send.reshape(dp_size, -1, piece_out), "dp", 0, 0, tiled=True)

    a_half = lax.dynamic_slice_in_dim(a_sel, core_idx * half, half, 1)
    grad_x = (base + dot(dlow, a_half, 1, 0)).astype(bf16)
    grad_a = dot(ga_got.reshape(dp_size * picked, column_total), onehot, 0, 0)
    up_map_gradient = jnp.sum(up_got.astype(f32), axis=0)
    return grad_x, grad_a, up_map_gradient


def local(*args):
    down_maps, up_maps = args[3], args[4]
    n, tp = lax.axis_size("dp"), lax.axis_size("tensor")
    out_width = up_maps.shape[1]
    kernels_fit = (
        n == 8
        and tp == 2
        and down_maps.shape[0] == out_width
        and down_maps.shape[1] == n * up_maps.shape[0]
        and out_width % (128 * tp) == 0
        and out_width == 4 * down_maps.shape[1]
        and args[1].shape[0] == 2 * args[0].shape[0] == down_maps.shape[1]
        and args[5].shape[1] * ADAPTER_RANK * n == 2 * down_maps.shape[1]
    )
    return (local_kernels if kernels_fit else local_plain)(*args)


def solution(mesh):
    in_specs = (
        P(("groups", "dp", "tensor"), None),
        P(("groups", "dp"), None),
        P("tensor", None),
        P(("groups", "dp"), None),
        P(("groups", "dp"), None),
        P("groups", None),
        P("groups", None),
        P("groups"),
        P("groups"),
    )
    out_specs = (
        P(("groups", "dp"), "tensor"),
        P(("groups", "dp"), None),
        P(("groups", "dp"), "tensor"),
    )
    return jax.shard_map(local, mesh=mesh, in_specs=in_specs, out_specs=out_specs, check_vma=False)
```

```python
import functools

import jax
import jax.numpy as jnp
from jax import lax
from jax.experimental import pallas as pl
from jax.experimental.pallas import tpu as pltpu
from jax.sharding import PartitionSpec as P

ADAPTER_RANK = 16
adapter_scale = 2.0

bf16, f32, i32 = jnp.bfloat16, jnp.float32, jnp.int32

HBM = pl.BlockSpec(memory_space=pltpu.HBM)
VMEM = pl.BlockSpec(memory_space=pltpu.VMEM)


def dot(a, b, ca, cb):
    return lax.dot_general(a, b, (((ca,), (cb,)), ((), ())), preferred_element_type=f32)


def params(mib):
    return pltpu.CompilerParams(vmem_limit_bytes=mib << 20)


def slot_rows(chosen_ref, slot_ref, ranks, width):
    lane = lax.broadcasted_iota(i32, (ADAPTER_RANK, width), 1)
    row = lax.broadcasted_iota(i32, (ADAPTER_RANK, width), 0)
    rows = []
    for rank in ranks:
        for k in range(chosen_ref.shape[0]):
            first = slot_ref[chosen_ref[k, rank]] * ADAPTER_RANK
            rows.append(jnp.where(lane == row + first, 1.0, 0.0))
    return jnp.concatenate(rows, axis=0).astype(bf16)


def start_all(sources, targets, sems, first=0):
    copies = [
        pltpu.make_async_copy(source, target, sems.at[first + k])
        for k, (source, target) in enumerate(zip(sources, targets))
    ]
    for copy in copies:
        copy.start()
    return copies


def wait_all(copies):
    for copy in copies:
        copy.wait()


def steps(n):
    return [(n - 1, n // 2 + 1), (3, n - 2), (2, n // 2), (1, 1)]


def partners(n, me, core):
    return [me] + [me ^ jnp.where(core == 0, a, b) for a, b in steps(n)]


def senders(n, me, core):
    passed = [me ^ jnp.where(core == 0, b, a) for a, b in steps(n) if a != b]
    return partners(n, me, core) + passed


def both_orders(n, me):
    return [me] + [me ^ d for step in steps(n) for d in sorted(set(step), key=step.index)]


def in_hbm(*arrays):
    return [pltpu.with_memory_space_constraint(array, pltpu.HBM) for array in arrays]


def pack_kernel(n, chosen_hbm, slot_hbm, down_hbm, up_hbm, *refs):
    count = n // 2 + 1
    send, (chosen_ref, slot_ref, down_ref, up_ref, sems) = refs[:count], refs[count:]
    tables = start_all([chosen_hbm, slot_hbm], [chosen_ref, slot_ref], sems)
    maps = start_all([down_hbm, up_hbm], [down_ref, up_ref], sems, 2)
    ranks = partners(n, lax.axis_index("dp"), lax.axis_index("tensor"))
    wait_all(tables)
    onehot = slot_rows(chosen_ref, slot_ref, ranks, down_ref.shape[1])
    picked = onehot.shape[0] // count
    wait_all(maps)
    columns = dot(onehot, down_ref[...], 1, 1).astype(bf16)
    for k in range(count):
        send[k][:picked, :] = columns[k * picked : (k + 1) * picked]
        send[k][picked:, :] = up_ref[...]


def stage_kernel(
    n, picked, start_hbm, chosen_hbm, slot_hbm, count_hbm, g_hbm, x_hbm, w_hbm,
    x_ref, kept_ref, start_ref, chosen_ref, slot_ref, count_ref, sems,
):
    rows, width = g_hbm.shape
    slots = width // 4
    me = lax.axis_index("dp")
    tables = start_all(
        [chosen_hbm, slot_hbm, start_hbm, count_hbm], [chosen_ref, slot_ref, start_ref, count_ref], sems
    )
    gradient = start_all([g_hbm], [kept_ref.at[pl.ds(0, rows)]], sems, 4)
    tokens = start_all([x_hbm], [x_ref], sems, 5)
    wait_all(tables)
    position = lax.broadcasted_iota(i32, (rows, slots), 0)
    group = lax.broadcasted_iota(i32, (rows, slots), 1) // ADAPTER_RANK
    segment = jnp.full((rows, slots), -1, i32)
    for k in range(start_ref.shape[0]):
        segment += jnp.where(position >= start_ref[k, me], 1, 0)
    kept_ref[rows:, :slots] = jnp.where(segment == group, 1.0, 0.0).astype(bf16)
    kept_ref[rows : rows + picked, slots : 2 * slots] = slot_rows(chosen_ref, slot_ref, [me], slots)
    every = slot_rows(chosen_ref, slot_ref, both_orders(n, me), slots)
    kept_ref[rows:, 2 * slots : 3 * slots] = every[:rows]
    kept_ref[rows:, 3 * slots :] = every[rows:]
    wait_all(gradient)
    live = lax.broadcasted_iota(i32, (rows, width), 0) < count_ref[me]
    g = kept_ref[:rows, :]
    kept_ref[:rows, :] = jnp.where(live, g, jnp.zeros_like(g))
    wait_all(tokens)


def picked_maps(kept_ref, b_ref, picked, ranks, messages):
    rows, slots = kept_ref.shape[0] // 2, kept_ref.shape[1] // 4
    b_ref[...] = jnp.zeros(b_ref.shape, bf16)
    for rank, message in zip(ranks, messages):
        b_ref[rank] = message[picked:, :]
    onehot = kept_ref[rows : rows + picked, slots : 2 * slots]
    return dot(onehot, b_ref[...].reshape(-1, b_ref.shape[2]), 1, 0).astype(bf16)


def low_terms(x_ref, picked, ranks, messages):
    total = jnp.zeros((x_ref.shape[0], picked), f32)
    for rank, message in zip(ranks, messages):
        width = message.shape[1]
        at = pl.ds(pl.multiple_of(rank * width, width), width)
        total += dot(x_ref[:, at], message[:picked, :], 1, 1)
    return total


def early_kernel(n, picked, kept_ref, x_mine, x_other, *refs):
    count = n // 2 + 1
    here, (x_ref, low_ref, dlow_ref, b_ref) = refs[:count], refs[count:]
    me, core, half = lax.axis_index("dp"), lax.axis_index("tensor"), x_mine.shape[0]
    ranks = senders(n, me, core)[:count]
    x_ref[pl.ds(pl.multiple_of(core * half, half), half), :] = x_mine[...]
    x_ref[pl.ds(pl.multiple_of((1 - core) * half, half), half), :] = x_other[...]
    b_sel = picked_maps(kept_ref, b_ref, picked, ranks, here)
    dlow_ref[...] = dot(kept_ref[: 2 * half, :], b_sel, 1, 1)
    low_ref[...] = low_terms(x_ref, picked, ranks, here)


def middle_kernel(n, kept_ref, x_ref, low_ref, dlow_part, *refs):
    count = n // 2 + 1
    got, dlow_ref, send = refs[: n - count], refs[n - count], refs[n - count + 1 : n + 1]
    b_ref, up_ref = refs[n + 1 :]
    me, core = lax.axis_index("dp"), lax.axis_index("tensor")
    rows, picked = dlow_ref.shape
    width = kept_ref.shape[1]
    slots = width // 4
    ranks = senders(n, me, core)[count:]
    in_seg = kept_ref[rows:, :picked].astype(f32) > 0.0
    g = kept_ref[:rows, :]
    onehot = kept_ref[rows : rows + picked, slots : 2 * slots]
    b_sel = picked_maps(kept_ref, b_ref, picked, ranks, got)
    dlow = dlow_part[...] + dot(g, b_sel, 1, 1)
    dlow = jnp.where(in_seg, adapter_scale * dlow, 0.0).astype(bf16)
    dlow_ref[...] = dlow
    targets = partners(n, me, core)
    for target, message in zip(targets, send):
        at = pl.ds(pl.multiple_of(target * width, width), width)
        message[:picked, :] = dot(dlow, x_ref[:, at], 0, 0).astype(bf16)

    low = low_ref[...] + low_terms(x_ref, picked, ranks, got)
    low = jnp.where(in_seg, low, 0.0).astype(bf16)
    low_wide = dot(low, onehot, 1, 0).astype(bf16)
    up = (adapter_scale * dot(low_wide, g, 0, 0)).astype(bf16)
    up_ref[...] = up.reshape(up_ref.shape)
    for target, message in zip(targets, send):
        message[picked:, :] = up_ref[target]


def grad_x_kernel(n, kept_ref, w_ref, dlow_ref, *refs):
    got, (out_hbm, a_ref, out_ref, sems) = refs[:n], refs[n:]
    me, core = lax.axis_index("dp"), lax.axis_index("tensor")
    picked, width = a_ref.shape[1:]
    for sender, message in zip(senders(n, me, core), got):
        a_ref[sender] = message[:picked, :]
    g = kept_ref[: out_ref.shape[0], :]
    done = []
    for j in range(n // 2):
        at = pl.ds(j * width, width)
        total = dot(g, w_ref[at, :], 1, 1) + dot(dlow_ref[...], a_ref[core * (n // 2) + j], 1, 0)
        out_ref[:, at] = total.astype(bf16)
        done += start_all([out_ref.at[:, at]], [out_hbm.at[:, at]], sems, j)
    wait_all(done)


def final_kernel(n, kept_ref, *refs):
    got, (a_ref, up_ref) = refs[:n], refs[n:]
    core = lax.axis_index("tensor")
    piece, picked = up_ref.shape[1], got[0].shape[0] - ADAPTER_RANK
    half, slots = kept_ref.shape[0] // 2, kept_ref.shape[1] // 4
    blocks, passed = [got[0][:picked, :]], iter(got[n // 2 + 1 :])
    for (a, b), message in zip(steps(n), got[1:]):
        mine = message[:picked, :]
        if a == b:
            blocks.append(mine)
        else:
            other = next(passed)[:picked, :]
            blocks += [jnp.where(core == 0, mine, other), jnp.where(core == 0, other, mine)]
    onehot = jnp.concatenate(
        [kept_ref[half:, 2 * slots : 3 * slots], kept_ref[half:, 3 * slots :]], axis=0
    )
    a_ref[...] = dot(jnp.concatenate(blocks, axis=0), onehot, 0, 0)
    at = pl.ds(pl.multiple_of(core * piece, piece), piece)
    up_ref[...] = sum(message[picked:, at].astype(f32) for message in got)


def exchange(messages, tied, beside):
    n = 2 * len(messages)
    got = [
        lax.ppermute(
            message,
            ("dp", "tensor"),
            [(2 * i + c, 2 * (i ^ step[c]) + c) for i in range(n) for c in range(2)],
        )
        for message, step in zip(messages, steps(n))
    ]
    for k in tied:
        got[k], beside = lax.optimization_barrier((got[k], beside))
    passed = [
        lax.ppermute(message, "tensor", [(0, 1), (1, 0)])
        for message, (a, b) in zip(got, steps(n))
        if a != b
    ]
    return got + passed, beside


def local_kernels(
    inputs,
    output_gradient,
    frozen_weight,
    down_maps,
    up_maps,
    segment_start,
    segment_adapter,
    adapter_slot,
    token_count,
):
    model_width = inputs.shape[1]
    tok_rows, out_width = output_gradient.shape
    column_total, slot_width = down_maps.shape
    half = frozen_weight.shape[0]
    n = lax.axis_size("dp")
    piece = out_width // lax.axis_size("tensor")
    segs = segment_start.shape[1]
    picked = segs * ADAPTER_RANK
    shape = jax.ShapeDtypeStruct
    message = shape((picked + ADAPTER_RANK, column_total), bf16)
    count = n // 2 + 1
    starts, chosen = segment_start.T, segment_adapter.T

    tables = [
        pltpu.SMEM(starts.shape, i32),
        pltpu.SMEM(chosen.shape, i32),
        pltpu.SMEM(adapter_slot.shape, i32),
        pltpu.SMEM(token_count.shape, i32),
    ]
    dma = pltpu.SemaphoreType.DMA

    own, *sent = pl.pallas_call(
        functools.partial(pack_kernel, n),
        out_shape=[message] * count,
        in_specs=[HBM] * 4,
        out_specs=[VMEM] * count,
        scratch_shapes=tables[1:3]
        + [pltpu.VMEM(down_maps.shape, bf16), pltpu.VMEM(up_maps.shape, bf16), dma((4,))],
        compiler_params=params(8),
    )(*in_hbm(chosen, adapter_slot, down_maps, up_maps))
    sent, x_late = lax.optimization_barrier((sent, inputs))
    x_other = lax.ppermute(x_late, "tensor", [(0, 1), (1, 0)])
    x_mine, kept = pl.pallas_call(
        functools.partial(stage_kernel, n, picked),
        out_shape=[shape(inputs.shape, bf16), shape((2 * tok_rows, out_width), bf16)],
        in_specs=[HBM] * 7,
        out_specs=[VMEM] * 2,
        scratch_shapes=tables + [dma((6,))],
        compiler_params=params(8),
        cost_estimate=pl.CostEstimate(flops=0, bytes_accessed=1 << 21, transcendentals=0),
    )(*in_hbm(starts, chosen, adapter_slot, token_count, output_gradient, inputs, frozen_weight))
    got, x_mine = exchange(sent, (0,), x_mine)
    low = shape((tok_rows, picked), f32)
    maps = pltpu.VMEM((n, ADAPTER_RANK, out_width), bf16)
    got = [own] + got
    x, low, dlow = pl.pallas_call(
        functools.partial(early_kernel, n, picked),
        out_shape=[shape((tok_rows, model_width), bf16), low, low],
        in_specs=[VMEM] * (3 + count),
        out_specs=[VMEM] * 3,
        scratch_shapes=[maps],
        compiler_params=params(8),
        cost_estimate=pl.CostEstimate(flops=0, bytes_accessed=1 << 21, transcendentals=0),
    )(kept, x_mine, x_other, *got[:count])

    dlow, *sent = pl.pallas_call(
        functools.partial(middle_kernel, n),
        out_shape=[shape((tok_rows, picked), bf16)] + [message] * count,
        in_specs=[VMEM] * (4 + n - count),
        out_specs=[VMEM] * (1 + count),
        scratch_shapes=[maps, maps],
        compiler_params=params(8),
    )(kept, x, low, dlow, *got[count:])
    own, *sent = sent

    grad_x = pl.pallas_call(
        functools.partial(grad_x_kernel, n),
        out_shape=shape((tok_rows, half), bf16),
        in_specs=[VMEM] * (3 + n),
        out_specs=HBM,
        scratch_shapes=[
            pltpu.VMEM((n, picked, column_total), bf16),
            pltpu.VMEM((tok_rows, half), bf16),
            dma((n // 2,)),
        ],
        compiler_params=params(8),
        cost_estimate=pl.CostEstimate(
            flops=2 * tok_rows * half * (out_width + picked),
            bytes_accessed=2 * half * (out_width + tok_rows),
            transcendentals=0,
        ),
    )(kept, frozen_weight, dlow, *got)

    got, grad_x = exchange(sent, (0,), grad_x)

    grad_a, up_map_gradient = pl.pallas_call(
        functools.partial(final_kernel, n),
        out_shape=[shape((column_total, slot_width), f32), shape((ADAPTER_RANK, piece), f32)],
        in_specs=[VMEM] * (1 + n),
        out_specs=[VMEM, VMEM],
        compiler_params=params(8),
    )(kept, own, *got)
    return grad_x, grad_a, up_map_gradient


def local_plain(
    inputs,
    output_gradient,
    frozen_weight,
    down_maps,
    up_maps,
    segment_start,
    segment_adapter,
    adapter_slot,
    token_count,
):
    tok_rows, out_width = output_gradient.shape
    column_total = down_maps.shape[0]
    adapter_list = adapter_slot.shape[0]
    segs = segment_start.shape[1]
    dp_size = lax.axis_size("dp")
    my_rank = lax.axis_index("dp")
    core_idx = lax.axis_index("tensor")
    picked = segs * ADAPTER_RANK
    piece_out = out_width // lax.axis_size("tensor")
    half = frozen_weight.shape[0]

    x_other = lax.ppermute(inputs, "tensor", [(0, 1), (1, 0)])
    adapter_ids = jnp.arange(adapter_list, dtype=i32)
    slot_table = jnp.sum(
        jnp.where(segment_adapter[..., None] == adapter_ids, adapter_slot, 0), axis=-1
    )
    column = slot_table[:, :, None] * ADAPTER_RANK + jnp.arange(ADAPTER_RANK, dtype=i32)
    onehot = (
        column.reshape(-1)[:, None] == jnp.arange(adapter_list * ADAPTER_RANK, dtype=i32)
    ).astype(bf16)

    a_send = dot(onehot, down_maps, 1, 1).astype(bf16).reshape(dp_size, picked, column_total)
    b_send = jnp.broadcast_to(up_maps[None], (dp_size,) + up_maps.shape)
    a_got = lax.all_to_all(a_send, "dp", 0, 0, tiled=True)
    b_got = lax.all_to_all(b_send, "dp", 0, 0, tiled=True)

    position = jnp.arange(tok_rows, dtype=i32)
    starts = lax.dynamic_index_in_dim(segment_start, my_rank, 0, keepdims=False)
    live = position < lax.dynamic_index_in_dim(token_count, my_rank, 0, keepdims=False)
    my_seg = jnp.sum((starts[None, :] <= position[:, None]).astype(i32), axis=1) - 1
    in_seg = my_seg[:, None] == (jnp.arange(picked, dtype=i32) // ADAPTER_RANK)[None, :]
    my_onehot = lax.dynamic_slice_in_dim(onehot, my_rank * picked, picked, 0)
    g = jnp.where(live[:, None], output_gradient, jnp.zeros_like(output_gradient))
    base = dot(g, frozen_weight, 1, 1)

    b_sel = dot(my_onehot, b_got.reshape(-1, out_width), 1, 0).astype(bf16)
    dlow = (adapter_scale * dot(g, b_sel, 1, 1)).astype(bf16)
    dlow = jnp.where(in_seg, dlow, jnp.zeros_like(dlow))
    a_sel = jnp.moveaxis(a_got, 0, 1).reshape(picked, -1)
    first = core_idx == 0
    x = jnp.concatenate(
        [jnp.where(first, inputs, x_other), jnp.where(first, x_other, inputs)], axis=0
    )
    low = dot(x, a_sel, 1, 1).astype(bf16)
    low = jnp.where(in_seg, low, jnp.zeros_like(low))
    low_wide = dot(low, my_onehot, 1, 0).astype(bf16)

    ga_send = dot(dlow, x, 0, 0).astype(bf16).reshape(picked, dp_size, column_total)
    ga_got = lax.all_to_all(jnp.moveaxis(ga_send, 1, 0), "dp", 0, 0, tiled=True)
    g_piece = lax.dynamic_slice_in_dim(g, core_idx * piece_out, piece_out, 1)
    up_send = (adapter_scale * dot(low_wide, g_piece, 0, 0)).astype(bf16)
    up_got = lax.all_to_all(up_send.reshape(dp_size, -1, piece_out), "dp", 0, 0, tiled=True)

    a_half = lax.dynamic_slice_in_dim(a_sel, core_idx * half, half, 1)
    grad_x = (base + dot(dlow, a_half, 1, 0)).astype(bf16)
    grad_a = dot(ga_got.reshape(dp_size * picked, column_total), onehot, 0, 0)
    up_map_gradient = jnp.sum(up_got.astype(f32), axis=0)
    return grad_x, grad_a, up_map_gradient


def local(*args):
    down_maps, up_maps = args[3], args[4]
    n, tp = lax.axis_size("dp"), lax.axis_size("tensor")
    out_width = up_maps.shape[1]
    kernels_fit = (
        n == 8
        and tp == 2
        and down_maps.shape[0] == out_width
        and down_maps.shape[1] == n * up_maps.shape[0]
        and out_width % (128 * tp) == 0
        and out_width == 4 * down_maps.shape[1]
        and args[1].shape[0] == 2 * args[0].shape[0] == down_maps.shape[1]
        and args[5].shape[1] * ADAPTER_RANK * n == 2 * down_maps.shape[1]
    )
    return (local_kernels if kernels_fit else local_plain)(*args)


def solution(mesh):
    in_specs = (
        P(("groups", "dp", "tensor"), None),
        P(("groups", "dp"), None),
        P("tensor", None),
        P(("groups", "dp"), None),
        P(("groups", "dp"), None),
        P("groups", None),
        P("groups", None),
        P("groups"),
        P("groups"),
    )
    out_specs = (
        P(("groups", "dp"), "tensor"),
        P(("groups", "dp"), None),
        P(("groups", "dp"), "tensor"),
    )
    return jax.shard_map(local, mesh=mesh, in_specs=in_specs, out_specs=out_specs, check_vma=False)
```

```python
import functools

import jax
import jax.numpy as jnp
from jax import lax
from jax.experimental import pallas as pl
from jax.experimental.pallas import tpu as pltpu
from jax.sharding import PartitionSpec as P

ADAPTER_RANK = 16
adapter_scale = 2.0

bf16, f32, i32 = jnp.bfloat16, jnp.float32, jnp.int32

HBM = pl.BlockSpec(memory_space=pltpu.HBM)
VMEM = pl.BlockSpec(memory_space=pltpu.VMEM)


def dot(a, b, ca, cb):
    return lax.dot_general(a, b, (((ca,), (cb,)), ((), ())), preferred_element_type=f32)


def params(mib):
    return pltpu.CompilerParams(vmem_limit_bytes=mib << 20)


def slot_rows(chosen_ref, slot_ref, ranks, width):
    lane = lax.broadcasted_iota(i32, (ADAPTER_RANK, width), 1)
    row = lax.broadcasted_iota(i32, (ADAPTER_RANK, width), 0)
    rows = []
    for rank in ranks:
        for k in range(chosen_ref.shape[0]):
            first = slot_ref[chosen_ref[k, rank]] * ADAPTER_RANK
            rows.append(jnp.where(lane == row + first, 1.0, 0.0))
    return jnp.concatenate(rows, axis=0).astype(bf16)


def start_all(sources, targets, sems, first=0):
    copies = [
        pltpu.make_async_copy(source, target, sems.at[first + k])
        for k, (source, target) in enumerate(zip(sources, targets))
    ]
    for copy in copies:
        copy.start()
    return copies


def wait_all(copies):
    for copy in copies:
        copy.wait()


def steps(n):
    return [(n - 1, n // 2 + 1), (2, n - 2), (3, n // 2), (1, 1)]


def partners(n, me, core):
    return [me] + [me ^ jnp.where(core == 0, a, b) for a, b in steps(n)]


def senders(n, me, core):
    passed = [me ^ jnp.where(core == 0, b, a) for a, b in steps(n) if a != b]
    return partners(n, me, core) + passed


def in_hbm(*arrays):
    return [pltpu.with_memory_space_constraint(array, pltpu.HBM) for array in arrays]


def pack_kernel(n, chosen_hbm, slot_hbm, down_hbm, up_hbm, *refs):
    count = n // 2 + 1
    send, (chosen_ref, slot_ref, down_ref, up_ref, sems) = refs[:count], refs[count:]
    tables = start_all([chosen_hbm, slot_hbm], [chosen_ref, slot_ref], sems)
    maps = start_all([down_hbm, up_hbm], [down_ref, up_ref], sems, 2)
    ranks = partners(n, lax.axis_index("dp"), lax.axis_index("tensor"))
    wait_all(tables)
    onehot = slot_rows(chosen_ref, slot_ref, ranks, down_ref.shape[1])
    picked = onehot.shape[0] // count
    wait_all(maps)
    columns = dot(onehot, down_ref[...], 1, 1).astype(bf16)
    for k in range(count):
        send[k][:picked, :] = columns[k * picked : (k + 1) * picked]
        send[k][picked:, :] = up_ref[...]


def stage_kernel(
    n, picked, start_hbm, chosen_hbm, slot_hbm, count_hbm, g_hbm, x_hbm, w_hbm,
    x_ref, kept_ref, start_ref, chosen_ref, slot_ref, count_ref, sems,
):
    rows, width = g_hbm.shape
    slots = width // 4
    me = lax.axis_index("dp")
    tables = start_all(
        [chosen_hbm, slot_hbm, start_hbm, count_hbm], [chosen_ref, slot_ref, start_ref, count_ref], sems
    )
    gradient = start_all([g_hbm], [kept_ref.at[pl.ds(0, rows)]], sems, 4)
    tokens = start_all([x_hbm], [x_ref], sems, 5)
    wait_all(tables)
    position = lax.broadcasted_iota(i32, (rows, slots), 0)
    group = lax.broadcasted_iota(i32, (rows, slots), 1) // ADAPTER_RANK
    segment = jnp.full((rows, slots), -1, i32)
    for k in range(start_ref.shape[0]):
        segment += jnp.where(position >= start_ref[k, me], 1, 0)
    kept_ref[rows:, :slots] = jnp.where(segment == group, 1.0, 0.0).astype(bf16)
    kept_ref[rows : rows + picked, slots : 2 * slots] = slot_rows(chosen_ref, slot_ref, [me], slots)
    every = slot_rows(chosen_ref, slot_ref, range(n), slots)
    kept_ref[rows:, 2 * slots : 3 * slots] = every[:rows]
    kept_ref[rows:, 3 * slots :] = every[rows:]
    wait_all(gradient)
    live = lax.broadcasted_iota(i32, (rows, width), 0) < count_ref[me]
    g = kept_ref[:rows, :]
    kept_ref[:rows, :] = jnp.where(live, g, jnp.zeros_like(g))
    wait_all(tokens)


def picked_maps(kept_ref, b_ref, picked, ranks, messages):
    rows, slots = kept_ref.shape[0] // 2, kept_ref.shape[1] // 4
    b_ref[...] = jnp.zeros(b_ref.shape, bf16)
    for rank, message in zip(ranks, messages):
        b_ref[rank] = message[picked:, :]
    onehot = kept_ref[rows : rows + picked, slots : 2 * slots]
    return dot(onehot, b_ref[...].reshape(-1, b_ref.shape[2]), 1, 0).astype(bf16)


def low_terms(x_ref, picked, ranks, messages):
    total = jnp.zeros((x_ref.shape[0], picked), f32)
    for rank, message in zip(ranks, messages):
        width = message.shape[1]
        at = pl.ds(pl.multiple_of(rank * width, width), width)
        total += dot(x_ref[:, at], message[:picked, :], 1, 1)
    return total


def early_kernel(n, picked, kept_ref, x_mine, x_other, *refs):
    count = n // 2 + 1
    here, (x_ref, low_ref, dlow_ref, b_ref) = refs[:count], refs[count:]
    me, core, half = lax.axis_index("dp"), lax.axis_index("tensor"), x_mine.shape[0]
    ranks = senders(n, me, core)[:count]
    x_ref[pl.ds(pl.multiple_of(core * half, half), half), :] = x_mine[...]
    x_ref[pl.ds(pl.multiple_of((1 - core) * half, half), half), :] = x_other[...]
    b_sel = picked_maps(kept_ref, b_ref, picked, ranks, here)
    dlow_ref[...] = dot(kept_ref[: 2 * half, :], b_sel, 1, 1)
    low_ref[...] = low_terms(x_ref, picked, ranks, here)


def middle_kernel(n, kept_ref, x_ref, low_ref, dlow_part, *refs):
    count = n // 2 + 1
    got, dlow_ref, send = refs[: n - count], refs[n - count], refs[n - count + 1 : n + 1]
    b_ref, up_ref = refs[n + 1 :]
    me, core = lax.axis_index("dp"), lax.axis_index("tensor")
    rows, picked = dlow_ref.shape
    width = kept_ref.shape[1]
    slots = width // 4
    ranks = senders(n, me, core)[count:]
    in_seg = kept_ref[rows:, :picked].astype(f32) > 0.0
    g = kept_ref[:rows, :]
    onehot = kept_ref[rows : rows + picked, slots : 2 * slots]
    b_sel = picked_maps(kept_ref, b_ref, picked, ranks, got)
    dlow = dlow_part[...] + dot(g, b_sel, 1, 1)
    dlow = jnp.where(in_seg, adapter_scale * dlow, 0.0).astype(bf16)
    dlow_ref[...] = dlow
    targets = partners(n, me, core)
    for target, message in zip(targets, send):
        at = pl.ds(pl.multiple_of(target * width, width), width)
        message[:picked, :] = dot(dlow, x_ref[:, at], 0, 0).astype(bf16)

    low = low_ref[...] + low_terms(x_ref, picked, ranks, got)
    low = jnp.where(in_seg, low, 0.0).astype(bf16)
    low_wide = dot(low, onehot, 1, 0).astype(bf16)
    up = (adapter_scale * dot(low_wide, g, 0, 0)).astype(bf16)
    up_ref[...] = up.reshape(up_ref.shape)
    for target, message in zip(targets, send):
        message[picked:, :] = up_ref[target]


def grad_x_kernel(n, kept_ref, w_ref, dlow_ref, *refs):
    got, (out_hbm, a_ref, out_ref, sems) = refs[:n], refs[n:]
    me, core = lax.axis_index("dp"), lax.axis_index("tensor")
    picked, width = a_ref.shape[1:]
    for sender, message in zip(senders(n, me, core), got):
        a_ref[sender] = message[:picked, :]
    g = kept_ref[: out_ref.shape[0], :]
    done = []
    for j in range(n // 2):
        at = pl.ds(j * width, width)
        total = dot(g, w_ref[at, :], 1, 1) + dot(dlow_ref[...], a_ref[core * (n // 2) + j], 1, 0)
        out_ref[:, at] = total.astype(bf16)
        done += start_all([out_ref.at[:, at]], [out_hbm.at[:, at]], sems, j)
    wait_all(done)


def final_kernel(n, kept_ref, *refs):
    got, (a_ref, up_ref, rows_ref) = refs[:n], refs[n:]
    me, core = lax.axis_index("dp"), lax.axis_index("tensor")
    piece, picked = up_ref.shape[1], rows_ref.shape[1] - ADAPTER_RANK
    half, slots = kept_ref.shape[0] // 2, kept_ref.shape[1] // 4
    for sender, message in zip(senders(n, me, core), got):
        rows_ref[sender] = message[...]
    rows = rows_ref[:, :picked, :].reshape(n * picked, rows_ref.shape[2])
    onehot = jnp.concatenate(
        [kept_ref[half:, 2 * slots : 3 * slots], kept_ref[half:, 3 * slots :]], axis=0
    )
    a_ref[...] = dot(rows, onehot, 0, 0)
    at = pl.ds(pl.multiple_of(core * piece, piece), piece)
    up_ref[...] = jnp.sum(rows_ref[:, picked:, at].astype(f32), axis=0)


def exchange(messages, tied, beside):
    n = 2 * len(messages)
    got = [
        lax.ppermute(
            message,
            ("dp", "tensor"),
            [(2 * i + c, 2 * (i ^ step[c]) + c) for i in range(n) for c in range(2)],
        )
        for message, step in zip(messages, steps(n))
    ]
    for k in tied:
        got[k], beside = lax.optimization_barrier((got[k], beside))
    passed = [
        lax.ppermute(message, "tensor", [(0, 1), (1, 0)])
        for message, (a, b) in zip(got, steps(n))
        if a != b
    ]
    return got + passed, beside


def local_kernels(
    inputs,
    output_gradient,
    frozen_weight,
    down_maps,
    up_maps,
    segment_start,
    segment_adapter,
    adapter_slot,
    token_count,
):
    model_width = inputs.shape[1]
    tok_rows, out_width = output_gradient.shape
    column_total, slot_width = down_maps.shape
    half = frozen_weight.shape[0]
    n = lax.axis_size("dp")
    piece = out_width // lax.axis_size("tensor")
    segs = segment_start.shape[1]
    picked = segs * ADAPTER_RANK
    shape = jax.ShapeDtypeStruct
    message = shape((picked + ADAPTER_RANK, column_total), bf16)
    count = n // 2 + 1
    starts, chosen = segment_start.T, segment_adapter.T

    tables = [
        pltpu.SMEM(starts.shape, i32),
        pltpu.SMEM(chosen.shape, i32),
        pltpu.SMEM(adapter_slot.shape, i32),
        pltpu.SMEM(token_count.shape, i32),
    ]
    dma = pltpu.SemaphoreType.DMA

    own, *sent = pl.pallas_call(
        functools.partial(pack_kernel, n),
        out_shape=[message] * count,
        in_specs=[HBM] * 4,
        out_specs=[VMEM] * count,
        scratch_shapes=tables[1:3]
        + [pltpu.VMEM(down_maps.shape, bf16), pltpu.VMEM(up_maps.shape, bf16), dma((4,))],
        compiler_params=params(8),
    )(*in_hbm(chosen, adapter_slot, down_maps, up_maps))
    sent, x_late = lax.optimization_barrier((sent, inputs))
    x_other = lax.ppermute(x_late, "tensor", [(0, 1), (1, 0)])
    x_mine, kept = pl.pallas_call(
        functools.partial(stage_kernel, n, picked),
        out_shape=[shape(inputs.shape, bf16), shape((2 * tok_rows, out_width), bf16)],
        in_specs=[HBM] * 7,
        out_specs=[VMEM] * 2,
        scratch_shapes=tables + [dma((6,))],
        compiler_params=params(8),
        cost_estimate=pl.CostEstimate(flops=0, bytes_accessed=1 << 21, transcendentals=0),
    )(*in_hbm(starts, chosen, adapter_slot, token_count, output_gradient, inputs, frozen_weight))
    got, x_mine = exchange(sent, (0,), x_mine)
    low = shape((tok_rows, picked), f32)
    maps = pltpu.VMEM((n, ADAPTER_RANK, out_width), bf16)
    got = [own] + got
    x, low, dlow = pl.pallas_call(
        functools.partial(early_kernel, n, picked),
        out_shape=[shape((tok_rows, model_width), bf16), low, low],
        in_specs=[VMEM] * (3 + count),
        out_specs=[VMEM] * 3,
        scratch_shapes=[maps],
        compiler_params=params(8),
        cost_estimate=pl.CostEstimate(flops=0, bytes_accessed=1 << 21, transcendentals=0),
    )(kept, x_mine, x_other, *got[:count])

    dlow, *sent = pl.pallas_call(
        functools.partial(middle_kernel, n),
        out_shape=[shape((tok_rows, picked), bf16)] + [message] * count,
        in_specs=[VMEM] * (4 + n - count),
        out_specs=[VMEM] * (1 + count),
        scratch_shapes=[maps, maps],
        compiler_params=params(8),
    )(kept, x, low, dlow, *got[count:])
    own, *sent = sent

    grad_x = pl.pallas_call(
        functools.partial(grad_x_kernel, n),
        out_shape=shape((tok_rows, half), bf16),
        in_specs=[VMEM] * (3 + n),
        out_specs=HBM,
        scratch_shapes=[
            pltpu.VMEM((n, picked, column_total), bf16),
            pltpu.VMEM((tok_rows, half), bf16),
            dma((n // 2,)),
        ],
        compiler_params=params(8),
        cost_estimate=pl.CostEstimate(
            flops=2 * tok_rows * half * (out_width + picked),
            bytes_accessed=2 * half * (out_width + tok_rows),
            transcendentals=0,
        ),
    )(kept, frozen_weight, dlow, *got)

    got, grad_x = exchange(sent, (0,), grad_x)

    grad_a, up_map_gradient = pl.pallas_call(
        functools.partial(final_kernel, n),
        out_shape=[shape((column_total, slot_width), f32), shape((ADAPTER_RANK, piece), f32)],
        in_specs=[VMEM] * (1 + n),
        out_specs=[VMEM, VMEM],
        scratch_shapes=[pltpu.VMEM((n,) + message.shape, bf16)],
        compiler_params=params(8),
    )(kept, own, *got)
    return grad_x, grad_a, up_map_gradient


def local_plain(
    inputs,
    output_gradient,
    frozen_weight,
    down_maps,
    up_maps,
    segment_start,
    segment_adapter,
    adapter_slot,
    token_count,
):
    tok_rows, out_width = output_gradient.shape
    column_total = down_maps.shape[0]
    adapter_list = adapter_slot.shape[0]
    segs = segment_start.shape[1]
    dp_size = lax.axis_size("dp")
    my_rank = lax.axis_index("dp")
    core_idx = lax.axis_index("tensor")
    picked = segs * ADAPTER_RANK
    piece_out = out_width // lax.axis_size("tensor")
    half = frozen_weight.shape[0]

    x_other = lax.ppermute(inputs, "tensor", [(0, 1), (1, 0)])
    adapter_ids = jnp.arange(adapter_list, dtype=i32)
    slot_table = jnp.sum(
        jnp.where(segment_adapter[..., None] == adapter_ids, adapter_slot, 0), axis=-1
    )
    column = slot_table[:, :, None] * ADAPTER_RANK + jnp.arange(ADAPTER_RANK, dtype=i32)
    onehot = (
        column.reshape(-1)[:, None] == jnp.arange(adapter_list * ADAPTER_RANK, dtype=i32)
    ).astype(bf16)

    a_send = dot(onehot, down_maps, 1, 1).astype(bf16).reshape(dp_size, picked, column_total)
    b_send = jnp.broadcast_to(up_maps[None], (dp_size,) + up_maps.shape)
    a_got = lax.all_to_all(a_send, "dp", 0, 0, tiled=True)
    b_got = lax.all_to_all(b_send, "dp", 0, 0, tiled=True)

    position = jnp.arange(tok_rows, dtype=i32)
    starts = lax.dynamic_index_in_dim(segment_start, my_rank, 0, keepdims=False)
    live = position < lax.dynamic_index_in_dim(token_count, my_rank, 0, keepdims=False)
    my_seg = jnp.sum((starts[None, :] <= position[:, None]).astype(i32), axis=1) - 1
    in_seg = my_seg[:, None] == (jnp.arange(picked, dtype=i32) // ADAPTER_RANK)[None, :]
    my_onehot = lax.dynamic_slice_in_dim(onehot, my_rank * picked, picked, 0)
    g = jnp.where(live[:, None], output_gradient, jnp.zeros_like(output_gradient))
    base = dot(g, frozen_weight, 1, 1)

    b_sel = dot(my_onehot, b_got.reshape(-1, out_width), 1, 0).astype(bf16)
    dlow = (adapter_scale * dot(g, b_sel, 1, 1)).astype(bf16)
    dlow = jnp.where(in_seg, dlow, jnp.zeros_like(dlow))
    a_sel = jnp.moveaxis(a_got, 0, 1).reshape(picked, -1)
    first = core_idx == 0
    x = jnp.concatenate(
        [jnp.where(first, inputs, x_other), jnp.where(first, x_other, inputs)], axis=0
    )
    low = dot(x, a_sel, 1, 1).astype(bf16)
    low = jnp.where(in_seg, low, jnp.zeros_like(low))
    low_wide = dot(low, my_onehot, 1, 0).astype(bf16)

    ga_send = dot(dlow, x, 0, 0).astype(bf16).reshape(picked, dp_size, column_total)
    ga_got = lax.all_to_all(jnp.moveaxis(ga_send, 1, 0), "dp", 0, 0, tiled=True)
    g_piece = lax.dynamic_slice_in_dim(g, core_idx * piece_out, piece_out, 1)
    up_send = (adapter_scale * dot(low_wide, g_piece, 0, 0)).astype(bf16)
    up_got = lax.all_to_all(up_send.reshape(dp_size, -1, piece_out), "dp", 0, 0, tiled=True)

    a_half = lax.dynamic_slice_in_dim(a_sel, core_idx * half, half, 1)
    grad_x = (base + dot(dlow, a_half, 1, 0)).astype(bf16)
    grad_a = dot(ga_got.reshape(dp_size * picked, column_total), onehot, 0, 0)
    up_map_gradient = jnp.sum(up_got.astype(f32), axis=0)
    return grad_x, grad_a, up_map_gradient


def local(*args):
    down_maps, up_maps = args[3], args[4]
    n, tp = lax.axis_size("dp"), lax.axis_size("tensor")
    out_width = up_maps.shape[1]
    kernels_fit = (
        n == 8
        and tp == 2
        and down_maps.shape[0] == out_width
        and down_maps.shape[1] == n * up_maps.shape[0]
        and out_width % (128 * tp) == 0
        and out_width == 4 * down_maps.shape[1]
        and args[1].shape[0] == 2 * args[0].shape[0] == down_maps.shape[1]
        and args[5].shape[1] * ADAPTER_RANK * n == 2 * down_maps.shape[1]
    )
    return (local_kernels if kernels_fit else local_plain)(*args)


def solution(mesh):
    in_specs = (
        P(("groups", "dp", "tensor"), None),
        P(("groups", "dp"), None),
        P("tensor", None),
        P(("groups", "dp"), None),
        P(("groups", "dp"), None),
        P("groups", None),
        P("groups", None),
        P("groups"),
        P("groups"),
    )
    out_specs = (
        P(("groups", "dp"), "tensor"),
        P(("groups", "dp"), None),
        P(("groups", "dp"), "tensor"),
    )
    return jax.shard_map(local, mesh=mesh, in_specs=in_specs, out_specs=out_specs, check_vma=False)
```

```python
import functools

import jax
import jax.numpy as jnp
from jax import lax
from jax.experimental import pallas as pl
from jax.experimental.pallas import tpu as pltpu
from jax.sharding import PartitionSpec as P

ADAPTER_RANK = 16
adapter_scale = 2.0

bf16, f32, i32 = jnp.bfloat16, jnp.float32, jnp.int32

HBM = pl.BlockSpec(memory_space=pltpu.HBM)
VMEM = pl.BlockSpec(memory_space=pltpu.VMEM)


def dot(a, b, ca, cb):
    return lax.dot_general(a, b, (((ca,), (cb,)), ((), ())), preferred_element_type=f32)


def params(mib):
    return pltpu.CompilerParams(vmem_limit_bytes=mib << 20)


def slot_rows(chosen_ref, slot_ref, ranks, width):
    lane = lax.broadcasted_iota(i32, (ADAPTER_RANK, width), 1)
    row = lax.broadcasted_iota(i32, (ADAPTER_RANK, width), 0)
    rows = []
    for rank in ranks:
        for k in range(chosen_ref.shape[0]):
            first = slot_ref[chosen_ref[k, rank]] * ADAPTER_RANK
            rows.append(jnp.where(lane == row + first, 1.0, 0.0))
    return jnp.concatenate(rows, axis=0).astype(bf16)


def start_all(sources, targets, sems, first=0):
    copies = [
        pltpu.make_async_copy(source, target, sems.at[first + k])
        for k, (source, target) in enumerate(zip(sources, targets))
    ]
    for copy in copies:
        copy.start()
    return copies


def wait_all(copies):
    for copy in copies:
        copy.wait()


def steps(n):
    return [(n - 1, n // 2 + 1), (3, n - 2), (2, n // 2), (1, 1)]


def partners(n, me, core):
    return [me] + [me ^ jnp.where(core == 0, a, b) for a, b in steps(n)]


def senders(n, me, core):
    passed = [me ^ jnp.where(core == 0, b, a) for a, b in steps(n) if a != b]
    return partners(n, me, core) + passed


def in_hbm(*arrays):
    return [pltpu.with_memory_space_constraint(array, pltpu.HBM) for array in arrays]


def pack_kernel(n, chosen_hbm, slot_hbm, down_hbm, up_hbm, *refs):
    count = n // 2 + 1
    send, (chosen_ref, slot_ref, down_ref, up_ref, sems) = refs[:count], refs[count:]
    tables = start_all([chosen_hbm, slot_hbm], [chosen_ref, slot_ref], sems)
    maps = start_all([down_hbm, up_hbm], [down_ref, up_ref], sems, 2)
    ranks = partners(n, lax.axis_index("dp"), lax.axis_index("tensor"))
    wait_all(tables)
    onehot = slot_rows(chosen_ref, slot_ref, ranks, down_ref.shape[1])
    picked = onehot.shape[0] // count
    wait_all(maps)
    columns = dot(onehot, down_ref[...], 1, 1).astype(bf16)
    for k in range(count):
        send[k][:picked, :] = columns[k * picked : (k + 1) * picked]
        send[k][picked:, :] = up_ref[...]


def stage_kernel(
    n, picked, start_hbm, chosen_hbm, slot_hbm, count_hbm, g_hbm, x_hbm, w_hbm,
    x_ref, kept_ref, start_ref, chosen_ref, slot_ref, count_ref, sems,
):
    rows, width = g_hbm.shape
    slots = width // 4
    me = lax.axis_index("dp")
    tables = start_all(
        [chosen_hbm, slot_hbm, start_hbm, count_hbm], [chosen_ref, slot_ref, start_ref, count_ref], sems
    )
    gradient = start_all([g_hbm], [kept_ref.at[pl.ds(0, rows)]], sems, 4)
    tokens = start_all([x_hbm], [x_ref], sems, 5)
    wait_all(tables)
    position = lax.broadcasted_iota(i32, (rows, slots), 0)
    group = lax.broadcasted_iota(i32, (rows, slots), 1) // ADAPTER_RANK
    segment = jnp.full((rows, slots), -1, i32)
    for k in range(start_ref.shape[0]):
        segment += jnp.where(position >= start_ref[k, me], 1, 0)
    kept_ref[rows:, :slots] = jnp.where(segment == group, 1.0, 0.0).astype(bf16)
    kept_ref[rows : rows + picked, slots : 2 * slots] = slot_rows(chosen_ref, slot_ref, [me], slots)
    every = slot_rows(chosen_ref, slot_ref, range(n), slots)
    kept_ref[rows:, 2 * slots : 3 * slots] = every[:rows]
    kept_ref[rows:, 3 * slots :] = every[rows:]
    wait_all(gradient)
    live = lax.broadcasted_iota(i32, (rows, width), 0) < count_ref[me]
    g = kept_ref[:rows, :]
    kept_ref[:rows, :] = jnp.where(live, g, jnp.zeros_like(g))
    wait_all(tokens)


def picked_maps(kept_ref, b_ref, picked, ranks, messages):
    rows, slots = kept_ref.shape[0] // 2, kept_ref.shape[1] // 4
    b_ref[...] = jnp.zeros(b_ref.shape, bf16)
    for rank, message in zip(ranks, messages):
        b_ref[rank] = message[picked:, :]
    onehot = kept_ref[rows : rows + picked, slots : 2 * slots]
    return dot(onehot, b_ref[...].reshape(-1, b_ref.shape[2]), 1, 0).astype(bf16)


def low_terms(x_ref, picked, ranks, messages):
    total = jnp.zeros((x_ref.shape[0], picked), f32)
    for rank, message in zip(ranks, messages):
        width = message.shape[1]
        at = pl.ds(pl.multiple_of(rank * width, width), width)
        total += dot(x_ref[:, at], message[:picked, :], 1, 1)
    return total


def early_kernel(n, picked, kept_ref, x_mine, x_other, *refs):
    count = n // 2 + 1
    here, (x_ref, low_ref, dlow_ref, b_ref) = refs[:count], refs[count:]
    me, core, half = lax.axis_index("dp"), lax.axis_index("tensor"), x_mine.shape[0]
    ranks = senders(n, me, core)[:count]
    x_ref[pl.ds(pl.multiple_of(core * half, half), half), :] = x_mine[...]
    x_ref[pl.ds(pl.multiple_of((1 - core) * half, half), half), :] = x_other[...]
    b_sel = picked_maps(kept_ref, b_ref, picked, ranks, here)
    dlow_ref[...] = dot(kept_ref[: 2 * half, :], b_sel, 1, 1)
    low_ref[...] = low_terms(x_ref, picked, ranks, here)


def middle_kernel(n, kept_ref, x_ref, low_ref, dlow_part, *refs):
    count = n // 2 + 1
    got, (dlow_ref, own_ref), send = refs[: n - count], refs[n - count :][:2], refs[n - count + 2 : n + 1]
    b_ref, up_ref = refs[n + 1 :]
    me, core = lax.axis_index("dp"), lax.axis_index("tensor")
    rows, picked = dlow_ref.shape
    width = kept_ref.shape[1]
    slots = width // 4
    ranks = senders(n, me, core)[count:]
    in_seg = kept_ref[rows:, :picked].astype(f32) > 0.0
    g = kept_ref[:rows, :]
    onehot = kept_ref[rows : rows + picked, slots : 2 * slots]
    b_sel = picked_maps(kept_ref, b_ref, picked, ranks, got)
    dlow = dlow_part[...] + dot(g, b_sel, 1, 1)
    dlow = jnp.where(in_seg, adapter_scale * dlow, 0.0).astype(bf16)
    dlow_ref[...] = dlow
    targets = partners(n, me, core)[1:]
    for target, message in zip(targets, send):
        at = pl.ds(pl.multiple_of(target * width, width), width)
        message[:picked, :] = dot(dlow, x_ref[:, at], 0, 0).astype(bf16)

    low = low_ref[...] + low_terms(x_ref, picked, ranks, got)
    low = jnp.where(in_seg, low, 0.0).astype(bf16)
    low_wide = dot(low, onehot, 1, 0).astype(bf16)
    up = (adapter_scale * dot(low_wide, g, 0, 0)).astype(bf16)
    up_ref[...] = up.reshape(up_ref.shape)
    own_ref[...] = up_ref[me]
    for target, message in zip(targets, send):
        message[picked:, :] = up_ref[target]


def grad_x_kernel(n, kept_ref, w_ref, x_ref, up_ref, dlow_ref, *refs):
    got, (out_hbm, own_ref, a_ref, out_ref, sems) = refs[:n], refs[n:]
    me, core = lax.axis_index("dp"), lax.axis_index("tensor")
    picked, width = a_ref.shape[1:]
    for sender, message in zip(senders(n, me, core), got):
        a_ref[sender] = message[:picked, :]
    g = kept_ref[: out_ref.shape[0], :]
    done = []
    for j in range(n // 2):
        at = pl.ds(j * width, width)
        total = dot(g, w_ref[at, :], 1, 1) + dot(dlow_ref[...], a_ref[core * (n // 2) + j], 1, 0)
        out_ref[:, at] = total.astype(bf16)
        done += start_all([out_ref.at[:, at]], [out_hbm.at[:, at]], sems, j)
    at = pl.ds(pl.multiple_of(me * width, width), width)
    own_ref[:picked, :] = dot(dlow_ref[...], x_ref[:, at], 0, 0).astype(bf16)
    own_ref[picked:, :] = up_ref[...]
    wait_all(done)


def final_kernel(n, kept_ref, *refs):
    got, (a_ref, up_ref, rows_ref) = refs[:n], refs[n:]
    me, core = lax.axis_index("dp"), lax.axis_index("tensor")
    piece, picked = up_ref.shape[1], rows_ref.shape[1] - ADAPTER_RANK
    half, slots = kept_ref.shape[0] // 2, kept_ref.shape[1] // 4
    for sender, message in zip(senders(n, me, core), got):
        rows_ref[sender] = message[...]
    rows = rows_ref[:, :picked, :].reshape(n * picked, rows_ref.shape[2])
    onehot = jnp.concatenate(
        [kept_ref[half:, 2 * slots : 3 * slots], kept_ref[half:, 3 * slots :]], axis=0
    )
    a_ref[...] = dot(rows, onehot, 0, 0)
    at = pl.ds(pl.multiple_of(core * piece, piece), piece)
    up_ref[...] = jnp.sum(rows_ref[:, picked:, at].astype(f32), axis=0)


def exchange(messages, tied, beside):
    n = 2 * len(messages)
    got = [
        lax.ppermute(
            message,
            ("dp", "tensor"),
            [(2 * i + c, 2 * (i ^ step[c]) + c) for i in range(n) for c in range(2)],
        )
        for message, step in zip(messages, steps(n))
    ]
    for k in tied:
        got[k], beside = lax.optimization_barrier((got[k], beside))
    passed = [
        lax.ppermute(message, "tensor", [(0, 1), (1, 0)])
        for message, (a, b) in zip(got, steps(n))
        if a != b
    ]
    return got + passed, beside


def local_kernels(
    inputs,
    output_gradient,
    frozen_weight,
    down_maps,
    up_maps,
    segment_start,
    segment_adapter,
    adapter_slot,
    token_count,
):
    model_width = inputs.shape[1]
    tok_rows, out_width = output_gradient.shape
    column_total, slot_width = down_maps.shape
    half = frozen_weight.shape[0]
    n = lax.axis_size("dp")
    piece = out_width // lax.axis_size("tensor")
    segs = segment_start.shape[1]
    picked = segs * ADAPTER_RANK
    shape = jax.ShapeDtypeStruct
    message = shape((picked + ADAPTER_RANK, column_total), bf16)
    count = n // 2 + 1
    starts, chosen = segment_start.T, segment_adapter.T

    tables = [
        pltpu.SMEM(starts.shape, i32),
        pltpu.SMEM(chosen.shape, i32),
        pltpu.SMEM(adapter_slot.shape, i32),
        pltpu.SMEM(token_count.shape, i32),
    ]
    dma = pltpu.SemaphoreType.DMA

    own, *sent = pl.pallas_call(
        functools.partial(pack_kernel, n),
        out_shape=[message] * count,
        in_specs=[HBM] * 4,
        out_specs=[VMEM] * count,
        scratch_shapes=tables[1:3]
        + [pltpu.VMEM(down_maps.shape, bf16), pltpu.VMEM(up_maps.shape, bf16), dma((4,))],
        compiler_params=params(8),
    )(*in_hbm(chosen, adapter_slot, down_maps, up_maps))
    sent, x_late = lax.optimization_barrier((sent, inputs))
    x_other = lax.ppermute(x_late, "tensor", [(0, 1), (1, 0)])
    x_mine, kept = pl.pallas_call(
        functools.partial(stage_kernel, n, picked),
        out_shape=[shape(inputs.shape, bf16), shape((2 * tok_rows, out_width), bf16)],
        in_specs=[HBM] * 7,
        out_specs=[VMEM] * 2,
        scratch_shapes=tables + [dma((6,))],
        compiler_params=params(8),
        cost_estimate=pl.CostEstimate(flops=0, bytes_accessed=1 << 21, transcendentals=0),
    )(*in_hbm(starts, chosen, adapter_slot, token_count, output_gradient, inputs, frozen_weight))
    got, x_mine = exchange(sent, (0,), x_mine)
    low = shape((tok_rows, picked), f32)
    maps = pltpu.VMEM((n, ADAPTER_RANK, out_width), bf16)
    got = [own] + got
    x, low, dlow = pl.pallas_call(
        functools.partial(early_kernel, n, picked),
        out_shape=[shape((tok_rows, model_width), bf16), low, low],
        in_specs=[VMEM] * (3 + count),
        out_specs=[VMEM] * 3,
        scratch_shapes=[maps],
        compiler_params=params(8),
        cost_estimate=pl.CostEstimate(flops=0, bytes_accessed=1 << 21, transcendentals=0),
    )(kept, x_mine, x_other, *got[:count])

    dlow, own_up, *sent = pl.pallas_call(
        functools.partial(middle_kernel, n),
        out_shape=[shape((tok_rows, picked), bf16), shape((ADAPTER_RANK, out_width), bf16)]
        + [message] * (count - 1),
        in_specs=[VMEM] * (4 + n - count),
        out_specs=[VMEM] * (1 + count),
        scratch_shapes=[maps, maps],
        compiler_params=params(8),
    )(kept, x, low, dlow, *got[count:])

    grad_x, own = pl.pallas_call(
        functools.partial(grad_x_kernel, n),
        out_shape=[shape((tok_rows, half), bf16), message],
        in_specs=[VMEM] * (5 + n),
        out_specs=[HBM, VMEM],
        scratch_shapes=[
            pltpu.VMEM((n, picked, column_total), bf16),
            pltpu.VMEM((tok_rows, half), bf16),
            dma((n // 2,)),
        ],
        compiler_params=params(8),
        cost_estimate=pl.CostEstimate(
            flops=2 * tok_rows * half * (out_width + picked),
            bytes_accessed=2 * half * (out_width + tok_rows),
            transcendentals=0,
        ),
    )(kept, frozen_weight, x, own_up, dlow, *got)

    got, grad_x = exchange(sent, (0,), grad_x)

    grad_a, up_map_gradient = pl.pallas_call(
        functools.partial(final_kernel, n),
        out_shape=[shape((column_total, slot_width), f32), shape((ADAPTER_RANK, piece), f32)],
        in_specs=[VMEM] * (1 + n),
        out_specs=[VMEM, VMEM],
        scratch_shapes=[pltpu.VMEM((n,) + message.shape, bf16)],
        compiler_params=params(8),
    )(kept, own, *got)
    return grad_x, grad_a, up_map_gradient


def local_plain(
    inputs,
    output_gradient,
    frozen_weight,
    down_maps,
    up_maps,
    segment_start,
    segment_adapter,
    adapter_slot,
    token_count,
):
    tok_rows, out_width = output_gradient.shape
    column_total = down_maps.shape[0]
    adapter_list = adapter_slot.shape[0]
    segs = segment_start.shape[1]
    dp_size = lax.axis_size("dp")
    my_rank = lax.axis_index("dp")
    core_idx = lax.axis_index("tensor")
    picked = segs * ADAPTER_RANK
    piece_out = out_width // lax.axis_size("tensor")
    half = frozen_weight.shape[0]

    x_other = lax.ppermute(inputs, "tensor", [(0, 1), (1, 0)])
    adapter_ids = jnp.arange(adapter_list, dtype=i32)
    slot_table = jnp.sum(
        jnp.where(segment_adapter[..., None] == adapter_ids, adapter_slot, 0), axis=-1
    )
    column = slot_table[:, :, None] * ADAPTER_RANK + jnp.arange(ADAPTER_RANK, dtype=i32)
    onehot = (
        column.reshape(-1)[:, None] == jnp.arange(adapter_list * ADAPTER_RANK, dtype=i32)
    ).astype(bf16)

    a_send = dot(onehot, down_maps, 1, 1).astype(bf16).reshape(dp_size, picked, column_total)
    b_send = jnp.broadcast_to(up_maps[None], (dp_size,) + up_maps.shape)
    a_got = lax.all_to_all(a_send, "dp", 0, 0, tiled=True)
    b_got = lax.all_to_all(b_send, "dp", 0, 0, tiled=True)

    position = jnp.arange(tok_rows, dtype=i32)
    starts = lax.dynamic_index_in_dim(segment_start, my_rank, 0, keepdims=False)
    live = position < lax.dynamic_index_in_dim(token_count, my_rank, 0, keepdims=False)
    my_seg = jnp.sum((starts[None, :] <= position[:, None]).astype(i32), axis=1) - 1
    in_seg = my_seg[:, None] == (jnp.arange(picked, dtype=i32) // ADAPTER_RANK)[None, :]
    my_onehot = lax.dynamic_slice_in_dim(onehot, my_rank * picked, picked, 0)
    g = jnp.where(live[:, None], output_gradient, jnp.zeros_like(output_gradient))
    base = dot(g, frozen_weight, 1, 1)

    b_sel = dot(my_onehot, b_got.reshape(-1, out_width), 1, 0).astype(bf16)
    dlow = (adapter_scale * dot(g, b_sel, 1, 1)).astype(bf16)
    dlow = jnp.where(in_seg, dlow, jnp.zeros_like(dlow))
    a_sel = jnp.moveaxis(a_got, 0, 1).reshape(picked, -1)
    first = core_idx == 0
    x = jnp.concatenate(
        [jnp.where(first, inputs, x_other), jnp.where(first, x_other, inputs)], axis=0
    )
    low = dot(x, a_sel, 1, 1).astype(bf16)
    low = jnp.where(in_seg, low, jnp.zeros_like(low))
    low_wide = dot(low, my_onehot, 1, 0).astype(bf16)

    ga_send = dot(dlow, x, 0, 0).astype(bf16).reshape(picked, dp_size, column_total)
    ga_got = lax.all_to_all(jnp.moveaxis(ga_send, 1, 0), "dp", 0, 0, tiled=True)
    g_piece = lax.dynamic_slice_in_dim(g, core_idx * piece_out, piece_out, 1)
    up_send = (adapter_scale * dot(low_wide, g_piece, 0, 0)).astype(bf16)
    up_got = lax.all_to_all(up_send.reshape(dp_size, -1, piece_out), "dp", 0, 0, tiled=True)

    a_half = lax.dynamic_slice_in_dim(a_sel, core_idx * half, half, 1)
    grad_x = (base + dot(dlow, a_half, 1, 0)).astype(bf16)
    grad_a = dot(ga_got.reshape(dp_size * picked, column_total), onehot, 0, 0)
    up_map_gradient = jnp.sum(up_got.astype(f32), axis=0)
    return grad_x, grad_a, up_map_gradient


def local(*args):
    down_maps, up_maps = args[3], args[4]
    n, tp = lax.axis_size("dp"), lax.axis_size("tensor")
    out_width = up_maps.shape[1]
    kernels_fit = (
        n == 8
        and tp == 2
        and down_maps.shape[0] == out_width
        and down_maps.shape[1] == n * up_maps.shape[0]
        and out_width % (128 * tp) == 0
        and out_width == 4 * down_maps.shape[1]
        and args[1].shape[0] == 2 * args[0].shape[0] == down_maps.shape[1]
        and args[5].shape[1] * ADAPTER_RANK * n == 2 * down_maps.shape[1]
    )
    return (local_kernels if kernels_fit else local_plain)(*args)


def solution(mesh):
    in_specs = (
        P(("groups", "dp", "tensor"), None),
        P(("groups", "dp"), None),
        P("tensor", None),
        P(("groups", "dp"), None),
        P(("groups", "dp"), None),
        P("groups", None),
        P("groups", None),
        P("groups"),
        P("groups"),
    )
    out_specs = (
        P(("groups", "dp"), "tensor"),
        P(("groups", "dp"), None),
        P(("groups", "dp"), "tensor"),
    )
    return jax.shard_map(local, mesh=mesh, in_specs=in_specs, out_specs=out_specs, check_vma=False)
```

```python
import functools

import jax
import jax.numpy as jnp
from jax import lax
from jax.experimental import pallas as pl
from jax.experimental.pallas import tpu as pltpu
from jax.sharding import PartitionSpec as P

ADAPTER_RANK = 16
adapter_scale = 2.0

bf16, f32, i32 = jnp.bfloat16, jnp.float32, jnp.int32

HBM = pl.BlockSpec(memory_space=pltpu.HBM)
VMEM = pl.BlockSpec(memory_space=pltpu.VMEM)


def dot(a, b, ca, cb):
    return lax.dot_general(a, b, (((ca,), (cb,)), ((), ())), preferred_element_type=f32)


def params(mib):
    return pltpu.CompilerParams(vmem_limit_bytes=mib << 20)


def slot_rows(chosen_ref, slot_ref, ranks, width):
    lane = lax.broadcasted_iota(i32, (ADAPTER_RANK, width), 1)
    row = lax.broadcasted_iota(i32, (ADAPTER_RANK, width), 0)
    rows = []
    for rank in ranks:
        for k in range(chosen_ref.shape[0]):
            first = slot_ref[chosen_ref[k, rank]] * ADAPTER_RANK
            rows.append(jnp.where(lane == row + first, 1.0, 0.0))
    return jnp.concatenate(rows, axis=0).astype(bf16)


def start_all(sources, targets, sems, first=0):
    copies = [
        pltpu.make_async_copy(source, target, sems.at[first + k])
        for k, (source, target) in enumerate(zip(sources, targets))
    ]
    for copy in copies:
        copy.start()
    return copies


def wait_all(copies):
    for copy in copies:
        copy.wait()


def steps(n):
    return [(n - 1, n // 2 + 1), (3, n - 2), (2, n // 2), (1, 1)]


def partners(n, me, core):
    return [me] + [me ^ jnp.where(core == 0, a, b) for a, b in steps(n)]


def senders(n, me, core):
    passed = [me ^ jnp.where(core == 0, b, a) for a, b in steps(n) if a != b]
    return partners(n, me, core) + passed


def in_hbm(*arrays):
    return [pltpu.with_memory_space_constraint(array, pltpu.HBM) for array in arrays]


def pack_kernel(n, chosen_hbm, slot_hbm, down_hbm, up_hbm, *refs):
    count = n // 2 + 1
    send, (chosen_ref, slot_ref, down_ref, sems) = refs[:count], refs[count:]
    tables = start_all([chosen_hbm, slot_hbm], [chosen_ref, slot_ref], sems)
    maps = start_all([down_hbm], [down_ref], sems, 2)
    picked = chosen_ref.shape[0] * ADAPTER_RANK
    tail = pl.ds(picked, ADAPTER_RANK)
    ups = start_all([up_hbm] * count, [message.at[tail] for message in send], sems, 3)
    ranks = partners(n, lax.axis_index("dp"), lax.axis_index("tensor"))
    wait_all(tables)
    onehot = slot_rows(chosen_ref, slot_ref, ranks, down_ref.shape[1])
    wait_all(maps)
    columns = dot(onehot, down_ref[...], 1, 1).astype(bf16)
    for k in range(count):
        send[k][:picked, :] = columns[k * picked : (k + 1) * picked]
    wait_all(ups)


def stage_kernel(
    n, picked, start_hbm, chosen_hbm, slot_hbm, count_hbm, g_hbm, x_hbm, w_hbm,
    x_ref, kept_ref, start_ref, chosen_ref, slot_ref, count_ref, sems,
):
    rows, width = g_hbm.shape
    slots = width // 4
    me = lax.axis_index("dp")
    tables = start_all(
        [chosen_hbm, slot_hbm, start_hbm, count_hbm], [chosen_ref, slot_ref, start_ref, count_ref], sems
    )
    gradient = start_all([g_hbm], [kept_ref.at[pl.ds(0, rows)]], sems, 4)
    tokens = start_all([x_hbm], [x_ref], sems, 5)
    wait_all(tables)
    position = lax.broadcasted_iota(i32, (rows, slots), 0)
    group = lax.broadcasted_iota(i32, (rows, slots), 1) // ADAPTER_RANK
    segment = jnp.full((rows, slots), -1, i32)
    for k in range(start_ref.shape[0]):
        segment += jnp.where(position >= start_ref[k, me], 1, 0)
    kept_ref[rows:, :slots] = jnp.where(segment == group, 1.0, 0.0).astype(bf16)
    kept_ref[rows : rows + picked, slots : 2 * slots] = slot_rows(chosen_ref, slot_ref, [me], slots)
    every = slot_rows(chosen_ref, slot_ref, range(n), slots)
    kept_ref[rows:, 2 * slots : 3 * slots] = every[:rows]
    kept_ref[rows:, 3 * slots :] = every[rows:]
    wait_all(gradient)
    live = lax.broadcasted_iota(i32, (rows, width), 0) < count_ref[me]
    g = kept_ref[:rows, :]
    kept_ref[:rows, :] = jnp.where(live, g, jnp.zeros_like(g))
    wait_all(tokens)


def picked_maps(kept_ref, b_ref, picked, ranks, messages):
    rows, slots = kept_ref.shape[0] // 2, kept_ref.shape[1] // 4
    b_ref[...] = jnp.zeros(b_ref.shape, bf16)
    for rank, message in zip(ranks, messages):
        b_ref[rank] = message[picked:, :]
    onehot = kept_ref[rows : rows + picked, slots : 2 * slots]
    return dot(onehot, b_ref[...].reshape(-1, b_ref.shape[2]), 1, 0).astype(bf16)


def low_terms(x_ref, picked, ranks, messages):
    total = jnp.zeros((x_ref.shape[0], picked), f32)
    for rank, message in zip(ranks, messages):
        width = message.shape[1]
        at = pl.ds(pl.multiple_of(rank * width, width), width)
        total += dot(x_ref[:, at], message[:picked, :], 1, 1)
    return total


def early_kernel(n, picked, kept_ref, x_mine, x_other, *refs):
    count = n // 2 + 1
    here, (x_ref, low_ref, dlow_ref, b_ref) = refs[:count], refs[count:]
    me, core, half = lax.axis_index("dp"), lax.axis_index("tensor"), x_mine.shape[0]
    ranks = senders(n, me, core)[:count]
    x_ref[pl.ds(pl.multiple_of(core * half, half), half), :] = x_mine[...]
    x_ref[pl.ds(pl.multiple_of((1 - core) * half, half), half), :] = x_other[...]
    b_sel = picked_maps(kept_ref, b_ref, picked, ranks, here)
    dlow_ref[...] = dot(kept_ref[: 2 * half, :], b_sel, 1, 1)
    low_ref[...] = low_terms(x_ref, picked, ranks, here)


def middle_kernel(n, kept_ref, x_ref, low_ref, dlow_part, *refs):
    count = n // 2 + 1
    got, dlow_ref, send = refs[: n - count], refs[n - count], refs[n - count + 1 : n + 1]
    b_ref, up_ref = refs[n + 1 :]
    me, core = lax.axis_index("dp"), lax.axis_index("tensor")
    rows, picked = dlow_ref.shape
    width = kept_ref.shape[1]
    slots = width // 4
    ranks = senders(n, me, core)[count:]
    in_seg = kept_ref[rows:, :picked].astype(f32) > 0.0
    g = kept_ref[:rows, :]
    onehot = kept_ref[rows : rows + picked, slots : 2 * slots]
    b_sel = picked_maps(kept_ref, b_ref, picked, ranks, got)
    dlow = dlow_part[...] + dot(g, b_sel, 1, 1)
    dlow = jnp.where(in_seg, adapter_scale * dlow, 0.0).astype(bf16)
    dlow_ref[...] = dlow
    targets = partners(n, me, core)
    for target, message in zip(targets, send):
        at = pl.ds(pl.multiple_of(target * width, width), width)
        message[:picked, :] = dot(dlow, x_ref[:, at], 0, 0).astype(bf16)

    low = low_ref[...] + low_terms(x_ref, picked, ranks, got)
    low = jnp.where(in_seg, low, 0.0).astype(bf16)
    low_wide = dot(low, onehot, 1, 0).astype(bf16)
    up = (adapter_scale * dot(low_wide, g, 0, 0)).astype(bf16)
    up_ref[...] = up.reshape(up_ref.shape)
    for target, message in zip(targets, send):
        message[picked:, :] = up_ref[target]


def grad_x_kernel(n, kept_ref, w_ref, dlow_ref, *refs):
    got, (out_hbm, a_ref, out_ref, sems) = refs[:n], refs[n:]
    me, core = lax.axis_index("dp"), lax.axis_index("tensor")
    picked, width = a_ref.shape[1:]
    for sender, message in zip(senders(n, me, core), got):
        a_ref[sender] = message[:picked, :]
    g = kept_ref[: out_ref.shape[0], :]
    done = []
    for j in range(n // 2):
        at = pl.ds(j * width, width)
        total = dot(g, w_ref[at, :], 1, 1) + dot(dlow_ref[...], a_ref[core * (n // 2) + j], 1, 0)
        out_ref[:, at] = total.astype(bf16)
        done += start_all([out_ref.at[:, at]], [out_hbm.at[:, at]], sems, j)
    wait_all(done)


def final_kernel(n, kept_ref, *refs):
    got, (a_ref, up_ref, rows_ref) = refs[:n], refs[n:]
    me, core = lax.axis_index("dp"), lax.axis_index("tensor")
    piece, picked = up_ref.shape[1], rows_ref.shape[1] - ADAPTER_RANK
    half, slots = kept_ref.shape[0] // 2, kept_ref.shape[1] // 4
    for sender, message in zip(senders(n, me, core), got):
        rows_ref[sender] = message[...]
    rows = rows_ref[:, :picked, :].reshape(n * picked, rows_ref.shape[2])
    onehot = jnp.concatenate(
        [kept_ref[half:, 2 * slots : 3 * slots], kept_ref[half:, 3 * slots :]], axis=0
    )
    a_ref[...] = dot(rows, onehot, 0, 0)
    at = pl.ds(pl.multiple_of(core * piece, piece), piece)
    up_ref[...] = jnp.sum(rows_ref[:, picked:, at].astype(f32), axis=0)


def exchange(messages, tied, beside):
    n = 2 * len(messages)
    got = [
        lax.ppermute(
            message,
            ("dp", "tensor"),
            [(2 * i + c, 2 * (i ^ step[c]) + c) for i in range(n) for c in range(2)],
        )
        for message, step in zip(messages, steps(n))
    ]
    for k in tied:
        got[k], beside = lax.optimization_barrier((got[k], beside))
    passed = [
        lax.ppermute(message, "tensor", [(0, 1), (1, 0)])
        for message, (a, b) in zip(got, steps(n))
        if a != b
    ]
    return got + passed, beside


def local_kernels(
    inputs,
    output_gradient,
    frozen_weight,
    down_maps,
    up_maps,
    segment_start,
    segment_adapter,
    adapter_slot,
    token_count,
):
    model_width = inputs.shape[1]
    tok_rows, out_width = output_gradient.shape
    column_total, slot_width = down_maps.shape
    half = frozen_weight.shape[0]
    n = lax.axis_size("dp")
    piece = out_width // lax.axis_size("tensor")
    segs = segment_start.shape[1]
    picked = segs * ADAPTER_RANK
    shape = jax.ShapeDtypeStruct
    message = shape((picked + ADAPTER_RANK, column_total), bf16)
    count = n // 2 + 1
    starts, chosen = segment_start.T, segment_adapter.T

    tables = [
        pltpu.SMEM(starts.shape, i32),
        pltpu.SMEM(chosen.shape, i32),
        pltpu.SMEM(adapter_slot.shape, i32),
        pltpu.SMEM(token_count.shape, i32),
    ]
    dma = pltpu.SemaphoreType.DMA

    own, *sent = pl.pallas_call(
        functools.partial(pack_kernel, n),
        out_shape=[message] * count,
        in_specs=[HBM] * 4,
        out_specs=[VMEM] * count,
        scratch_shapes=tables[1:3]
        + [pltpu.VMEM(down_maps.shape, bf16), dma((3 + count,))],
        compiler_params=params(8),
    )(*in_hbm(chosen, adapter_slot, down_maps, up_maps))
    sent, x_late = lax.optimization_barrier((sent, inputs))
    x_other = lax.ppermute(x_late, "tensor", [(0, 1), (1, 0)])
    x_mine, kept = pl.pallas_call(
        functools.partial(stage_kernel, n, picked),
        out_shape=[shape(inputs.shape, bf16), shape((2 * tok_rows, out_width), bf16)],
        in_specs=[HBM] * 7,
        out_specs=[VMEM] * 2,
        scratch_shapes=tables + [dma((6,))],
        compiler_params=params(8),
        cost_estimate=pl.CostEstimate(flops=0, bytes_accessed=1 << 21, transcendentals=0),
    )(*in_hbm(starts, chosen, adapter_slot, token_count, output_gradient, inputs, frozen_weight))
    got, x_mine = exchange(sent, (0,), x_mine)
    low = shape((tok_rows, picked), f32)
    maps = pltpu.VMEM((n, ADAPTER_RANK, out_width), bf16)
    got = [own] + got
    x, low, dlow = pl.pallas_call(
        functools.partial(early_kernel, n, picked),
        out_shape=[shape((tok_rows, model_width), bf16), low, low],
        in_specs=[VMEM] * (3 + count),
        out_specs=[VMEM] * 3,
        scratch_shapes=[maps],
        compiler_params=params(8),
        cost_estimate=pl.CostEstimate(flops=0, bytes_accessed=1 << 21, transcendentals=0),
    )(kept, x_mine, x_other, *got[:count])

    dlow, *sent = pl.pallas_call(
        functools.partial(middle_kernel, n),
        out_shape=[shape((tok_rows, picked), bf16)] + [message] * count,
        in_specs=[VMEM] * (4 + n - count),
        out_specs=[VMEM] * (1 + count),
        scratch_shapes=[maps, maps],
        compiler_params=params(8),
    )(kept, x, low, dlow, *got[count:])
    own, *sent = sent

    grad_x = pl.pallas_call(
        functools.partial(grad_x_kernel, n),
        out_shape=shape((tok_rows, half), bf16),
        in_specs=[VMEM] * (3 + n),
        out_specs=HBM,
        scratch_shapes=[
            pltpu.VMEM((n, picked, column_total), bf16),
            pltpu.VMEM((tok_rows, half), bf16),
            dma((n // 2,)),
        ],
        compiler_params=params(8),
        cost_estimate=pl.CostEstimate(
            flops=2 * tok_rows * half * (out_width + picked),
            bytes_accessed=2 * half * (out_width + tok_rows),
            transcendentals=0,
        ),
    )(kept, frozen_weight, dlow, *got)

    got, grad_x = exchange(sent, (0,), grad_x)

    grad_a, up_map_gradient = pl.pallas_call(
        functools.partial(final_kernel, n),
        out_shape=[shape((column_total, slot_width), f32), shape((ADAPTER_RANK, piece), f32)],
        in_specs=[VMEM] * (1 + n),
        out_specs=[VMEM, VMEM],
        scratch_shapes=[pltpu.VMEM((n,) + message.shape, bf16)],
        compiler_params=params(8),
    )(kept, own, *got)
    return grad_x, grad_a, up_map_gradient


def local_plain(
    inputs,
    output_gradient,
    frozen_weight,
    down_maps,
    up_maps,
    segment_start,
    segment_adapter,
    adapter_slot,
    token_count,
):
    tok_rows, out_width = output_gradient.shape
    column_total = down_maps.shape[0]
    adapter_list = adapter_slot.shape[0]
    segs = segment_start.shape[1]
    dp_size = lax.axis_size("dp")
    my_rank = lax.axis_index("dp")
    core_idx = lax.axis_index("tensor")
    picked = segs * ADAPTER_RANK
    piece_out = out_width // lax.axis_size("tensor")
    half = frozen_weight.shape[0]

    x_other = lax.ppermute(inputs, "tensor", [(0, 1), (1, 0)])
    adapter_ids = jnp.arange(adapter_list, dtype=i32)
    slot_table = jnp.sum(
        jnp.where(segment_adapter[..., None] == adapter_ids, adapter_slot, 0), axis=-1
    )
    column = slot_table[:, :, None] * ADAPTER_RANK + jnp.arange(ADAPTER_RANK, dtype=i32)
    onehot = (
        column.reshape(-1)[:, None] == jnp.arange(adapter_list * ADAPTER_RANK, dtype=i32)
    ).astype(bf16)

    a_send = dot(onehot, down_maps, 1, 1).astype(bf16).reshape(dp_size, picked, column_total)
    b_send = jnp.broadcast_to(up_maps[None], (dp_size,) + up_maps.shape)
    a_got = lax.all_to_all(a_send, "dp", 0, 0, tiled=True)
    b_got = lax.all_to_all(b_send, "dp", 0, 0, tiled=True)

    position = jnp.arange(tok_rows, dtype=i32)
    starts = lax.dynamic_index_in_dim(segment_start, my_rank, 0, keepdims=False)
    live = position < lax.dynamic_index_in_dim(token_count, my_rank, 0, keepdims=False)
    my_seg = jnp.sum((starts[None, :] <= position[:, None]).astype(i32), axis=1) - 1
    in_seg = my_seg[:, None] == (jnp.arange(picked, dtype=i32) // ADAPTER_RANK)[None, :]
    my_onehot = lax.dynamic_slice_in_dim(onehot, my_rank * picked, picked, 0)
    g = jnp.where(live[:, None], output_gradient, jnp.zeros_like(output_gradient))
    base = dot(g, frozen_weight, 1, 1)

    b_sel = dot(my_onehot, b_got.reshape(-1, out_width), 1, 0).astype(bf16)
    dlow = (adapter_scale * dot(g, b_sel, 1, 1)).astype(bf16)
    dlow = jnp.where(in_seg, dlow, jnp.zeros_like(dlow))
    a_sel = jnp.moveaxis(a_got, 0, 1).reshape(picked, -1)
    first = core_idx == 0
    x = jnp.concatenate(
        [jnp.where(first, inputs, x_other), jnp.where(first, x_other, inputs)], axis=0
    )
    low = dot(x, a_sel, 1, 1).astype(bf16)
    low = jnp.where(in_seg, low, jnp.zeros_like(low))
    low_wide = dot(low, my_onehot, 1, 0).astype(bf16)

    ga_send = dot(dlow, x, 0, 0).astype(bf16).reshape(picked, dp_size, column_total)
    ga_got = lax.all_to_all(jnp.moveaxis(ga_send, 1, 0), "dp", 0, 0, tiled=True)
    g_piece = lax.dynamic_slice_in_dim(g, core_idx * piece_out, piece_out, 1)
    up_send = (adapter_scale * dot(low_wide, g_piece, 0, 0)).astype(bf16)
    up_got = lax.all_to_all(up_send.reshape(dp_size, -1, piece_out), "dp", 0, 0, tiled=True)

    a_half = lax.dynamic_slice_in_dim(a_sel, core_idx * half, half, 1)
    grad_x = (base + dot(dlow, a_half, 1, 0)).astype(bf16)
    grad_a = dot(ga_got.reshape(dp_size * picked, column_total), onehot, 0, 0)
    up_map_gradient = jnp.sum(up_got.astype(f32), axis=0)
    return grad_x, grad_a, up_map_gradient


def local(*args):
    down_maps, up_maps = args[3], args[4]
    n, tp = lax.axis_size("dp"), lax.axis_size("tensor")
    out_width = up_maps.shape[1]
    kernels_fit = (
        n == 8
        and tp == 2
        and down_maps.shape[0] == out_width
        and down_maps.shape[1] == n * up_maps.shape[0]
        and out_width % (128 * tp) == 0
        and out_width == 4 * down_maps.shape[1]
        and args[1].shape[0] == 2 * args[0].shape[0] == down_maps.shape[1]
        and args[5].shape[1] * ADAPTER_RANK * n == 2 * down_maps.shape[1]
    )
    return (local_kernels if kernels_fit else local_plain)(*args)


def solution(mesh):
    in_specs = (
        P(("groups", "dp", "tensor"), None),
        P(("groups", "dp"), None),
        P("tensor", None),
        P(("groups", "dp"), None),
        P(("groups", "dp"), None),
        P("groups", None),
        P("groups", None),
        P("groups"),
        P("groups"),
    )
    out_specs = (
        P(("groups", "dp"), "tensor"),
        P(("groups", "dp"), None),
        P(("groups", "dp"), "tensor"),
    )
    return jax.shard_map(local, mesh=mesh, in_specs=in_specs, out_specs=out_specs, check_vma=False)
```

```python
import functools

import jax
import jax.numpy as jnp
from jax import lax
from jax.experimental import pallas as pl
from jax.experimental.pallas import tpu as pltpu
from jax.sharding import PartitionSpec as P

ADAPTER_RANK = 16
adapter_scale = 2.0

bf16, f32, i32 = jnp.bfloat16, jnp.float32, jnp.int32

HBM = pl.BlockSpec(memory_space=pltpu.HBM)
VMEM = pl.BlockSpec(memory_space=pltpu.VMEM)


def dot(a, b, ca, cb):
    return lax.dot_general(a, b, (((ca,), (cb,)), ((), ())), preferred_element_type=f32)


def params(mib):
    return pltpu.CompilerParams(vmem_limit_bytes=mib << 20)


def slot_rows(chosen_ref, slot_ref, ranks, width):
    lane = lax.broadcasted_iota(i32, (ADAPTER_RANK, width), 1)
    row = lax.broadcasted_iota(i32, (ADAPTER_RANK, width), 0)
    rows = []
    for rank in ranks:
        for k in range(chosen_ref.shape[0]):
            first = slot_ref[chosen_ref[k, rank]] * ADAPTER_RANK
            rows.append(jnp.where(lane == row + first, 1.0, 0.0))
    return jnp.concatenate(rows, axis=0).astype(bf16)


def start_all(sources, targets, sems, first=0):
    copies = [
        pltpu.make_async_copy(source, target, sems.at[first + k])
        for k, (source, target) in enumerate(zip(sources, targets))
    ]
    for copy in copies:
        copy.start()
    return copies


def wait_all(copies):
    for copy in copies:
        copy.wait()


def steps(n):
    return [(n - 1, n // 2 + 1), (3, n - 2), (2, n // 2), (1, 1)]


def partners(n, me, core):
    return [me] + [me ^ jnp.where(core == 0, a, b) for a, b in steps(n)]


def senders(n, me, core):
    passed = [me ^ jnp.where(core == 0, b, a) for a, b in steps(n) if a != b]
    return partners(n, me, core) + passed


def in_hbm(*arrays):
    return [pltpu.with_memory_space_constraint(array, pltpu.HBM) for array in arrays]


def pack_kernel(n, chosen_hbm, slot_hbm, down_hbm, up_hbm, *refs):
    count = n // 2 + 1
    send, (chosen_ref, slot_ref, down_ref, up_ref, sems) = refs[:count], refs[count:]
    maps = start_all([down_hbm, up_hbm], [down_ref, up_ref], sems, 2)
    tables = start_all([chosen_hbm, slot_hbm], [chosen_ref, slot_ref], sems)
    ranks = partners(n, lax.axis_index("dp"), lax.axis_index("tensor"))
    wait_all(tables)
    onehot = slot_rows(chosen_ref, slot_ref, ranks, down_ref.shape[1])
    picked = onehot.shape[0] // count
    wait_all(maps)
    columns = dot(onehot, down_ref[...], 1, 1).astype(bf16)
    for k in range(count):
        send[k][:picked, :] = columns[k * picked : (k + 1) * picked]
        send[k][picked:, :] = up_ref[...]


def stage_kernel(
    n, picked, start_hbm, chosen_hbm, slot_hbm, count_hbm, g_hbm, x_hbm, w_hbm,
    x_ref, kept_ref, start_ref, chosen_ref, slot_ref, count_ref, sems,
):
    rows, width = g_hbm.shape
    slots = width // 4
    me = lax.axis_index("dp")
    tables = start_all(
        [chosen_hbm, slot_hbm, start_hbm, count_hbm], [chosen_ref, slot_ref, start_ref, count_ref], sems
    )
    gradient = start_all([g_hbm], [kept_ref.at[pl.ds(0, rows)]], sems, 4)
    tokens = start_all([x_hbm], [x_ref], sems, 5)
    wait_all(tables)
    position = lax.broadcasted_iota(i32, (rows, slots), 0)
    group = lax.broadcasted_iota(i32, (rows, slots), 1) // ADAPTER_RANK
    segment = jnp.full((rows, slots), -1, i32)
    for k in range(start_ref.shape[0]):
        segment += jnp.where(position >= start_ref[k, me], 1, 0)
    kept_ref[rows:, :slots] = jnp.where(segment == group, 1.0, 0.0).astype(bf16)
    kept_ref[rows : rows + picked, slots : 2 * slots] = slot_rows(chosen_ref, slot_ref, [me], slots)
    every = slot_rows(chosen_ref, slot_ref, range(n), slots)
    kept_ref[rows:, 2 * slots : 3 * slots] = every[:rows]
    kept_ref[rows:, 3 * slots :] = every[rows:]
    wait_all(gradient)
    live = lax.broadcasted_iota(i32, (rows, width), 0) < count_ref[me]
    g = kept_ref[:rows, :]
    kept_ref[:rows, :] = jnp.where(live, g, jnp.zeros_like(g))
    wait_all(tokens)


def picked_maps(kept_ref, b_ref, picked, ranks, messages):
    rows, slots = kept_ref.shape[0] // 2, kept_ref.shape[1] // 4
    b_ref[...] = jnp.zeros(b_ref.shape, bf16)
    for rank, message in zip(ranks, messages):
        b_ref[rank] = message[picked:, :]
    onehot = kept_ref[rows : rows + picked, slots : 2 * slots]
    return dot(onehot, b_ref[...].reshape(-1, b_ref.shape[2]), 1, 0).astype(bf16)


def low_terms(x_ref, picked, ranks, messages):
    total = jnp.zeros((x_ref.shape[0], picked), f32)
    for rank, message in zip(ranks, messages):
        width = message.shape[1]
        at = pl.ds(pl.multiple_of(rank * width, width), width)
        total += dot(x_ref[:, at], message[:picked, :], 1, 1)
    return total


def early_kernel(n, picked, kept_ref, x_mine, x_other, *refs):
    count = n // 2 + 1
    here, (x_ref, low_ref, dlow_ref, b_ref) = refs[:count], refs[count:]
    me, core, half = lax.axis_index("dp"), lax.axis_index("tensor"), x_mine.shape[0]
    ranks = senders(n, me, core)[:count]
    x_ref[pl.ds(pl.multiple_of(core * half, half), half), :] = x_mine[...]
    x_ref[pl.ds(pl.multiple_of((1 - core) * half, half), half), :] = x_other[...]
    b_sel = picked_maps(kept_ref, b_ref, picked, ranks, here)
    dlow_ref[...] = dot(kept_ref[: 2 * half, :], b_sel, 1, 1)
    low_ref[...] = low_terms(x_ref, picked, ranks, here)


def middle_kernel(n, kept_ref, x_ref, low_ref, dlow_part, *refs):
    count = n // 2 + 1
    got, dlow_ref, send = refs[: n - count], refs[n - count], refs[n - count + 1 : n + 1]
    b_ref, up_ref = refs[n + 1 :]
    me, core = lax.axis_index("dp"), lax.axis_index("tensor")
    rows, picked = dlow_ref.shape
    width = kept_ref.shape[1]
    slots = width // 4
    ranks = senders(n, me, core)[count:]
    in_seg = kept_ref[rows:, :picked].astype(f32) > 0.0
    g = kept_ref[:rows, :]
    onehot = kept_ref[rows : rows + picked, slots : 2 * slots]
    b_sel = picked_maps(kept_ref, b_ref, picked, ranks, got)
    dlow = dlow_part[...] + dot(g, b_sel, 1, 1)
    dlow = jnp.where(in_seg, adapter_scale * dlow, 0.0).astype(bf16)
    dlow_ref[...] = dlow
    targets = partners(n, me, core)
    for target, message in zip(targets, send):
        at = pl.ds(pl.multiple_of(target * width, width), width)
        message[:picked, :] = dot(dlow, x_ref[:, at], 0, 0).astype(bf16)

    low = low_ref[...] + low_terms(x_ref, picked, ranks, got)
    low = jnp.where(in_seg, low, 0.0).astype(bf16)
    low_wide = dot(low, onehot, 1, 0).astype(bf16)
    up = (adapter_scale * dot(low_wide, g, 0, 0)).astype(bf16)
    up_ref[...] = up.reshape(up_ref.shape)
    for target, message in zip(targets, send):
        message[picked:, :] = up_ref[target]


def grad_x_kernel(n, kept_ref, w_ref, dlow_ref, *refs):
    got, (out_hbm, a_ref, out_ref, sems) = refs[:n], refs[n:]
    me, core = lax.axis_index("dp"), lax.axis_index("tensor")
    picked, width = a_ref.shape[1:]
    for sender, message in zip(senders(n, me, core), got):
        a_ref[sender] = message[:picked, :]
    g = kept_ref[: out_ref.shape[0], :]
    done = []
    for j in range(n // 2):
        at = pl.ds(j * width, width)
        total = dot(g, w_ref[at, :], 1, 1) + dot(dlow_ref[...], a_ref[core * (n // 2) + j], 1, 0)
        out_ref[:, at] = total.astype(bf16)
        done += start_all([out_ref.at[:, at]], [out_hbm.at[:, at]], sems, j)
    wait_all(done)


def final_kernel(n, kept_ref, *refs):
    got, (a_ref, up_ref, rows_ref) = refs[:n], refs[n:]
    me, core = lax.axis_index("dp"), lax.axis_index("tensor")
    piece, picked = up_ref.shape[1], rows_ref.shape[1] - ADAPTER_RANK
    half, slots = kept_ref.shape[0] // 2, kept_ref.shape[1] // 4
    for sender, message in zip(senders(n, me, core), got):
        rows_ref[sender] = message[...]
    rows = rows_ref[:, :picked, :].reshape(n * picked, rows_ref.shape[2])
    onehot = jnp.concatenate(
        [kept_ref[half:, 2 * slots : 3 * slots], kept_ref[half:, 3 * slots :]], axis=0
    )
    a_ref[...] = dot(rows, onehot, 0, 0)
    at = pl.ds(pl.multiple_of(core * piece, piece), piece)
    up_ref[...] = jnp.sum(rows_ref[:, picked:, at].astype(f32), axis=0)


def exchange(messages, tied, beside):
    n = 2 * len(messages)
    got = [
        lax.ppermute(
            message,
            ("dp", "tensor"),
            [(2 * i + c, 2 * (i ^ step[c]) + c) for i in range(n) for c in range(2)],
        )
        for message, step in zip(messages, steps(n))
    ]
    for k in tied:
        got[k], beside = lax.optimization_barrier((got[k], beside))
    passed = [
        lax.ppermute(message, "tensor", [(0, 1), (1, 0)])
        for message, (a, b) in zip(got, steps(n))
        if a != b
    ]
    return got + passed, beside


def local_kernels(
    inputs,
    output_gradient,
    frozen_weight,
    down_maps,
    up_maps,
    segment_start,
    segment_adapter,
    adapter_slot,
    token_count,
):
    model_width = inputs.shape[1]
    tok_rows, out_width = output_gradient.shape
    column_total, slot_width = down_maps.shape
    half = frozen_weight.shape[0]
    n = lax.axis_size("dp")
    piece = out_width // lax.axis_size("tensor")
    segs = segment_start.shape[1]
    picked = segs * ADAPTER_RANK
    shape = jax.ShapeDtypeStruct
    message = shape((picked + ADAPTER_RANK, column_total), bf16)
    count = n // 2 + 1
    starts, chosen = segment_start.T, segment_adapter.T

    tables = [
        pltpu.SMEM(starts.shape, i32),
        pltpu.SMEM(chosen.shape, i32),
        pltpu.SMEM(adapter_slot.shape, i32),
        pltpu.SMEM(token_count.shape, i32),
    ]
    dma = pltpu.SemaphoreType.DMA

    own, *sent = pl.pallas_call(
        functools.partial(pack_kernel, n),
        out_shape=[message] * count,
        in_specs=[HBM] * 4,
        out_specs=[VMEM] * count,
        scratch_shapes=tables[1:3]
        + [pltpu.VMEM(down_maps.shape, bf16), pltpu.VMEM(up_maps.shape, bf16), dma((4,))],
        compiler_params=params(8),
    )(*in_hbm(chosen, adapter_slot, down_maps, up_maps))
    sent, x_late = lax.optimization_barrier((sent, inputs))
    x_other = lax.ppermute(x_late, "tensor", [(0, 1), (1, 0)])
    x_mine, kept = pl.pallas_call(
        functools.partial(stage_kernel, n, picked),
        out_shape=[shape(inputs.shape, bf16), shape((2 * tok_rows, out_width), bf16)],
        in_specs=[HBM] * 7,
        out_specs=[VMEM] * 2,
        scratch_shapes=tables + [dma((6,))],
        compiler_params=params(8),
        cost_estimate=pl.CostEstimate(flops=0, bytes_accessed=1 << 21, transcendentals=0),
    )(*in_hbm(starts, chosen, adapter_slot, token_count, output_gradient, inputs, frozen_weight))
    got, x_mine = exchange(sent, (0,), x_mine)
    low = shape((tok_rows, picked), f32)
    maps = pltpu.VMEM((n, ADAPTER_RANK, out_width), bf16)
    got = [own] + got
    x, low, dlow = pl.pallas_call(
        functools.partial(early_kernel, n, picked),
        out_shape=[shape((tok_rows, model_width), bf16), low, low],
        in_specs=[VMEM] * (3 + count),
        out_specs=[VMEM] * 3,
        scratch_shapes=[maps],
        compiler_params=params(8),
        cost_estimate=pl.CostEstimate(flops=0, bytes_accessed=1 << 21, transcendentals=0),
    )(kept, x_mine, x_other, *got[:count])

    dlow, *sent = pl.pallas_call(
        functools.partial(middle_kernel, n),
        out_shape=[shape((tok_rows, picked), bf16)] + [message] * count,
        in_specs=[VMEM] * (4 + n - count),
        out_specs=[VMEM] * (1 + count),
        scratch_shapes=[maps, maps],
        compiler_params=params(8),
    )(kept, x, low, dlow, *got[count:])
    own, *sent = sent

    grad_x = pl.pallas_call(
        functools.partial(grad_x_kernel, n),
        out_shape=shape((tok_rows, half), bf16),
        in_specs=[VMEM] * (3 + n),
        out_specs=HBM,
        scratch_shapes=[
            pltpu.VMEM((n, picked, column_total), bf16),
            pltpu.VMEM((tok_rows, half), bf16),
            dma((n // 2,)),
        ],
        compiler_params=params(8),
        cost_estimate=pl.CostEstimate(
            flops=2 * tok_rows * half * (out_width + picked),
            bytes_accessed=2 * half * (out_width + tok_rows),
            transcendentals=0,
        ),
    )(kept, frozen_weight, dlow, *got)

    got, grad_x = exchange(sent, (0,), grad_x)

    grad_a, up_map_gradient = pl.pallas_call(
        functools.partial(final_kernel, n),
        out_shape=[shape((column_total, slot_width), f32), shape((ADAPTER_RANK, piece), f32)],
        in_specs=[VMEM] * (1 + n),
        out_specs=[VMEM, VMEM],
        scratch_shapes=[pltpu.VMEM((n,) + message.shape, bf16)],
        compiler_params=params(8),
    )(kept, own, *got)
    return grad_x, grad_a, up_map_gradient


def local_plain(
    inputs,
    output_gradient,
    frozen_weight,
    down_maps,
    up_maps,
    segment_start,
    segment_adapter,
    adapter_slot,
    token_count,
):
    tok_rows, out_width = output_gradient.shape
    column_total = down_maps.shape[0]
    adapter_list = adapter_slot.shape[0]
    segs = segment_start.shape[1]
    dp_size = lax.axis_size("dp")
    my_rank = lax.axis_index("dp")
    core_idx = lax.axis_index("tensor")
    picked = segs * ADAPTER_RANK
    piece_out = out_width // lax.axis_size("tensor")
    half = frozen_weight.shape[0]

    x_other = lax.ppermute(inputs, "tensor", [(0, 1), (1, 0)])
    adapter_ids = jnp.arange(adapter_list, dtype=i32)
    slot_table = jnp.sum(
        jnp.where(segment_adapter[..., None] == adapter_ids, adapter_slot, 0), axis=-1
    )
    column = slot_table[:, :, None] * ADAPTER_RANK + jnp.arange(ADAPTER_RANK, dtype=i32)
    onehot = (
        column.reshape(-1)[:, None] == jnp.arange(adapter_list * ADAPTER_RANK, dtype=i32)
    ).astype(bf16)

    a_send = dot(onehot, down_maps, 1, 1).astype(bf16).reshape(dp_size, picked, column_total)
    b_send = jnp.broadcast_to(up_maps[None], (dp_size,) + up_maps.shape)
    a_got = lax.all_to_all(a_send, "dp", 0, 0, tiled=True)
    b_got = lax.all_to_all(b_send, "dp", 0, 0, tiled=True)

    position = jnp.arange(tok_rows, dtype=i32)
    starts = lax.dynamic_index_in_dim(segment_start, my_rank, 0, keepdims=False)
    live = position < lax.dynamic_index_in_dim(token_count, my_rank, 0, keepdims=False)
    my_seg = jnp.sum((starts[None, :] <= position[:, None]).astype(i32), axis=1) - 1
    in_seg = my_seg[:, None] == (jnp.arange(picked, dtype=i32) // ADAPTER_RANK)[None, :]
    my_onehot = lax.dynamic_slice_in_dim(onehot, my_rank * picked, picked, 0)
    g = jnp.where(live[:, None], output_gradient, jnp.zeros_like(output_gradient))
    base = dot(g, frozen_weight, 1, 1)

    b_sel = dot(my_onehot, b_got.reshape(-1, out_width), 1, 0).astype(bf16)
    dlow = (adapter_scale * dot(g, b_sel, 1, 1)).astype(bf16)
    dlow = jnp.where(in_seg, dlow, jnp.zeros_like(dlow))
    a_sel = jnp.moveaxis(a_got, 0, 1).reshape(picked, -1)
    first = core_idx == 0
    x = jnp.concatenate(
        [jnp.where(first, inputs, x_other), jnp.where(first, x_other, inputs)], axis=0
    )
    low = dot(x, a_sel, 1, 1).astype(bf16)
    low = jnp.where(in_seg, low, jnp.zeros_like(low))
    low_wide = dot(low, my_onehot, 1, 0).astype(bf16)

    ga_send = dot(dlow, x, 0, 0).astype(bf16).reshape(picked, dp_size, column_total)
    ga_got = lax.all_to_all(jnp.moveaxis(ga_send, 1, 0), "dp", 0, 0, tiled=True)
    g_piece = lax.dynamic_slice_in_dim(g, core_idx * piece_out, piece_out, 1)
    up_send = (adapter_scale * dot(low_wide, g_piece, 0, 0)).astype(bf16)
    up_got = lax.all_to_all(up_send.reshape(dp_size, -1, piece_out), "dp", 0, 0, tiled=True)

    a_half = lax.dynamic_slice_in_dim(a_sel, core_idx * half, half, 1)
    grad_x = (base + dot(dlow, a_half, 1, 0)).astype(bf16)
    grad_a = dot(ga_got.reshape(dp_size * picked, column_total), onehot, 0, 0)
    up_map_gradient = jnp.sum(up_got.astype(f32), axis=0)
    return grad_x, grad_a, up_map_gradient


def local(*args):
    down_maps, up_maps = args[3], args[4]
    n, tp = lax.axis_size("dp"), lax.axis_size("tensor")
    out_width = up_maps.shape[1]
    kernels_fit = (
        n == 8
        and tp == 2
        and down_maps.shape[0] == out_width
        and down_maps.shape[1] == n * up_maps.shape[0]
        and out_width % (128 * tp) == 0
        and out_width == 4 * down_maps.shape[1]
        and args[1].shape[0] == 2 * args[0].shape[0] == down_maps.shape[1]
        and args[5].shape[1] * ADAPTER_RANK * n == 2 * down_maps.shape[1]
    )
    return (local_kernels if kernels_fit else local_plain)(*args)


def solution(mesh):
    in_specs = (
        P(("groups", "dp", "tensor"), None),
        P(("groups", "dp"), None),
        P("tensor", None),
        P(("groups", "dp"), None),
        P(("groups", "dp"), None),
        P("groups", None),
        P("groups", None),
        P("groups"),
        P("groups"),
    )
    out_specs = (
        P(("groups", "dp"), "tensor"),
        P(("groups", "dp"), None),
        P(("groups", "dp"), "tensor"),
    )
    return jax.shard_map(local, mesh=mesh, in_specs=in_specs, out_specs=out_specs, check_vma=False)
```
